32 devices in a mesh: row: 4 (over z), blk: 8 (over y, x, core).
Axes of the slice: x: 2, y: 2, z: 4, core: 2. Of those that a mesh axis runs over, the one named last changes fastest.
Arguments:
- tokens: bfloat16 [16, 1024, 768], P('row', 'blk'), may hold values from -6 to 6
- lengths: int32 [16, 8], P('row'), may hold values from 20 to 884, as said below
- norm_gain: bfloat16 [768], P('blk'), may hold values from 0.5 to 1.5
- qkv_weight: bfloat16 [768, 2304], P('blk', 'row'), may hold values from -0.21875 to 0.21875
- out_weight: bfloat16 [768, 768], P('blk', 'row'), may hold values from -6 to 6
- mlp_gain: bfloat16 [768], P('blk'), may hold values from 0.5 to 1.5
- in_weight: bfloat16 [768, 2304], P('blk', 'row'), may hold values from -0.21875 to 0.21875
- down_weight: bfloat16 [1152, 768], P('blk', 'row'), may hold values from -0.1875 to 0.1875
- cotangent: bfloat16 [16, 1024, 768], P('row', 'blk'), may hold values from -6 to 6
Outputs:
- output: bfloat16 [16, 1024, 768], P('row', 'blk')
- input_grad: bfloat16 [16, 1024, 768], P('row', 'blk')
- norm_gain_grad: float32 [768], P('blk')
- qkv_grad: float32 [768, 2304], P('blk', 'row')
- out_grad: float32 [768, 768], P('blk', 'row')
- mlp_gain_grad: float32 [768], P('blk')
- in_grad: float32 [768, 2304], P('blk', 'row')
- down_grad: float32 [1152, 768], P('blk', 'row')
The draws below stay inside these ranges and needn't reach their ends.
Inputs may be any that keep to these rules, and one draw needn't show every extreme that they name: Each packed row holds 8 positive document lengths that sum to 1024.
All inputs are finite; a program needn't handle non-finite values.
Results may differ from the reference program's by a relative error of at most 0.03.
Values may be sent and summed in bfloat16 or wider, within the bound.
No kernel may reach another device: no remote copies, remote signals or barrier semaphores. Data moves between devices by JAX's collectives and lax.ppermute only.
A program may use at most 256 MiB of HBM per device.

```python
import math
import jax
import jax.numpy as jnp
from jax import lax

D = 768
HEADS = 12
HD = 64
FF = 1152
TOK_DEV = 128
ROWS_DEV = 4
NDOC = 8
SEQ = 1024
ROWS = 16


def draw_lengths(key, part):
    key = jax.random.fold_in(key, 11)
    short_key, place_key, edge_key, pick_key = jax.random.split(key, 4)
    least = min(20, SEQ // (2 * NDOC))
    shorts = jax.random.randint(short_key, (ROWS, NDOC), least, SEQ // NDOC, dtype=jnp.int32)
    placed = jax.random.randint(place_key, (ROWS, 1), 0, NDOC, dtype=jnp.int32)
    chosen = jnp.arange(NDOC, dtype=jnp.int32)[None, :] == placed
    others = jnp.sum(jnp.where(chosen, 0, shorts), axis=1, keepdims=True)
    spread_row = jnp.where(chosen, SEQ - others, shorts)
    front = NDOC // 2
    edge_most = (TOK_DEV - 1) // front
    edge_least = min(20, edge_most)
    edges = jax.random.randint(edge_key, (ROWS, NDOC), edge_least, edge_most + 1, dtype=jnp.int32)
    first_group = jnp.arange(ROWS, dtype=jnp.int32) // ROWS_DEV == 0
    edges = jnp.where(first_group[:, None], edge_least, edges)
    middle = jnp.arange(NDOC, dtype=jnp.int32)[None, :] == front
    edge_total = jnp.sum(jnp.where(middle, 0, edges), axis=1, keepdims=True)
    span_row = jnp.where(middle, SEQ - edge_total, edges)
    picked = jax.random.randint(pick_key, (ROWS // ROWS_DEV,), 0, ROWS_DEV, dtype=jnp.int32)
    spanning = jnp.arange(ROWS, dtype=jnp.int32) % ROWS_DEV == jnp.repeat(picked, ROWS_DEV)
    return jnp.where(spanning[:, None], span_row, spread_row).astype(jnp.int32)


def steps_of(rng, dims, shards, low, high):
    factor_of, own = 1.0, jax.random.fold_in(rng, 6)
    for dim, parts in shards:
        steps = jnp.exp(jax.random.uniform(jax.random.fold_in(own, dim), (parts,), jnp.float32, low / len(shards), high / len(shards)))
        factor_of = factor_of * jnp.repeat(steps, dims[dim] // parts).reshape([-1 if axis == dim else 1 for axis in range(len(dims))])
    return factor_of


def noise(stream_key, extent, width, limit, cuts=(), kind=jnp.bfloat16):
    drawn = jax.random.normal(stream_key, extent, jnp.float32) * width
    if len(cuts) > 0:
        drawn = steps_of(stream_key, extent, cuts, -0.22, 0.18) * drawn
    return jnp.clip(drawn, min=-limit, max=limit).astype(kind)


def setup_inputs(seed: int = 0) -> dict:
    arg_keys = jax.random.split(jax.random.key(seed), 10)
    return {
        "tokens": noise(arg_keys[0], (ROWS, SEQ, D), 1.0, 6.0, ((0, 4), (1, 8))),
        "lengths": draw_lengths(jax.random.fold_in(arg_keys[9], 71), 0),
        "norm_gain": jnp.clip(1.0 + 0.1 * jax.random.normal(arg_keys[2], (D,), jnp.float32), 0.5, 1.5).astype(jnp.bfloat16),
        "qkv_weight": noise(arg_keys[3], (D, 3 * D), D ** -0.5, 0.21875, ((0, 8), (1, 4))),
        "out_weight": noise(arg_keys[4], (D, D), 1.0, 6.0, ((0, 8), (1, 4))),
        "mlp_gain": jnp.clip(1.0 + 0.1 * jax.random.normal(arg_keys[5], (D,), jnp.float32), 0.5, 1.5).astype(jnp.bfloat16),
        "in_weight": noise(arg_keys[6], (D, 2 * FF), D ** -0.5, 0.21875, ((0, 8), (1, 4))),
        "down_weight": noise(arg_keys[7], (FF, D), FF ** -0.5, 0.1875, ((0, 8), (1, 4))),
        "cotangent": noise(arg_keys[8], (ROWS, SEQ, D), 1.0, 6.0, ((0, 4), (1, 8))),
    }


ROPE_BASE = 160000.0
NORM_EPSILON = 1e-05
MASKED = -1e+30
HIGH = lax.Precision.HIGHEST

@jax.custom_vjp
def low(v):
    return lax.optimization_barrier(v.astype(jnp.bfloat16)).astype(jnp.float32)

@jax.custom_vjp
def low_back(v):
    return v

def low_keep(v):
    return (low(v), None)

def low_pass(kept, grad):
    return (grad,)

def back_keep(v):
    return (v, None)

def back_low(kept, grad):
    return (low(grad),)
low.defvjp(low_keep, low_pass)
low_back.defvjp(back_keep, back_low)

def layer_norm(values, gain_vec):
    average = lax.optimization_barrier(jnp.mean(values, axis=-1, keepdims=True))
    centred = values - average
    variance = lax.optimization_barrier(jnp.mean(centred * centred, axis=-1, keepdims=True))
    return centred * lax.rsqrt(variance + NORM_EPSILON) * gain_vec

def doc_tables(lengths, first_tok, tok_count):
    doc_ends = jnp.cumsum(lengths, axis=-1).astype(jnp.int32)
    places = (first_tok + jnp.arange(tok_count, dtype=jnp.int32)).astype(jnp.int32)
    passed = places[None, :, None] >= doc_ends[:, None, :]
    docs = lax.optimization_barrier(jnp.sum(passed.astype(jnp.int32), axis=2)).astype(jnp.int32)
    starts = lax.optimization_barrier(jnp.sum(jnp.where(passed, lengths[:, None, :], 0), axis=2)).astype(jnp.int32)
    return (docs, (places[None, :] - starts).astype(jnp.int32))

def rotate(values, positions, direction):
    half_dim = HD // 2
    inverse = ROPE_BASE ** (-(jnp.arange(half_dim, dtype=jnp.float32) * (2.0 / HD)))
    angles = positions.astype(jnp.float32)[..., None] * inverse
    cosine = jnp.cos(angles)[..., None, :]
    sine_part = direction * jnp.sin(angles)[..., None, :]
    front_half = values[..., :half_dim]
    back_half = values[..., half_dim:]
    return jnp.concatenate([front_half * cosine - back_half * sine_part, back_half * cosine + front_half * sine_part], axis=-1)

def row_attention(inputs):
    queries, keys, values, docs = inputs
    block_rows = math.gcd(SEQ, 512)
    scale_factor = 1.0 / math.sqrt(HD)
    query_blocks = queries.reshape(SEQ // block_rows, block_rows, HEADS, HD)
    doc_blocks = docs.reshape(SEQ // block_rows, block_rows)

    def attend_block(block):
        query_block, query_docs = block
        scores = jnp.einsum('qhd,khd->hqk', query_block, keys, precision=HIGH) * scale_factor
        scores = low_back(scores)
        same_doc = query_docs[None, :, None] == docs[None, None, :]
        scores = jnp.where(same_doc, scores, MASKED)
        top_score = lax.optimization_barrier(jnp.max(scores, axis=-1, keepdims=True))
        log_total = top_score + jnp.log(lax.optimization_barrier(jnp.sum(jnp.exp(scores - top_score), axis=-1, keepdims=True)))
        probs = low(jnp.exp(scores - log_total))
        return jnp.einsum('hqk,khd->qhd', probs, values, precision=HIGH)
    outputs = lax.map(jax.checkpoint(attend_block), (query_blocks, doc_blocks))
    return outputs.reshape(SEQ, HEADS, HD)

def reference(tokens, lengths, norm_gain, qkv_weight, out_weight, mlp_gain, in_weight, down_weight, cotangent):
    docs, positions = doc_tables(lengths, 0, SEQ)
    heads_shape = (ROWS, SEQ, HEADS, HD)

    def forward(inputs, gain_one, w_qkv, w_out, gain_two, w_in, w_down):
        normed_one = low(layer_norm(inputs, gain_one))
        projected = low_back(jnp.einsum('rsd,de->rse', normed_one, w_qkv, precision=HIGH))
        queries = low(rotate(projected[..., :D].reshape(heads_shape), positions, 1.0))
        keys = low(rotate(projected[..., D:2 * D].reshape(heads_shape), positions, 1.0))
        values = low(projected[..., 2 * D:].reshape(heads_shape))
        attended = lax.map(jax.checkpoint(row_attention), (queries, keys, values, docs))
        attn = low(low_back(attended.reshape(ROWS, SEQ, D)))
        branch = low_back(jnp.einsum('rsd,de->rse', attn, w_out, precision=HIGH))
        hidden = inputs + branch
        normed_two = low(layer_norm(hidden, gain_two))
        gate_up = low_back(jnp.einsum('rsd,de->rse', normed_two, w_in, precision=HIGH))
        middle = low(jax.nn.gelu(gate_up[..., :FF], approximate=False) * gate_up[..., FF:])
        mixed = low_back(jnp.einsum('rsf,fd->rsd', middle, w_down, precision=HIGH))
        return hidden + mixed
    primal = (tokens.astype(jnp.float32), norm_gain.astype(jnp.float32), qkv_weight.astype(jnp.float32), out_weight.astype(jnp.float32), mlp_gain.astype(jnp.float32), in_weight.astype(jnp.float32), down_weight.astype(jnp.float32))
    result, pull = jax.vjp(forward, *primal)
    grads = pull(cotangent.astype(jnp.float32))
    return (result.astype(jnp.bfloat16), grads[0].astype(jnp.bfloat16), grads[1], grads[2], grads[3], grads[4], grads[5], grads[6])
```

```python
import functools
import math

import jax
import jax.numpy as jnp
import numpy as np
from jax import lax
from jax.experimental import pallas as pl
from jax.experimental.pallas import tpu as pltpu
from jax.sharding import PartitionSpec as P

D = 768
HEADS = 12
HD = 64
FF = 1152
NDOC = 8
PAIRS = HEADS // 2
EXT = 3 * D + 128

ROPE_BASE = 160000.0
NORM_EPSILON = 1e-05
MASKED = -1e30
F32 = jnp.float32
BF16 = jnp.bfloat16
NN = (((1,), (0,)), ((), ()))
NT = (((1,), (1,)), ((), ()))
TN = (((0,), (0,)), ((), ()))
VMEM_BYTES = 56 * 1024 * 1024
SMEM = pl.BlockSpec(memory_space=pltpu.SMEM)
ANY = pl.BlockSpec(memory_space=pl.ANY)
VMEM = pl.BlockSpec(memory_space=pltpu.VMEM)


def dot(a, b, dims):
    return lax.dot_general(a, b, dims, preferred_element_type=F32)


def shape_of(dims, dtype):
    return jax.ShapeDtypeStruct(tuple(dims), dtype)


def params():
    return pltpu.CompilerParams(vmem_limit_bytes=VMEM_BYTES)


def cost(flops, moved, exps=0):
    return pl.CostEstimate(flops=int(flops), bytes_accessed=int(moved), transcendentals=int(exps))


class Plan:
    def __init__(self, mesh, rows, tok):
        self.nrow = mesh.shape["row"]
        self.nblk = mesh.shape["blk"]
        self.rows = rows
        self.tok = tok
        self.local = rows * tok
        self.chips = self.nblk // 2
        self.bits = self.chips.bit_length() - 1
        self.groups = self.nblk // rows
        self.r = D // self.nblk
        self.rf = FF // self.nblk
        self.cw = D // self.nrow
        self.aligned = self.r % 16 == 0 and self.rf % 16 == 0
        self.packed = 4 * self.r + self.rf
        rows_, chips, nrow = self.rows, self.chips, self.nrow
        self.at_pick = 0
        self.at_base = self.at_pick + rows_
        self.at_own = self.at_base + self.groups * rows_
        self.at_other = self.at_own + chips
        self.at_z = self.at_other + chips
        self.at_lo = self.at_z + nrow
        self.size = self.at_lo + 1
        table = np.zeros((nrow, self.nblk, self.size), np.int32)
        for z in range(nrow):
            for blk in range(self.nblk):
                chip, core = blk // 2, blk % 2
                low = chip % rows_
                entry = table[z, blk]
                for j in range(rows_):
                    entry[self.at_pick + j] = low ^ j
                for e in range(self.groups):
                    other = blk ^ self.member(e)
                    for j in range(rows_):
                        entry[self.at_base + e * rows_ + j] = (2 * ((other // 2) ^ j) + other % 2) * tok
                for j in range(chips):
                    entry[self.at_own + j] = 2 * (chip ^ self.order(core, j)) + core
                    entry[self.at_other + j] = 2 * (chip ^ self.order(1 - core, j)) + 1 - core
                for other in range(nrow):
                    entry[self.at_z + other] = other ^ z
                entry[self.at_lo] = low
        self.table = table

    def member(self, e):
        return (e & 1) | ((e >> 1) * 2 * self.rows)

    def order(self, core, j):
        if core == 0:
            return j
        return int(format(j, "0%db" % self.bits)[::-1], 2) if self.bits else 0

    def step_pairs(self, step):
        def flip(blk):
            bit = step if blk % 2 == 0 else self.bits - 1 - step
            return 2 * ((blk // 2) ^ (1 << bit)) + blk % 2

        return [(blk, flip(blk)) for blk in range(self.nblk)]

    def xor_pairs(self, mask):
        return [(blk, blk ^ mask) for blk in range(self.nblk)]

    def z_pairs(self, mask):
        return [(z, z ^ mask) for z in range(self.nrow)]


def swap_cores(plan, value):
    return lax.ppermute(value, "blk", plan.xor_pairs(1))


def gather_z(plan, value):
    return [value] + [lax.ppermute(value, "row", plan.z_pairs(j)) for j in range(1, plan.nrow)]


def exchange_rows(plan, pieces):
    return [pieces[0]] + [
        lax.ppermute(pieces[j], "blk", plan.xor_pairs(2 * j)) for j in range(1, plan.rows)
    ]


def gather_xy(plan, value):
    pieces = [value]
    others = [swap_cores(plan, value)]
    for step in range(plan.bits):
        pairs = plan.step_pairs(step)
        more = [lax.ppermute(piece, "blk", pairs) for piece in pieces]
        pieces = pieces + more
        others = others + [swap_cores(plan, piece) for piece in more]
    return pieces, others


def add_low(a, b):
    return (a.astype(F32) + b.astype(F32)).astype(BF16)


def reduce_xy(plan, keep, send):
    half = plan.chips // 2
    if half == 0:
        return add_low(keep, swap_cores(plan, send))[0]
    high = add_low(keep[half:], swap_cores(plan, send[half:]))
    total = add_low(keep[:half], swap_cores(plan, send[:half]))
    for step in reversed(range(plan.bits)):
        moved = lax.ppermute(high, "blk", plan.step_pairs(step))
        half = half // 2
        if step == 0:
            return add_low(total, moved)[0]
        high = add_low(total[half:], moved[half:])
        total = add_low(total[:half], moved[:half])


def layer_norm(values):
    average = jnp.mean(values, axis=-1, keepdims=True)
    centred = values - average
    inv_std = lax.rsqrt(jnp.mean(centred * centred, axis=-1, keepdims=True) + NORM_EPSILON)
    return centred * inv_std, inv_std


def norm_backward(grad_out, normalized, inv_std, gain):
    scaled = grad_out * gain
    inner = jnp.mean(scaled * normalized, axis=-1, keepdims=True)
    outer = jnp.mean(scaled, axis=-1, keepdims=True)
    return inv_std * (scaled - outer - normalized * inner)


def swap_halves(values):
    lane = lax.broadcasted_iota(jnp.int32, values.shape, 1)
    width = values.shape[1]
    half = HD // 2
    return jnp.where(
        (lane & half) == 0, pltpu.roll(values, width - half, 1), pltpu.roll(values, half, 1)
    )


def rotate_pair(values, cosine, sine, direction):
    return values * cosine + swap_halves(values) * (direction * sine)


def rotate_all(values, cosine, sine, direction):
    return jnp.concatenate(
        [
            rotate_pair(values[:, 128 * p : 128 * (p + 1)], cosine, sine, direction)
            for p in range(PAIRS)
        ],
        axis=1,
    )


def pick_kernel(plan, meta, tokens, cotangent, *refs):
    outs, sems = refs[: plan.rows], refs[plan.rows]
    copies = []
    for j in range(plan.rows):
        row = meta[plan.at_pick + j]
        copies.append(pltpu.make_async_copy(tokens.at[row], outs[j].at[0], sems.at[2 * j]))
        copies.append(pltpu.make_async_copy(cotangent.at[row], outs[j].at[1], sems.at[2 * j + 1]))
    for copy in copies:
        copy.start()
    for copy in copies:
        copy.wait()


def pick(plan, meta, tokens, cotangent):
    return pl.pallas_call(
        functools.partial(pick_kernel, plan),
        in_specs=[SMEM, ANY, ANY],
        out_specs=[ANY] * plan.rows,
        out_shape=[shape_of((2, plan.tok, D), BF16)] * plan.rows,
        scratch_shapes=[pltpu.SemaphoreType.DMA((2 * plan.rows,))],
        compiler_params=params(),
        cost_estimate=cost(0, 4 * plan.local * D * 2),
        name="pick_rows",
    )(meta, tokens, cotangent)


def place_kernel(plan, meta, *refs):
    pieces, out, sems = refs[: plan.rows], refs[plan.rows], refs[plan.rows + 1]
    copies = []
    for j in range(plan.rows):
        row = meta[plan.at_pick + j]
        copies.append(pltpu.make_async_copy(pieces[j], out.at[row], sems.at[j]))
    for copy in copies:
        copy.start()
    for copy in copies:
        copy.wait()


def place(plan, meta, pieces):
    return pl.pallas_call(
        functools.partial(place_kernel, plan),
        in_specs=[SMEM] + [ANY] * plan.rows,
        out_specs=ANY,
        out_shape=shape_of((plan.rows, plan.tok, D), BF16),
        scratch_shapes=[pltpu.SemaphoreType.DMA((plan.rows,))],
        compiler_params=params(),
        cost_estimate=cost(0, 2 * plan.local * D * 2),
        name="place_rows",
    )(meta, *pieces)


def ordered(plan, meta, pieces):
    stacked = jnp.stack(pieces)
    return [
        lax.dynamic_index_in_dim(stacked, meta[plan.at_z + z], 0, keepdims=False)
        for z in range(plan.nrow)
    ]


def join_qkv_kernel(plan, meta, gains, *refs):
    pieces, out, held = refs[: plan.nrow], refs[plan.nrow], refs[plan.nrow + 1]
    width = 3 * plan.cw
    for j in range(plan.nrow):
        held[j] = pieces[j][...]
    for z in range(plan.nrow):
        out[:, width * z : width * (z + 1)] = held[meta[plan.at_z + z]]
    out[:, 3 * D :] = gains[...]


def join_qkv(plan, meta, gains, pieces):
    if not plan.aligned:
        return jnp.concatenate(ordered(plan, meta, pieces) + [gains], axis=1)
    return pl.pallas_call(
        functools.partial(join_qkv_kernel, plan),
        in_specs=[SMEM] + [VMEM] * (1 + plan.nrow),
        out_specs=VMEM,
        out_shape=shape_of((plan.r, EXT), BF16),
        scratch_shapes=[pltpu.VMEM((plan.nrow, plan.r, 3 * plan.cw), BF16)],
        compiler_params=params(),
        cost_estimate=cost(0, 2 * plan.r * EXT * 2),
        name="join_qkv",
    )(meta, gains, *pieces)


def pack_rest(plan, w_out, w_in, w_down):
    cw = plan.cw
    left = jnp.concatenate([w_in[:, :cw], w_in[:, cw : 2 * cw], w_out], axis=0)
    blank = jnp.zeros((2 * plan.r - plan.rf, cw), BF16)
    right = jnp.concatenate([w_in[:, 2 * cw :], w_down, blank], axis=0)
    return jnp.concatenate([left, right], axis=1)


def unpack_rest(plan, piece):
    r, rf, cw = plan.r, plan.rf, plan.cw
    parts_in = [piece[:r, :cw], piece[r : 2 * r, :cw], piece[:r, cw:]]
    return parts_in, piece[2 * r : 3 * r, :cw], piece[r : r + rf, cw:]


def join_rest_kernel(plan, meta, *refs):
    pieces, out, held = refs[: plan.nrow], refs[plan.nrow], refs[plan.nrow + 1]
    r, cw = plan.r, plan.cw
    for j in range(plan.nrow):
        held[j] = pieces[j][...]
    for z in range(plan.nrow):
        parts_in, part_out, part_down = unpack_rest(plan, held[meta[plan.at_z + z]])
        out[:r, cw * z : cw * (z + 1)] = part_out
        for i in range(3):
            block, place_at = (3 * z + i) // plan.nrow, (3 * z + i) % plan.nrow
            out[r * (1 + block) : r * (2 + block), cw * place_at : cw * (place_at + 1)] = parts_in[i]
        out[4 * r :, cw * z : cw * (z + 1)] = part_down


def join_rest(plan, meta, pieces):
    if not plan.aligned:
        parts = [unpack_rest(plan, piece) for piece in ordered(plan, meta, pieces)]
        w_in = jnp.concatenate([part for item in parts for part in item[0]], axis=1)
        blocks = [jnp.concatenate([item[1] for item in parts], axis=1)]
        blocks += [w_in[:, D * t : D * (t + 1)] for t in range(3)]
        blocks += [jnp.concatenate([item[2] for item in parts], axis=1)]
        return jnp.concatenate(blocks, axis=0)
    return pl.pallas_call(
        functools.partial(join_rest_kernel, plan),
        in_specs=[SMEM] + [VMEM] * plan.nrow,
        out_specs=VMEM,
        out_shape=shape_of((plan.packed, D), BF16),
        scratch_shapes=[pltpu.VMEM((plan.nrow, 3 * plan.r, 2 * plan.cw), BF16)],
        compiler_params=params(),
        cost_estimate=cost(0, 2 * plan.packed * D * 2),
        name="join_rest",
    )(meta, *pieces)


def by_block(plan, meta, own, other):
    stacked = jnp.stack(own + other)
    places = meta[plan.at_own : plan.at_other + plan.chips]
    return jnp.zeros_like(stacked).at[places].set(stacked)


def split_blocks(plan, meta, blocks):
    own = jnp.take(blocks, meta[plan.at_own : plan.at_own + plan.chips], axis=0)
    other = jnp.take(blocks, meta[plan.at_other : plan.at_other + plan.chips], axis=0)
    return own, other


def qkv_sources(plan, meta, own, other):
    if plan.aligned:
        return own + other
    return [by_block(plan, meta, own, other).reshape(D, EXT)]


def rest_sources(plan, meta, own, other):
    if plan.aligned:
        return own + other
    blocks = by_block(plan, meta, own, other)
    r = plan.r
    parts = [blocks[:, r * i : r * (i + 1)].reshape(D, D) for i in range(4)]
    parts.append(blocks[:, 4 * r :].reshape(FF, D))
    return [jnp.concatenate(parts, axis=0)]


def block_size(plan):
    return (plan.r, plan.rf) if plan.aligned else (D, FF)


def block_of(plan, meta, index):
    return meta[plan.at_own + index] if plan.aligned else 0


def rows_at(index, size):
    if isinstance(index, int):
        return pl.ds(index * size, size)
    return pl.ds(pl.multiple_of(index * size, size), size)


def qkv_copies(plan, meta, sources, w_ref, sems):
    r, _ = block_size(plan)
    return [
        pltpu.make_async_copy(source, w_ref.at[rows_at(block_of(plan, meta, i), r)], sems.at[i])
        for i, source in enumerate(sources)
    ]


def rest_copies(plan, meta, sources, w_out, w_in, w_down, sems):
    r, rf = block_size(plan)
    found = [[], [], []]
    for i, source in enumerate(sources):
        block = block_of(plan, meta, i)
        rows = rows_at(block, r)
        found[0].append(
            pltpu.make_async_copy(source.at[pl.ds(0, r)], w_out.at[rows], sems.at[5 * i])
        )
        for t in range(3):
            found[1].append(
                pltpu.make_async_copy(
                    source.at[pl.ds((1 + t) * r, r)], w_in.at[t, rows], sems.at[5 * i + 1 + t]
                )
            )
        found[2].append(
            pltpu.make_async_copy(
                source.at[pl.ds(4 * r, rf)], w_down.at[rows_at(block, rf)], sems.at[5 * i + 4]
            )
        )
    return found


def source_count(plan):
    return 2 * plan.chips if plan.aligned else 1


def qkv_kernel(plan, meta, cos_ref, sin_ref, *refs):
    x_refs = refs[: plan.rows]
    count = source_count(plan)
    sources = refs[plan.rows : plan.rows + count]
    q_ref, kv_ref, n_ref, gain_ref, w_ref, sems = refs[plan.rows + count :]
    copies = qkv_copies(plan, meta, sources, w_ref, sems)
    for copy in copies:
        copy.start()
    units = [layer_norm(x_refs[j][0].astype(F32))[0] for j in range(plan.rows)]
    for copy in copies:
        copy.wait()
    gain_ref[...] = w_ref[:, 3 * D :].astype(F32).T[:8, :]
    for j in range(plan.rows):
        n_ref[plan.tok * j : plan.tok * (j + 1), :] = (units[j] * gain_ref[0:1, :]).astype(BF16)
    cosine, sine = cos_ref[...], sin_ref[...]
    normed = n_ref[...]
    queries = dot(normed, w_ref[:, :D], NN)
    q_ref[...] = rotate_all(queries, cosine, sine, 1.0).astype(BF16)
    keys = dot(normed, w_ref[:, D : 2 * D], NN)
    kv_ref[0] = rotate_all(keys, cosine, sine, 1.0).astype(BF16)
    kv_ref[1] = dot(normed, w_ref[:, 2 * D : 3 * D], NN).astype(BF16)


def project(plan, meta, cosine, sine, pieces, sources):
    local = plan.local
    count = len(sources)
    return pl.pallas_call(
        functools.partial(qkv_kernel, plan),
        in_specs=[SMEM, VMEM, VMEM] + [VMEM] * plan.rows + [ANY] * count,
        out_specs=[VMEM] * 4,
        out_shape=[
            shape_of((local, D), BF16),
            shape_of((2, local, D), BF16),
            shape_of((local, D), BF16),
            shape_of((8, D), F32),
        ],
        scratch_shapes=[pltpu.VMEM((D, EXT), BF16), pltpu.SemaphoreType.DMA((count,))],
        compiler_params=params(),
        cost_estimate=cost(2 * local * D * 3 * D, 2 * (D * EXT + 6 * local * D)),
        name="project",
    )(meta, cosine, sine, *pieces, *sources)


def fill_docs(plan, meta, lengths, kdoc, qdoc):
    low = meta[plan.at_lo]
    ends = []
    passed = jnp.int32(0)
    for n in range(NDOC):
        passed = passed + lengths[low, n]
        ends.append(passed)

    def docs(places):
        total = jnp.zeros(places.shape, jnp.int32)
        for end in ends:
            total = total + (places >= end).astype(jnp.int32)
        return total

    tok = plan.tok
    for i in range(plan.groups * plan.rows):
        first = meta[plan.at_base + i]
        kdoc[i * tok : (i + 1) * tok, :] = docs(
            first + lax.broadcasted_iota(jnp.int32, (tok, 128), 0)
        )
    for i in range(plan.rows):
        first = meta[plan.at_base + i]
        qdoc[:, i * tok : (i + 1) * tok] = docs(
            first + lax.broadcasted_iota(jnp.int32, (8, tok), 1)
        )


def head_part(pair, head):
    lane = lax.broadcasted_iota(jnp.int32, pair.shape, 1)
    keep = (lane < HD) if head == 0 else (lane >= HD)
    return jnp.where(keep, pair, jnp.zeros_like(pair))


def same_docs(kdoc, qdoc, first, size, q0, width):
    key_docs = jnp.concatenate([kdoc[first : first + size, :]] * (width // 128), axis=1)
    return key_docs == qdoc[0:1, q0 : q0 + width]


def attend_kernel(plan, width, meta, lengths, q_ref, *refs):
    groups, local = plan.groups, plan.local
    kv = refs[:groups]
    o_ref, low_ref, lse_ref, kdoc, qdoc, s_ref = refs[groups:]

    @pl.when(pl.program_id(0) == 0)
    def _():
        fill_docs(plan, meta, lengths, kdoc, qdoc)

    values_t = [kv[e][1].T for e in range(groups)]
    for first in range(0, local, width):
        rows = slice(first, first + width)
        queries = q_ref[rows, :] * jnp.asarray(1.0 / math.sqrt(HD), BF16)
        parts = []
        for h in range(2):
            head_queries = head_part(queries, h)
            top = jnp.full((1, width), MASKED, F32)
            for e in range(groups):
                scores = dot(kv[e][0], head_queries, NT)
                mask = same_docs(kdoc, qdoc, e * local, local, first, width)
                scores = jnp.where(mask, scores, MASKED)
                s_ref[h, e * local : (e + 1) * local, :] = scores
                top = jnp.maximum(top, jnp.max(scores, axis=0, keepdims=True))
            total = jnp.zeros((1, width), F32)
            weighted = jnp.zeros((HD, width), F32)
            for e in range(groups):
                probs = jnp.exp(s_ref[h, e * local : (e + 1) * local, :] - top)
                total = total + jnp.sum(probs, axis=0, keepdims=True)
                weighted = weighted + dot(
                    values_t[e][h * HD : (h + 1) * HD, :], probs.astype(BF16), NN
                )
            parts.append(weighted / total)
            lse_ref[0, h : h + 1, rows] = top + jnp.log(total)
        heads = jnp.concatenate(parts, axis=0).T
        o_ref[rows, :] = heads
        low_ref[rows, :] = heads.astype(BF16)


def attend(plan, meta, lengths, queries, kv):
    local, groups = plan.local, plan.groups
    width = min(512, local)
    pair = pl.BlockSpec((local, 128), lambda p: (0, p))
    pair_kv = pl.BlockSpec((2, local, 128), lambda p: (0, 0, p))
    return pl.pallas_call(
        functools.partial(attend_kernel, plan, width),
        grid=(PAIRS,),
        in_specs=[SMEM, SMEM, pair] + [pair_kv] * groups,
        out_specs=[pair, pair, pl.BlockSpec((1, 2, local), lambda p: (p, 0, 0))],
        out_shape=[
            shape_of((local, D), F32),
            shape_of((local, D), BF16),
            shape_of((PAIRS, 2, local), F32),
        ],
        scratch_shapes=[
            pltpu.VMEM((groups * local, 128), jnp.int32),
            pltpu.VMEM((8, local), jnp.int32),
            pltpu.VMEM((2, groups * local, width), F32),
        ],
        compiler_params=params(),
        cost_estimate=cost(16 * local * local * groups * D, 2 * local * D * (4 + 2 * groups)),
        name="attend",
    )(meta, lengths, queries, *kv)


def attend_back_kernel(
    plan, width, meta, lengths, q_ref, do_ref, o_ref, lse_ref, cos_ref, sin_ref, *refs
):
    groups, local = plan.groups, plan.local
    kv = refs[:groups]
    dq_ref = refs[groups]
    dkv = refs[groups + 1 : 2 * groups + 1]
    kdoc, qdoc, held = refs[2 * groups + 1 :]

    @pl.when(pl.program_id(0) == 0)
    def _():
        fill_docs(plan, meta, lengths, kdoc, qdoc)

    keys_t = [kv[e][0].T for e in range(groups)]
    scale = 1.0 / math.sqrt(HD)
    for first in range(0, local, width):
        rows = slice(first, first + width)
        queries = q_ref[rows, :] * jnp.asarray(scale, BF16)
        dout = do_ref[rows, :]
        product = (dout.astype(F32) * o_ref[rows, :]).T
        parts = []
        for h in range(2):
            head_queries = head_part(queries, h)
            head_dout = head_part(dout, h)
            lse = lse_ref[0, h : h + 1, rows]
            delta = jnp.sum(product[h * HD : (h + 1) * HD, :], axis=0, keepdims=True)
            grad_queries = jnp.zeros((HD, width), F32)
            for e in range(groups):
                scores = dot(kv[e][0], head_queries, NT)
                mask = same_docs(kdoc, qdoc, e * local, local, first, width)
                probs = jnp.exp(jnp.where(mask, scores, MASKED) - lse)
                dprobs = dot(kv[e][1], head_dout, NT)
                dscores = (probs * (dprobs - delta)).astype(BF16)
                grad_values = dot(probs.astype(BF16), head_dout, NN)
                grad_keys = dot(dscores, head_queries, NN)
                if first == 0 and h == 0:
                    held[e, 0] = grad_keys
                    held[e, 1] = grad_values
                else:
                    held[e, 0] += grad_keys
                    held[e, 1] += grad_values
                grad_queries = grad_queries + dot(
                    keys_t[e][h * HD : (h + 1) * HD, :], dscores, NN
                )
            parts.append(grad_queries)
        grad = jnp.concatenate(parts, axis=0).T * scale
        dq_ref[rows, :] = rotate_pair(grad, cos_ref[rows, :], sin_ref[rows, :], -1.0).astype(BF16)
    for e in range(groups):
        dkv[e][...] = held[e].astype(BF16)


def attend_back(plan, meta, lengths, queries, dout, heads, lse, cosine, sine, kv):
    local, groups = plan.local, plan.groups
    width = min(256, local)
    pair = pl.BlockSpec((local, 128), lambda p: (0, p))
    table = pl.BlockSpec((local, 128), lambda p: (0, 0))
    pair_kv = pl.BlockSpec((2, local, 128), lambda p: (0, 0, p))
    return pl.pallas_call(
        functools.partial(attend_back_kernel, plan, width),
        grid=(PAIRS,),
        in_specs=[
            SMEM,
            SMEM,
            pair,
            pair,
            pair,
            pl.BlockSpec((1, 2, local), lambda p: (p, 0, 0)),
            table,
            table,
        ]
        + [pair_kv] * groups,
        out_specs=[pair] + [pair_kv] * groups,
        out_shape=[shape_of((local, D), BF16)] + [shape_of((2, local, D), BF16)] * groups,
        scratch_shapes=[
            pltpu.VMEM((groups * local, 128), jnp.int32),
            pltpu.VMEM((8, local), jnp.int32),
            pltpu.VMEM((groups, 2, local, 128), F32),
        ],
        compiler_params=params(),
        cost_estimate=cost(40 * local * local * groups * D, 2 * local * D * (6 + 4 * groups)),
        name="attend_back",
    )(meta, lengths, queries, dout, heads, lse, cosine, sine, *kv)


def middle_kernel(plan, meta, low_ref, gain_ref, *refs):
    rows, tok, local = plan.rows, plan.tok, plan.local
    count = source_count(plan)
    x_refs = refs[:rows]
    sources = refs[rows : rows + count]
    refs = refs[rows + count :]
    out_refs = refs[:rows]
    do_ref, dh_ref, gain_grad_ref = refs[rows : rows + 3]
    grads = refs[rows + 3 : rows + 3 + (2 if plan.aligned else 1)]
    (
        w_out,
        w_in,
        w_down,
        h_ref,
        n_ref,
        gu_ref,
        mid_ref,
        dgu_ref,
        g_out,
        g_in,
        g_down,
        in_sems,
        out_sems,
    ) = refs[rows + 3 + len(grads) :]
    copies = rest_copies(plan, meta, sources, w_out, w_in, w_down, in_sems)
    for group in copies:
        for copy in group:
            copy.start()
    for copy in copies[0]:
        copy.wait()
    branch = dot(low_ref[...], w_out[...], NN)
    for j in range(rows):
        part = slice(tok * j, tok * (j + 1))
        h_ref[part, :] = x_refs[j][0].astype(F32) + branch[part, :]
    gain = gain_ref[1:2, :]
    unit, inv_std = layer_norm(h_ref[...])
    n_ref[...] = (unit * gain).astype(BF16)
    for copy in copies[1]:
        copy.wait()
    for t in range(3):
        gu_ref[:, D * t : D * (t + 1)] = dot(n_ref[...], w_in[t], NN)
    for copy in copies[2]:
        copy.wait()
    dy = jnp.concatenate([x_refs[j][1] for j in range(rows)], axis=0)
    size = FF // 3
    for f in range(3):
        cols = slice(size * f, size * (f + 1))
        up_cols = slice(FF + size * f, FF + size * (f + 1))
        gate = gu_ref[:, cols]
        up = gu_ref[:, up_cols]
        below = 0.5 + 0.5 * lax.erf(gate * math.sqrt(0.5))
        active = gate * below
        mid_ref[:, cols] = (active * up).astype(BF16)
        slope = below + gate * jnp.exp(-0.5 * gate * gate) * (1.0 / math.sqrt(2.0 * math.pi))
        dmid = dot(dy, w_down[cols, :], NT)
        dgu_ref[:, cols] = (dmid * up * slope).astype(BF16)
        dgu_ref[:, up_cols] = (dmid * active).astype(BF16)
    mixed = dot(mid_ref[...], w_down[...], NN)
    for j in range(rows):
        part = slice(tok * j, tok * (j + 1))
        out_refs[j][...] = (h_ref[part, :] + mixed[part, :]).astype(BF16)
    grad_normed = dot(dgu_ref[:, :D], w_in[0], NT)
    for t in range(1, 3):
        grad_normed = grad_normed + dot(dgu_ref[:, D * t : D * (t + 1)], w_in[t], NT)
    unit, inv_std = layer_norm(h_ref[...])
    gain_grad_ref[...] = jnp.broadcast_to(
        jnp.sum(grad_normed * unit, axis=0, keepdims=True), (8, D)
    )
    grad_hidden = dy.astype(F32) + norm_backward(grad_normed, unit, inv_std, gain)
    dh_ref[...] = grad_hidden
    branch_grad = grad_hidden.astype(BF16)
    do_ref[...] = dot(branch_grad, w_out[...], NT).astype(BF16)
    g_out[...] = dot(low_ref[...], branch_grad, TN).astype(BF16)
    for t in range(3):
        g_in[t] = dot(n_ref[...], dgu_ref[:, D * t : D * (t + 1)], TN).astype(BF16)
    g_down[...] = dot(mid_ref[...], dy, TN).astype(BF16)
    r, rf = block_size(plan)
    done = []
    for i in range(count):
        block = block_of(plan, meta, i)
        target = grads[i // plan.chips].at[i % plan.chips] if plan.aligned else grads[0]
        at = rows_at(block, r)
        done.append(
            pltpu.make_async_copy(g_out.at[at], target.at[pl.ds(0, r)], out_sems.at[5 * i])
        )
        for t in range(3):
            done.append(
                pltpu.make_async_copy(
                    g_in.at[t, at], target.at[pl.ds((1 + t) * r, r)], out_sems.at[5 * i + 1 + t]
                )
            )
        done.append(
            pltpu.make_async_copy(
                g_down.at[rows_at(block, rf)], target.at[pl.ds(4 * r, rf)], out_sems.at[5 * i + 4]
            )
        )
    for copy in done:
        copy.start()
    for copy in done:
        copy.wait()


def middle(plan, meta, low, gains, pieces, sources):
    local, rows, tok = plan.local, plan.rows, plan.tok
    count = len(sources)
    total = 4 * D + FF
    if plan.aligned:
        grads = [shape_of((plan.chips, plan.packed, D), BF16)] * 2
    else:
        grads = [shape_of((total, D), BF16)]
    return pl.pallas_call(
        functools.partial(middle_kernel, plan),
        in_specs=[SMEM, VMEM, VMEM] + [VMEM] * rows + [ANY] * count,
        out_specs=[VMEM] * (rows + 3) + [ANY] * len(grads),
        out_shape=[shape_of((tok, D), BF16)] * rows
        + [shape_of((local, D), BF16), shape_of((local, D), F32), shape_of((8, D), F32)]
        + grads,
        scratch_shapes=[
            pltpu.VMEM((D, D), BF16),
            pltpu.VMEM((3, D, D), BF16),
            pltpu.VMEM((FF, D), BF16),
            pltpu.VMEM((local, D), F32),
            pltpu.VMEM((local, D), BF16),
            pltpu.VMEM((local, 2 * FF), F32),
            pltpu.VMEM((local, FF), BF16),
            pltpu.VMEM((local, 2 * FF), BF16),
            pltpu.VMEM((D, D), BF16),
            pltpu.VMEM((3, D, D), BF16),
            pltpu.VMEM((FF, D), BF16),
            pltpu.SemaphoreType.DMA((5 * count,)),
            pltpu.SemaphoreType.DMA((5 * count,)),
        ],
        compiler_params=params(),
        cost_estimate=cost(6 * local * D * total, 4 * total * D + 12 * local * D),
        name="middle",
    )(meta, low, gains, *pieces, *sources)


def back_kernel(plan, meta, cos_ref, sin_ref, dq_ref, n_ref, dh_ref, gain_ref, g2_ref, *refs):
    rows, tok, groups = plan.rows, plan.tok, plan.groups
    count = source_count(plan)
    dkv = refs[:groups]
    x_refs = refs[groups : groups + rows]
    sources = refs[groups + rows : groups + rows + count]
    refs = refs[groups + rows + count :]
    in_refs = refs[:rows]
    grads = refs[rows : rows + (2 if plan.aligned else 1)]
    w_ref, dp_ref, g_ref, in_sems, out_sems = refs[rows + len(grads) :]
    copies = qkv_copies(plan, meta, sources, w_ref, in_sems)
    for copy in copies:
        copy.start()
    grad_keys = dkv[0][0].astype(F32)
    grad_values = dkv[0][1].astype(F32)
    for e in range(1, groups):
        grad_keys = grad_keys + dkv[e][0].astype(F32)
        grad_values = grad_values + dkv[e][1].astype(F32)
    dp_ref[0] = dq_ref[...]
    dp_ref[1] = rotate_all(grad_keys, cos_ref[...], sin_ref[...], -1.0).astype(BF16)
    dp_ref[2] = grad_values.astype(BF16)
    for t in range(3):
        g_ref[:, D * t : D * (t + 1)] = dot(n_ref[...], dp_ref[t], TN).astype(BF16)
    for copy in copies:
        copy.wait()
    grad_normed = dot(dp_ref[0], w_ref[:, :D], NT)
    for t in range(1, 3):
        grad_normed = grad_normed + dot(dp_ref[t], w_ref[:, D * t : D * (t + 1)], NT)
    gain_grad = jnp.zeros((1, D), F32)
    for j in range(rows):
        part = slice(tok * j, tok * (j + 1))
        unit, inv_std = layer_norm(x_refs[j][0].astype(F32))
        grad = grad_normed[part, :]
        gain_grad = gain_grad + jnp.sum(grad * unit, axis=0, keepdims=True)
        back = norm_backward(grad, unit, inv_std, gain_ref[0:1, :])
        in_refs[j][...] = (dh_ref[part, :] + back).astype(BF16)
    which = lax.broadcasted_iota(jnp.int32, (128, D), 0)
    both = jnp.where(which == 0, gain_grad, jnp.where(which == 1, g2_ref[0:1, :], 0.0))
    g_ref[:, 3 * D :] = both.T.astype(BF16)
    r, _ = block_size(plan)
    done = []
    for i in range(count):
        target = grads[i // plan.chips].at[i % plan.chips] if plan.aligned else grads[0]
        at = rows_at(block_of(plan, meta, i), r)
        done.append(pltpu.make_async_copy(g_ref.at[at], target, out_sems.at[i]))
    for copy in done:
        copy.start()
    for copy in done:
        copy.wait()


def back(plan, meta, cosine, sine, dq, normed, dhidden, gains, gain_two, dkv, pieces, sources):
    local, rows, tok = plan.local, plan.rows, plan.tok
    count = len(sources)
    if plan.aligned:
        grads = [shape_of((plan.chips, plan.r, EXT), BF16)] * 2
    else:
        grads = [shape_of((D, EXT), BF16)]
    return pl.pallas_call(
        functools.partial(back_kernel, plan),
        in_specs=[SMEM] + [VMEM] * (7 + plan.groups + rows) + [ANY] * count,
        out_specs=[VMEM] * rows + [ANY] * len(grads),
        out_shape=[shape_of((tok, D), BF16)] * rows + grads,
        scratch_shapes=[
            pltpu.VMEM((D, EXT), BF16),
            pltpu.VMEM((3, local, D), BF16),
            pltpu.VMEM((D, EXT), BF16),
            pltpu.SemaphoreType.DMA((count,)),
            pltpu.SemaphoreType.DMA((count,)),
        ],
        compiler_params=params(),
        cost_estimate=cost(4 * local * D * 3 * D, 4 * D * EXT + 20 * local * D),
        name="back",
    )(meta, cosine, sine, dq, normed, dhidden, gains, gain_two, *dkv, *pieces, *sources)


def pad_width(plan):
    return -(-(3 * plan.cw + 2) // 128) * 128


def cut_qkv_kernel(plan, meta, total, *refs):
    outs, held = refs[: plan.nrow], refs[plan.nrow]
    width, wide = 3 * plan.cw, pad_width(plan)
    for z in range(plan.nrow):
        place_at = meta[plan.at_z + z]
        held[place_at, :, :width] = total[:, width * z : width * (z + 1)]
        held[place_at, :, width:] = total[:, 3 * D : 3 * D + wide - width]
    for j in range(plan.nrow):
        outs[j][...] = held[j]


def cut_qkv(plan, meta, total):
    width, wide = 3 * plan.cw, pad_width(plan)
    if not plan.aligned:
        parts = [
            jnp.concatenate(
                [total[:, width * z : width * (z + 1)], total[:, 3 * D : 3 * D + wide - width]],
                axis=1,
            )
            for z in range(plan.nrow)
        ]
        return ordered(plan, meta, parts)
    return pl.pallas_call(
        functools.partial(cut_qkv_kernel, plan),
        in_specs=[SMEM, VMEM],
        out_specs=[VMEM] * plan.nrow,
        out_shape=[shape_of((plan.r, wide), BF16)] * plan.nrow,
        scratch_shapes=[pltpu.VMEM((plan.nrow, plan.r, wide), BF16)],
        compiler_params=params(),
        cost_estimate=cost(0, 4 * plan.r * EXT),
        name="cut_qkv",
    )(meta, total)


def cut_rest_kernel(plan, meta, total, *refs):
    outs, held = refs[: plan.nrow], refs[plan.nrow]
    r, rf, cw = plan.r, plan.rf, plan.cw
    for z in range(plan.nrow):
        place_at = meta[plan.at_z + z]
        cols = slice(cw * z, cw * (z + 1))
        parts = []
        for i in range(3):
            block, at = (3 * z + i) // plan.nrow, (3 * z + i) % plan.nrow
            parts.append(total[r * (1 + block) : r * (2 + block), cw * at : cw * (at + 1)])
        held[place_at, :r, :] = jnp.concatenate([parts[0], parts[2]], axis=1)
        held[place_at, r : 2 * r, :] = jnp.concatenate(
            [parts[1], total[4 * r : 5 * r, cols]], axis=1
        )
        rest = total[5 * r : 4 * r + rf, cols]
        blank = jnp.zeros((2 * r - rf, cw), BF16)
        held[place_at, 2 * r :, :] = jnp.concatenate(
            [total[:r, cols], jnp.concatenate([rest, blank], axis=0)], axis=1
        )
    for j in range(plan.nrow):
        outs[j][...] = held[j]


def cut_rest(plan, meta, total):
    r, cw = plan.r, plan.cw
    if not plan.aligned:
        grad_in = jnp.concatenate([total[r * (1 + t) : r * (2 + t)] for t in range(3)], axis=1)
        parts = [
            pack_rest(
                plan,
                total[:r, cw * z : cw * (z + 1)],
                grad_in[:, 3 * cw * z : 3 * cw * (z + 1)],
                total[4 * r :, cw * z : cw * (z + 1)],
            )
            for z in range(plan.nrow)
        ]
        return ordered(plan, meta, parts)
    return pl.pallas_call(
        functools.partial(cut_rest_kernel, plan),
        in_specs=[SMEM, VMEM],
        out_specs=[VMEM] * plan.nrow,
        out_shape=[shape_of((3 * r, 2 * cw), BF16)] * plan.nrow,
        scratch_shapes=[pltpu.VMEM((plan.nrow, 3 * r, 2 * cw), BF16)],
        compiler_params=params(),
        cost_estimate=cost(0, 4 * plan.packed * D),
        name="cut_rest",
    )(meta, total)


def reduce_z(plan, pieces):
    return [pieces[0]] + [
        lax.ppermute(pieces[j], "row", plan.z_pairs(j)) for j in range(1, plan.nrow)
    ]


def sum_pieces(pieces):
    total = pieces[0].astype(F32)
    for piece in pieces[1:]:
        total = total + piece.astype(F32)
    return total


def end_rest_kernel(plan, *refs):
    pieces, (g_out, g_in, g_down) = refs[: plan.nrow], refs[plan.nrow :]
    total = sum_pieces([piece[...] for piece in pieces])
    parts_in, part_out, part_down = unpack_rest(plan, total)
    g_out[...] = part_out
    g_in[...] = jnp.concatenate(parts_in, axis=1)
    g_down[...] = part_down


def end_rest(plan, pieces):
    if not plan.aligned:
        parts_in, part_out, part_down = unpack_rest(plan, sum_pieces(pieces))
        return part_out, jnp.concatenate(parts_in, axis=1), part_down
    return pl.pallas_call(
        functools.partial(end_rest_kernel, plan),
        in_specs=[VMEM] * plan.nrow,
        out_specs=[VMEM] * 3,
        out_shape=[
            shape_of((plan.r, plan.cw), F32),
            shape_of((plan.r, 3 * plan.cw), F32),
            shape_of((plan.rf, plan.cw), F32),
        ],
        compiler_params=params(),
        cost_estimate=cost(0, 6 * plan.packed * D),
        name="end_rest",
    )(*pieces)


def end_qkv_kernel(plan, *refs):
    pieces, (g_qkv, g_gain) = refs[: plan.nrow], refs[plan.nrow :]
    width, wide = 3 * plan.cw, pad_width(plan)
    total = sum_pieces([piece[...] for piece in pieces])
    g_qkv[...] = total[:, :width]
    tail = total[:, wide - 128 :]
    g_gain[...] = tail.T


def end_qkv(plan, pieces):
    width, wide = 3 * plan.cw, pad_width(plan)
    if not plan.aligned:
        total = sum_pieces(pieces)
        return total[:, :width], total[:, width], total[:, width + 1]
    grad, gain = pl.pallas_call(
        functools.partial(end_qkv_kernel, plan),
        in_specs=[VMEM] * plan.nrow,
        out_specs=[VMEM] * 2,
        out_shape=[shape_of((plan.r, width), F32), shape_of((128, plan.r), F32)],
        compiler_params=params(),
        cost_estimate=cost(0, 6 * plan.r * EXT),
        name="end_qkv",
    )(*pieces)
    at = width - (wide - 128)
    return grad, gain[at], gain[at + 1]


def rotation_tables(plan, meta, lengths):
    ends = jnp.cumsum(lax.dynamic_index_in_dim(lengths, meta[plan.at_lo], 0, keepdims=False))
    starts = jnp.concatenate([jnp.zeros((1,), jnp.int32), ends[:-1]])
    bases = meta[plan.at_base : plan.at_base + plan.rows]
    places = (bases[:, None] + jnp.arange(plan.tok, dtype=jnp.int32)[None, :]).reshape(-1)
    passed = places[:, None] >= starts[None, :]
    positions = places - jnp.max(jnp.where(passed, starts[None, :], 0), axis=1)
    half = HD // 2
    inverse = ROPE_BASE ** (-(jnp.arange(half, dtype=F32) * (2.0 / HD)))
    angles = positions.astype(F32)[:, None] * inverse
    cosine, sine = jnp.cos(angles), jnp.sin(angles)
    return (
        jnp.concatenate([cosine] * 4, axis=1),
        jnp.concatenate([-sine, sine, -sine, sine], axis=1),
    )


def body(
    plan,
    tokens,
    lengths,
    norm_gain,
    qkv_weight,
    out_weight,
    mlp_gain,
    in_weight,
    down_weight,
    cotangent,
):
    blk, row = lax.axis_index("blk"), lax.axis_index("row")
    meta = lax.dynamic_slice(
        jnp.asarray(plan.table), (row, blk, 0), (1, 1, plan.size)
    ).reshape(plan.size)
    qkv_parts = gather_z(plan, qkv_weight)
    pieces = exchange_rows(plan, pick(plan, meta, tokens, cotangent))
    rest_parts = gather_z(plan, pack_rest(plan, out_weight, in_weight, down_weight))
    gains = jnp.pad(jnp.stack([norm_gain, mlp_gain], axis=1), ((0, 0), (0, 126)))
    cosine, sine = rotation_tables(plan, meta, lengths)
    qkv_own, qkv_other = gather_xy(plan, join_qkv(plan, meta, gains, qkv_parts))
    qkv_from = qkv_sources(plan, meta, qkv_own, qkv_other)
    queries, kv, normed, gains = project(plan, meta, cosine, sine, pieces, qkv_from)
    kv_all = [kv] + [
        lax.ppermute(kv, "blk", plan.xor_pairs(plan.member(e))) for e in range(1, plan.groups)
    ]
    rest_own, rest_other = gather_xy(plan, join_rest(plan, meta, rest_parts))
    rest_from = rest_sources(plan, meta, rest_own, rest_other)
    heads, low, lse = attend(plan, meta, lengths, queries, kv_all)
    results = middle(plan, meta, low, gains, pieces, rest_from)
    outs, (dout, dhidden, gain_two) = results[: plan.rows], results[plan.rows : plan.rows + 3]
    rest_grads = results[plan.rows + 3 :]
    if not plan.aligned:
        r, rf, nblk = plan.r, plan.rf, plan.nblk
        whole = rest_grads[0]
        blocks = [whole[D * i : D * (i + 1)].reshape(nblk, r, D) for i in range(4)]
        blocks.append(whole[4 * D :].reshape(nblk, rf, D))
        rest_grads = split_blocks(plan, meta, jnp.concatenate(blocks, axis=1))
    output = place(plan, meta, exchange_rows(plan, outs))
    rest_sum = reduce_xy(plan, *rest_grads)
    back_results = attend_back(
        plan, meta, lengths, queries, dout, heads, lse, cosine, sine, kv_all
    )
    dq, dkv = back_results[0], list(back_results[1:])
    for e in range(1, plan.groups):
        dkv[e] = lax.ppermute(dkv[e], "blk", plan.xor_pairs(plan.member(e)))
    rest_pieces = reduce_z(plan, cut_rest(plan, meta, rest_sum))
    out_grad, in_grad, down_grad = end_rest(plan, rest_pieces)
    results = back(
        plan, meta, cosine, sine, dq, normed, dhidden, gains, gain_two, dkv, pieces, qkv_from
    )
    qkv_grads = results[plan.rows :]
    if not plan.aligned:
        qkv_grads = split_blocks(plan, meta, qkv_grads[0].reshape(plan.nblk, plan.r, EXT))
    qkv_sum = reduce_xy(plan, *qkv_grads)
    input_grad = place(plan, meta, exchange_rows(plan, results[: plan.rows]))
    qkv_pieces = reduce_z(plan, cut_qkv(plan, meta, qkv_sum))
    qkv_grad, norm_gain_grad, mlp_gain_grad = end_qkv(plan, qkv_pieces)
    return (
        output,
        input_grad,
        norm_gain_grad,
        qkv_grad,
        out_grad,
        mlp_gain_grad,
        in_grad,
        down_grad,
    )


def solution(mesh):
    weights = P("blk", "row")
    acts = P("row", "blk", None)

    def run(*args):
        rows = args[0].shape[0] // mesh.shape["row"]
        tok = args[0].shape[1] // mesh.shape["blk"]
        plan = Plan(mesh, rows, tok)
        return jax.shard_map(
            functools.partial(body, plan),
            mesh=mesh,
            in_specs=(acts, P("row", None), P("blk"), weights, weights, P("blk"), weights, weights, acts),
            out_specs=(acts, acts, P("blk"), weights, weights, P("blk"), weights, weights),
            check_vma=False,
        )(*args)

    return run
```

```python
import functools
import math

import jax
import jax.numpy as jnp
import numpy as np
from jax import lax
from jax.experimental import pallas as pl
from jax.experimental.pallas import tpu as pltpu
from jax.sharding import PartitionSpec as P

D = 768
HEADS = 12
HD = 64
FF = 1152
NDOC = 8
PAIRS = HEADS // 2
EXT = 3 * D + 128

ROPE_BASE = 160000.0
NORM_EPSILON = 1e-05
MASKED = -1e30
F32 = jnp.float32
BF16 = jnp.bfloat16
NN = (((1,), (0,)), ((), ()))
NT = (((1,), (1,)), ((), ()))
TN = (((0,), (0,)), ((), ()))
VMEM_BYTES = 56 * 1024 * 1024
HALVES = 2
HALF_PAIRS = PAIRS // HALVES
HALF = D // HALVES
COSTS = {
    "prepare": 4,
    "place_rows": 2,
    "join_qkv": 2,
    "join_rest": 2,
    "project": 7,
    "attend": 9,
    "middle": 20,
    "attend_back": 12,
    "back": 12,
    "cut_qkv": 2,
    "cut_rest": 2,
    "end_rest": 2,
    "end_qkv": 2,
}
SMEM = pl.BlockSpec(memory_space=pltpu.SMEM)
ANY = pl.BlockSpec(memory_space=pl.ANY)
VMEM = pl.BlockSpec(memory_space=pltpu.VMEM)


def dot(a, b, dims):
    return lax.dot_general(a, b, dims, preferred_element_type=F32)


def shape_of(dims, dtype):
    return jax.ShapeDtypeStruct(tuple(dims), dtype)


def params():
    return pltpu.CompilerParams(vmem_limit_bytes=VMEM_BYTES)


def cost(microseconds):
    return pl.CostEstimate(
        flops=int(microseconds * 1.15e9), bytes_accessed=1 << 16, transcendentals=0
    )


def after_inputs(kernel, inputs, extra):
    def ordered_kernel(*refs):
        kernel(*refs[:inputs], *refs[inputs + extra :])

    return ordered_kernel if extra else kernel


class Plan:
    def __init__(self, mesh, rows, tok):
        self.nrow = mesh.shape["row"]
        self.nblk = mesh.shape["blk"]
        self.rows = rows
        self.tok = tok
        self.local = rows * tok
        self.chips = self.nblk // 2
        self.bits = self.chips.bit_length() - 1
        self.groups = self.nblk // rows
        self.r = D // self.nblk
        self.rf = FF // self.nblk
        self.cw = D // self.nrow
        self.aligned = self.r % 16 == 0 and self.rf % 16 == 0
        self.packed = 4 * self.r + self.rf
        rows_, chips, nrow = self.rows, self.chips, self.nrow
        self.at_pick = 0
        self.at_base = self.at_pick + rows_
        self.at_own = self.at_base + self.groups * rows_
        self.at_other = self.at_own + chips
        self.at_z = self.at_other + chips
        self.at_lo = self.at_z + nrow
        self.size = self.at_lo + 1
        table = np.zeros((nrow, self.nblk, self.size), np.int32)
        for z in range(nrow):
            for blk in range(self.nblk):
                chip, core = blk // 2, blk % 2
                low = chip % rows_
                entry = table[z, blk]
                for j in range(rows_):
                    entry[self.at_pick + j] = low ^ j
                for e in range(self.groups):
                    other = blk ^ self.member(e)
                    for j in range(rows_):
                        entry[self.at_base + e * rows_ + j] = (2 * ((other // 2) ^ j) + other % 2) * tok
                for j in range(chips):
                    entry[self.at_own + j] = 2 * (chip ^ self.order(core, j)) + core
                    entry[self.at_other + j] = 2 * (chip ^ self.order(1 - core, j)) + 1 - core
                for other in range(nrow):
                    entry[self.at_z + other] = other ^ z
                entry[self.at_lo] = low
        self.table = table

    def member(self, e):
        return (e & 1) | ((e >> 1) * 2 * self.rows)

    def order(self, core, j):
        if core == 0:
            return j
        return int(format(j, "0%db" % self.bits)[::-1], 2) if self.bits else 0

    def step_pairs(self, step):
        def flip(blk):
            bit = step if blk % 2 == 0 else self.bits - 1 - step
            return 2 * ((blk // 2) ^ (1 << bit)) + blk % 2

        return [(blk, flip(blk)) for blk in range(self.nblk)]

    def xor_pairs(self, mask):
        return [(blk, blk ^ mask) for blk in range(self.nblk)]

    def z_pairs(self, mask):
        return [(z, z ^ mask) for z in range(self.nrow)]


def swap_cores(plan, value):
    return lax.ppermute(value, "blk", plan.xor_pairs(1))


def gather_z(plan, value):
    return [value] + [lax.ppermute(value, "row", plan.z_pairs(j)) for j in range(1, plan.nrow)]


def exchange_rows(plan, pieces):
    return [pieces[0]] + [
        lax.ppermute(pieces[j], "blk", plan.xor_pairs(2 * j)) for j in range(1, plan.rows)
    ]


def gather_xy(plan, value):
    pieces = [value]
    others = [swap_cores(plan, value)]
    for step in range(plan.bits):
        pairs = plan.step_pairs(step)
        more = [lax.ppermute(piece, "blk", pairs) for piece in pieces]
        pieces = pieces + more
        others = others + [swap_cores(plan, piece) for piece in more]
    return pieces, others


def add_low(a, b):
    return (a.astype(F32) + b.astype(F32)).astype(BF16)


def reduce_start(plan, grads):
    keep_low, keep_high, send_low, send_high = grads
    high = add_low(keep_high, swap_cores(plan, send_high))
    low = add_low(keep_low, swap_cores(plan, send_low))
    return low, high


def reduce_step(plan, step, low, high):
    moved = lax.ppermute(high, "blk", plan.step_pairs(step))
    half = low.shape[0] // 2
    if half == 0:
        return add_low(low, moved)[0], None
    high = add_low(low[half:], moved[half:])
    return add_low(low[:half], moved[:half]), high


def layer_norm(values):
    average = jnp.mean(values, axis=-1, keepdims=True)
    centred = values - average
    inv_std = lax.rsqrt(jnp.mean(centred * centred, axis=-1, keepdims=True) + NORM_EPSILON)
    return centred * inv_std, inv_std


def norm_backward(grad_out, normalized, inv_std, gain):
    scaled = grad_out * gain
    inner = jnp.mean(scaled * normalized, axis=-1, keepdims=True)
    outer = jnp.mean(scaled, axis=-1, keepdims=True)
    return inv_std * (scaled - outer - normalized * inner)


def swap_halves(values):
    lane = lax.broadcasted_iota(jnp.int32, values.shape, 1)
    width = values.shape[1]
    half = HD // 2
    return jnp.where(
        (lane & half) == 0, pltpu.roll(values, width - half, 1), pltpu.roll(values, half, 1)
    )


def rotate_pair(values, cosine, sine, direction):
    return values * cosine + swap_halves(values) * (direction * sine)


def rotate_all(values, cosine, sine, direction):
    return jnp.concatenate(
        [
            rotate_pair(values[:, 128 * p : 128 * (p + 1)], cosine, sine, direction)
            for p in range(values.shape[1] // 128)
        ],
        axis=1,
    )


def prepare_kernel(plan, meta, tokens, cotangent, w_out, w_in, w_down, *refs):
    outs = refs[: plan.rows]
    for j in range(plan.rows):
        row = meta[plan.at_pick + j]
        outs[j][0] = tokens[row]
        outs[j][1] = cotangent[row]
    if plan.aligned:
        refs[plan.rows][...] = pack_rest(plan, w_out[...], w_in[...], w_down[...])


def prepare(plan, meta, tokens, cotangent, w_out, w_in, w_down):
    shapes = [shape_of((2, plan.tok, D), BF16)] * plan.rows
    if plan.aligned:
        shapes.append(shape_of((3 * plan.r, 2 * plan.cw), BF16))
    results = pl.pallas_call(
        functools.partial(prepare_kernel, plan),
        in_specs=[SMEM] + [VMEM] * 5,
        out_specs=[VMEM] * len(shapes),
        out_shape=shapes,
        compiler_params=params(),
        cost_estimate=cost(COSTS["prepare"]),
        name="prepare",
    )(meta, tokens, cotangent, w_out, w_in, w_down)
    packed = results[plan.rows] if plan.aligned else pack_rest(plan, w_out, w_in, w_down)
    return results[: plan.rows], packed


def place_kernel(plan, meta, *refs):
    pieces, out = refs[: plan.rows], refs[plan.rows]
    for j in range(plan.rows):
        out[meta[plan.at_pick + j]] = pieces[j][...]


def place(plan, meta, pieces):
    return pl.pallas_call(
        functools.partial(place_kernel, plan),
        in_specs=[SMEM] + [VMEM] * plan.rows,
        out_specs=VMEM,
        out_shape=shape_of((plan.rows, plan.tok, D), BF16),
        compiler_params=params(),
        cost_estimate=cost(COSTS["place_rows"]),
        name="place_rows",
    )(meta, *pieces)


def ordered(plan, meta, pieces):
    stacked = jnp.stack(pieces)
    return [
        lax.dynamic_index_in_dim(stacked, meta[plan.at_z + z], 0, keepdims=False)
        for z in range(plan.nrow)
    ]


def join_qkv_kernel(plan, meta, gains, *refs):
    pieces, out, held = refs[: plan.nrow], refs[plan.nrow], refs[plan.nrow + 1]
    width = 3 * plan.cw
    for j in range(plan.nrow):
        held[j] = pieces[j][...]
    for z in range(plan.nrow):
        out[:, width * z : width * (z + 1)] = held[meta[plan.at_z + z]]
    out[:, 3 * D :] = gains[...]


def join_qkv(plan, meta, gains, pieces):
    if not plan.aligned:
        return jnp.concatenate(ordered(plan, meta, pieces) + [gains], axis=1)
    return pl.pallas_call(
        functools.partial(join_qkv_kernel, plan),
        in_specs=[SMEM] + [VMEM] * (1 + plan.nrow),
        out_specs=VMEM,
        out_shape=shape_of((plan.r, EXT), BF16),
        scratch_shapes=[pltpu.VMEM((plan.nrow, plan.r, 3 * plan.cw), BF16)],
        compiler_params=params(),
        cost_estimate=cost(COSTS["join_qkv"]),
        name="join_qkv",
    )(meta, gains, *pieces)


def pack_rest(plan, w_out, w_in, w_down):
    cw = plan.cw
    left = jnp.concatenate([w_in[:, :cw], w_in[:, cw : 2 * cw], w_out], axis=0)
    blank = jnp.zeros((2 * plan.r - plan.rf, cw), BF16)
    right = jnp.concatenate([w_in[:, 2 * cw :], w_down, blank], axis=0)
    return jnp.concatenate([left, right], axis=1)


def unpack_rest(plan, piece):
    r, rf, cw = plan.r, plan.rf, plan.cw
    parts_in = [piece[:r, :cw], piece[r : 2 * r, :cw], piece[:r, cw:]]
    return parts_in, piece[2 * r : 3 * r, :cw], piece[r : r + rf, cw:]


def join_rest_kernel(plan, meta, *refs):
    pieces, out, held = refs[: plan.nrow], refs[plan.nrow], refs[plan.nrow + 1]
    r, cw = plan.r, plan.cw
    for j in range(plan.nrow):
        held[j] = pieces[j][...]
    for z in range(plan.nrow):
        parts_in, part_out, part_down = unpack_rest(plan, held[meta[plan.at_z + z]])
        out[:r, cw * z : cw * (z + 1)] = part_out
        for i in range(3):
            block, place_at = (3 * z + i) // plan.nrow, (3 * z + i) % plan.nrow
            out[r * (1 + block) : r * (2 + block), cw * place_at : cw * (place_at + 1)] = parts_in[i]
        out[4 * r :, cw * z : cw * (z + 1)] = part_down


def join_rest(plan, meta, pieces):
    if not plan.aligned:
        parts = [unpack_rest(plan, piece) for piece in ordered(plan, meta, pieces)]
        w_in = jnp.concatenate([part for item in parts for part in item[0]], axis=1)
        blocks = [jnp.concatenate([item[1] for item in parts], axis=1)]
        blocks += [w_in[:, D * t : D * (t + 1)] for t in range(3)]
        blocks += [jnp.concatenate([item[2] for item in parts], axis=1)]
        return jnp.concatenate(blocks, axis=0)
    return pl.pallas_call(
        functools.partial(join_rest_kernel, plan),
        in_specs=[SMEM] + [VMEM] * plan.nrow,
        out_specs=VMEM,
        out_shape=shape_of((plan.packed, D), BF16),
        scratch_shapes=[pltpu.VMEM((plan.nrow, 3 * plan.r, 2 * plan.cw), BF16)],
        compiler_params=params(),
        cost_estimate=cost(COSTS["join_rest"]),
        name="join_rest",
    )(meta, *pieces)


def by_block(plan, meta, own, other):
    stacked = jnp.stack(own + other)
    places = meta[plan.at_own : plan.at_other + plan.chips]
    return jnp.zeros_like(stacked).at[places].set(stacked)


def split_blocks(plan, meta, blocks):
    half = plan.chips // 2
    return [
        jnp.take(blocks, meta[plan.at_own + half * i : plan.at_own + half * (i + 1)], axis=0)
        for i in range(4)
    ]


def qkv_sources(plan, meta, own, other):
    if plan.aligned:
        return own + other
    return [by_block(plan, meta, own, other).reshape(D, EXT)]


def rest_sources(plan, meta, own, other):
    if plan.aligned:
        return own + other
    blocks = by_block(plan, meta, own, other)
    r = plan.r
    parts = [blocks[:, r * i : r * (i + 1)].reshape(D, D) for i in range(4)]
    parts.append(blocks[:, 4 * r :].reshape(FF, D))
    return [jnp.concatenate(parts, axis=0)]


def block_size(plan):
    return (plan.r, plan.rf) if plan.aligned else (D, FF)


def block_of(plan, meta, index):
    return meta[plan.at_own + index] if plan.aligned else 0


def rows_at(index, size):
    if isinstance(index, int):
        return pl.ds(index * size, size)
    return pl.ds(pl.multiple_of(index * size, size), size)


def qkv_copies(plan, meta, sources, w_ref, sems):
    r, _ = block_size(plan)
    return [
        pltpu.make_async_copy(source, w_ref.at[rows_at(block_of(plan, meta, i), r)], sems.at[i])
        for i, source in enumerate(sources)
    ]


def rest_copies(plan, meta, sources, w_out, w_in, w_down, sems):
    r, rf = block_size(plan)
    found = [[], [], []]
    for i, source in enumerate(sources):
        block = block_of(plan, meta, i)
        rows = rows_at(block, r)
        found[0].append(
            pltpu.make_async_copy(source.at[pl.ds(0, r)], w_out.at[rows], sems.at[5 * i])
        )
        for t in range(3):
            found[1].append(
                pltpu.make_async_copy(
                    source.at[pl.ds((1 + t) * r, r)], w_in.at[t, rows], sems.at[5 * i + 1 + t]
                )
            )
        found[2].append(
            pltpu.make_async_copy(
                source.at[pl.ds(4 * r, rf)], w_down.at[rows_at(block, rf)], sems.at[5 * i + 4]
            )
        )
    return found


def grad_target(plan, grads, index):
    if not plan.aligned:
        return grads[0]
    half = plan.chips // 2
    return grads[index // half].at[index % half]


def grad_blocks(plan, height, width):
    return [shape_of((plan.chips // 2, height, width), BF16)] * 4


def source_count(plan):
    return 2 * plan.chips if plan.aligned else 1


def qkv_kernel(plan, meta, cos_ref, sin_ref, *refs):
    x_refs = refs[: plan.rows]
    count = source_count(plan)
    sources = refs[plan.rows : plan.rows + count]
    q_ref = refs[plan.rows + count]
    kv_refs = refs[plan.rows + count + 1 : plan.rows + count + 1 + HALVES]
    n_ref, gain_ref, w_ref, sems = refs[plan.rows + count + 1 + HALVES :]
    copies = qkv_copies(plan, meta, sources, w_ref, sems)
    for copy in copies:
        copy.start()
    units = [layer_norm(x_refs[j][0].astype(F32))[0] for j in range(plan.rows)]
    for copy in copies:
        copy.wait()
    gain_ref[...] = w_ref[:, 3 * D :].astype(F32).T[:8, :]
    for j in range(plan.rows):
        n_ref[plan.tok * j : plan.tok * (j + 1), :] = (units[j] * gain_ref[0:1, :]).astype(BF16)
    cosine, sine = cos_ref[...], sin_ref[...]
    normed = n_ref[...]
    queries = dot(normed, w_ref[:, :D], NN)
    q_ref[...] = rotate_all(queries, cosine, sine, 1.0).astype(BF16)
    keys = rotate_all(dot(normed, w_ref[:, D : 2 * D], NN), cosine, sine, 1.0).astype(BF16)
    values = dot(normed, w_ref[:, 2 * D : 3 * D], NN).astype(BF16)
    for h in range(HALVES):
        kv_refs[h][0] = keys[:, HALF * h : HALF * (h + 1)]
        kv_refs[h][1] = values[:, HALF * h : HALF * (h + 1)]


def project(plan, meta, cosine, sine, pieces, sources, after):
    local = plan.local
    count = len(sources)
    inputs = [meta, cosine, sine, *pieces, *sources]
    return pl.pallas_call(
        after_inputs(functools.partial(qkv_kernel, plan), len(inputs), len(after)),
        in_specs=[SMEM, VMEM, VMEM] + [VMEM] * plan.rows + [ANY] * (count + len(after)),
        out_specs=[VMEM] * (3 + HALVES),
        out_shape=[shape_of((local, D), BF16)]
        + [shape_of((2, local, HALF), BF16)] * HALVES
        + [shape_of((local, D), BF16), shape_of((8, D), F32)],
        scratch_shapes=[pltpu.VMEM((D, EXT), BF16), pltpu.SemaphoreType.DMA((count,))],
        compiler_params=params(),
        cost_estimate=cost(COSTS["project"]),
        name="project",
    )(*inputs, *after)


def fill_docs(plan, meta, lengths, kdoc, qdoc):
    low = meta[plan.at_lo]
    ends = []
    passed = jnp.int32(0)
    for n in range(NDOC):
        passed = passed + lengths[low, n]
        ends.append(passed)

    def docs(places):
        total = jnp.zeros(places.shape, jnp.int32)
        for end in ends:
            total = total + (places >= end).astype(jnp.int32)
        return total

    tok = plan.tok
    for i in range(plan.groups * plan.rows):
        first = meta[plan.at_base + i]
        kdoc[i * tok : (i + 1) * tok, :] = docs(
            first + lax.broadcasted_iota(jnp.int32, (tok, 128), 0)
        )
    for i in range(plan.rows):
        first = meta[plan.at_base + i]
        qdoc[:, i * tok : (i + 1) * tok] = docs(
            first + lax.broadcasted_iota(jnp.int32, (8, tok), 1)
        )


def head_part(pair, head):
    lane = lax.broadcasted_iota(jnp.int32, pair.shape, 1)
    keep = (lane < HD) if head == 0 else (lane >= HD)
    return jnp.where(keep, pair, jnp.zeros_like(pair))


def same_docs(kdoc, qdoc, first, size, q0, width):
    key_docs = jnp.concatenate([kdoc[first : first + size, :]] * (width // 128), axis=1)
    return key_docs == qdoc[0:1, q0 : q0 + width]


def attend_kernel(plan, width, meta, lengths, q_ref, *refs):
    groups, local = plan.groups, plan.local
    kv = refs[:groups]
    o_ref, low_ref, lse_ref, kdoc, qdoc, s_ref = refs[groups:]

    @pl.when(pl.program_id(0) == 0)
    def _():
        fill_docs(plan, meta, lengths, kdoc, qdoc)

    values_t = [kv[e][1].T for e in range(groups)]
    for first in range(0, local, width):
        rows = slice(first, first + width)
        queries = q_ref[rows, :] * jnp.asarray(1.0 / math.sqrt(HD), BF16)
        parts = []
        for h in range(2):
            head_queries = head_part(queries, h)
            top = jnp.full((1, width), MASKED, F32)
            for e in range(groups):
                scores = dot(kv[e][0], head_queries, NT)
                mask = same_docs(kdoc, qdoc, e * local, local, first, width)
                scores = jnp.where(mask, scores, MASKED)
                s_ref[h, e * local : (e + 1) * local, :] = scores
                top = jnp.maximum(top, jnp.max(scores, axis=0, keepdims=True))
            total = jnp.zeros((1, width), F32)
            weighted = jnp.zeros((HD, width), F32)
            for e in range(groups):
                probs = jnp.exp(s_ref[h, e * local : (e + 1) * local, :] - top)
                total = total + jnp.sum(probs, axis=0, keepdims=True)
                weighted = weighted + dot(
                    values_t[e][h * HD : (h + 1) * HD, :], probs.astype(BF16), NN
                )
            parts.append(weighted / total)
            lse_ref[0, h : h + 1, rows] = top + jnp.log(total)
        heads = jnp.concatenate(parts, axis=0).T
        o_ref[rows, :] = heads
        low_ref[rows, :] = heads.astype(BF16)


def attend(plan, part, meta, lengths, queries, kv, after):
    local, groups = plan.local, plan.groups
    width = min(512, local)
    skip = part * HALF_PAIRS
    pair = pl.BlockSpec((local, 128), lambda p: (0, p))
    pair_q = pl.BlockSpec((local, 128), lambda p: (0, p + skip))
    pair_kv = pl.BlockSpec((2, local, 128), lambda p: (0, 0, p))
    inputs = [meta, lengths, queries, *kv]
    return pl.pallas_call(
        after_inputs(
            functools.partial(attend_kernel, plan, width), len(inputs), len(after)
        ),
        grid=(HALF_PAIRS,),
        in_specs=[SMEM, SMEM, pair_q] + [pair_kv] * groups + [ANY] * len(after),
        out_specs=[pair, pair, pl.BlockSpec((1, 2, local), lambda p: (p, 0, 0))],
        out_shape=[
            shape_of((local, HALF), F32),
            shape_of((local, HALF), BF16),
            shape_of((HALF_PAIRS, 2, local), F32),
        ],
        scratch_shapes=[
            pltpu.VMEM((groups * local, 128), jnp.int32),
            pltpu.VMEM((8, local), jnp.int32),
            pltpu.VMEM((2, groups * local, width), F32),
        ],
        compiler_params=params(),
        cost_estimate=cost(COSTS["attend"]),
        name="attend",
    )(*inputs, *after)


def attend_back_kernel(
    plan, width, meta, lengths, q_ref, do_ref, o_ref, lse_ref, cos_ref, sin_ref, *refs
):
    groups, local = plan.groups, plan.local
    kv = refs[:groups]
    dq_ref = refs[groups]
    dkv = refs[groups + 1 : 2 * groups + 1]
    kdoc, qdoc, held = refs[2 * groups + 1 :]

    @pl.when(pl.program_id(0) == 0)
    def _():
        fill_docs(plan, meta, lengths, kdoc, qdoc)

    keys_t = [kv[e][0].T for e in range(groups)]
    scale = 1.0 / math.sqrt(HD)
    for first in range(0, local, width):
        rows = slice(first, first + width)
        queries = q_ref[rows, :] * jnp.asarray(scale, BF16)
        dout = do_ref[rows, :]
        product = (dout.astype(F32) * o_ref[rows, :]).T
        parts = []
        for h in range(2):
            head_queries = head_part(queries, h)
            head_dout = head_part(dout, h)
            lse = lse_ref[0, h : h + 1, rows]
            delta = jnp.sum(product[h * HD : (h + 1) * HD, :], axis=0, keepdims=True)
            grad_queries = jnp.zeros((HD, width), F32)
            for e in range(groups):
                scores = dot(kv[e][0], head_queries, NT)
                mask = same_docs(kdoc, qdoc, e * local, local, first, width)
                probs = jnp.exp(jnp.where(mask, scores, MASKED) - lse)
                dprobs = dot(kv[e][1], head_dout, NT)
                dscores = (probs * (dprobs - delta)).astype(BF16)
                grad_values = dot(probs.astype(BF16), head_dout, NN)
                grad_keys = dot(dscores, head_queries, NN)
                if first == 0 and h == 0:
                    held[e, 0] = grad_keys
                    held[e, 1] = grad_values
                else:
                    held[e, 0] += grad_keys
                    held[e, 1] += grad_values
                grad_queries = grad_queries + dot(
                    keys_t[e][h * HD : (h + 1) * HD, :], dscores, NN
                )
            parts.append(grad_queries)
        grad = jnp.concatenate(parts, axis=0).T * scale
        dq_ref[rows, :] = rotate_pair(grad, cos_ref[rows, :], sin_ref[rows, :], -1.0).astype(BF16)
    for e in range(groups):
        dkv[e][...] = held[e].astype(BF16)


def attend_back(plan, part, meta, lengths, queries, dout, heads, lse, cosine, sine, kv, after):
    local, groups = plan.local, plan.groups
    width = min(256, local)
    skip = part * HALF_PAIRS
    pair = pl.BlockSpec((local, 128), lambda p: (0, p))
    pair_q = pl.BlockSpec((local, 128), lambda p: (0, p + skip))
    inputs = [meta, lengths, queries, dout, heads, lse, cosine, sine, *kv]
    table = pl.BlockSpec((local, 128), lambda p: (0, 0))
    pair_kv = pl.BlockSpec((2, local, 128), lambda p: (0, 0, p))
    return pl.pallas_call(
        after_inputs(
            functools.partial(attend_back_kernel, plan, width), len(inputs), len(after)
        ),
        grid=(HALF_PAIRS,),
        in_specs=[
            SMEM,
            SMEM,
            pair_q,
            pair_q,
            pair,
            pl.BlockSpec((1, 2, local), lambda p: (p, 0, 0)),
            table,
            table,
        ]
        + [pair_kv] * groups
        + [ANY] * len(after),
        out_specs=[pair] + [pair_kv] * groups,
        out_shape=[shape_of((local, HALF), BF16)] + [shape_of((2, local, HALF), BF16)] * groups,
        scratch_shapes=[
            pltpu.VMEM((groups * local, 128), jnp.int32),
            pltpu.VMEM((8, local), jnp.int32),
            pltpu.VMEM((groups, 2, local, 128), F32),
        ],
        compiler_params=params(),
        cost_estimate=cost(COSTS["attend_back"]),
        name="attend_back",
    )(*inputs, *after)


def middle_kernel(plan, meta, gain_ref, *refs):
    rows, tok, local = plan.rows, plan.tok, plan.local
    low_refs, refs = refs[:HALVES], refs[HALVES:]
    count = source_count(plan)
    x_refs = refs[:rows]
    sources = refs[rows : rows + count]
    refs = refs[rows + count :]
    out_refs = refs[:rows]
    do_ref, dh_ref, gain_grad_ref = refs[rows : rows + 3]
    grads = refs[rows + 3 : rows + 3 + (4 if plan.aligned else 1)]
    (
        w_out,
        w_in,
        w_down,
        h_ref,
        n_ref,
        gu_ref,
        mid_ref,
        dgu_ref,
        g_out,
        g_in,
        g_down,
        in_sems,
        out_sems,
    ) = refs[rows + 3 + len(grads) :]
    copies = rest_copies(plan, meta, sources, w_out, w_in, w_down, in_sems)
    for group in copies:
        for copy in group:
            copy.start()
    for copy in copies[0]:
        copy.wait()
    low = jnp.concatenate([low_ref[...] for low_ref in low_refs], axis=1)
    branch = dot(low, w_out[...], NN)
    for j in range(rows):
        part = slice(tok * j, tok * (j + 1))
        h_ref[part, :] = x_refs[j][0].astype(F32) + branch[part, :]
    gain = gain_ref[1:2, :]
    unit, inv_std = layer_norm(h_ref[...])
    n_ref[...] = (unit * gain).astype(BF16)
    for copy in copies[1]:
        copy.wait()
    for t in range(3):
        gu_ref[:, D * t : D * (t + 1)] = dot(n_ref[...], w_in[t], NN)
    for copy in copies[2]:
        copy.wait()
    dy = jnp.concatenate([x_refs[j][1] for j in range(rows)], axis=0)
    size = FF // 3
    for f in range(3):
        cols = slice(size * f, size * (f + 1))
        up_cols = slice(FF + size * f, FF + size * (f + 1))
        gate = gu_ref[:, cols]
        up = gu_ref[:, up_cols]
        below = 0.5 + 0.5 * lax.erf(gate * math.sqrt(0.5))
        active = gate * below
        mid_ref[:, cols] = (active * up).astype(BF16)
        slope = below + gate * jnp.exp(-0.5 * gate * gate) * (1.0 / math.sqrt(2.0 * math.pi))
        dmid = dot(dy, w_down[cols, :], NT)
        dgu_ref[:, cols] = (dmid * up * slope).astype(BF16)
        dgu_ref[:, up_cols] = (dmid * active).astype(BF16)
    mixed = dot(mid_ref[...], w_down[...], NN)
    for j in range(rows):
        part = slice(tok * j, tok * (j + 1))
        out_refs[j][...] = (h_ref[part, :] + mixed[part, :]).astype(BF16)
    grad_normed = dot(dgu_ref[:, :D], w_in[0], NT)
    for t in range(1, 3):
        grad_normed = grad_normed + dot(dgu_ref[:, D * t : D * (t + 1)], w_in[t], NT)
    unit, inv_std = layer_norm(h_ref[...])
    gain_grad_ref[...] = jnp.broadcast_to(
        jnp.sum(grad_normed * unit, axis=0, keepdims=True), (8, D)
    )
    grad_hidden = dy.astype(F32) + norm_backward(grad_normed, unit, inv_std, gain)
    dh_ref[...] = grad_hidden
    branch_grad = grad_hidden.astype(BF16)
    do_ref[...] = dot(branch_grad, w_out[...], NT).astype(BF16)
    for h in range(HALVES):
        g_out[HALF * h : HALF * (h + 1), :] = dot(low_refs[h][...], branch_grad, TN).astype(BF16)
    for t in range(3):
        g_in[t] = dot(n_ref[...], dgu_ref[:, D * t : D * (t + 1)], TN).astype(BF16)
    g_down[...] = dot(mid_ref[...], dy, TN).astype(BF16)
    r, rf = block_size(plan)
    done = []
    for i in range(count):
        block = block_of(plan, meta, i)
        target = grad_target(plan, grads, i)
        at = rows_at(block, r)
        done.append(
            pltpu.make_async_copy(g_out.at[at], target.at[pl.ds(0, r)], out_sems.at[5 * i])
        )
        for t in range(3):
            done.append(
                pltpu.make_async_copy(
                    g_in.at[t, at], target.at[pl.ds((1 + t) * r, r)], out_sems.at[5 * i + 1 + t]
                )
            )
        done.append(
            pltpu.make_async_copy(
                g_down.at[rows_at(block, rf)], target.at[pl.ds(4 * r, rf)], out_sems.at[5 * i + 4]
            )
        )
    for copy in done:
        copy.start()
    for copy in done:
        copy.wait()


def middle(plan, meta, low, gains, pieces, sources):
    local, rows, tok = plan.local, plan.rows, plan.tok
    count = len(sources)
    total = 4 * D + FF
    if plan.aligned:
        grads = grad_blocks(plan, plan.packed, D)
    else:
        grads = [shape_of((total, D), BF16)]
    return pl.pallas_call(
        functools.partial(middle_kernel, plan),
        in_specs=[SMEM, VMEM] + [VMEM] * (HALVES + rows) + [ANY] * count,
        out_specs=[VMEM] * (rows + 3) + [ANY] * len(grads),
        out_shape=[shape_of((tok, D), BF16)] * rows
        + [shape_of((local, D), BF16), shape_of((local, D), F32), shape_of((8, D), F32)]
        + grads,
        scratch_shapes=[
            pltpu.VMEM((D, D), BF16),
            pltpu.VMEM((3, D, D), BF16),
            pltpu.VMEM((FF, D), BF16),
            pltpu.VMEM((local, D), F32),
            pltpu.VMEM((local, D), BF16),
            pltpu.VMEM((local, 2 * FF), F32),
            pltpu.VMEM((local, FF), BF16),
            pltpu.VMEM((local, 2 * FF), BF16),
            pltpu.VMEM((D, D), BF16),
            pltpu.VMEM((3, D, D), BF16),
            pltpu.VMEM((FF, D), BF16),
            pltpu.SemaphoreType.DMA((5 * count,)),
            pltpu.SemaphoreType.DMA((5 * count,)),
        ],
        compiler_params=params(),
        cost_estimate=cost(COSTS["middle"]),
        name="middle",
    )(meta, gains, *low, *pieces, *sources)


def back_kernel(plan, meta, cos_ref, sin_ref, n_ref, dh_ref, gain_ref, g2_ref, *refs):
    rows, tok, groups = plan.rows, plan.tok, plan.groups
    count = source_count(plan)
    dq_refs, refs = refs[:HALVES], refs[HALVES:]
    dkv, refs = refs[: HALVES * groups], refs[HALVES * groups :]
    x_refs = refs[:rows]
    sources = refs[rows : rows + count]
    refs = refs[rows + count :]
    in_refs = refs[:rows]
    grads = refs[rows : rows + (4 if plan.aligned else 1)]
    w_ref, dp_ref, g_ref, in_sems, out_sems = refs[rows + len(grads) :]
    copies = qkv_copies(plan, meta, sources, w_ref, in_sems)
    for copy in copies:
        copy.start()
    for h in range(HALVES):
        cols = slice(HALF * h, HALF * (h + 1))
        parts = dkv[groups * h : groups * (h + 1)]
        grad_keys = sum_pieces([part[0] for part in parts])
        dp_ref[0, :, cols] = dq_refs[h][...]
        dp_ref[1, :, cols] = rotate_all(grad_keys, cos_ref[...], sin_ref[...], -1.0).astype(BF16)
        dp_ref[2, :, cols] = sum_pieces([part[1] for part in parts]).astype(BF16)
    for t in range(3):
        g_ref[:, D * t : D * (t + 1)] = dot(n_ref[...], dp_ref[t], TN).astype(BF16)
    for copy in copies:
        copy.wait()
    grad_normed = dot(dp_ref[0], w_ref[:, :D], NT)
    for t in range(1, 3):
        grad_normed = grad_normed + dot(dp_ref[t], w_ref[:, D * t : D * (t + 1)], NT)
    gain_grad = jnp.zeros((1, D), F32)
    for j in range(rows):
        part = slice(tok * j, tok * (j + 1))
        unit, inv_std = layer_norm(x_refs[j][0].astype(F32))
        grad = grad_normed[part, :]
        gain_grad = gain_grad + jnp.sum(grad * unit, axis=0, keepdims=True)
        back = norm_backward(grad, unit, inv_std, gain_ref[0:1, :])
        in_refs[j][...] = (dh_ref[part, :] + back).astype(BF16)
    which = lax.broadcasted_iota(jnp.int32, (128, D), 0)
    both = jnp.where(which == 0, gain_grad, jnp.where(which == 1, g2_ref[0:1, :], 0.0))
    g_ref[:, 3 * D :] = both.T.astype(BF16)
    r, _ = block_size(plan)
    done = []
    for i in range(count):
        target = grad_target(plan, grads, i)
        at = rows_at(block_of(plan, meta, i), r)
        done.append(pltpu.make_async_copy(g_ref.at[at], target, out_sems.at[i]))
    for copy in done:
        copy.start()
    for copy in done:
        copy.wait()


def back(
    plan, meta, cosine, sine, normed, dhidden, gains, gain_two, dq, dkv, pieces, sources, after
):
    local, rows, tok = plan.local, plan.rows, plan.tok
    count = len(sources)
    inputs = [meta, cosine, sine, normed, dhidden, gains, gain_two, *dq, *dkv, *pieces, *sources]
    if plan.aligned:
        grads = grad_blocks(plan, plan.r, EXT)
    else:
        grads = [shape_of((D, EXT), BF16)]
    return pl.pallas_call(
        after_inputs(functools.partial(back_kernel, plan), len(inputs), len(after)),
        in_specs=[SMEM]
        + [VMEM] * (6 + HALVES * (1 + plan.groups) + rows)
        + [ANY] * (count + len(after)),
        out_specs=[VMEM] * rows + [ANY] * len(grads),
        out_shape=[shape_of((tok, D), BF16)] * rows + grads,
        scratch_shapes=[
            pltpu.VMEM((D, EXT), BF16),
            pltpu.VMEM((3, local, D), BF16),
            pltpu.VMEM((D, EXT), BF16),
            pltpu.SemaphoreType.DMA((count,)),
            pltpu.SemaphoreType.DMA((count,)),
        ],
        compiler_params=params(),
        cost_estimate=cost(COSTS["back"]),
        name="back",
    )(*inputs, *after)


def pad_width(plan):
    return -(-(3 * plan.cw + 2) // 128) * 128


def cut_qkv_kernel(plan, meta, total, *refs):
    outs, held = refs[: plan.nrow], refs[plan.nrow]
    width, wide = 3 * plan.cw, pad_width(plan)
    for z in range(plan.nrow):
        place_at = meta[plan.at_z + z]
        held[place_at, :, :width] = total[:, width * z : width * (z + 1)]
        held[place_at, :, width:] = total[:, 3 * D : 3 * D + wide - width]
    for j in range(plan.nrow):
        outs[j][...] = held[j]


def cut_qkv(plan, meta, total):
    width, wide = 3 * plan.cw, pad_width(plan)
    if not plan.aligned:
        parts = [
            jnp.concatenate(
                [total[:, width * z : width * (z + 1)], total[:, 3 * D : 3 * D + wide - width]],
                axis=1,
            )
            for z in range(plan.nrow)
        ]
        return ordered(plan, meta, parts)
    return pl.pallas_call(
        functools.partial(cut_qkv_kernel, plan),
        in_specs=[SMEM, VMEM],
        out_specs=[VMEM] * plan.nrow,
        out_shape=[shape_of((plan.r, wide), BF16)] * plan.nrow,
        scratch_shapes=[pltpu.VMEM((plan.nrow, plan.r, wide), BF16)],
        compiler_params=params(),
        cost_estimate=cost(COSTS["cut_qkv"]),
        name="cut_qkv",
    )(meta, total)


def cut_rest_kernel(plan, meta, total, *refs):
    outs, held = refs[: plan.nrow], refs[plan.nrow]
    r, rf, cw = plan.r, plan.rf, plan.cw
    for z in range(plan.nrow):
        place_at = meta[plan.at_z + z]
        cols = slice(cw * z, cw * (z + 1))
        parts = []
        for i in range(3):
            block, at = (3 * z + i) // plan.nrow, (3 * z + i) % plan.nrow
            parts.append(total[r * (1 + block) : r * (2 + block), cw * at : cw * (at + 1)])
        held[place_at, :r, :] = jnp.concatenate([parts[0], parts[2]], axis=1)
        held[place_at, r : 2 * r, :] = jnp.concatenate(
            [parts[1], total[4 * r : 5 * r, cols]], axis=1
        )
        rest = total[5 * r : 4 * r + rf, cols]
        blank = jnp.zeros((2 * r - rf, cw), BF16)
        held[place_at, 2 * r :, :] = jnp.concatenate(
            [total[:r, cols], jnp.concatenate([rest, blank], axis=0)], axis=1
        )
    for j in range(plan.nrow):
        outs[j][...] = held[j]


def cut_rest(plan, meta, total):
    r, cw = plan.r, plan.cw
    if not plan.aligned:
        grad_in = jnp.concatenate([total[r * (1 + t) : r * (2 + t)] for t in range(3)], axis=1)
        parts = [
            pack_rest(
                plan,
                total[:r, cw * z : cw * (z + 1)],
                grad_in[:, 3 * cw * z : 3 * cw * (z + 1)],
                total[4 * r :, cw * z : cw * (z + 1)],
            )
            for z in range(plan.nrow)
        ]
        return ordered(plan, meta, parts)
    return pl.pallas_call(
        functools.partial(cut_rest_kernel, plan),
        in_specs=[SMEM, VMEM],
        out_specs=[VMEM] * plan.nrow,
        out_shape=[shape_of((3 * r, 2 * cw), BF16)] * plan.nrow,
        scratch_shapes=[pltpu.VMEM((plan.nrow, 3 * r, 2 * cw), BF16)],
        compiler_params=params(),
        cost_estimate=cost(COSTS["cut_rest"]),
        name="cut_rest",
    )(meta, total)


def reduce_z(plan, pieces):
    return [pieces[0]] + [
        lax.ppermute(pieces[j], "row", plan.z_pairs(j)) for j in range(1, plan.nrow)
    ]


def sum_pieces(pieces):
    total = pieces[0].astype(F32)
    for piece in pieces[1:]:
        total = total + piece.astype(F32)
    return total


def end_rest_kernel(plan, *refs):
    pieces, (g_out, g_in, g_down) = refs[: plan.nrow], refs[plan.nrow :]
    total = sum_pieces([piece[...] for piece in pieces])
    parts_in, part_out, part_down = unpack_rest(plan, total)
    g_out[...] = part_out
    g_in[...] = jnp.concatenate(parts_in, axis=1)
    g_down[...] = part_down


def end_rest(plan, pieces):
    if not plan.aligned:
        parts_in, part_out, part_down = unpack_rest(plan, sum_pieces(pieces))
        return part_out, jnp.concatenate(parts_in, axis=1), part_down
    return pl.pallas_call(
        functools.partial(end_rest_kernel, plan),
        in_specs=[VMEM] * plan.nrow,
        out_specs=[VMEM] * 3,
        out_shape=[
            shape_of((plan.r, plan.cw), F32),
            shape_of((plan.r, 3 * plan.cw), F32),
            shape_of((plan.rf, plan.cw), F32),
        ],
        compiler_params=params(),
        cost_estimate=cost(COSTS["end_rest"]),
        name="end_rest",
    )(*pieces)


def end_qkv_kernel(plan, *refs):
    pieces, (g_qkv, g_gain) = refs[: plan.nrow], refs[plan.nrow :]
    width, wide = 3 * plan.cw, pad_width(plan)
    total = sum_pieces([piece[...] for piece in pieces])
    g_qkv[...] = total[:, :width]
    tail = total[:, wide - 128 :]
    g_gain[...] = tail.T


def end_qkv(plan, pieces):
    width, wide = 3 * plan.cw, pad_width(plan)
    if not plan.aligned:
        total = sum_pieces(pieces)
        return total[:, :width], total[:, width], total[:, width + 1]
    grad, gain = pl.pallas_call(
        functools.partial(end_qkv_kernel, plan),
        in_specs=[VMEM] * plan.nrow,
        out_specs=[VMEM] * 2,
        out_shape=[shape_of((plan.r, width), F32), shape_of((128, plan.r), F32)],
        compiler_params=params(),
        cost_estimate=cost(COSTS["end_qkv"]),
        name="end_qkv",
    )(*pieces)
    at = width - (wide - 128)
    return grad, gain[at], gain[at + 1]


def rotation_tables(plan, meta, lengths):
    ends = jnp.cumsum(lax.dynamic_index_in_dim(lengths, meta[plan.at_lo], 0, keepdims=False))
    starts = jnp.concatenate([jnp.zeros((1,), jnp.int32), ends[:-1]])
    bases = meta[plan.at_base : plan.at_base + plan.rows]
    places = (bases[:, None] + jnp.arange(plan.tok, dtype=jnp.int32)[None, :]).reshape(-1)
    passed = places[:, None] >= starts[None, :]
    positions = places - jnp.max(jnp.where(passed, starts[None, :], 0), axis=1)
    half = HD // 2
    inverse = ROPE_BASE ** (-(jnp.arange(half, dtype=F32) * (2.0 / HD)))
    angles = positions.astype(F32)[:, None] * inverse
    cosine, sine = jnp.cos(angles), jnp.sin(angles)
    return (
        jnp.concatenate([cosine] * 4, axis=1),
        jnp.concatenate([-sine, sine, -sine, sine], axis=1),
    )


def body(
    plan,
    tokens,
    lengths,
    norm_gain,
    qkv_weight,
    out_weight,
    mlp_gain,
    in_weight,
    down_weight,
    cotangent,
):
    blk, row = lax.axis_index("blk"), lax.axis_index("row")
    meta = lax.dynamic_slice(
        jnp.asarray(plan.table), (row, blk, 0), (1, 1, plan.size)
    ).reshape(plan.size)
    qkv_parts = gather_z(plan, qkv_weight)
    cut, packed = prepare(plan, meta, tokens, cotangent, out_weight, in_weight, down_weight)
    pieces = exchange_rows(plan, cut)
    rest_parts = gather_z(plan, packed)
    gains = jnp.pad(jnp.stack([norm_gain, mlp_gain], axis=1), ((0, 0), (0, 126)))
    cosine, sine = rotation_tables(plan, meta, lengths)
    qkv_own, qkv_other = gather_xy(plan, join_qkv(plan, meta, gains, qkv_parts))
    qkv_from = qkv_sources(plan, meta, qkv_own, qkv_other)
    joined = join_rest(plan, meta, rest_parts)
    results = project(plan, meta, cosine, sine, pieces, qkv_from, [joined])
    queries, kv, (normed, gains) = results[0], results[1 : 1 + HALVES], results[1 + HALVES :]
    kv = [
        [part]
        + [
            lax.ppermute(part, "blk", plan.xor_pairs(plan.member(e)))
            for e in range(1, plan.groups)
        ]
        for part in kv
    ]
    rest_own, rest_other = gather_xy(plan, joined)
    rest_from = rest_sources(plan, meta, rest_own, rest_other)
    heads, low, lse = [None] * HALVES, [None] * HALVES, [None] * HALVES
    for h in range(HALVES):
        after = [] if h == 0 else [low[h - 1]] + rest_own[1:3] + rest_other[:1]
        heads[h], low[h], lse[h] = attend(plan, h, meta, lengths, queries, kv[h], after)
    results = middle(plan, meta, low, gains, pieces, rest_from)
    outs, (dout, dhidden, gain_two) = results[: plan.rows], results[plan.rows : plan.rows + 3]
    rest_grads = results[plan.rows + 3 :]
    if not plan.aligned:
        r, rf, nblk = plan.r, plan.rf, plan.nblk
        whole = rest_grads[0]
        blocks = [whole[D * i : D * (i + 1)].reshape(nblk, r, D) for i in range(4)]
        blocks.append(whole[4 * D :].reshape(nblk, rf, D))
        rest_grads = split_blocks(plan, meta, jnp.concatenate(blocks, axis=1))
    outs = exchange_rows(plan, outs)
    rest_low, rest_high = reduce_start(plan, rest_grads)
    dq, dkv = [None] * HALVES, [None] * HALVES
    for h in range(HALVES):
        after = [] if h == 0 else [dq[h - 1], rest_low, rest_high]
        results = attend_back(
            plan, h, meta, lengths, queries, dout, heads[h], lse[h], cosine, sine, kv[h], after
        )
        dq[h], dkv[h] = results[0], list(results[1:])
        for e in range(1, plan.groups):
            dkv[h][e] = lax.ppermute(dkv[h][e], "blk", plan.xor_pairs(plan.member(e)))
    for step in reversed(range(plan.bits)):
        rest_low, rest_high = reduce_step(plan, step, rest_low, rest_high)
        if step == plan.bits - 1:
            after = [rest_low] + ([rest_high] if plan.bits > 1 else [])
    output = place(plan, meta, outs)
    dkv = [part for parts in dkv for part in parts]
    results = back(
        plan,
        meta,
        cosine,
        sine,
        normed,
        dhidden,
        gains,
        gain_two,
        dq,
        dkv,
        pieces,
        qkv_from,
        after + [output],
    )
    rest_pieces = reduce_z(plan, cut_rest(plan, meta, rest_low))
    out_grad, in_grad, down_grad = end_rest(plan, rest_pieces)
    qkv_grads = results[plan.rows :]
    if not plan.aligned:
        qkv_grads = split_blocks(plan, meta, qkv_grads[0].reshape(plan.nblk, plan.r, EXT))
    qkv_low, qkv_high = reduce_start(plan, qkv_grads)
    for step in reversed(range(plan.bits)):
        qkv_low, qkv_high = reduce_step(plan, step, qkv_low, qkv_high)
    input_grad = place(plan, meta, exchange_rows(plan, results[: plan.rows]))
    qkv_pieces = reduce_z(plan, cut_qkv(plan, meta, qkv_low))
    qkv_grad, norm_gain_grad, mlp_gain_grad = end_qkv(plan, qkv_pieces)
    return (
        output,
        input_grad,
        norm_gain_grad,
        qkv_grad,
        out_grad,
        mlp_gain_grad,
        in_grad,
        down_grad,
    )


def solution(mesh):
    weights = P("blk", "row")
    acts = P("row", "blk", None)

    def run(*args):
        rows = args[0].shape[0] // mesh.shape["row"]
        tok = args[0].shape[1] // mesh.shape["blk"]
        plan = Plan(mesh, rows, tok)
        return jax.shard_map(
            functools.partial(body, plan),
            mesh=mesh,
            in_specs=(acts, P("row", None), P("blk"), weights, weights, P("blk"), weights, weights, acts),
            out_specs=(acts, acts, P("blk"), weights, weights, P("blk"), weights, weights),
            check_vma=False,
        )(*args)

    return run
```

```python
import functools
import math

import jax
import jax.numpy as jnp
import numpy as np
from jax import lax
from jax.experimental import pallas as pl
from jax.experimental.pallas import tpu as pltpu
from jax.sharding import PartitionSpec as P

D = 768
HEADS = 12
HD = 64
FF = 1152
NDOC = 8
PAIRS = HEADS // 2
EXT = 3 * D + 128

ROPE_BASE = 160000.0
NORM_EPSILON = 1e-05
MASKED = -1e30
F32 = jnp.float32
BF16 = jnp.bfloat16
NN = (((1,), (0,)), ((), ()))
NT = (((1,), (1,)), ((), ()))
TN = (((0,), (0,)), ((), ()))
VMEM_BYTES = 56 * 1024 * 1024
HALVES = 2
HALF_PAIRS = PAIRS // HALVES
HALF = D // HALVES
BACK_PARTS = ((0, 0, 1), (0, 1, 2), (1, 0, 3))
COSTS = {
    "prepare": 4,
    "place_rows": 2,
    "join_qkv": 2,
    "join_rest": 2,
    "project": 7,
    "attend": 9,
    "middle": 20,
    "attend_back": 12,
    "back_in": 7,
    "back_weight": 6,
    "cut_qkv": 2,
    "cut_rest": 2,
    "end_rest": 2,
    "end_qkv": 2,
}
SMEM = pl.BlockSpec(memory_space=pltpu.SMEM)
ANY = pl.BlockSpec(memory_space=pl.ANY)
VMEM = pl.BlockSpec(memory_space=pltpu.VMEM)


def dot(a, b, dims):
    return lax.dot_general(a, b, dims, preferred_element_type=F32)


def shape_of(dims, dtype):
    return jax.ShapeDtypeStruct(tuple(dims), dtype)


def params():
    return pltpu.CompilerParams(vmem_limit_bytes=VMEM_BYTES)


def cost(microseconds):
    return pl.CostEstimate(
        flops=int(microseconds * 1e6), bytes_accessed=1 << 10, transcendentals=0
    )


def tie(value, *others):
    return lax.optimization_barrier((value, *others))[0]


class Plan:
    def __init__(self, mesh, rows, tok):
        self.nrow = mesh.shape["row"]
        self.nblk = mesh.shape["blk"]
        self.rows = rows
        self.tok = tok
        self.local = rows * tok
        self.chips = self.nblk // 2
        self.bits = self.chips.bit_length() - 1
        self.groups = self.nblk // rows
        self.r = D // self.nblk
        self.rf = FF // self.nblk
        self.cw = D // self.nrow
        self.aligned = self.r % 16 == 0 and self.rf % 16 == 0
        self.packed = 4 * self.r + self.rf
        rows_, chips, nrow = self.rows, self.chips, self.nrow
        self.at_pick = 0
        self.at_base = self.at_pick + rows_
        self.at_own = self.at_base + self.groups * rows_
        self.at_other = self.at_own + chips
        self.at_z = self.at_other + chips
        self.at_lo = self.at_z + nrow
        self.size = self.at_lo + 1
        table = np.zeros((nrow, self.nblk, self.size), np.int32)
        for z in range(nrow):
            for blk in range(self.nblk):
                chip, core = blk // 2, blk % 2
                low = chip % rows_
                entry = table[z, blk]
                for j in range(rows_):
                    entry[self.at_pick + j] = low ^ j
                for e in range(self.groups):
                    other = blk ^ self.member(e)
                    for j in range(rows_):
                        entry[self.at_base + e * rows_ + j] = (2 * ((other // 2) ^ j) + other % 2) * tok
                for j in range(chips):
                    entry[self.at_own + j] = 2 * (chip ^ self.order(core, j)) + core
                    entry[self.at_other + j] = 2 * (chip ^ self.order(1 - core, j)) + 1 - core
                for other in range(nrow):
                    entry[self.at_z + other] = other ^ z
                entry[self.at_lo] = low
        self.table = table

    def member(self, e):
        return (e & 1) | ((e >> 1) * 2 * self.rows)

    def order(self, core, j):
        if core == 0:
            return j
        return int(format(j, "0%db" % self.bits)[::-1], 2) if self.bits else 0

    def step_pairs(self, step):
        def flip(blk):
            bit = step if blk % 2 == 0 else self.bits - 1 - step
            return 2 * ((blk // 2) ^ (1 << bit)) + blk % 2

        return [(blk, flip(blk)) for blk in range(self.nblk)]

    def xor_pairs(self, mask):
        return [(blk, blk ^ mask) for blk in range(self.nblk)]

    def z_pairs(self, mask):
        return [(z, z ^ mask) for z in range(self.nrow)]


def swap_cores(plan, value):
    return lax.ppermute(value, "blk", plan.xor_pairs(1))


def gather_z(plan, value, behind=None):
    pieces = [value]
    for j in range(1, plan.nrow):
        source = value if behind is None else tie(value, behind[j])
        pieces.append(lax.ppermute(source, "row", plan.z_pairs(j)))
    return pieces


def exchange_rows(plan, pieces):
    return [pieces[0]] + [
        lax.ppermute(pieces[j], "blk", plan.xor_pairs(2 * j)) for j in range(1, plan.rows)
    ]


def gather_start(plan, value):
    pairs = [plan.step_pairs(step) for step in range(plan.bits)]
    first = lax.ppermute(value, "blk", pairs[0])
    second = [lax.ppermute(value, "blk", pairs[1])] if plan.bits > 1 else []
    return [value, first] + second


def gather_more(plan, pieces):
    for step in range(1, plan.bits):
        have = 1 << step
        missing = pieces[len(pieces) - have :] if step > 1 else pieces[1:2]
        pieces = pieces + [lax.ppermute(piece, "blk", plan.step_pairs(step)) for piece in missing]
    return pieces


def add_low(a, b):
    return (a.astype(F32) + b.astype(F32)).astype(BF16)


def reduce_start(plan, grads):
    keep_low, keep_high, send_low, send_high = grads
    other_high = swap_cores(plan, send_high)
    return keep_low, keep_high, swap_cores(plan, send_low), other_high


def reduce_step(plan, step, low, high):
    moved = lax.ppermute(high, "blk", plan.step_pairs(step))
    half = low.shape[0] // 2
    if half == 0:
        return add_low(low, moved)[0], None
    high = add_low(low[half:], moved[half:])
    return add_low(low[:half], moved[:half]), high


def layer_norm(values):
    average = jnp.mean(values, axis=-1, keepdims=True)
    centred = values - average
    inv_std = lax.rsqrt(jnp.mean(centred * centred, axis=-1, keepdims=True) + NORM_EPSILON)
    return centred * inv_std, inv_std


def norm_backward(grad_out, normalized, inv_std, gain):
    scaled = grad_out * gain
    inner = jnp.mean(scaled * normalized, axis=-1, keepdims=True)
    outer = jnp.mean(scaled, axis=-1, keepdims=True)
    return inv_std * (scaled - outer - normalized * inner)


def swap_halves(values):
    lane = lax.broadcasted_iota(jnp.int32, values.shape, 1)
    width = values.shape[1]
    half = HD // 2
    return jnp.where(
        (lane & half) == 0, pltpu.roll(values, width - half, 1), pltpu.roll(values, half, 1)
    )


def rotate_pair(values, cosine, sine, direction):
    return values * cosine + swap_halves(values) * (direction * sine)


def rotate_all(values, cosine, sine, direction):
    return jnp.concatenate(
        [
            rotate_pair(values[:, 128 * p : 128 * (p + 1)], cosine, sine, direction)
            for p in range(values.shape[1] // 128)
        ],
        axis=1,
    )


def prepare_kernel(plan, meta, tokens, cotangent, w_out, w_in, w_down, *refs):
    rows = plan.rows
    for j in range(rows):
        row = meta[plan.at_pick + j]
        refs[j][0] = tokens[row]
        refs[j][1] = cotangent[row]
    if plan.aligned:
        refs[rows][...] = pack_rest(plan, w_out[...], w_in[...], w_down[...])


def prepare(plan, meta, tokens, cotangent, w_out, w_in, w_down):
    rows = plan.rows
    shapes = [shape_of((2, plan.tok, D), BF16)] * rows
    if plan.aligned:
        shapes.append(shape_of((3 * plan.r, 2 * plan.cw), BF16))
    results = pl.pallas_call(
        functools.partial(prepare_kernel, plan),
        in_specs=[SMEM] + [VMEM] * 5,
        out_specs=[VMEM] * len(shapes),
        out_shape=shapes,
        compiler_params=params(),
        cost_estimate=cost(COSTS["prepare"]),
        name="prepare",
    )(meta, tokens, cotangent, w_out, w_in, w_down)
    packed = results[rows] if plan.aligned else pack_rest(plan, w_out, w_in, w_down)
    return results[:rows], packed


def place_kernel(plan, meta, *refs):
    pieces, out = refs[: plan.rows], refs[plan.rows]
    for j in range(plan.rows):
        out[meta[plan.at_pick + j]] = pieces[j][...]


def place(plan, meta, pieces):
    return pl.pallas_call(
        functools.partial(place_kernel, plan),
        in_specs=[SMEM] + [VMEM] * plan.rows,
        out_specs=VMEM,
        out_shape=shape_of((plan.rows, plan.tok, D), BF16),
        compiler_params=params(),
        cost_estimate=cost(COSTS["place_rows"]),
        name="place_rows",
    )(meta, *pieces)


def ordered(plan, meta, pieces):
    stacked = jnp.stack(pieces)
    return [
        lax.dynamic_index_in_dim(stacked, meta[plan.at_z + z], 0, keepdims=False)
        for z in range(plan.nrow)
    ]


def join_qkv_kernel(plan, meta, gains, *refs):
    pieces, out, held = refs[: plan.nrow], refs[plan.nrow], refs[plan.nrow + 1]
    width = 3 * plan.cw
    for j in range(plan.nrow):
        held[j] = pieces[j][...]
    for z in range(plan.nrow):
        out[:, width * z : width * (z + 1)] = held[meta[plan.at_z + z]]
    out[:, 3 * D :] = gains[...]


def join_qkv(plan, meta, gains, pieces):
    if not plan.aligned:
        return jnp.concatenate(ordered(plan, meta, pieces) + [gains], axis=1)
    return pl.pallas_call(
        functools.partial(join_qkv_kernel, plan),
        in_specs=[SMEM] + [VMEM] * (1 + plan.nrow),
        out_specs=VMEM,
        out_shape=shape_of((plan.r, EXT), BF16),
        scratch_shapes=[pltpu.VMEM((plan.nrow, plan.r, 3 * plan.cw), BF16)],
        compiler_params=params(),
        cost_estimate=cost(COSTS["join_qkv"]),
        name="join_qkv",
    )(meta, gains, *pieces)


def pack_rest(plan, w_out, w_in, w_down, blank=None):
    cw = plan.cw
    left = jnp.concatenate([w_in[:, :cw], w_in[:, cw : 2 * cw], w_out], axis=0)
    if blank is None:
        blank = jnp.zeros((2 * plan.r - plan.rf, cw), BF16)
    right = jnp.concatenate([w_in[:, 2 * cw :], w_down, blank], axis=0)
    return jnp.concatenate([left, right], axis=1)


def unpack_rest(plan, piece):
    r, rf, cw = plan.r, plan.rf, plan.cw
    parts_in = [piece[:r, :cw], piece[r : 2 * r, :cw], piece[:r, cw:]]
    return parts_in, piece[2 * r : 3 * r, :cw], piece[r : r + rf, cw:]


def join_rest_kernel(plan, meta, *refs):
    pieces, out, held = refs[: plan.nrow], refs[plan.nrow], refs[plan.nrow + 1]
    r, cw = plan.r, plan.cw
    for j in range(plan.nrow):
        held[j] = pieces[j][...]
    for z in range(plan.nrow):
        parts_in, part_out, part_down = unpack_rest(plan, held[meta[plan.at_z + z]])
        out[:r, cw * z : cw * (z + 1)] = part_out
        for i in range(3):
            block, place_at = (3 * z + i) // plan.nrow, (3 * z + i) % plan.nrow
            out[r * (1 + block) : r * (2 + block), cw * place_at : cw * (place_at + 1)] = parts_in[i]
        out[4 * r :, cw * z : cw * (z + 1)] = part_down


def join_rest(plan, meta, pieces):
    if not plan.aligned:
        parts = [unpack_rest(plan, piece) for piece in ordered(plan, meta, pieces)]
        w_in = jnp.concatenate([part for item in parts for part in item[0]], axis=1)
        blocks = [jnp.concatenate([item[1] for item in parts], axis=1)]
        blocks += [w_in[:, D * t : D * (t + 1)] for t in range(3)]
        blocks += [jnp.concatenate([item[2] for item in parts], axis=1)]
        return jnp.concatenate(blocks, axis=0)
    return pl.pallas_call(
        functools.partial(join_rest_kernel, plan),
        in_specs=[SMEM] + [VMEM] * plan.nrow,
        out_specs=VMEM,
        out_shape=shape_of((plan.packed, D), BF16),
        scratch_shapes=[pltpu.VMEM((plan.nrow, 3 * plan.r, 2 * plan.cw), BF16)],
        compiler_params=params(),
        cost_estimate=cost(COSTS["join_rest"]),
        name="join_rest",
    )(meta, *pieces)


def by_block(plan, meta, own, other):
    stacked = jnp.stack(own + other)
    places = meta[plan.at_own : plan.at_other + plan.chips]
    return jnp.zeros_like(stacked).at[places].set(stacked)


def split_blocks(plan, meta, blocks):
    half = plan.chips // 2
    return [
        jnp.take(blocks, meta[plan.at_own + half * i : plan.at_own + half * (i + 1)], axis=0)
        for i in range(4)
    ]


def qkv_sources(plan, meta, own, other):
    if plan.aligned:
        return own + other
    return [by_block(plan, meta, own, other).reshape(D, EXT)]


def rest_sources(plan, meta, own, other):
    if plan.aligned:
        return own + other
    blocks = by_block(plan, meta, own, other)
    r = plan.r
    parts = [blocks[:, r * i : r * (i + 1)].reshape(D, D) for i in range(4)]
    parts.append(blocks[:, 4 * r :].reshape(FF, D))
    return [jnp.concatenate(parts, axis=0)]


def block_size(plan):
    return (plan.r, plan.rf) if plan.aligned else (D, FF)


def block_of(plan, meta, index):
    return meta[plan.at_own + index] if plan.aligned else 0


def rows_at(index, size):
    if isinstance(index, int):
        return pl.ds(index * size, size)
    return pl.ds(pl.multiple_of(index * size, size), size)


def qkv_copies(plan, meta, sources, w_ref, sems):
    r, _ = block_size(plan)
    return [
        pltpu.make_async_copy(source, w_ref.at[rows_at(block_of(plan, meta, i), r)], sems.at[i])
        for i, source in enumerate(sources)
    ]


def rest_copies(plan, meta, sources, w_out, w_in, w_down, sems):
    r, rf = block_size(plan)
    found = [[], [], []]
    for i, source in enumerate(sources):
        block = block_of(plan, meta, i)
        rows = rows_at(block, r)
        found[0].append(
            pltpu.make_async_copy(source.at[pl.ds(0, r)], w_out.at[rows], sems.at[5 * i])
        )
        for t in range(3):
            found[1].append(
                pltpu.make_async_copy(
                    source.at[pl.ds((1 + t) * r, r)], w_in.at[t, rows], sems.at[5 * i + 1 + t]
                )
            )
        found[2].append(
            pltpu.make_async_copy(
                source.at[pl.ds(4 * r, rf)], w_down.at[rows_at(block, rf)], sems.at[5 * i + 4]
            )
        )
    return found


def grad_target(plan, grads, index):
    if not plan.aligned:
        return grads[0]
    half = plan.chips // 2
    return grads[index // half].at[index % half]


def grad_blocks(plan, height, width):
    return [shape_of((plan.chips // 2, height, width), BF16)] * 4


def source_count(plan):
    return 2 * plan.chips if plan.aligned else 1


def qkv_kernel(plan, meta, cos_ref, sin_ref, *refs):
    x_refs = refs[: plan.rows]
    count = source_count(plan)
    sources = refs[plan.rows : plan.rows + count]
    q_ref = refs[plan.rows + count]
    kv_refs = refs[plan.rows + count + 1 : plan.rows + count + 1 + HALVES]
    n_ref, gain_ref, w_ref, sems = refs[plan.rows + count + 1 + HALVES :]
    copies = qkv_copies(plan, meta, sources, w_ref, sems)
    for copy in copies:
        copy.start()
    units = [layer_norm(x_refs[j][0].astype(F32))[0] for j in range(plan.rows)]
    for copy in copies:
        copy.wait()
    gain_ref[...] = w_ref[:, 3 * D :].astype(F32).T[:8, :]
    for j in range(plan.rows):
        n_ref[plan.tok * j : plan.tok * (j + 1), :] = (units[j] * gain_ref[0:1, :]).astype(BF16)
    cosine, sine = cos_ref[...], sin_ref[...]
    normed = n_ref[...]
    queries = dot(normed, w_ref[:, :D], NN)
    q_ref[...] = rotate_all(queries, cosine, sine, 1.0).astype(BF16)
    keys = rotate_all(dot(normed, w_ref[:, D : 2 * D], NN), cosine, sine, 1.0).astype(BF16)
    values = dot(normed, w_ref[:, 2 * D : 3 * D], NN).astype(BF16)
    for h in range(HALVES):
        kv_refs[h][0] = keys[:, HALF * h : HALF * (h + 1)]
        kv_refs[h][1] = values[:, HALF * h : HALF * (h + 1)]


def project(plan, meta, cosine, sine, pieces, sources):
    local = plan.local
    count = len(sources)
    inputs = [meta, cosine, sine, *pieces, *sources]
    return pl.pallas_call(
        functools.partial(qkv_kernel, plan),
        in_specs=[SMEM, VMEM, VMEM] + [VMEM] * plan.rows + [ANY] * count,
        out_specs=[VMEM] * (3 + HALVES),
        out_shape=[shape_of((local, D), BF16)]
        + [shape_of((2, local, HALF), BF16)] * HALVES
        + [shape_of((local, D), BF16), shape_of((8, D), F32)],
        scratch_shapes=[pltpu.VMEM((D, EXT), BF16), pltpu.SemaphoreType.DMA((count,))],
        compiler_params=params(),
        cost_estimate=cost(COSTS["project"]),
        name="project",
    )(*inputs)


def fill_docs(plan, meta, lengths, kdoc, qdoc):
    low = meta[plan.at_lo]
    ends = []
    passed = jnp.int32(0)
    for n in range(NDOC):
        passed = passed + lengths[low, n]
        ends.append(passed)

    def docs(places):
        total = jnp.zeros(places.shape, jnp.int32)
        for end in ends:
            total = total + (places >= end).astype(jnp.int32)
        return total

    tok = plan.tok
    for i in range(plan.groups * plan.rows):
        first = meta[plan.at_base + i]
        kdoc[i * tok : (i + 1) * tok, :] = docs(
            first + lax.broadcasted_iota(jnp.int32, (tok, 128), 0)
        )
    for i in range(plan.rows):
        first = meta[plan.at_base + i]
        qdoc[:, i * tok : (i + 1) * tok] = docs(
            first + lax.broadcasted_iota(jnp.int32, (8, tok), 1)
        )


def head_part(pair, head):
    lane = lax.broadcasted_iota(jnp.int32, pair.shape, 1)
    keep = (lane < HD) if head == 0 else (lane >= HD)
    return jnp.where(keep, pair, jnp.zeros_like(pair))


def same_docs(kdoc, qdoc, first, size, q0, width):
    key_docs = jnp.concatenate([kdoc[first : first + size, :]] * (width // 128), axis=1)
    return key_docs == qdoc[0:1, q0 : q0 + width]


def attend_kernel(plan, width, meta, lengths, q_ref, *refs):
    groups, local = plan.groups, plan.local
    kv = refs[:groups]
    o_ref, low_ref, lse_ref, kdoc, qdoc, s_ref = refs[groups:]

    @pl.when(pl.program_id(0) == 0)
    def _():
        fill_docs(plan, meta, lengths, kdoc, qdoc)

    values_t = [kv[e][1].T for e in range(groups)]
    for first in range(0, local, width):
        rows = slice(first, first + width)
        queries = q_ref[rows, :] * jnp.asarray(1.0 / math.sqrt(HD), BF16)
        parts = []
        for h in range(2):
            head_queries = head_part(queries, h)
            top = jnp.full((1, width), MASKED, F32)
            for e in range(groups):
                scores = dot(kv[e][0], head_queries, NT)
                mask = same_docs(kdoc, qdoc, e * local, local, first, width)
                scores = jnp.where(mask, scores, MASKED)
                s_ref[h, e * local : (e + 1) * local, :] = scores
                top = jnp.maximum(top, jnp.max(scores, axis=0, keepdims=True))
            total = jnp.zeros((1, width), F32)
            weighted = jnp.zeros((HD, width), F32)
            for e in range(groups):
                probs = jnp.exp(s_ref[h, e * local : (e + 1) * local, :] - top)
                total = total + jnp.sum(probs, axis=0, keepdims=True)
                weighted = weighted + dot(
                    values_t[e][h * HD : (h + 1) * HD, :], probs.astype(BF16), NN
                )
            parts.append(weighted / total)
            lse_ref[0, h : h + 1, rows] = top + jnp.log(total)
        heads = jnp.concatenate(parts, axis=0).T
        o_ref[rows, :] = heads
        low_ref[rows, :] = heads.astype(BF16)


def attend(plan, part, meta, lengths, queries, kv):
    local, groups = plan.local, plan.groups
    width = min(512, local)
    skip = part * HALF_PAIRS
    pair = pl.BlockSpec((local, 128), lambda p: (0, p))
    pair_q = pl.BlockSpec((local, 128), lambda p: (0, p + skip))
    pair_kv = pl.BlockSpec((2, local, 128), lambda p: (0, 0, p))
    inputs = [meta, lengths, queries, *kv]
    return pl.pallas_call(
        functools.partial(attend_kernel, plan, width),
        grid=(HALF_PAIRS,),
        in_specs=[SMEM, SMEM, pair_q] + [pair_kv] * groups,
        out_specs=[pair, pair, pl.BlockSpec((1, 2, local), lambda p: (p, 0, 0))],
        out_shape=[
            shape_of((local, HALF), F32),
            shape_of((local, HALF), BF16),
            shape_of((HALF_PAIRS, 2, local), F32),
        ],
        scratch_shapes=[
            pltpu.VMEM((groups * local, 128), jnp.int32),
            pltpu.VMEM((8, local), jnp.int32),
            pltpu.VMEM((2, groups * local, width), F32),
        ],
        compiler_params=params(),
        cost_estimate=cost(COSTS["attend"]),
        name="attend",
    )(*inputs)


def attend_back_kernel(
    plan, width, meta, lengths, q_ref, do_ref, o_ref, lse_ref, cos_ref, sin_ref, *refs
):
    groups, local = plan.groups, plan.local
    kv = refs[:groups]
    dq_ref = refs[groups]
    dkv = refs[groups + 1 : 2 * groups + 1]
    kdoc, qdoc, held = refs[2 * groups + 1 :]

    @pl.when(pl.program_id(0) == 0)
    def _():
        fill_docs(plan, meta, lengths, kdoc, qdoc)

    keys_t = [kv[e][0].T for e in range(groups)]
    scale = 1.0 / math.sqrt(HD)
    for first in range(0, local, width):
        rows = slice(first, first + width)
        queries = q_ref[rows, :] * jnp.asarray(scale, BF16)
        dout = do_ref[rows, :]
        product = (dout.astype(F32) * o_ref[rows, :]).T
        parts = []
        for h in range(2):
            head_queries = head_part(queries, h)
            head_dout = head_part(dout, h)
            lse = lse_ref[0, h : h + 1, rows]
            delta = jnp.sum(product[h * HD : (h + 1) * HD, :], axis=0, keepdims=True)
            grad_queries = jnp.zeros((HD, width), F32)
            for e in range(groups):
                scores = dot(kv[e][0], head_queries, NT)
                mask = same_docs(kdoc, qdoc, e * local, local, first, width)
                probs = jnp.exp(jnp.where(mask, scores, MASKED) - lse)
                dprobs = dot(kv[e][1], head_dout, NT)
                dscores = (probs * (dprobs - delta)).astype(BF16)
                grad_values = dot(probs.astype(BF16), head_dout, NN)
                grad_keys = dot(dscores, head_queries, NN)
                if first == 0 and h == 0:
                    held[e, 0] = grad_keys
                    held[e, 1] = grad_values
                else:
                    held[e, 0] += grad_keys
                    held[e, 1] += grad_values
                grad_queries = grad_queries + dot(
                    keys_t[e][h * HD : (h + 1) * HD, :], dscores, NN
                )
            parts.append(grad_queries)
        grad = jnp.concatenate(parts, axis=0).T * scale
        dq_ref[rows, :] = rotate_pair(grad, cos_ref[rows, :], sin_ref[rows, :], -1.0).astype(BF16)
    for e in range(groups):
        dkv[e][...] = held[e].astype(BF16)


def attend_back(plan, part, meta, lengths, queries, dout, heads, lse, cosine, sine, kv):
    local, groups = plan.local, plan.groups
    width = min(256, local)
    half, first, count = part
    skip = half * HALF_PAIRS + first
    wide = 128 * count
    pair = pl.BlockSpec((local, 128), lambda p: (0, p))
    pair_h = pl.BlockSpec((local, 128), lambda p: (0, p + first))
    pair_q = pl.BlockSpec((local, 128), lambda p: (0, p + skip))
    inputs = [meta, lengths, queries, dout, heads, lse, cosine, sine, *kv]
    table = pl.BlockSpec((local, 128), lambda p: (0, 0))
    pair_kv = pl.BlockSpec((2, local, 128), lambda p: (0, 0, p))
    pair_kv_h = pl.BlockSpec((2, local, 128), lambda p: (0, 0, p + first))
    return pl.pallas_call(
        functools.partial(attend_back_kernel, plan, width),
        grid=(count,),
        in_specs=[
            SMEM,
            SMEM,
            pair_q,
            pair_q,
            pair_h,
            pl.BlockSpec((1, 2, local), lambda p: (p + first, 0, 0)),
            table,
            table,
        ]
        + [pair_kv_h] * groups,
        out_specs=[pair] + [pair_kv] * groups,
        out_shape=[shape_of((local, wide), BF16)] + [shape_of((2, local, wide), BF16)] * groups,
        scratch_shapes=[
            pltpu.VMEM((groups * local, 128), jnp.int32),
            pltpu.VMEM((8, local), jnp.int32),
            pltpu.VMEM((groups, 2, local, 128), F32),
        ],
        compiler_params=params(),
        cost_estimate=cost(4 * count),
        name="attend_back",
    )(*inputs)


def middle_kernel(plan, meta, gain_ref, *refs):
    rows, tok, local = plan.rows, plan.tok, plan.local
    low_refs, refs = refs[:HALVES], refs[HALVES:]
    count = source_count(plan)
    x_refs = refs[:rows]
    sources = refs[rows : rows + count]
    refs = refs[rows + count :]
    out_refs = refs[:rows]
    do_ref, dh_ref = refs[rows : rows + 2]
    grads = refs[rows + 2 : rows + 2 + (4 if plan.aligned else 1)]
    (
        w_out,
        w_in,
        w_down,
        h_ref,
        n_ref,
        gu_ref,
        mid_ref,
        dgu_ref,
        g_out,
        g_in,
        g_down,
        in_sems,
        out_sems,
    ) = refs[rows + 2 + len(grads) :]
    copies = rest_copies(plan, meta, sources, w_out, w_in, w_down, in_sems)
    for group in copies:
        for copy in group:
            copy.start()
    for copy in copies[0]:
        copy.wait()
    low = jnp.concatenate([low_ref[...] for low_ref in low_refs], axis=1)
    branch = dot(low, w_out[...], NN)
    for j in range(rows):
        part = slice(tok * j, tok * (j + 1))
        h_ref[part, :] = x_refs[j][0].astype(F32) + branch[part, :]
    gain = gain_ref[1:2, :]
    unit, inv_std = layer_norm(h_ref[...])
    n_ref[...] = (unit * gain).astype(BF16)
    for copy in copies[1]:
        copy.wait()
    for t in range(3):
        gu_ref[:, D * t : D * (t + 1)] = dot(n_ref[...], w_in[t], NN)
    for copy in copies[2]:
        copy.wait()
    dy = jnp.concatenate([x_refs[j][1] for j in range(rows)], axis=0)
    size = FF // 3
    for f in range(3):
        cols = slice(size * f, size * (f + 1))
        up_cols = slice(FF + size * f, FF + size * (f + 1))
        gate = gu_ref[:, cols]
        up = gu_ref[:, up_cols]
        below = 0.5 + 0.5 * lax.erf(gate * math.sqrt(0.5))
        active = gate * below
        mid_ref[:, cols] = (active * up).astype(BF16)
        slope = below + gate * jnp.exp(-0.5 * gate * gate) * (1.0 / math.sqrt(2.0 * math.pi))
        dmid = dot(dy, w_down[cols, :], NT)
        dgu_ref[:, cols] = (dmid * up * slope).astype(BF16)
        dgu_ref[:, up_cols] = (dmid * active).astype(BF16)
    mixed = dot(mid_ref[...], w_down[...], NN)
    for j in range(rows):
        part = slice(tok * j, tok * (j + 1))
        out_refs[j][...] = (h_ref[part, :] + mixed[part, :]).astype(BF16)
    grad_normed = dot(dgu_ref[:, :D], w_in[0], NT)
    for t in range(1, 3):
        grad_normed = grad_normed + dot(dgu_ref[:, D * t : D * (t + 1)], w_in[t], NT)
    unit, inv_std = layer_norm(h_ref[...])
    grad_hidden = dy.astype(F32) + norm_backward(grad_normed, unit, inv_std, gain)
    dh_ref[...] = grad_hidden
    branch_grad = grad_hidden.astype(BF16)
    do_ref[...] = dot(branch_grad, w_out[...], NT).astype(BF16)
    for h in range(HALVES):
        g_out[HALF * h : HALF * (h + 1), :] = dot(low_refs[h][...], branch_grad, TN).astype(BF16)
    for t in range(3):
        g_in[t] = dot(n_ref[...], dgu_ref[:, D * t : D * (t + 1)], TN).astype(BF16)
    g_down[...] = dot(mid_ref[...], dy, TN).astype(BF16)
    r, rf = block_size(plan)
    done = []
    for i in range(count):
        block = block_of(plan, meta, i)
        target = grad_target(plan, grads, i)
        at = rows_at(block, r)
        done.append(
            pltpu.make_async_copy(g_out.at[at], target.at[pl.ds(0, r)], out_sems.at[5 * i])
        )
        for t in range(3):
            done.append(
                pltpu.make_async_copy(
                    g_in.at[t, at], target.at[pl.ds((1 + t) * r, r)], out_sems.at[5 * i + 1 + t]
                )
            )
        done.append(
            pltpu.make_async_copy(
                g_down.at[rows_at(block, rf)], target.at[pl.ds(4 * r, rf)], out_sems.at[5 * i + 4]
            )
        )
    for copy in done:
        copy.start()
    for copy in done:
        copy.wait()


def middle(plan, meta, low, gains, pieces, sources):
    local, rows, tok = plan.local, plan.rows, plan.tok
    count = len(sources)
    total = 4 * D + FF
    if plan.aligned:
        grads = grad_blocks(plan, plan.packed, D)
    else:
        grads = [shape_of((total, D), BF16)]
    return pl.pallas_call(
        functools.partial(middle_kernel, plan),
        in_specs=[SMEM, VMEM] + [VMEM] * (HALVES + rows) + [ANY] * count,
        out_specs=[VMEM] * (rows + 2) + [ANY] * len(grads),
        out_shape=[shape_of((tok, D), BF16)] * rows
        + [shape_of((local, D), BF16), shape_of((local, D), F32)]
        + grads,
        scratch_shapes=[
            pltpu.VMEM((D, D), BF16),
            pltpu.VMEM((3, D, D), BF16),
            pltpu.VMEM((FF, D), BF16),
            pltpu.VMEM((local, D), F32),
            pltpu.VMEM((local, D), BF16),
            pltpu.VMEM((local, 2 * FF), F32),
            pltpu.VMEM((local, FF), BF16),
            pltpu.VMEM((local, 2 * FF), BF16),
            pltpu.VMEM((D, D), BF16),
            pltpu.VMEM((3, D, D), BF16),
            pltpu.VMEM((FF, D), BF16),
            pltpu.SemaphoreType.DMA((5 * count,)),
            pltpu.SemaphoreType.DMA((5 * count,)),
        ],
        compiler_params=params(),
        cost_estimate=cost(COSTS["middle"]),
        name="middle",
    )(meta, gains, *low, *pieces, *sources)


def back_weight_kernel(plan, meta, cos_ref, sin_ref, n_ref, *refs):
    groups = plan.groups
    count = len(BACK_PARTS)
    dq_refs, refs = refs[:count], refs[count:]
    dkv, refs = refs[: count * groups], refs[count * groups :]
    dp_ref, refs = refs[0], refs[1:]
    grads = refs[: 4 if plan.aligned else 1]
    g_ref, out_sems = refs[len(grads) :]
    for i, (half, first, pairs) in enumerate(BACK_PARTS):
        at = HALF * half + 128 * first
        cols = slice(at, at + 128 * pairs)
        parts = dkv[groups * i : groups * (i + 1)]
        grad_keys = sum_pieces([part[0] for part in parts])
        dp_ref[0, :, cols] = dq_refs[i][...]
        dp_ref[1, :, cols] = rotate_all(grad_keys, cos_ref[...], sin_ref[...], -1.0).astype(BF16)
        dp_ref[2, :, cols] = sum_pieces([part[1] for part in parts]).astype(BF16)
    for t in range(3):
        g_ref[:, D * t : D * (t + 1)] = dot(n_ref[...], dp_ref[t], TN).astype(BF16)
    r, _ = block_size(plan)
    done = []
    for i in range(source_count(plan)):
        at = rows_at(block_of(plan, meta, i), r)
        target = grad_target(plan, grads, i)
        done.append(pltpu.make_async_copy(g_ref.at[at], target, out_sems.at[i]))
    for copy in done:
        copy.start()
    for copy in done:
        copy.wait()


def back_weight(plan, meta, cosine, sine, normed, dq, dkv):
    if plan.aligned:
        grads = grad_blocks(plan, plan.r, 3 * D)
    else:
        grads = [shape_of((D, 3 * D), BF16)]
    results = pl.pallas_call(
        functools.partial(back_weight_kernel, plan),
        in_specs=[SMEM] + [VMEM] * (3 + len(BACK_PARTS) * (1 + plan.groups)),
        out_specs=[VMEM] + [ANY] * len(grads),
        out_shape=[shape_of((3, plan.local, D), BF16)] + grads,
        scratch_shapes=[
            pltpu.VMEM((D, 3 * D), BF16),
            pltpu.SemaphoreType.DMA((source_count(plan),)),
        ],
        compiler_params=params(),
        cost_estimate=cost(COSTS["back_weight"]),
        name="back_weight",
    )(meta, cosine, sine, normed, *dq, *dkv)
    return results[0], results[1:]


def back_in_kernel(plan, meta, dp_ref, dh_ref, gain_ref, *refs):
    rows, tok = plan.rows, plan.tok
    count = source_count(plan)
    x_refs = refs[:rows]
    sources = refs[rows : rows + count]
    refs = refs[rows + count :]
    in_refs = refs[:rows]
    w_ref, in_sems = refs[rows:]
    copies = qkv_copies(plan, meta, sources, w_ref, in_sems)
    for copy in copies:
        copy.start()
    for copy in copies:
        copy.wait()
    grad_normed = dot(dp_ref[0], w_ref[:, :D], NT)
    for t in range(1, 3):
        grad_normed = grad_normed + dot(dp_ref[t], w_ref[:, D * t : D * (t + 1)], NT)
    for j in range(rows):
        part = slice(tok * j, tok * (j + 1))
        unit, inv_std = layer_norm(x_refs[j][0].astype(F32))
        grad = grad_normed[part, :]
        back = norm_backward(grad, unit, inv_std, gain_ref[0:1, :])
        in_refs[j][...] = (dh_ref[part, :] + back).astype(BF16)


def back_in(plan, meta, dprojected, dhidden, gains, pieces, sources):
    rows, tok = plan.rows, plan.tok
    count = len(sources)
    return pl.pallas_call(
        functools.partial(back_in_kernel, plan),
        in_specs=[SMEM] + [VMEM] * (3 + rows) + [ANY] * count,
        out_specs=[VMEM] * rows,
        out_shape=[shape_of((tok, D), BF16)] * rows,
        scratch_shapes=[pltpu.VMEM((D, EXT), BF16), pltpu.SemaphoreType.DMA((count,))],
        compiler_params=params(),
        cost_estimate=cost(COSTS["back_in"]),
        name="back_in",
    )(meta, dprojected, dhidden, gains, *pieces, *sources)


def gain_columns(weight, grad):
    total = jnp.sum(weight.astype(F32) * grad.astype(F32), axis=1, keepdims=True)
    high = total.astype(BF16)
    return high, (total - high.astype(F32)).astype(BF16)


def pad_width(plan):
    return -(-(3 * plan.cw + 2) // 128) * 128


def gain_tail(plan, weight, grad):
    width = pad_width(plan) - 3 * plan.cw
    high, rest = gain_columns(weight, grad)
    lane = lax.broadcasted_iota(jnp.int32, (plan.r, width), 1)
    return jnp.where(lane == 0, high, jnp.where(lane == 1, rest, jnp.zeros_like(high)))


def cut_qkv_kernel(plan, meta, total, weight, *refs):
    outs, held = refs[: plan.nrow], refs[plan.nrow]
    width = 3 * plan.cw
    tail = gain_tail(plan, weight[:, : 3 * D], total[...])
    for z in range(plan.nrow):
        place_at = meta[plan.at_z + z]
        held[place_at, :, :width] = total[:, width * z : width * (z + 1)]
        held[place_at, :, width:] = tail
    for j in range(plan.nrow):
        outs[j][...] = held[j]


def cut_qkv(plan, meta, total, weight):
    width, wide = 3 * plan.cw, pad_width(plan)
    if not plan.aligned:
        tail = gain_tail(plan, weight[:, : 3 * D], total)
        parts = [
            jnp.concatenate([total[:, width * z : width * (z + 1)], tail], axis=1)
            for z in range(plan.nrow)
        ]
        return ordered(plan, meta, parts)
    return pl.pallas_call(
        functools.partial(cut_qkv_kernel, plan),
        in_specs=[SMEM, VMEM, VMEM],
        out_specs=[VMEM] * plan.nrow,
        out_shape=[shape_of((plan.r, wide), BF16)] * plan.nrow,
        scratch_shapes=[pltpu.VMEM((plan.nrow, plan.r, wide), BF16)],
        compiler_params=params(),
        cost_estimate=cost(COSTS["cut_qkv"]),
        name="cut_qkv",
    )(meta, total, weight)


def gain_blank(plan, weight, grad):
    r, blank = plan.r, 2 * plan.r - plan.rf
    cols = [weight[r * t : r * (t + 1)] for t in range(1, 4)]
    grads = [grad[r * t : r * (t + 1)] for t in range(1, 4)]
    high, rest = gain_columns(jnp.concatenate(cols, axis=1), jnp.concatenate(grads, axis=1))
    lane = lax.broadcasted_iota(jnp.int32, (blank, plan.cw), 1)
    found = jnp.zeros((blank, plan.cw), BF16)
    for i in range(r // blank):
        part = slice(blank * i, blank * (i + 1))
        found = jnp.where(lane == 2 * i, high[part], found)
        found = jnp.where(lane == 2 * i + 1, rest[part], found)
    return found


def cut_rest_kernel(plan, meta, total, weight, *refs):
    outs, held = refs[: plan.nrow], refs[plan.nrow]
    r, rf, cw = plan.r, plan.rf, plan.cw
    blank = gain_blank(plan, weight[...], total[...])
    for z in range(plan.nrow):
        place_at = meta[plan.at_z + z]
        cols = slice(cw * z, cw * (z + 1))
        parts = []
        for i in range(3):
            block, at = (3 * z + i) // plan.nrow, (3 * z + i) % plan.nrow
            parts.append(total[r * (1 + block) : r * (2 + block), cw * at : cw * (at + 1)])
        held[place_at, :r, :] = jnp.concatenate([parts[0], parts[2]], axis=1)
        held[place_at, r : 2 * r, :] = jnp.concatenate(
            [parts[1], total[4 * r : 5 * r, cols]], axis=1
        )
        rest = total[5 * r : 4 * r + rf, cols]
        held[place_at, 2 * r :, :] = jnp.concatenate(
            [total[:r, cols], jnp.concatenate([rest, blank], axis=0)], axis=1
        )
    for j in range(plan.nrow):
        outs[j][...] = held[j]


def cut_rest(plan, meta, total, weight):
    r, cw = plan.r, plan.cw
    if not plan.aligned:
        grad_in = jnp.concatenate([total[r * (1 + t) : r * (2 + t)] for t in range(3)], axis=1)
        blank = gain_blank(plan, weight, total)
        parts = [
            pack_rest(
                plan,
                total[:r, cw * z : cw * (z + 1)],
                grad_in[:, 3 * cw * z : 3 * cw * (z + 1)],
                total[4 * r :, cw * z : cw * (z + 1)],
                blank,
            )
            for z in range(plan.nrow)
        ]
        return ordered(plan, meta, parts)
    return pl.pallas_call(
        functools.partial(cut_rest_kernel, plan),
        in_specs=[SMEM, VMEM, VMEM],
        out_specs=[VMEM] * plan.nrow,
        out_shape=[shape_of((3 * r, 2 * cw), BF16)] * plan.nrow,
        scratch_shapes=[pltpu.VMEM((plan.nrow, 3 * r, 2 * cw), BF16)],
        compiler_params=params(),
        cost_estimate=cost(COSTS["cut_rest"]),
        name="cut_rest",
    )(meta, total, weight)


def reduce_z(plan, pieces):
    return [pieces[0]] + [
        lax.ppermute(pieces[j], "row", plan.z_pairs(j)) for j in range(1, plan.nrow)
    ]


def sum_pieces(pieces):
    total = pieces[0].astype(F32)
    for piece in pieces[1:]:
        total = total + piece.astype(F32)
    return total


def end_rest_kernel(plan, *refs):
    pieces, (g_out, g_in, g_down, g_gain) = refs[: plan.nrow], refs[plan.nrow :]
    total = sum_pieces([piece[...] for piece in pieces])
    parts_in, part_out, part_down = unpack_rest(plan, total)
    g_out[...] = part_out
    g_in[...] = jnp.concatenate(parts_in, axis=1)
    g_down[...] = part_down
    blank = 2 * plan.r - plan.rf
    g_gain[...] = total[3 * plan.r - blank :, plan.cw : plan.cw + 128].T[:8, :]


def end_rest(plan, pieces):
    r, blank = plan.r, 2 * plan.r - plan.rf
    if not plan.aligned:
        total = sum_pieces(pieces)
        parts_in, out_grad, down_grad = unpack_rest(plan, total)
        in_grad = jnp.concatenate(parts_in, axis=1)
        gain = total[3 * r - blank :, plan.cw : plan.cw + 8].T
    else:
        out_grad, in_grad, down_grad, gain = pl.pallas_call(
            functools.partial(end_rest_kernel, plan),
            in_specs=[VMEM] * plan.nrow,
            out_specs=[VMEM] * 4,
            out_shape=[
                shape_of((r, plan.cw), F32),
                shape_of((r, 3 * plan.cw), F32),
                shape_of((plan.rf, plan.cw), F32),
                shape_of((8, blank), F32),
            ],
            compiler_params=params(),
            cost_estimate=cost(COSTS["end_rest"]),
            name="end_rest",
        )(*pieces)
    gain = jnp.concatenate([gain[2 * i] + gain[2 * i + 1] for i in range(r // blank)])
    return out_grad, in_grad, down_grad, gain


def end_qkv_kernel(plan, gain_ref, *refs):
    pieces, (g_qkv, g_gain) = refs[: plan.nrow], refs[plan.nrow :]
    width, wide = 3 * plan.cw, pad_width(plan)
    total = sum_pieces([piece[...] for piece in pieces])
    g_qkv[...] = total[:, :width]
    tail = total[:, wide - 128 :].T
    at = width - (wide - 128)
    g_gain[...] = (tail[at : at + 1, :] + tail[at + 1 : at + 2, :]) / gain_ref[...]


def end_qkv(plan, gain, pieces):
    width, wide = 3 * plan.cw, pad_width(plan)
    if not plan.aligned:
        total = sum_pieces(pieces)
        return total[:, :width], (total[:, width] + total[:, width + 1]) / gain[0]
    grad, gain_grad = pl.pallas_call(
        functools.partial(end_qkv_kernel, plan),
        in_specs=[VMEM] * (1 + plan.nrow),
        out_specs=[VMEM] * 2,
        out_shape=[shape_of((plan.r, width), F32), shape_of((1, plan.r), F32)],
        compiler_params=params(),
        cost_estimate=cost(COSTS["end_qkv"]),
        name="end_qkv",
    )(gain, *pieces)
    return grad, gain_grad.reshape(plan.r)


def rotation_tables(plan, meta, lengths):
    ends = jnp.cumsum(lax.dynamic_index_in_dim(lengths, meta[plan.at_lo], 0, keepdims=False))
    starts = jnp.concatenate([jnp.zeros((1,), jnp.int32), ends[:-1]])
    bases = meta[plan.at_base : plan.at_base + plan.rows]
    places = (bases[:, None] + jnp.arange(plan.tok, dtype=jnp.int32)[None, :]).reshape(-1)
    passed = places[:, None] >= starts[None, :]
    positions = places - jnp.max(jnp.where(passed, starts[None, :], 0), axis=1)
    half = HD // 2
    inverse = ROPE_BASE ** (-(jnp.arange(half, dtype=F32) * (2.0 / HD)))
    angles = positions.astype(F32)[:, None] * inverse
    cosine, sine = jnp.cos(angles), jnp.sin(angles)
    return (
        jnp.concatenate([cosine] * 4, axis=1),
        jnp.concatenate([-sine, sine, -sine, sine], axis=1),
    )


def body(
    plan,
    tokens,
    lengths,
    norm_gain,
    qkv_weight,
    out_weight,
    mlp_gain,
    in_weight,
    down_weight,
    cotangent,
):
    blk, row = lax.axis_index("blk"), lax.axis_index("row")
    meta = lax.dynamic_slice(
        jnp.asarray(plan.table), (row, blk, 0), (1, 1, plan.size)
    ).reshape(plan.size)
    qkv_parts = gather_z(plan, qkv_weight)
    cut, packed = prepare(plan, meta, tokens, cotangent, out_weight, in_weight, down_weight)
    pieces = exchange_rows(plan, cut)
    rest_parts = gather_z(plan, packed, behind=qkv_parts)
    gains = jnp.pad(jnp.stack([norm_gain, mlp_gain], axis=1), ((0, 0), (0, 126)))
    cosine, sine = rotation_tables(plan, meta, lengths)
    qkv_parts[0] = tie(qkv_parts[0], rest_parts[1], *pieces[1:])
    qkv_joined = join_qkv(plan, meta, gains, qkv_parts)
    qkv_own = gather_start(plan, qkv_joined)
    qkv_own[1] = tie(qkv_own[1], *rest_parts[2:])
    qkv_own = gather_more(plan, qkv_own)
    qkv_other = [swap_cores(plan, piece) for piece in qkv_own]
    qkv_from = qkv_sources(plan, meta, qkv_own, qkv_other)
    rest_parts[0] = tie(rest_parts[0], qkv_joined)
    joined = join_rest(plan, meta, rest_parts)
    results = project(plan, tie(meta, joined), cosine, sine, pieces, qkv_from)
    queries, kv, (normed, gains) = results[0], results[1 : 1 + HALVES], results[1 + HALVES :]
    kv = [
        [part]
        + [
            lax.ppermute(part, "blk", plan.xor_pairs(plan.member(e)))
            for e in range(1, plan.groups)
        ]
        for part in kv
    ]
    rest_own = gather_start(plan, joined)
    heads, low, lse = [None] * HALVES, [None] * HALVES, [None] * HALVES
    heads[0], low[0], lse[0] = attend(plan, 0, meta, lengths, queries, kv[0])
    order = tie(meta, low[0], *rest_own[1:])
    rest_own[1:] = [tie(piece, low[0]) for piece in rest_own[1:]]
    rest_other = [swap_cores(plan, piece) for piece in rest_own]
    rest_more = gather_more(plan, rest_own)[len(rest_own) :]
    heads[1], low[1], lse[1] = attend(plan, 1, order, lengths, queries, kv[1])
    rest_more = [tie(piece, low[1]) for piece in rest_more]
    rest_own = rest_own + rest_more
    rest_other = rest_other + [swap_cores(plan, piece) for piece in rest_more]
    rest_from = rest_sources(plan, meta, rest_own, rest_other)
    results = middle(plan, meta, low, gains, pieces, rest_from)
    outs, (dout, dhidden), rest_grads = (
        results[: plan.rows],
        results[plan.rows : plan.rows + 2],
        results[plan.rows + 2 :],
    )
    if not plan.aligned:
        r, rf, nblk = plan.r, plan.rf, plan.nblk
        whole = rest_grads[0]
        blocks = [whole[D * i : D * (i + 1)].reshape(nblk, r, D) for i in range(4)]
        blocks.append(whole[4 * D :].reshape(nblk, rf, D))
        rest_grads = split_blocks(plan, meta, jnp.concatenate(blocks, axis=1))
    keep_low, keep_high, other_low, other_high = reduce_start(plan, rest_grads)
    dq, dkv = [], []
    order = meta
    for i, part in enumerate(BACK_PARTS):
        half = part[0]
        results = attend_back(
            plan, part, order, lengths, queries, dout, heads[half], lse[half], cosine, sine, kv[half]
        )
        dq.append(results[0])
        dkv.append(results[1])
        dkv += [
            lax.ppermute(results[1 + e], "blk", plan.xor_pairs(plan.member(e)))
            for e in range(1, plan.groups)
        ]
        if i == 0:
            rest_high = add_low(tie(keep_high, dq[0]), other_high)
            rest_low = add_low(tie(keep_low, dq[0]), other_low)
            order = tie(meta, dq[0], rest_high, rest_low)
        else:
            order = tie(meta, dq[i], *dkv[1 : plan.groups])
    rest_low, rest_high = reduce_step(plan, plan.bits - 1, tie(rest_low, dq[-1]), rest_high)
    order = tie(meta, rest_low) if rest_high is None else tie(meta, rest_low, rest_high)
    dprojected, qkv_grads = back_weight(plan, order, cosine, sine, normed, dq, dkv)
    if not plan.aligned:
        qkv_grads = split_blocks(plan, meta, qkv_grads[0].reshape(plan.nblk, plan.r, 3 * D))
    rest_low = tie(rest_low, dprojected)
    for step in reversed(range(plan.bits - 1)):
        rest_low, rest_high = reduce_step(plan, step, rest_low, rest_high)
    rest_cut = cut_rest(plan, meta, rest_low, joined)
    keep_low, keep_high, other_low, other_high = reduce_start(plan, qkv_grads)
    qkv_high = add_low(tie(keep_high, *rest_cut), other_high)
    qkv_low = add_low(keep_low, other_low)
    order = tie(meta, qkv_high, qkv_low, *rest_cut)
    in_pieces = back_in(plan, order, dprojected, dhidden, gains, pieces, qkv_from)
    rest_pieces = reduce_z(plan, rest_cut)
    qkv_low = tie(qkv_low, in_pieces[0], *rest_pieces[1:3])
    for step in reversed(range(plan.bits)):
        if step == 0:
            qkv_low = tie(qkv_low, *rest_pieces[3:])
        qkv_low, qkv_high = reduce_step(plan, step, qkv_low, qkv_high)
    in_pieces = exchange_rows(plan, [tie(piece, qkv_low) for piece in in_pieces])
    outs = exchange_rows(plan, [tie(piece, qkv_low) for piece in outs])
    qkv_cut = cut_qkv(plan, meta, tie(qkv_low, *rest_pieces[1:]), qkv_joined)
    qkv_pieces = reduce_z(plan, qkv_cut)
    rest_pieces[0] = tie(rest_pieces[0], *qkv_cut)
    out_grad, in_grad, down_grad, mlp_gain_grad = end_rest(plan, rest_pieces)
    output = place(plan, meta, [tie(outs[0], *qkv_cut)] + outs[1:])
    input_grad = place(plan, meta, [tie(in_pieces[0], *qkv_cut)] + in_pieces[1:])
    gain_row = norm_gain.astype(F32)[None]
    qkv_grad, norm_gain_grad = end_qkv(plan, tie(gain_row, output, input_grad, in_grad), qkv_pieces)
    mlp_gain_grad = mlp_gain_grad / mlp_gain.astype(F32)
    return (
        output,
        input_grad,
        norm_gain_grad,
        qkv_grad,
        out_grad,
        mlp_gain_grad,
        in_grad,
        down_grad,
    )


def solution(mesh):
    weights = P("blk", "row")
    acts = P("row", "blk", None)

    def run(*args):
        rows = args[0].shape[0] // mesh.shape["row"]
        tok = args[0].shape[1] // mesh.shape["blk"]
        plan = Plan(mesh, rows, tok)
        return jax.shard_map(
            functools.partial(body, plan),
            mesh=mesh,
            in_specs=(acts, P("row", None), P("blk"), weights, weights, P("blk"), weights, weights, acts),
            out_specs=(acts, acts, P("blk"), weights, weights, P("blk"), weights, weights),
            check_vma=False,
        )(*args)

    return run
```

```python
import functools
import math

import jax
import jax.numpy as jnp
import numpy as np
from jax import lax
from jax.experimental import pallas as pl
from jax.experimental.pallas import tpu as pltpu
from jax.sharding import PartitionSpec as P

D = 768
HEADS = 12
HD = 64
FF = 1152
NDOC = 8
PAIRS = HEADS // 2
EXT = 3 * D + 128

ROPE_BASE = 160000.0
NORM_EPSILON = 1e-05
MASKED = -1e30
F32 = jnp.float32
BF16 = jnp.bfloat16
NN = (((1,), (0,)), ((), ()))
NT = (((1,), (1,)), ((), ()))
TN = (((0,), (0,)), ((), ()))
VMEM_BYTES = 56 * 1024 * 1024
HALVES = 2
HALF_PAIRS = PAIRS // HALVES
HALF = D // HALVES
BACK_PARTS = ((0, 0, 1), (0, 1, 2), (1, 0, 3))
COSTS = {
    "prepare": 4,
    "place_rows": 2,
    "join_qkv": 2,
    "join_rest": 2,
    "project": 7,
    "attend": 9,
    "middle": 20,
    "attend_back": 12,
    "back_in": 7,
    "back_weight": 6,
    "cut_qkv": 2,
    "cut_rest": 2,
    "end_rest": 2,
    "end_qkv": 2,
}
SMEM = pl.BlockSpec(memory_space=pltpu.SMEM)
ANY = pl.BlockSpec(memory_space=pl.ANY)
VMEM = pl.BlockSpec(memory_space=pltpu.VMEM)


def dot(a, b, dims):
    return lax.dot_general(a, b, dims, preferred_element_type=F32)


def shape_of(dims, dtype):
    return jax.ShapeDtypeStruct(tuple(dims), dtype)


def params():
    return pltpu.CompilerParams(vmem_limit_bytes=VMEM_BYTES)


def cost(microseconds):
    return pl.CostEstimate(
        flops=int(microseconds * 1e6), bytes_accessed=1 << 10, transcendentals=0
    )


def tie(value, *others):
    return lax.optimization_barrier((value, *others))[0]


class Plan:
    def __init__(self, mesh, rows, tok):
        self.nrow = mesh.shape["row"]
        self.nblk = mesh.shape["blk"]
        self.rows = rows
        self.tok = tok
        self.local = rows * tok
        self.chips = self.nblk // 2
        self.bits = self.chips.bit_length() - 1
        self.groups = self.nblk // rows
        self.r = D // self.nblk
        self.rf = FF // self.nblk
        self.cw = D // self.nrow
        self.aligned = self.r % 16 == 0 and self.rf % 16 == 0
        self.packed = 4 * self.r + self.rf
        rows_, chips, nrow = self.rows, self.chips, self.nrow
        self.at_pick = 0
        self.at_base = self.at_pick + rows_
        self.at_own = self.at_base + self.groups * rows_
        self.at_other = self.at_own + chips
        self.at_z = self.at_other + chips
        self.at_lo = self.at_z + nrow
        self.size = self.at_lo + 1
        table = np.zeros((nrow, self.nblk, self.size), np.int32)
        for z in range(nrow):
            for blk in range(self.nblk):
                chip, core = blk // 2, blk % 2
                low = chip % rows_
                entry = table[z, blk]
                for j in range(rows_):
                    entry[self.at_pick + j] = low ^ j
                for e in range(self.groups):
                    other = blk ^ self.member(e)
                    for j in range(rows_):
                        entry[self.at_base + e * rows_ + j] = (2 * ((other // 2) ^ j) + other % 2) * tok
                for j in range(chips):
                    entry[self.at_own + j] = 2 * (chip ^ self.order(core, j)) + core
                    entry[self.at_other + j] = 2 * (chip ^ self.order(1 - core, j)) + 1 - core
                for other in range(nrow):
                    entry[self.at_z + other] = other ^ z
                entry[self.at_lo] = low
        self.table = table

    def member(self, e):
        return (e & 1) | ((e >> 1) * 2 * self.rows)

    def order(self, core, j):
        if core == 0:
            return j
        return int(format(j, "0%db" % self.bits)[::-1], 2) if self.bits else 0

    def step_pairs(self, step):
        def flip(blk):
            bit = step if blk % 2 == 0 else self.bits - 1 - step
            return 2 * ((blk // 2) ^ (1 << bit)) + blk % 2

        return [(blk, flip(blk)) for blk in range(self.nblk)]

    def xor_pairs(self, mask):
        return [(blk, blk ^ mask) for blk in range(self.nblk)]

    def z_pairs(self, mask):
        return [(z, z ^ mask) for z in range(self.nrow)]


def swap_cores(plan, value):
    return lax.ppermute(value, "blk", plan.xor_pairs(1))


def gather_z(plan, value, behind=None):
    pieces = [value]
    for j in range(1, plan.nrow):
        source = value if behind is None else tie(value, behind[j])
        pieces.append(lax.ppermute(source, "row", plan.z_pairs(j)))
    return pieces


def exchange_rows(plan, pieces):
    return [pieces[0]] + [
        lax.ppermute(pieces[j], "blk", plan.xor_pairs(2 * j)) for j in range(1, plan.rows)
    ]


def gather_start(plan, value):
    pairs = [plan.step_pairs(step) for step in range(plan.bits)]
    first = lax.ppermute(value, "blk", pairs[0])
    second = [lax.ppermute(value, "blk", pairs[1])] if plan.bits > 1 else []
    return [value, first] + second


def gather_more(plan, pieces):
    for step in range(1, plan.bits):
        have = 1 << step
        missing = pieces[len(pieces) - have :] if step > 1 else pieces[1:2]
        pieces = pieces + [lax.ppermute(piece, "blk", plan.step_pairs(step)) for piece in missing]
    return pieces


def add_low(a, b):
    return (a.astype(F32) + b.astype(F32)).astype(BF16)


def reduce_start(plan, grads):
    keep_low, keep_high, send_low, send_high = grads
    other_high = swap_cores(plan, send_high)
    return keep_low, keep_high, swap_cores(plan, send_low), other_high


def reduce_step(plan, step, low, high):
    moved = lax.ppermute(high, "blk", plan.step_pairs(step))
    half = low.shape[0] // 2
    if half == 0:
        return add_low(low, moved)[0], None
    high = add_low(low[half:], moved[half:])
    return add_low(low[:half], moved[:half]), high


def layer_norm(values):
    average = jnp.mean(values, axis=-1, keepdims=True)
    centred = values - average
    inv_std = lax.rsqrt(jnp.mean(centred * centred, axis=-1, keepdims=True) + NORM_EPSILON)
    return centred * inv_std, inv_std


def norm_backward(grad_out, normalized, inv_std, gain):
    scaled = grad_out * gain
    inner = jnp.mean(scaled * normalized, axis=-1, keepdims=True)
    outer = jnp.mean(scaled, axis=-1, keepdims=True)
    return inv_std * (scaled - outer - normalized * inner)


def swap_halves(values):
    lane = lax.broadcasted_iota(jnp.int32, values.shape, 1)
    width = values.shape[1]
    half = HD // 2
    return jnp.where(
        (lane & half) == 0, pltpu.roll(values, width - half, 1), pltpu.roll(values, half, 1)
    )


def rotate_pair(values, cosine, sine, direction):
    return values * cosine + swap_halves(values) * (direction * sine)


def rotate_all(values, cosine, sine, direction):
    return jnp.concatenate(
        [
            rotate_pair(values[:, 128 * p : 128 * (p + 1)], cosine, sine, direction)
            for p in range(values.shape[1] // 128)
        ],
        axis=1,
    )


def prepare_kernel(plan, meta, tokens, cotangent, w_out, w_in, w_down, *refs):
    rows = plan.rows
    for j in range(rows):
        row = meta[plan.at_pick + j]
        refs[j][0] = tokens[row]
        refs[j][1] = cotangent[row]
    if plan.aligned:
        refs[rows][...] = pack_rest(plan, w_out[...], w_in[...], w_down[...])


def prepare(plan, meta, tokens, cotangent, w_out, w_in, w_down):
    rows = plan.rows
    shapes = [shape_of((2, plan.tok, D), BF16)] * rows
    if plan.aligned:
        shapes.append(shape_of((3 * plan.r, 2 * plan.cw), BF16))
    results = pl.pallas_call(
        functools.partial(prepare_kernel, plan),
        in_specs=[SMEM] + [VMEM] * 5,
        out_specs=[VMEM] * len(shapes),
        out_shape=shapes,
        compiler_params=params(),
        cost_estimate=cost(COSTS["prepare"]),
        name="prepare",
    )(meta, tokens, cotangent, w_out, w_in, w_down)
    packed = results[rows] if plan.aligned else pack_rest(plan, w_out, w_in, w_down)
    return results[:rows], packed


def place_kernel(plan, meta, *refs):
    pieces, (out, grad) = refs[: plan.rows], refs[plan.rows :]
    for j in range(plan.rows):
        row = meta[plan.at_pick + j]
        out[row] = pieces[j][0]
        grad[row] = pieces[j][1]


def place(plan, meta, pieces):
    return pl.pallas_call(
        functools.partial(place_kernel, plan),
        in_specs=[SMEM] + [VMEM] * plan.rows,
        out_specs=[VMEM] * 2,
        out_shape=[shape_of((plan.rows, plan.tok, D), BF16)] * 2,
        compiler_params=params(),
        cost_estimate=cost(COSTS["place_rows"]),
        name="place_rows",
    )(meta, *pieces)


def ordered(plan, meta, pieces):
    stacked = jnp.stack(pieces)
    return [
        lax.dynamic_index_in_dim(stacked, meta[plan.at_z + z], 0, keepdims=False)
        for z in range(plan.nrow)
    ]


def join_qkv_kernel(plan, meta, gains, *refs):
    pieces, out, held = refs[: plan.nrow], refs[plan.nrow], refs[plan.nrow + 1]
    width = 3 * plan.cw
    for j in range(plan.nrow):
        held[j] = pieces[j][...]
    for z in range(plan.nrow):
        out[:, width * z : width * (z + 1)] = held[meta[plan.at_z + z]]
    out[:, 3 * D :] = gains[...]


def join_qkv(plan, meta, gains, pieces):
    if not plan.aligned:
        return jnp.concatenate(ordered(plan, meta, pieces) + [gains], axis=1)
    return pl.pallas_call(
        functools.partial(join_qkv_kernel, plan),
        in_specs=[SMEM] + [VMEM] * (1 + plan.nrow),
        out_specs=VMEM,
        out_shape=shape_of((plan.r, EXT), BF16),
        scratch_shapes=[pltpu.VMEM((plan.nrow, plan.r, 3 * plan.cw), BF16)],
        compiler_params=params(),
        cost_estimate=cost(COSTS["join_qkv"]),
        name="join_qkv",
    )(meta, gains, *pieces)


def pack_rest(plan, w_out, w_in, w_down, blank=None):
    cw = plan.cw
    left = jnp.concatenate([w_in[:, :cw], w_in[:, cw : 2 * cw], w_out], axis=0)
    if blank is None:
        blank = jnp.zeros((2 * plan.r - plan.rf, cw), BF16)
    right = jnp.concatenate([w_in[:, 2 * cw :], w_down, blank], axis=0)
    return jnp.concatenate([left, right], axis=1)


def unpack_rest(plan, piece):
    r, rf, cw = plan.r, plan.rf, plan.cw
    parts_in = [piece[:r, :cw], piece[r : 2 * r, :cw], piece[:r, cw:]]
    return parts_in, piece[2 * r : 3 * r, :cw], piece[r : r + rf, cw:]


def join_rest_kernel(plan, meta, *refs):
    pieces, out, held = refs[: plan.nrow], refs[plan.nrow], refs[plan.nrow + 1]
    r, cw = plan.r, plan.cw
    for j in range(plan.nrow):
        held[j] = pieces[j][...]
    for z in range(plan.nrow):
        parts_in, part_out, part_down = unpack_rest(plan, held[meta[plan.at_z + z]])
        out[:r, cw * z : cw * (z + 1)] = part_out
        for i in range(3):
            block, place_at = (3 * z + i) // plan.nrow, (3 * z + i) % plan.nrow
            out[r * (1 + block) : r * (2 + block), cw * place_at : cw * (place_at + 1)] = parts_in[i]
        out[4 * r :, cw * z : cw * (z + 1)] = part_down


def join_rest(plan, meta, pieces):
    if not plan.aligned:
        parts = [unpack_rest(plan, piece) for piece in ordered(plan, meta, pieces)]
        w_in = jnp.concatenate([part for item in parts for part in item[0]], axis=1)
        blocks = [jnp.concatenate([item[1] for item in parts], axis=1)]
        blocks += [w_in[:, D * t : D * (t + 1)] for t in range(3)]
        blocks += [jnp.concatenate([item[2] for item in parts], axis=1)]
        return jnp.concatenate(blocks, axis=0)
    return pl.pallas_call(
        functools.partial(join_rest_kernel, plan),
        in_specs=[SMEM] + [VMEM] * plan.nrow,
        out_specs=VMEM,
        out_shape=shape_of((plan.packed, D), BF16),
        scratch_shapes=[pltpu.VMEM((plan.nrow, 3 * plan.r, 2 * plan.cw), BF16)],
        compiler_params=params(),
        cost_estimate=cost(COSTS["join_rest"]),
        name="join_rest",
    )(meta, *pieces)


def by_block(plan, meta, own, other):
    stacked = jnp.stack(own + other)
    places = meta[plan.at_own : plan.at_other + plan.chips]
    return jnp.zeros_like(stacked).at[places].set(stacked)


def split_blocks(plan, meta, blocks):
    half = plan.chips // 2
    return [
        jnp.take(blocks, meta[plan.at_own + half * i : plan.at_own + half * (i + 1)], axis=0)
        for i in range(4)
    ]


def qkv_sources(plan, meta, own, other):
    if plan.aligned:
        return own + other
    return [by_block(plan, meta, own, other).reshape(D, EXT)]


def rest_sources(plan, meta, own, other):
    if plan.aligned:
        return own + other
    blocks = by_block(plan, meta, own, other)
    r = plan.r
    parts = [blocks[:, r * i : r * (i + 1)].reshape(D, D) for i in range(4)]
    parts.append(blocks[:, 4 * r :].reshape(FF, D))
    return [jnp.concatenate(parts, axis=0)]


def block_size(plan):
    return (plan.r, plan.rf) if plan.aligned else (D, FF)


def block_of(plan, meta, index):
    return meta[plan.at_own + index] if plan.aligned else 0


def rows_at(index, size):
    if isinstance(index, int):
        return pl.ds(index * size, size)
    return pl.ds(pl.multiple_of(index * size, size), size)


class Mover:
    def __init__(self, sems):
        self.sems = sems
        self.used = 0
        self.open = []

    def start(self, source, target):
        copy = pltpu.make_async_copy(source, target, self.sems.at[self.used])
        self.used += 1
        copy.start()
        return copy

    def send(self, source, target):
        self.open.append(self.start(source, target))

    def finish(self):
        for copy in self.open:
            copy.wait()


def wait_all(copies):
    for copy in copies:
        copy.wait()


def qkv_copies(plan, meta, sources, w_ref, sems):
    r, _ = block_size(plan)
    return [
        pltpu.make_async_copy(source, w_ref.at[rows_at(block_of(plan, meta, i), r)], sems.at[i])
        for i, source in enumerate(sources)
    ]


def grad_target(plan, grads, index):
    if not plan.aligned:
        return grads[0]
    half = plan.chips // 2
    return grads[index // half].at[index % half]


def grad_blocks(plan, height, width):
    return [shape_of((plan.chips // 2, height, width), BF16)] * 4


def source_count(plan):
    return 2 * plan.chips if plan.aligned else 1


def qkv_kernel(plan, meta, cos_ref, sin_ref, *refs):
    x_refs = refs[: plan.rows]
    count = source_count(plan)
    sources = refs[plan.rows : plan.rows + count]
    q_ref = refs[plan.rows + count]
    kv_refs = refs[plan.rows + count + 1 : plan.rows + count + 1 + HALVES]
    n_ref, gain_ref, w_ref, sems = refs[plan.rows + count + 1 + HALVES :]
    copies = qkv_copies(plan, meta, sources, w_ref, sems)
    for copy in copies:
        copy.start()
    units = [layer_norm(x_refs[j][0].astype(F32))[0] for j in range(plan.rows)]
    for copy in copies:
        copy.wait()
    gain_ref[...] = w_ref[:, 3 * D :].astype(F32).T[:8, :]
    for j in range(plan.rows):
        n_ref[plan.tok * j : plan.tok * (j + 1), :] = (units[j] * gain_ref[0:1, :]).astype(BF16)
    cosine, sine = cos_ref[...], sin_ref[...]
    normed = n_ref[...]
    queries = dot(normed, w_ref[:, :D], NN)
    q_ref[...] = rotate_all(queries, cosine, sine, 1.0).astype(BF16)
    keys = rotate_all(dot(normed, w_ref[:, D : 2 * D], NN), cosine, sine, 1.0).astype(BF16)
    values = dot(normed, w_ref[:, 2 * D : 3 * D], NN).astype(BF16)
    for h in range(HALVES):
        kv_refs[h][0] = keys[:, HALF * h : HALF * (h + 1)]
        kv_refs[h][1] = values[:, HALF * h : HALF * (h + 1)]


def project(plan, meta, cosine, sine, pieces, sources):
    local = plan.local
    count = len(sources)
    inputs = [meta, cosine, sine, *pieces, *sources]
    return pl.pallas_call(
        functools.partial(qkv_kernel, plan),
        in_specs=[SMEM, VMEM, VMEM] + [VMEM] * plan.rows + [ANY] * count,
        out_specs=[VMEM] * (3 + HALVES),
        out_shape=[shape_of((local, D), BF16)]
        + [shape_of((2, local, HALF), BF16)] * HALVES
        + [shape_of((local, D), BF16), shape_of((8, D), F32)],
        scratch_shapes=[pltpu.VMEM((D, EXT), BF16), pltpu.SemaphoreType.DMA((count,))],
        compiler_params=params(),
        cost_estimate=cost(COSTS["project"]),
        name="project",
    )(*inputs)


def fill_docs(plan, meta, lengths, kmask, qmask):
    low = meta[plan.at_lo]
    ends = []
    passed = jnp.int32(0)
    for n in range(NDOC):
        passed = passed + lengths[low, n]
        ends.append(passed)

    tok = plan.tok
    lane = lax.broadcasted_iota(jnp.int32, (tok, 128), 1) & (HD - 1)
    for i in range(plan.groups * plan.rows):
        places = meta[plan.at_base + i] + lax.broadcasted_iota(jnp.int32, (tok, 128), 0)
        docs = jnp.zeros((tok, 128), jnp.int32)
        for end in ends:
            docs = docs + (places >= end).astype(jnp.int32)
        part = slice(i * tok, (i + 1) * tok)
        same = docs == lane
        kmask[part, :] = jnp.where((lane < NDOC) & ~same, MASKED, 0.0).astype(BF16)
        if i < plan.rows:
            qmask[part, :] = jnp.where(same, 1.0, 0.0).astype(BF16)


def masks(plan, meta, lengths):
    keys = plan.groups * plan.local
    return pl.pallas_call(
        functools.partial(fill_docs, plan),
        in_specs=[SMEM, SMEM],
        out_specs=[VMEM, VMEM],
        out_shape=[shape_of((keys, 128), BF16), shape_of((plan.local, 128), BF16)],
        compiler_params=params(),
        cost_estimate=cost(1),
        name="masks",
    )(meta, lengths)


def head_part(pair, head, other=None):
    lane = lax.broadcasted_iota(jnp.int32, pair.shape, 1)
    keep = (lane < HD) if head == 0 else (lane >= HD)
    return jnp.where(keep, pair, jnp.zeros_like(pair) if other is None else other)


def attend_kernel(plan, width, order, kmask, qmask, q_ref, *refs):
    groups, local = plan.groups, plan.local
    kv = refs[:groups]
    o_ref, low_ref, lse_ref, s_ref, p_ref = refs[groups:]
    total_keys = groups * local
    chunk = 128
    values_t = []
    row = lax.broadcasted_iota(jnp.int32, (HD + 8, total_keys), 0)
    pair_t = jnp.concatenate([kv[e][1].T for e in range(groups)], axis=1)
    for h in range(2):
        head = pair_t[h * HD : (h + 1) * HD, :]
        values_t.append(jnp.concatenate([head, jnp.ones((8, total_keys), BF16)], axis=0))
    for first in range(0, local, width):
        rows = slice(first, first + width)
        queries = q_ref[rows, :] * jnp.asarray(1.0 / math.sqrt(HD), BF16)
        tops = []
        for h in range(2):
            head_queries = head_part(queries, h, qmask[rows, :])
            top = jnp.full((8, width), MASKED, F32)
            for e in range(groups):
                for c in range(0, local, 2 * chunk):
                    part = slice(e * local + c, e * local + c + 2 * chunk)
                    keys = head_part(kv[e][0, c : c + 2 * chunk, :], h, kmask[part, :])
                    scores = dot(keys, head_queries, NT)
                    s_ref[h, part, :] = scores
                    top = jnp.maximum(top, jnp.max(scores.reshape(-1, 8, width), axis=0))
            tops.append(jnp.max(top, axis=0, keepdims=True))
        parts = []
        for h in range(2):
            for c in range(0, total_keys, chunk):
                part = slice(c, c + chunk)
                p_ref[h, part, :] = jnp.exp(s_ref[h, part, :] - tops[h]).astype(BF16)
            weighted = dot(values_t[h], p_ref[h], NN)
            total = weighted[HD : HD + 1, :]
            parts.append(weighted[:HD, :] / total)
            lse_ref[0, h : h + 1, rows] = tops[h] + jnp.log(total)
        heads = jnp.concatenate(parts, axis=0).T
        o_ref[rows, :] = heads
        low_ref[rows, :] = heads.astype(BF16)


def attend(plan, part, meta, mask, queries, kv):
    local, groups = plan.local, plan.groups
    width = min(512, local)
    skip = part * HALF_PAIRS
    pair = pl.BlockSpec((local, 128), lambda p: (0, p))
    pair_q = pl.BlockSpec((local, 128), lambda p: (0, p + skip))
    pair_kv = pl.BlockSpec((2, local, 128), lambda p: (0, 0, p))
    whole_k = pl.BlockSpec((groups * local, 128), lambda p: (0, 0))
    whole_q = pl.BlockSpec((local, 128), lambda p: (0, 0))
    inputs = [meta, *mask, queries, *kv]
    return pl.pallas_call(
        functools.partial(attend_kernel, plan, width),
        grid=(HALF_PAIRS,),
        in_specs=[SMEM, whole_k, whole_q, pair_q] + [pair_kv] * groups,
        out_specs=[pair, pair, pl.BlockSpec((1, 2, local), lambda p: (p, 0, 0))],
        out_shape=[
            shape_of((local, HALF), F32),
            shape_of((local, HALF), BF16),
            shape_of((HALF_PAIRS, 2, local), F32),
        ],
        scratch_shapes=[
            pltpu.VMEM((2, groups * local, width), F32),
            pltpu.VMEM((2, groups * local, width), BF16),
        ],
        compiler_params=params(),
        cost_estimate=cost(COSTS["attend"]),
        name="attend",
    )(*inputs)


def attend_back_kernel(
    plan, width, order, kmask, qmask, q_ref, do_ref, o_ref, lse_ref, cos_ref, sin_ref, *refs
):
    groups, local = plan.groups, plan.local
    kv = refs[:groups]
    dq_ref = refs[groups]
    dkv = refs[groups + 1 : 2 * groups + 1]
    held, p_ref, ds_ref = refs[2 * groups + 1 :]
    keys_t = [kv[e][0].T for e in range(groups)]
    scale = 1.0 / math.sqrt(HD)
    chunk = 128
    for first in range(0, local, width):
        rows = slice(first, first + width)
        queries = q_ref[rows, :] * jnp.asarray(scale, BF16)
        dout = do_ref[rows, :]
        product = (dout.astype(F32) * o_ref[rows, :]).T
        parts = []
        for h in range(2):
            masked_queries = head_part(queries, h, qmask[rows, :])
            head_queries = head_part(queries, h)
            head_dout = head_part(dout, h)
            lse = lse_ref[0, h : h + 1, rows]
            delta = jnp.sum(product[h * HD : (h + 1) * HD, :], axis=0, keepdims=True)
            grad_queries = jnp.zeros((HD, width), F32)
            for e in range(groups):
                for c in range(0, local, chunk):
                    part = slice(c, c + chunk)
                    mask = kmask[e * local + c : e * local + c + chunk, :]
                    scores = dot(head_part(kv[e][0, part, :], h, mask), masked_queries, NT)
                    dprobs = dot(kv[e][1, part, :], head_dout, NT)
                    probs = jnp.exp(scores - lse)
                    p_ref[h, e, part, :] = probs.astype(BF16)
                    ds_ref[h, e, part, :] = (probs * (dprobs - delta)).astype(BF16)
                grad_values = dot(p_ref[h, e], head_dout, NN)
                grad_keys = dot(ds_ref[h, e], head_queries, NN)
                if first == 0 and h == 0:
                    held[e, 0] = grad_keys
                    held[e, 1] = grad_values
                else:
                    held[e, 0] += grad_keys
                    held[e, 1] += grad_values
                grad_queries = grad_queries + dot(
                    keys_t[e][h * HD : (h + 1) * HD, :], ds_ref[h, e], NN
                )
            parts.append(grad_queries)
        grad = jnp.concatenate(parts, axis=0).T * scale
        dq_ref[rows, :] = rotate_pair(grad, cos_ref[rows, :], sin_ref[rows, :], -1.0).astype(BF16)
    for e in range(groups):
        dkv[e][...] = held[e].astype(BF16)


def attend_back(plan, part, meta, mask, queries, dout, heads, lse, cosine, sine, kv):
    local, groups = plan.local, plan.groups
    width = min(512, local)
    half, first, count = part
    skip = half * HALF_PAIRS + first
    wide = 128 * count
    pair = pl.BlockSpec((local, 128), lambda p: (0, p))
    pair_h = pl.BlockSpec((local, 128), lambda p: (0, p + first))
    pair_q = pl.BlockSpec((local, 128), lambda p: (0, p + skip))
    whole_k = pl.BlockSpec((groups * local, 128), lambda p: (0, 0))
    inputs = [meta, *mask, queries, dout, heads, lse, cosine, sine, *kv]
    table = pl.BlockSpec((local, 128), lambda p: (0, 0))
    pair_kv = pl.BlockSpec((2, local, 128), lambda p: (0, 0, p))
    pair_kv_h = pl.BlockSpec((2, local, 128), lambda p: (0, 0, p + first))
    return pl.pallas_call(
        functools.partial(attend_back_kernel, plan, width),
        grid=(count,),
        in_specs=[
            SMEM,
            whole_k,
            table,
            pair_q,
            pair_q,
            pair_h,
            pl.BlockSpec((1, 2, local), lambda p: (p + first, 0, 0)),
            table,
            table,
        ]
        + [pair_kv_h] * groups,
        out_specs=[pair] + [pair_kv] * groups,
        out_shape=[shape_of((local, wide), BF16)] + [shape_of((2, local, wide), BF16)] * groups,
        scratch_shapes=[
            pltpu.VMEM((groups, 2, local, 128), F32),
            pltpu.VMEM((2, groups, local, width), BF16),
            pltpu.VMEM((2, groups, local, width), BF16),
        ],
        compiler_params=params(),
        cost_estimate=cost(4 * count),
        name="attend_back",
    )(*inputs)


def middle_kernel(plan, meta, gain_ref, *refs):
    rows, tok, local = plan.rows, plan.tok, plan.local
    count = source_count(plan)
    low_refs, refs = refs[:HALVES], refs[HALVES:]
    x_refs, refs = refs[:rows], refs[rows:]
    sources, refs = refs[:count], refs[count:]
    out_refs, refs = refs[:rows], refs[rows:]
    do_out, dh_out, refs = refs[0], refs[1], refs[2:]
    grads, refs = refs[: 4 if plan.aligned else 1], refs[4 if plan.aligned else 1 :]
    low_ref, x_ref, dy_ref, w_out, w_in, w_down, h_ref, unit_ref, n_ref, gu_ref = refs[:10]
    mid_ref, dgu_ref, out_ref, do_ref, dh_ref, da_ref, g_out, g_in, g_down, sems = refs[10:]
    mover = Mover(sems)
    r, rf = block_size(plan)
    blocks = [block_of(plan, meta, i) for i in range(count)]
    low_in = [
        mover.start(low_refs[h], low_ref.at[:, pl.ds(HALF * h, HALF)]) for h in range(HALVES)
    ]
    out_in = [
        mover.start(source.at[pl.ds(0, r)], w_out.at[rows_at(block, r)])
        for source, block in zip(sources, blocks)
    ]
    x_in = [mover.start(x_refs[j].at[0], x_ref.at[pl.ds(tok * j, tok)]) for j in range(rows)]

    def fetch_in(t):
        return [
            mover.start(source.at[pl.ds((1 + t) * r, r)], w_in.at[t, rows_at(block, r)])
            for source, block in zip(sources, blocks)
        ]

    wait_all(low_in)
    in_in = [fetch_in(0)]
    wait_all(out_in)
    wait_all(x_in)
    in_in.append(fetch_in(1))
    gain = gain_ref[1:2, :]
    inv_stds = []
    for j in range(rows):
        part = slice(tok * j, tok * (j + 1))
        hidden = x_ref[part, :].astype(F32) + dot(low_ref[part, :], w_out[...], NN)
        h_ref[part, :] = hidden
        unit, inv_std = layer_norm(hidden)
        inv_stds.append(inv_std)
        unit_ref[part, :] = unit
        n_ref[part, :] = (unit * gain).astype(BF16)
    for t in range(3):
        wait_all(in_in[t])
        if t == 0:
            in_in.append(fetch_in(2))
        if t == 1:
            dy_in = [
                mover.start(x_refs[j].at[1], dy_ref.at[pl.ds(tok * j, tok)]) for j in range(rows)
            ]
            down_in = [
                mover.start(source.at[pl.ds(4 * r, rf)], w_down.at[rows_at(block, rf)])
                for source, block in zip(sources, blocks)
            ]
        gu_ref[:, D * t : D * (t + 1)] = dot(n_ref[...], w_in[t], NN)
    wait_all(dy_in)
    wait_all(down_in)
    dy = dy_ref[...]
    size = FF // 3
    for f in range(3):
        cols = slice(size * f, size * (f + 1))
        up_cols = slice(FF + size * f, FF + size * (f + 1))
        gate = gu_ref[:, cols]
        up = gu_ref[:, up_cols]
        below = 0.5 + 0.5 * lax.erf(gate * math.sqrt(0.5))
        active = gate * below
        mid_ref[:, cols] = (active * up).astype(BF16)
        slope = below + gate * jnp.exp(-0.5 * gate * gate) * (1.0 / math.sqrt(2.0 * math.pi))
        dmid = dot(dy, w_down[cols, :], NT)
        dgu_ref[:, cols] = (dmid * up * slope).astype(BF16)
        dgu_ref[:, up_cols] = (dmid * active).astype(BF16)
    targets = [grad_target(plan, grads, i) for i in range(count)]
    g_down[...] = dot(mid_ref[...], dy, TN).astype(BF16)
    for target, block in zip(targets, blocks):
        mover.send(g_down.at[rows_at(block, rf)], target.at[pl.ds(4 * r, rf)])
    out_ref[...] = (h_ref[...] + dot(mid_ref[...], w_down[...], NN)).astype(BF16)
    for j in range(rows):
        mover.send(out_ref.at[pl.ds(tok * j, tok)], out_refs[j])
    grad_normed = dot(dgu_ref[:, :D], w_in[0], NT)
    for t in range(1, 3):
        grad_normed = grad_normed + dot(dgu_ref[:, D * t : D * (t + 1)], w_in[t], NT)
    dh_ref[...] = grad_normed

    def grad_in(t):
        g_in[t] = dot(n_ref[...], dgu_ref[:, D * t : D * (t + 1)], TN).astype(BF16)
        for target, block in zip(targets, blocks):
            mover.send(g_in.at[t, rows_at(block, r)], target.at[pl.ds((1 + t) * r, r)])

    for j in range(rows):
        part = slice(tok * j, tok * (j + 1))
        grad_hidden = dy[part, :].astype(F32) + norm_backward(
            dh_ref[part, :], unit_ref[part, :], inv_stds[j], gain
        )
        dh_ref[part, :] = grad_hidden
        da_ref[part, :] = grad_hidden.astype(BF16)
        if j < 3:
            grad_in(j)
    for t in range(rows, 3):
        grad_in(t)
    mover.send(dh_ref, dh_out)
    do_ref[...] = dot(da_ref[...], w_out[...], NT).astype(BF16)
    mover.send(do_ref, do_out)
    g_out[...] = dot(low_ref[...], da_ref[...], TN).astype(BF16)
    for target, block in zip(targets, blocks):
        mover.send(g_out.at[rows_at(block, r)], target.at[pl.ds(0, r)])
    mover.finish()


def middle(plan, meta, low, gains, pieces, sources):
    local, rows, tok = plan.local, plan.rows, plan.tok
    count = len(sources)
    total = 4 * D + FF
    if plan.aligned:
        grads = grad_blocks(plan, plan.packed, D)
    else:
        grads = [shape_of((total, D), BF16)]
    return pl.pallas_call(
        functools.partial(middle_kernel, plan),
        in_specs=[SMEM, VMEM] + [ANY] * (HALVES + rows + count),
        out_specs=[ANY] * (rows + 2 + len(grads)),
        out_shape=[shape_of((tok, D), BF16)] * rows
        + [shape_of((local, D), BF16), shape_of((local, D), F32)]
        + grads,
        scratch_shapes=[
            pltpu.VMEM((local, D), BF16),
            pltpu.VMEM((local, D), BF16),
            pltpu.VMEM((local, D), BF16),
            pltpu.VMEM((D, D), BF16),
            pltpu.VMEM((3, D, D), BF16),
            pltpu.VMEM((FF, D), BF16),
            pltpu.VMEM((local, D), F32),
            pltpu.VMEM((local, D), F32),
            pltpu.VMEM((local, D), BF16),
            pltpu.VMEM((local, 2 * FF), F32),
            pltpu.VMEM((local, FF), BF16),
            pltpu.VMEM((local, 2 * FF), BF16),
            pltpu.VMEM((local, D), BF16),
            pltpu.VMEM((local, D), BF16),
            pltpu.VMEM((local, D), F32),
            pltpu.VMEM((local, D), BF16),
            pltpu.VMEM((D, D), BF16),
            pltpu.VMEM((3, D, D), BF16),
            pltpu.VMEM((FF, D), BF16),
            pltpu.SemaphoreType.DMA((HALVES + 3 * rows + 2 + 10 * count,)),
        ],
        compiler_params=params(),
        cost_estimate=cost(COSTS["middle"]),
        name="middle",
    )(meta, gains, *low, *pieces, *sources)


def back_weight_kernel(plan, meta, *refs):
    groups, local = plan.groups, plan.local
    count = len(BACK_PARTS)
    cos_ref, sin_ref, n_in, refs = refs[0], refs[1], refs[2], refs[3:]
    dq_refs, refs = refs[:count], refs[count:]
    dkv, refs = refs[: count * groups], refs[count * groups :]
    dp_out, refs = refs[0], refs[1:]
    grads, refs = refs[: 4 if plan.aligned else 1], refs[4 if plan.aligned else 1 :]
    cos, sin, n_ref, dkv_ref, dp_ref, g_ref, sems = refs
    mover = Mover(sems)
    columns = []
    for half, first, pairs in BACK_PARTS:
        columns.append(pl.ds(HALF * half + 128 * first, 128 * pairs))
    first_in = [mover.start(n_in, n_ref)]
    for i in range(count):
        first_in.append(mover.start(dq_refs[i], dp_ref.at[0, :, columns[i]]))
    rest_in = [mover.start(cos_ref, cos), mover.start(sin_ref, sin)]
    for i in range(count):
        for e in range(groups):
            rest_in.append(
                mover.start(dkv[groups * i + e], dkv_ref.at[e, :, :, columns[i]])
            )
    r, _ = block_size(plan)

    def send_grad(t):
        cols = pl.ds(D * t, D)
        for i in range(source_count(plan)):
            at = rows_at(block_of(plan, meta, i), r)
            mover.send(g_ref.at[at, cols], grad_target(plan, grads, i).at[:, cols])

    wait_all(first_in)
    normed = n_ref[...]
    g_ref[:, :D] = dot(normed, dp_ref[0], TN).astype(BF16)
    send_grad(0)
    wait_all(rest_in)
    dp_ref[2] = sum_pieces([dkv_ref[e, 1] for e in range(groups)]).astype(BF16)
    g_ref[:, 2 * D : 3 * D] = dot(normed, dp_ref[2], TN).astype(BF16)
    send_grad(2)
    grad_keys = sum_pieces([dkv_ref[e, 0] for e in range(groups)])
    dp_ref[1] = rotate_all(grad_keys, cos[...], sin[...], -1.0).astype(BF16)
    mover.send(dp_ref, dp_out)
    g_ref[:, D : 2 * D] = dot(normed, dp_ref[1], TN).astype(BF16)
    send_grad(1)
    mover.finish()


def back_weight(plan, meta, cosine, sine, normed, dq, dkv):
    local, groups, count = plan.local, plan.groups, len(BACK_PARTS)
    if plan.aligned:
        grads = grad_blocks(plan, plan.r, 3 * D)
    else:
        grads = [shape_of((D, 3 * D), BF16)]
    results = pl.pallas_call(
        functools.partial(back_weight_kernel, plan),
        in_specs=[SMEM] + [ANY] * (3 + count * (1 + groups)),
        out_specs=[ANY] * (1 + len(grads)),
        out_shape=[shape_of((3, local, D), BF16)] + grads,
        scratch_shapes=[
            pltpu.VMEM((local, 128), F32),
            pltpu.VMEM((local, 128), F32),
            pltpu.VMEM((local, D), BF16),
            pltpu.VMEM((groups, 2, local, D), BF16),
            pltpu.VMEM((3, local, D), BF16),
            pltpu.VMEM((D, 3 * D), BF16),
            pltpu.SemaphoreType.DMA((4 + count * (1 + groups) + 3 * source_count(plan),)),
        ],
        compiler_params=params(),
        cost_estimate=cost(COSTS["back_weight"]),
        name="back_weight",
    )(meta, cosine, sine, normed, *dq, *dkv)
    return results[0], results[1:]


def back_in_kernel(plan, meta, dp_ref, dh_ref, gain_ref, *refs):
    rows, tok = plan.rows, plan.tok
    count = source_count(plan)
    x_refs, refs = refs[:rows], refs[rows:]
    out_refs, refs = refs[:rows], refs[rows:]
    sources, refs = refs[:count], refs[count:]
    both_refs = refs[:rows]
    w_ref, in_sems = refs[rows:]
    copies = qkv_copies(plan, meta, sources, w_ref, in_sems)
    for copy in copies:
        copy.start()
    for copy in copies:
        copy.wait()
    grad_normed = dot(dp_ref[0], w_ref[:, :D], NT)
    for t in range(1, 3):
        grad_normed = grad_normed + dot(dp_ref[t], w_ref[:, D * t : D * (t + 1)], NT)
    for j in range(rows):
        part = slice(tok * j, tok * (j + 1))
        unit, inv_std = layer_norm(x_refs[j][0].astype(F32))
        grad = grad_normed[part, :]
        back = norm_backward(grad, unit, inv_std, gain_ref[0:1, :])
        both_refs[j][0] = out_refs[j][...]
        both_refs[j][1] = (dh_ref[part, :] + back).astype(BF16)


def back_in(plan, meta, dprojected, dhidden, gains, pieces, outs, sources):
    rows, tok = plan.rows, plan.tok
    count = len(sources)
    return pl.pallas_call(
        functools.partial(back_in_kernel, plan),
        in_specs=[SMEM] + [VMEM] * (3 + 2 * rows) + [ANY] * count,
        out_specs=[VMEM] * rows,
        out_shape=[shape_of((2, tok, D), BF16)] * rows,
        scratch_shapes=[pltpu.VMEM((D, EXT), BF16), pltpu.SemaphoreType.DMA((count,))],
        compiler_params=params(),
        cost_estimate=cost(COSTS["back_in"]),
        name="back_in",
    )(meta, dprojected, dhidden, gains, *pieces, *outs, *sources)


def gain_columns(weight, grad):
    total = jnp.sum(weight.astype(F32) * grad.astype(F32), axis=1, keepdims=True)
    high = total.astype(BF16)
    return high, (total - high.astype(F32)).astype(BF16)


def pad_width(plan):
    return -(-(3 * plan.cw + 2) // 128) * 128


def gain_tail(plan, weight, grad):
    width = pad_width(plan) - 3 * plan.cw
    high, rest = gain_columns(weight, grad)
    lane = lax.broadcasted_iota(jnp.int32, (plan.r, width), 1)
    return jnp.where(lane == 0, high, jnp.where(lane == 1, rest, jnp.zeros_like(high)))


def cut_qkv_kernel(plan, meta, total, weight, *refs):
    outs, held = refs[: plan.nrow], refs[plan.nrow]
    width = 3 * plan.cw
    tail = gain_tail(plan, weight[:, : 3 * D], total[...])
    for z in range(plan.nrow):
        place_at = meta[plan.at_z + z]
        held[place_at, :, :width] = total[:, width * z : width * (z + 1)]
        held[place_at, :, width:] = tail
    for j in range(plan.nrow):
        outs[j][...] = held[j]


def cut_qkv(plan, meta, total, weight):
    width, wide = 3 * plan.cw, pad_width(plan)
    if not plan.aligned:
        tail = gain_tail(plan, weight[:, : 3 * D], total)
        parts = [
            jnp.concatenate([total[:, width * z : width * (z + 1)], tail], axis=1)
            for z in range(plan.nrow)
        ]
        return ordered(plan, meta, parts)
    return pl.pallas_call(
        functools.partial(cut_qkv_kernel, plan),
        in_specs=[SMEM, VMEM, VMEM],
        out_specs=[VMEM] * plan.nrow,
        out_shape=[shape_of((plan.r, wide), BF16)] * plan.nrow,
        scratch_shapes=[pltpu.VMEM((plan.nrow, plan.r, wide), BF16)],
        compiler_params=params(),
        cost_estimate=cost(COSTS["cut_qkv"]),
        name="cut_qkv",
    )(meta, total, weight)


def gain_blank(plan, weight, grad):
    r, blank = plan.r, 2 * plan.r - plan.rf
    cols = [weight[r * t : r * (t + 1)] for t in range(1, 4)]
    grads = [grad[r * t : r * (t + 1)] for t in range(1, 4)]
    high, rest = gain_columns(jnp.concatenate(cols, axis=1), jnp.concatenate(grads, axis=1))
    lane = lax.broadcasted_iota(jnp.int32, (blank, plan.cw), 1)
    found = jnp.zeros((blank, plan.cw), BF16)
    for i in range(r // blank):
        part = slice(blank * i, blank * (i + 1))
        found = jnp.where(lane == 2 * i, high[part], found)
        found = jnp.where(lane == 2 * i + 1, rest[part], found)
    return found


def cut_rest_kernel(plan, meta, total, weight, *refs):
    outs, held = refs[: plan.nrow], refs[plan.nrow]
    r, rf, cw = plan.r, plan.rf, plan.cw
    blank = gain_blank(plan, weight[...], total[...])
    for z in range(plan.nrow):
        place_at = meta[plan.at_z + z]
        cols = slice(cw * z, cw * (z + 1))
        parts = []
        for i in range(3):
            block, at = (3 * z + i) // plan.nrow, (3 * z + i) % plan.nrow
            parts.append(total[r * (1 + block) : r * (2 + block), cw * at : cw * (at + 1)])
        held[place_at, :r, :] = jnp.concatenate([parts[0], parts[2]], axis=1)
        held[place_at, r : 2 * r, :] = jnp.concatenate(
            [parts[1], total[4 * r : 5 * r, cols]], axis=1
        )
        rest = total[5 * r : 4 * r + rf, cols]
        held[place_at, 2 * r :, :] = jnp.concatenate(
            [total[:r, cols], jnp.concatenate([rest, blank], axis=0)], axis=1
        )
    for j in range(plan.nrow):
        outs[j][...] = held[j]


def cut_rest(plan, meta, total, weight):
    r, cw = plan.r, plan.cw
    if not plan.aligned:
        grad_in = jnp.concatenate([total[r * (1 + t) : r * (2 + t)] for t in range(3)], axis=1)
        blank = gain_blank(plan, weight, total)
        parts = [
            pack_rest(
                plan,
                total[:r, cw * z : cw * (z + 1)],
                grad_in[:, 3 * cw * z : 3 * cw * (z + 1)],
                total[4 * r :, cw * z : cw * (z + 1)],
                blank,
            )
            for z in range(plan.nrow)
        ]
        return ordered(plan, meta, parts)
    return pl.pallas_call(
        functools.partial(cut_rest_kernel, plan),
        in_specs=[SMEM, VMEM, VMEM],
        out_specs=[VMEM] * plan.nrow,
        out_shape=[shape_of((3 * r, 2 * cw), BF16)] * plan.nrow,
        scratch_shapes=[pltpu.VMEM((plan.nrow, 3 * r, 2 * cw), BF16)],
        compiler_params=params(),
        cost_estimate=cost(COSTS["cut_rest"]),
        name="cut_rest",
    )(meta, total, weight)


def reduce_z(plan, pieces):
    return [pieces[0]] + [
        lax.ppermute(pieces[j], "row", plan.z_pairs(j)) for j in range(1, plan.nrow)
    ]


def sum_pieces(pieces):
    total = pieces[0].astype(F32)
    for piece in pieces[1:]:
        total = total + piece.astype(F32)
    return total


def end_rest_kernel(plan, *refs):
    pieces, (g_out, g_in, g_down, g_gain) = refs[: plan.nrow], refs[plan.nrow :]
    total = sum_pieces([piece[...] for piece in pieces])
    parts_in, part_out, part_down = unpack_rest(plan, total)
    g_out[...] = part_out
    g_in[...] = jnp.concatenate(parts_in, axis=1)
    g_down[...] = part_down
    blank = 2 * plan.r - plan.rf
    g_gain[...] = total[3 * plan.r - blank :, plan.cw : plan.cw + 128].T[:8, :]


def end_rest(plan, pieces):
    r, blank = plan.r, 2 * plan.r - plan.rf
    if not plan.aligned:
        total = sum_pieces(pieces)
        parts_in, out_grad, down_grad = unpack_rest(plan, total)
        in_grad = jnp.concatenate(parts_in, axis=1)
        gain = total[3 * r - blank :, plan.cw : plan.cw + 8].T
    else:
        out_grad, in_grad, down_grad, gain = pl.pallas_call(
            functools.partial(end_rest_kernel, plan),
            in_specs=[VMEM] * plan.nrow,
            out_specs=[VMEM] * 4,
            out_shape=[
                shape_of((r, plan.cw), F32),
                shape_of((r, 3 * plan.cw), F32),
                shape_of((plan.rf, plan.cw), F32),
                shape_of((8, blank), F32),
            ],
            compiler_params=params(),
            cost_estimate=cost(COSTS["end_rest"]),
            name="end_rest",
        )(*pieces)
    gain = jnp.concatenate([gain[2 * i] + gain[2 * i + 1] for i in range(r // blank)])
    return out_grad, in_grad, down_grad, gain


def end_qkv_kernel(plan, gain_ref, *refs):
    pieces, (g_qkv, g_gain) = refs[: plan.nrow], refs[plan.nrow :]
    width, wide = 3 * plan.cw, pad_width(plan)
    total = sum_pieces([piece[...] for piece in pieces])
    g_qkv[...] = total[:, :width]
    tail = total[:, wide - 128 :].T
    at = width - (wide - 128)
    g_gain[...] = (tail[at : at + 1, :] + tail[at + 1 : at + 2, :]) / gain_ref[...]


def end_qkv(plan, gain, pieces):
    width, wide = 3 * plan.cw, pad_width(plan)
    if not plan.aligned:
        total = sum_pieces(pieces)
        return total[:, :width], (total[:, width] + total[:, width + 1]) / gain[0]
    grad, gain_grad = pl.pallas_call(
        functools.partial(end_qkv_kernel, plan),
        in_specs=[VMEM] * (1 + plan.nrow),
        out_specs=[VMEM] * 2,
        out_shape=[shape_of((plan.r, width), F32), shape_of((1, plan.r), F32)],
        compiler_params=params(),
        cost_estimate=cost(COSTS["end_qkv"]),
        name="end_qkv",
    )(gain, *pieces)
    return grad, gain_grad.reshape(plan.r)


def rotation_tables(plan, meta, lengths):
    ends = jnp.cumsum(lax.dynamic_index_in_dim(lengths, meta[plan.at_lo], 0, keepdims=False))
    starts = jnp.concatenate([jnp.zeros((1,), jnp.int32), ends[:-1]])
    bases = meta[plan.at_base : plan.at_base + plan.rows]
    places = (bases[:, None] + jnp.arange(plan.tok, dtype=jnp.int32)[None, :]).reshape(-1)
    passed = places[:, None] >= starts[None, :]
    positions = places - jnp.max(jnp.where(passed, starts[None, :], 0), axis=1)
    half = HD // 2
    inverse = ROPE_BASE ** (-(jnp.arange(half, dtype=F32) * (2.0 / HD)))
    angles = positions.astype(F32)[:, None] * inverse
    cosine, sine = jnp.cos(angles), jnp.sin(angles)
    return (
        jnp.concatenate([cosine] * 4, axis=1),
        jnp.concatenate([-sine, sine, -sine, sine], axis=1),
    )


def body(
    plan,
    tokens,
    lengths,
    norm_gain,
    qkv_weight,
    out_weight,
    mlp_gain,
    in_weight,
    down_weight,
    cotangent,
):
    blk, row = lax.axis_index("blk"), lax.axis_index("row")
    meta = lax.dynamic_slice(
        jnp.asarray(plan.table), (row, blk, 0), (1, 1, plan.size)
    ).reshape(plan.size)
    qkv_parts = gather_z(plan, qkv_weight)
    cut, packed = prepare(plan, meta, tokens, cotangent, out_weight, in_weight, down_weight)
    pieces = exchange_rows(plan, cut)
    rest_parts = gather_z(plan, packed, behind=qkv_parts)
    gains = jnp.pad(jnp.stack([norm_gain, mlp_gain], axis=1), ((0, 0), (0, 126)))
    cosine, sine = rotation_tables(plan, meta, lengths)
    mask = masks(plan, meta, lengths)
    qkv_parts[0] = tie(qkv_parts[0], rest_parts[1])
    qkv_joined = join_qkv(plan, meta, gains, qkv_parts)
    qkv_own = gather_start(plan, qkv_joined)
    qkv_own[1] = tie(qkv_own[1], *rest_parts[2:], *pieces[1:], cosine, sine, *mask)
    qkv_own = gather_more(plan, qkv_own)
    qkv_other = [swap_cores(plan, piece) for piece in qkv_own]
    qkv_from = qkv_sources(plan, meta, qkv_own, qkv_other)
    rest_parts[0] = tie(rest_parts[0], qkv_joined, *qkv_other[:-1])
    joined = join_rest(plan, meta, rest_parts)
    results = project(plan, tie(meta, joined), cosine, sine, pieces, qkv_from)
    queries, kv, (normed, gains) = results[0], results[1 : 1 + HALVES], results[1 + HALVES :]
    kv = [
        [part]
        + [
            lax.ppermute(part, "blk", plan.xor_pairs(plan.member(e)))
            for e in range(1, plan.groups)
        ]
        for part in kv
    ]
    rest_own = gather_start(plan, joined)
    heads, low, lse = [None] * HALVES, [None] * HALVES, [None] * HALVES
    heads[0], low[0], lse[0] = attend(plan, 0, meta, mask, queries, kv[0])
    order = tie(meta, low[0], *rest_own[1:])
    rest_own[1:] = [tie(piece, low[0]) for piece in rest_own[1:]]
    rest_other = [swap_cores(plan, piece) for piece in rest_own]
    rest_more = gather_more(plan, rest_own)[len(rest_own) :]
    heads[1], low[1], lse[1] = attend(plan, 1, order, mask, queries, kv[1])
    rest_more = [tie(piece, low[1]) for piece in rest_more]
    rest_own = rest_own + rest_more
    rest_other = rest_other + [swap_cores(plan, piece) for piece in rest_more]
    rest_from = rest_sources(plan, meta, rest_own, rest_other)
    results = middle(plan, meta, low, gains, pieces, rest_from)
    outs, (dout, dhidden), rest_grads = (
        results[: plan.rows],
        results[plan.rows : plan.rows + 2],
        results[plan.rows + 2 :],
    )
    if not plan.aligned:
        r, rf, nblk = plan.r, plan.rf, plan.nblk
        whole = rest_grads[0]
        blocks = [whole[D * i : D * (i + 1)].reshape(nblk, r, D) for i in range(4)]
        blocks.append(whole[4 * D :].reshape(nblk, rf, D))
        rest_grads = split_blocks(plan, meta, jnp.concatenate(blocks, axis=1))
    keep_low, keep_high, other_low, other_high = reduce_start(plan, rest_grads)
    dq, dkv = [], []
    order = meta
    for i, part in enumerate(BACK_PARTS):
        half = part[0]
        results = attend_back(
            plan, part, order, mask, queries, dout, heads[half], lse[half], cosine, sine, kv[half]
        )
        dq.append(results[0])
        dkv.append(results[1])
        dkv += [
            lax.ppermute(results[1 + e], "blk", plan.xor_pairs(plan.member(e)))
            for e in range(1, plan.groups)
        ]
        if i == 0:
            rest_high = add_low(tie(keep_high, dq[0]), other_high)
            rest_low = add_low(tie(keep_low, dq[0]), other_low)
            order = tie(meta, dq[0], rest_high, rest_low)
        else:
            order = tie(meta, dq[i], *dkv[1 : plan.groups])
    rest_low, rest_high = reduce_step(plan, plan.bits - 1, tie(rest_low, dq[-1]), rest_high)
    order = tie(meta, rest_low) if rest_high is None else tie(meta, rest_low, rest_high)
    dprojected, qkv_grads = back_weight(plan, order, cosine, sine, normed, dq, dkv)
    if not plan.aligned:
        qkv_grads = split_blocks(plan, meta, qkv_grads[0].reshape(plan.nblk, plan.r, 3 * D))
    rest_low = tie(rest_low, dprojected)
    for step in reversed(range(plan.bits - 1)):
        rest_low, rest_high = reduce_step(plan, step, rest_low, rest_high)
    keep_low, keep_high, other_low, other_high = reduce_start(plan, qkv_grads)
    qkv_high = add_low(tie(keep_high, rest_low), other_high)
    qkv_low = add_low(keep_low, other_low)
    rest_cut = cut_rest(plan, meta, tie(rest_low, qkv_high), joined)
    order = tie(meta, qkv_high, qkv_low, *rest_cut)
    both = back_in(plan, order, dprojected, dhidden, gains, pieces, outs, qkv_from)
    rest_pieces = reduce_z(plan, rest_cut)
    qkv_low = tie(qkv_low, both[0], *rest_pieces[1:3])
    for step in reversed(range(plan.bits)):
        if step == 0:
            qkv_low = tie(qkv_low, *rest_pieces[3:])
        qkv_low, qkv_high = reduce_step(plan, step, qkv_low, qkv_high)
    both = exchange_rows(plan, [tie(piece, qkv_low) for piece in both])
    qkv_cut = cut_qkv(plan, meta, tie(qkv_low, *rest_pieces[1:]), qkv_joined)
    qkv_pieces = reduce_z(plan, qkv_cut)
    rest_pieces[0] = tie(rest_pieces[0], *qkv_cut)
    out_grad, in_grad, down_grad, mlp_gain_grad = end_rest(plan, rest_pieces)
    output, input_grad = place(plan, meta, [tie(both[0], *qkv_cut)] + both[1:])
    gain_row = norm_gain.astype(F32)[None]
    qkv_grad, norm_gain_grad = end_qkv(plan, tie(gain_row, output, input_grad, in_grad), qkv_pieces)
    mlp_gain_grad = mlp_gain_grad / mlp_gain.astype(F32)
    return (
        output,
        input_grad,
        norm_gain_grad,
        qkv_grad,
        out_grad,
        mlp_gain_grad,
        in_grad,
        down_grad,
    )


def solution(mesh):
    weights = P("blk", "row")
    acts = P("row", "blk", None)

    def run(*args):
        rows = args[0].shape[0] // mesh.shape["row"]
        tok = args[0].shape[1] // mesh.shape["blk"]
        plan = Plan(mesh, rows, tok)
        return jax.shard_map(
            functools.partial(body, plan),
            mesh=mesh,
            in_specs=(acts, P("row", None), P("blk"), weights, weights, P("blk"), weights, weights, acts),
            out_specs=(acts, acts, P("blk"), weights, weights, P("blk"), weights, weights),
            check_vma=False,
        )(*args)

    return run
```

```python
import functools
import math

import jax
import jax.numpy as jnp
import numpy as np
from jax import lax
from jax.experimental import pallas as pl
from jax.experimental.pallas import tpu as pltpu
from jax.sharding import PartitionSpec as P

D = 768
HEADS = 12
HD = 64
FF = 1152
NDOC = 8
PAIRS = HEADS // 2
EXT = 3 * D + 128

ROPE_BASE = 160000.0
NORM_EPSILON = 1e-05
MASKED = -1e30
F32 = jnp.float32
BF16 = jnp.bfloat16
NN = (((1,), (0,)), ((), ()))
NT = (((1,), (1,)), ((), ()))
TN = (((0,), (0,)), ((), ()))
VMEM_BYTES = 40 * 1024 * 1024
HALVES = 2
HALF_PAIRS = PAIRS // HALVES
HALF = D // HALVES
BACK_PARTS = ((0, 0, 1), (0, 1, 2), (1, 0, 3))
COSTS = {
    "prepare": 4,
    "place_rows": 2,
    "join_qkv": 2,
    "join_rest": 2,
    "project": 7,
    "attend": 9,
    "middle": 20,
    "attend_back": 12,
    "back_in": 7,
    "back_weight": 6,
    "cut_qkv": 2,
    "cut_rest": 2,
    "end_rest": 2,
    "end_qkv": 2,
}
SMEM = pl.BlockSpec(memory_space=pltpu.SMEM)
ANY = pl.BlockSpec(memory_space=pl.ANY)
VMEM = pl.BlockSpec(memory_space=pltpu.VMEM)


def dot(a, b, dims):
    return lax.dot_general(a, b, dims, preferred_element_type=F32)


def shape_of(dims, dtype):
    return jax.ShapeDtypeStruct(tuple(dims), dtype)


def params():
    return pltpu.CompilerParams(vmem_limit_bytes=VMEM_BYTES)


def cost(microseconds):
    return pl.CostEstimate(
        flops=int(microseconds * 1e6), bytes_accessed=1 << 10, transcendentals=0
    )


def tie(value, *others):
    return lax.optimization_barrier((value, *others))[0]


class Plan:
    def __init__(self, mesh, rows, tok):
        self.nrow = mesh.shape["row"]
        self.nblk = mesh.shape["blk"]
        self.rows = rows
        self.tok = tok
        self.local = rows * tok
        self.chips = self.nblk // 2
        self.bits = self.chips.bit_length() - 1
        self.groups = self.nblk // rows
        self.r = D // self.nblk
        self.rf = FF // self.nblk
        self.cw = D // self.nrow
        self.aligned = self.r % 16 == 0 and self.rf % 16 == 0
        self.packed = 4 * self.r + self.rf
        rows_, chips, nrow = self.rows, self.chips, self.nrow
        self.at_pick = 0
        self.at_base = self.at_pick + rows_
        self.at_own = self.at_base + self.groups * rows_
        self.at_other = self.at_own + chips
        self.at_z = self.at_other + chips
        self.at_lo = self.at_z + nrow
        self.size = self.at_lo + 1
        table = np.zeros((nrow, self.nblk, self.size), np.int32)
        for z in range(nrow):
            for blk in range(self.nblk):
                chip, core = blk // 2, blk % 2
                low = chip % rows_
                entry = table[z, blk]
                for j in range(rows_):
                    entry[self.at_pick + j] = low ^ j
                for e in range(self.groups):
                    other = blk ^ self.member(e)
                    for j in range(rows_):
                        entry[self.at_base + e * rows_ + j] = (2 * ((other // 2) ^ j) + other % 2) * tok
                for j in range(chips):
                    entry[self.at_own + j] = 2 * (chip ^ self.order(core, j)) + core
                    entry[self.at_other + j] = 2 * (chip ^ self.order(1 - core, j)) + 1 - core
                for other in range(nrow):
                    entry[self.at_z + other] = other ^ z
                entry[self.at_lo] = low
        self.table = table

    def member(self, e):
        return (e & 1) | ((e >> 1) * 2 * self.rows)

    def order(self, core, j):
        if core == 0:
            return j
        return int(format(j, "0%db" % self.bits)[::-1], 2) if self.bits else 0

    def step_pairs(self, step):
        def flip(blk):
            bit = step if blk % 2 == 0 else self.bits - 1 - step
            return 2 * ((blk // 2) ^ (1 << bit)) + blk % 2

        return [(blk, flip(blk)) for blk in range(self.nblk)]

    def xor_pairs(self, mask):
        return [(blk, blk ^ mask) for blk in range(self.nblk)]

    def z_pairs(self, mask):
        return [(z, z ^ mask) for z in range(self.nrow)]


def swap_cores(plan, value):
    return lax.ppermute(value, "blk", plan.xor_pairs(1))


def gather_z(plan, value, behind=None):
    pieces = [value]
    for j in range(1, plan.nrow):
        source = value if behind is None else tie(value, behind[j])
        pieces.append(lax.ppermute(source, "row", plan.z_pairs(j)))
    return pieces


def exchange_rows(plan, pieces):
    return [pieces[0]] + [
        lax.ppermute(pieces[j], "blk", plan.xor_pairs(2 * j)) for j in range(1, plan.rows)
    ]


def gather_start(plan, value, behind=()):
    pairs = [plan.step_pairs(step) for step in range(plan.bits)]
    first = lax.ppermute(value, "blk", pairs[0])
    second = [lax.ppermute(tie(value, *behind), "blk", pairs[1])] if plan.bits > 1 else []
    return [value, first] + second


def gather_more(plan, pieces):
    for step in range(1, plan.bits):
        have = 1 << step
        missing = pieces[len(pieces) - have :] if step > 1 else pieces[1:2]
        pieces = pieces + [lax.ppermute(piece, "blk", plan.step_pairs(step)) for piece in missing]
    return pieces


def add_low(a, b):
    return (a.astype(F32) + b.astype(F32)).astype(BF16)


def reduce_start(plan, grads):
    keep_low, keep_high, send_low, send_high = grads
    other_high = swap_cores(plan, send_high)
    return keep_low, keep_high, swap_cores(plan, send_low), other_high


def reduce_step(plan, step, low, high):
    moved = lax.ppermute(high, "blk", plan.step_pairs(step))
    half = low.shape[0] // 2
    if half == 0:
        return add_low(low, moved)[0], None
    high = add_low(low[half:], moved[half:])
    return add_low(low[:half], moved[:half]), high


def layer_norm(values):
    average = jnp.mean(values, axis=-1, keepdims=True)
    centred = values - average
    inv_std = lax.rsqrt(jnp.mean(centred * centred, axis=-1, keepdims=True) + NORM_EPSILON)
    return centred * inv_std, inv_std


def norm_backward(grad_out, normalized, inv_std, gain):
    scaled = grad_out * gain
    inner = jnp.mean(scaled * normalized, axis=-1, keepdims=True)
    outer = jnp.mean(scaled, axis=-1, keepdims=True)
    return inv_std * (scaled - outer - normalized * inner)


def swap_halves(values):
    lane = lax.broadcasted_iota(jnp.int32, values.shape, 1)
    width = values.shape[1]
    half = HD // 2
    return jnp.where(
        (lane & half) == 0, pltpu.roll(values, width - half, 1), pltpu.roll(values, half, 1)
    )


def rotate_pair(values, cosine, sine, direction):
    return values * cosine + swap_halves(values) * (direction * sine)


def rotate_all(values, cosine, sine, direction):
    return jnp.concatenate(
        [
            rotate_pair(values[:, 128 * p : 128 * (p + 1)], cosine, sine, direction)
            for p in range(values.shape[1] // 128)
        ],
        axis=1,
    )


def prepare_kernel(plan, meta, tokens, cotangent, w_out, w_in, w_down, *refs):
    rows = plan.rows
    for j in range(rows):
        row = meta[plan.at_pick + j]
        refs[j][0] = tokens[row]
        refs[j][1] = cotangent[row]
    if plan.aligned:
        refs[rows][...] = pack_rest(plan, w_out[...], w_in[...], w_down[...])


def prepare(plan, meta, tokens, cotangent, w_out, w_in, w_down):
    rows = plan.rows
    shapes = [shape_of((2, plan.tok, D), BF16)] * rows
    if plan.aligned:
        shapes.append(shape_of((3 * plan.r, 2 * plan.cw), BF16))
    results = pl.pallas_call(
        functools.partial(prepare_kernel, plan),
        in_specs=[SMEM] + [VMEM] * 5,
        out_specs=[VMEM] * len(shapes),
        out_shape=shapes,
        compiler_params=params(),
        cost_estimate=cost(COSTS["prepare"]),
        name="prepare",
    )(meta, tokens, cotangent, w_out, w_in, w_down)
    packed = results[rows] if plan.aligned else pack_rest(plan, w_out, w_in, w_down)
    return results[:rows], packed


def place_kernel(plan, meta, *refs):
    pieces, (out, grad) = refs[: plan.rows], refs[plan.rows :]
    for j in range(plan.rows):
        row = meta[plan.at_pick + j]
        out[row] = pieces[j][0]
        grad[row] = pieces[j][1]


def place(plan, meta, pieces):
    return pl.pallas_call(
        functools.partial(place_kernel, plan),
        in_specs=[SMEM] + [VMEM] * plan.rows,
        out_specs=[VMEM] * 2,
        out_shape=[shape_of((plan.rows, plan.tok, D), BF16)] * 2,
        compiler_params=params(),
        cost_estimate=cost(COSTS["place_rows"]),
        name="place_rows",
    )(meta, *pieces)


def ordered(plan, meta, pieces):
    stacked = jnp.stack(pieces)
    return [
        lax.dynamic_index_in_dim(stacked, meta[plan.at_z + z], 0, keepdims=False)
        for z in range(plan.nrow)
    ]


def join_qkv_kernel(plan, meta, gains, *refs):
    pieces, out, held = refs[: plan.nrow], refs[plan.nrow], refs[plan.nrow + 1]
    width = 3 * plan.cw
    for j in range(plan.nrow):
        held[j] = pieces[j][...]
    for z in range(plan.nrow):
        out[:, width * z : width * (z + 1)] = held[meta[plan.at_z + z]]
    out[:, 3 * D :] = gains[...]


def join_qkv(plan, meta, gains, pieces):
    if not plan.aligned:
        return jnp.concatenate(ordered(plan, meta, pieces) + [gains], axis=1)
    return pl.pallas_call(
        functools.partial(join_qkv_kernel, plan),
        in_specs=[SMEM] + [VMEM] * (1 + plan.nrow),
        out_specs=VMEM,
        out_shape=shape_of((plan.r, EXT), BF16),
        scratch_shapes=[pltpu.VMEM((plan.nrow, plan.r, 3 * plan.cw), BF16)],
        compiler_params=params(),
        cost_estimate=cost(COSTS["join_qkv"]),
        name="join_qkv",
    )(meta, gains, *pieces)


def pack_rest(plan, w_out, w_in, w_down, blank=None):
    cw = plan.cw
    left = jnp.concatenate([w_in[:, :cw], w_in[:, cw : 2 * cw], w_out], axis=0)
    if blank is None:
        blank = jnp.zeros((2 * plan.r - plan.rf, cw), BF16)
    right = jnp.concatenate([w_in[:, 2 * cw :], w_down, blank], axis=0)
    return jnp.concatenate([left, right], axis=1)


def unpack_rest(plan, piece):
    r, rf, cw = plan.r, plan.rf, plan.cw
    parts_in = [piece[:r, :cw], piece[r : 2 * r, :cw], piece[:r, cw:]]
    return parts_in, piece[2 * r : 3 * r, :cw], piece[r : r + rf, cw:]


def join_rest_kernel(plan, meta, *refs):
    pieces, out, held = refs[: plan.nrow], refs[plan.nrow], refs[plan.nrow + 1]
    r, cw = plan.r, plan.cw
    for j in range(plan.nrow):
        held[j] = pieces[j][...]
    for z in range(plan.nrow):
        parts_in, part_out, part_down = unpack_rest(plan, held[meta[plan.at_z + z]])
        out[:r, cw * z : cw * (z + 1)] = part_out
        for i in range(3):
            block, place_at = (3 * z + i) // plan.nrow, (3 * z + i) % plan.nrow
            out[r * (1 + block) : r * (2 + block), cw * place_at : cw * (place_at + 1)] = parts_in[i]
        out[4 * r :, cw * z : cw * (z + 1)] = part_down


def join_rest(plan, meta, pieces):
    if not plan.aligned:
        parts = [unpack_rest(plan, piece) for piece in ordered(plan, meta, pieces)]
        w_in = jnp.concatenate([part for item in parts for part in item[0]], axis=1)
        blocks = [jnp.concatenate([item[1] for item in parts], axis=1)]
        blocks += [w_in[:, D * t : D * (t + 1)] for t in range(3)]
        blocks += [jnp.concatenate([item[2] for item in parts], axis=1)]
        return jnp.concatenate(blocks, axis=0)
    return pl.pallas_call(
        functools.partial(join_rest_kernel, plan),
        in_specs=[SMEM] + [VMEM] * plan.nrow,
        out_specs=VMEM,
        out_shape=shape_of((plan.packed, D), BF16),
        scratch_shapes=[pltpu.VMEM((plan.nrow, 3 * plan.r, 2 * plan.cw), BF16)],
        compiler_params=params(),
        cost_estimate=cost(COSTS["join_rest"]),
        name="join_rest",
    )(meta, *pieces)


def by_block(plan, meta, own, other):
    stacked = jnp.stack(own + other)
    places = meta[plan.at_own : plan.at_other + plan.chips]
    return jnp.zeros_like(stacked).at[places].set(stacked)


def split_blocks(plan, meta, blocks):
    half = plan.chips // 2
    return [
        jnp.take(blocks, meta[plan.at_own + half * i : plan.at_own + half * (i + 1)], axis=0)
        for i in range(4)
    ]


def qkv_sources(plan, meta, own, other):
    if plan.aligned:
        return own + other
    return [by_block(plan, meta, own, other).reshape(D, EXT)]


def rest_sources(plan, meta, own, other):
    if plan.aligned:
        return own + other
    blocks = by_block(plan, meta, own, other)
    r = plan.r
    parts = [blocks[:, r * i : r * (i + 1)].reshape(D, D) for i in range(4)]
    parts.append(blocks[:, 4 * r :].reshape(FF, D))
    return [jnp.concatenate(parts, axis=0)]


def block_size(plan):
    return (plan.r, plan.rf) if plan.aligned else (D, FF)


def block_of(plan, meta, index):
    return meta[plan.at_own + index] if plan.aligned else 0


def rows_at(index, size):
    if isinstance(index, int):
        return pl.ds(index * size, size)
    return pl.ds(pl.multiple_of(index * size, size), size)


class Mover:
    def __init__(self, sems):
        self.sems = sems
        self.used = 0
        self.open = []

    def start(self, source, target):
        copy = pltpu.make_async_copy(source, target, self.sems.at[self.used])
        self.used += 1
        copy.start()
        return copy

    def send(self, source, target):
        self.open.append(self.start(source, target))

    def finish(self):
        for copy in self.open:
            copy.wait()


def wait_all(copies):
    for copy in copies:
        copy.wait()


def qkv_copies(plan, meta, sources, w_ref, sems):
    r, _ = block_size(plan)
    return [
        pltpu.make_async_copy(source, w_ref.at[rows_at(block_of(plan, meta, i), r)], sems.at[i])
        for i, source in enumerate(sources)
    ]


def grad_target(plan, grads, index):
    if not plan.aligned:
        return grads[0]
    half = plan.chips // 2
    return grads[index // half].at[index % half]


def grad_blocks(plan, height, width):
    return [shape_of((plan.chips // 2, height, width), BF16)] * 4


def source_count(plan):
    return 2 * plan.chips if plan.aligned else 1


def qkv_kernel(plan, meta, cos_ref, sin_ref, *refs):
    x_refs = refs[: plan.rows]
    count = source_count(plan)
    sources = refs[plan.rows : plan.rows + count]
    q_ref = refs[plan.rows + count]
    kv_refs = refs[plan.rows + count + 1 : plan.rows + count + 1 + HALVES]
    n_ref, gain_ref, w_ref, sems = refs[plan.rows + count + 1 + HALVES :]
    copies = qkv_copies(plan, meta, sources, w_ref, sems)
    for copy in copies:
        copy.start()
    units = [layer_norm(x_refs[j][0].astype(F32))[0] for j in range(plan.rows)]
    for copy in copies:
        copy.wait()
    gain_ref[...] = w_ref[:, 3 * D :].astype(F32).T[:8, :]
    for j in range(plan.rows):
        n_ref[plan.tok * j : plan.tok * (j + 1), :] = (units[j] * gain_ref[0:1, :]).astype(BF16)
    cosine, sine = cos_ref[...], sin_ref[...]
    normed = n_ref[...]
    queries = dot(normed, w_ref[:, :D], NN)
    q_ref[...] = rotate_all(queries, cosine, sine, 1.0).astype(BF16)
    keys = rotate_all(dot(normed, w_ref[:, D : 2 * D], NN), cosine, sine, 1.0).astype(BF16)
    values = dot(normed, w_ref[:, 2 * D : 3 * D], NN).astype(BF16)
    for h in range(HALVES):
        kv_refs[h][0] = keys[:, HALF * h : HALF * (h + 1)]
        kv_refs[h][1] = values[:, HALF * h : HALF * (h + 1)]


def project(plan, meta, cosine, sine, pieces, sources):
    local = plan.local
    count = len(sources)
    inputs = [meta, cosine, sine, *pieces, *sources]
    return pl.pallas_call(
        functools.partial(qkv_kernel, plan),
        in_specs=[SMEM, VMEM, VMEM] + [VMEM] * plan.rows + [ANY] * count,
        out_specs=[VMEM] * (3 + HALVES),
        out_shape=[shape_of((local, D), BF16)]
        + [shape_of((2, local, HALF), BF16)] * HALVES
        + [shape_of((local, D), BF16), shape_of((8, D), F32)],
        scratch_shapes=[pltpu.VMEM((D, EXT), BF16), pltpu.SemaphoreType.DMA((count,))],
        compiler_params=params(),
        cost_estimate=cost(COSTS["project"]),
        name="project",
    )(*inputs)


def fill_docs(plan, meta, lengths, kmask, qmask):
    low = meta[plan.at_lo]
    ends = []
    passed = jnp.int32(0)
    for n in range(NDOC):
        passed = passed + lengths[low, n]
        ends.append(passed)

    tok = plan.tok
    lane = lax.broadcasted_iota(jnp.int32, (tok, 128), 1) & (HD - 1)
    for i in range(plan.groups * plan.rows):
        places = meta[plan.at_base + i] + lax.broadcasted_iota(jnp.int32, (tok, 128), 0)
        docs = jnp.zeros((tok, 128), jnp.int32)
        for end in ends:
            docs = docs + (places >= end).astype(jnp.int32)
        part = slice(i * tok, (i + 1) * tok)
        same = docs == lane
        kmask[part, :] = jnp.where((lane < NDOC) & ~same, MASKED, 0.0).astype(BF16)
        if i < plan.rows:
            qmask[part, :] = jnp.where(same, 1.0, 0.0).astype(BF16)


def masks(plan, meta, lengths):
    keys = plan.groups * plan.local
    return pl.pallas_call(
        functools.partial(fill_docs, plan),
        in_specs=[SMEM, SMEM],
        out_specs=[VMEM, VMEM],
        out_shape=[shape_of((keys, 128), BF16), shape_of((plan.local, 128), BF16)],
        compiler_params=params(),
        cost_estimate=cost(1),
        name="masks",
    )(meta, lengths)


def head_part(pair, head, other=None):
    lane = lax.broadcasted_iota(jnp.int32, pair.shape, 1)
    keep = (lane < HD) if head == 0 else (lane >= HD)
    return jnp.where(keep, pair, jnp.zeros_like(pair) if other is None else other)


def attend_kernel(plan, width, order, kmask, qmask, q_ref, *refs):
    groups, local = plan.groups, plan.local
    kv = refs[:groups]
    o_ref, low_ref, lse_ref, s_ref, p_ref = refs[groups:]
    total_keys = groups * local
    chunk = 128
    values_t = []
    row = lax.broadcasted_iota(jnp.int32, (HD + 8, total_keys), 0)
    pair_t = jnp.concatenate([kv[e][1].T for e in range(groups)], axis=1)
    for h in range(2):
        head = pair_t[h * HD : (h + 1) * HD, :]
        values_t.append(jnp.concatenate([head, jnp.ones((8, total_keys), BF16)], axis=0))
    for first in range(0, local, width):
        rows = slice(first, first + width)
        queries = q_ref[rows, :] * jnp.asarray(1.0 / math.sqrt(HD), BF16)
        tops = []
        for h in range(2):
            head_queries = head_part(queries, h, qmask[rows, :])
            top = jnp.full((8, width), MASKED, F32)
            for e in range(groups):
                for c in range(0, local, 2 * chunk):
                    part = slice(e * local + c, e * local + c + 2 * chunk)
                    keys = head_part(kv[e][0, c : c + 2 * chunk, :], h, kmask[part, :])
                    scores = dot(keys, head_queries, NT)
                    s_ref[h, part, :] = scores
                    top = jnp.maximum(top, jnp.max(scores.reshape(-1, 8, width), axis=0))
            tops.append(jnp.max(top, axis=0, keepdims=True))
        parts = []
        for h in range(2):
            for c in range(0, total_keys, chunk):
                part = slice(c, c + chunk)
                p_ref[h, part, :] = jnp.exp(s_ref[h, part, :] - tops[h]).astype(BF16)
            weighted = dot(values_t[h], p_ref[h], NN)
            total = weighted[HD : HD + 1, :]
            parts.append(weighted[:HD, :] / total)
            lse_ref[0, h : h + 1, rows] = tops[h] + jnp.log(total)
        heads = jnp.concatenate(parts, axis=0).T
        o_ref[rows, :] = heads
        low_ref[rows, :] = heads.astype(BF16)


def attend(plan, part, meta, mask, queries, kv):
    local, groups = plan.local, plan.groups
    width = min(512, local)
    skip = part * HALF_PAIRS
    pair = pl.BlockSpec((local, 128), lambda p: (0, p))
    pair_q = pl.BlockSpec((local, 128), lambda p: (0, p + skip))
    pair_kv = pl.BlockSpec((2, local, 128), lambda p: (0, 0, p))
    whole_k = pl.BlockSpec((groups * local, 128), lambda p: (0, 0))
    whole_q = pl.BlockSpec((local, 128), lambda p: (0, 0))
    inputs = [meta, *mask, queries, *kv]
    return pl.pallas_call(
        functools.partial(attend_kernel, plan, width),
        grid=(HALF_PAIRS,),
        in_specs=[SMEM, whole_k, whole_q, pair_q] + [pair_kv] * groups,
        out_specs=[pair, pair, pl.BlockSpec((1, 2, local), lambda p: (p, 0, 0))],
        out_shape=[
            shape_of((local, HALF), F32),
            shape_of((local, HALF), BF16),
            shape_of((HALF_PAIRS, 2, local), F32),
        ],
        scratch_shapes=[
            pltpu.VMEM((2, groups * local, width), F32),
            pltpu.VMEM((2, groups * local, width), BF16),
        ],
        compiler_params=params(),
        cost_estimate=cost(COSTS["attend"]),
        name="attend",
    )(*inputs)


def attend_back_kernel(
    plan, width, order, kmask, qmask, q_ref, do_ref, o_ref, lse_ref, cos_ref, sin_ref, *refs
):
    groups, local = plan.groups, plan.local
    kv = refs[:groups]
    dq_ref = refs[groups]
    dkv = refs[groups + 1 : 2 * groups + 1]
    held, p_ref, ds_ref = refs[2 * groups + 1 :]
    keys_t = [kv[e][0].T for e in range(groups)]
    scale = 1.0 / math.sqrt(HD)
    chunk = 128
    for first in range(0, local, width):
        rows = slice(first, first + width)
        queries = q_ref[rows, :] * jnp.asarray(scale, BF16)
        dout = do_ref[rows, :]
        product = (dout.astype(F32) * o_ref[rows, :]).T
        parts = []
        for h in range(2):
            masked_queries = head_part(queries, h, qmask[rows, :])
            head_queries = head_part(queries, h)
            head_dout = head_part(dout, h)
            lse = lse_ref[0, h : h + 1, rows]
            delta = jnp.sum(product[h * HD : (h + 1) * HD, :], axis=0, keepdims=True)
            grad_queries = jnp.zeros((HD, width), F32)
            for e in range(groups):
                for c in range(0, local, chunk):
                    part = slice(c, c + chunk)
                    mask = kmask[e * local + c : e * local + c + chunk, :]
                    scores = dot(head_part(kv[e][0, part, :], h, mask), masked_queries, NT)
                    dprobs = dot(kv[e][1, part, :], head_dout, NT)
                    probs = jnp.exp(scores - lse)
                    p_ref[h, e, part, :] = probs.astype(BF16)
                    ds_ref[h, e, part, :] = (probs * (dprobs - delta)).astype(BF16)
                grad_values = dot(p_ref[h, e], head_dout, NN)
                grad_keys = dot(ds_ref[h, e], head_queries, NN)
                if first == 0 and h == 0:
                    held[e, 0] = grad_keys
                    held[e, 1] = grad_values
                else:
                    held[e, 0] += grad_keys
                    held[e, 1] += grad_values
                grad_queries = grad_queries + dot(
                    keys_t[e][h * HD : (h + 1) * HD, :], ds_ref[h, e], NN
                )
            parts.append(grad_queries)
        grad = jnp.concatenate(parts, axis=0).T * scale
        dq_ref[rows, :] = rotate_pair(grad, cos_ref[rows, :], sin_ref[rows, :], -1.0).astype(BF16)
    for e in range(groups):
        dkv[e][...] = held[e].astype(BF16)


def attend_back(plan, part, meta, mask, queries, dout, heads, lse, cosine, sine, kv):
    local, groups = plan.local, plan.groups
    width = min(512, local)
    half, first, count = part
    skip = half * HALF_PAIRS + first
    wide = 128 * count
    pair = pl.BlockSpec((local, 128), lambda p: (0, p))
    pair_h = pl.BlockSpec((local, 128), lambda p: (0, p + first))
    pair_q = pl.BlockSpec((local, 128), lambda p: (0, p + skip))
    whole_k = pl.BlockSpec((groups * local, 128), lambda p: (0, 0))
    inputs = [meta, *mask, queries, dout, heads, lse, cosine, sine, *kv]
    table = pl.BlockSpec((local, 128), lambda p: (0, 0))
    pair_kv = pl.BlockSpec((2, local, 128), lambda p: (0, 0, p))
    pair_kv_h = pl.BlockSpec((2, local, 128), lambda p: (0, 0, p + first))
    return pl.pallas_call(
        functools.partial(attend_back_kernel, plan, width),
        grid=(count,),
        in_specs=[
            SMEM,
            whole_k,
            table,
            pair_q,
            pair_q,
            pair_h,
            pl.BlockSpec((1, 2, local), lambda p: (p + first, 0, 0)),
            table,
            table,
        ]
        + [pair_kv_h] * groups,
        out_specs=[pair] + [pair_kv] * groups,
        out_shape=[shape_of((local, wide), BF16)] + [shape_of((2, local, wide), BF16)] * groups,
        scratch_shapes=[
            pltpu.VMEM((groups, 2, local, 128), F32),
            pltpu.VMEM((2, groups, local, width), BF16),
            pltpu.VMEM((2, groups, local, width), BF16),
        ],
        compiler_params=params(),
        cost_estimate=cost(4 * count),
        name="attend_back",
    )(*inputs)


def middle_kernel(plan, meta, gain_ref, *refs):
    rows, tok, local = plan.rows, plan.tok, plan.local
    count = source_count(plan)
    low_refs, refs = refs[:HALVES], refs[HALVES:]
    x_refs, refs = refs[:rows], refs[rows:]
    sources, refs = refs[:count], refs[count:]
    out_refs, refs = refs[:rows], refs[rows:]
    do_out, dh_out, refs = refs[0], refs[1], refs[2:]
    grads, refs = refs[: 4 if plan.aligned else 1], refs[4 if plan.aligned else 1 :]
    low_ref, x_ref, dy_ref, w_out, w_in, w_down, h_ref, unit_ref, n_ref, gu_ref = refs[:10]
    mid_ref, dgu_ref, out_ref, do_ref, dh_ref, da_ref, g_out, g_in, g_down, sems = refs[10:]
    mover = Mover(sems)
    r, rf = block_size(plan)
    blocks = [block_of(plan, meta, i) for i in range(count)]
    low_in = [
        mover.start(low_refs[h], low_ref.at[:, pl.ds(HALF * h, HALF)]) for h in range(HALVES)
    ]
    out_in = [
        mover.start(source.at[pl.ds(0, r)], w_out.at[rows_at(block, r)])
        for source, block in zip(sources, blocks)
    ]
    x_in = [mover.start(x_refs[j].at[0], x_ref.at[pl.ds(tok * j, tok)]) for j in range(rows)]

    def fetch_in(t):
        return [
            mover.start(source.at[pl.ds((1 + t) * r, r)], w_in.at[t, rows_at(block, r)])
            for source, block in zip(sources, blocks)
        ]

    wait_all(low_in)
    in_in = [fetch_in(0)]
    wait_all(out_in)
    wait_all(x_in)
    in_in.append(fetch_in(1))
    gain = gain_ref[1:2, :]
    inv_stds = []
    for j in range(rows):
        part = slice(tok * j, tok * (j + 1))
        hidden = x_ref[part, :].astype(F32) + dot(low_ref[part, :], w_out[...], NN)
        h_ref[part, :] = hidden
        unit, inv_std = layer_norm(hidden)
        inv_stds.append(inv_std)
        unit_ref[part, :] = unit
        n_ref[part, :] = (unit * gain).astype(BF16)
    for t in range(3):
        wait_all(in_in[t])
        if t == 0:
            in_in.append(fetch_in(2))
        if t == 1:
            dy_in = [
                mover.start(x_refs[j].at[1], dy_ref.at[pl.ds(tok * j, tok)]) for j in range(rows)
            ]
            down_in = [
                mover.start(source.at[pl.ds(4 * r, rf)], w_down.at[rows_at(block, rf)])
                for source, block in zip(sources, blocks)
            ]
        gu_ref[:, D * t : D * (t + 1)] = dot(n_ref[...], w_in[t], NN)
    wait_all(dy_in)
    wait_all(down_in)
    dy = dy_ref[...]
    size = FF // 3
    for f in range(3):
        cols = slice(size * f, size * (f + 1))
        up_cols = slice(FF + size * f, FF + size * (f + 1))
        gate = gu_ref[:, cols]
        up = gu_ref[:, up_cols]
        below = 0.5 + 0.5 * lax.erf(gate * math.sqrt(0.5))
        active = gate * below
        mid_ref[:, cols] = (active * up).astype(BF16)
        slope = below + gate * jnp.exp(-0.5 * gate * gate) * (1.0 / math.sqrt(2.0 * math.pi))
        dmid = dot(dy, w_down[cols, :], NT)
        dgu_ref[:, cols] = (dmid * up * slope).astype(BF16)
        dgu_ref[:, up_cols] = (dmid * active).astype(BF16)
    targets = [grad_target(plan, grads, i) for i in range(count)]
    g_down[...] = dot(mid_ref[...], dy, TN).astype(BF16)
    for target, block in zip(targets, blocks):
        mover.send(g_down.at[rows_at(block, rf)], target.at[pl.ds(4 * r, rf)])
    out_ref[...] = (h_ref[...] + dot(mid_ref[...], w_down[...], NN)).astype(BF16)
    for j in range(rows):
        mover.send(out_ref.at[pl.ds(tok * j, tok)], out_refs[j])
    grad_normed = dot(dgu_ref[:, :D], w_in[0], NT)
    for t in range(1, 3):
        grad_normed = grad_normed + dot(dgu_ref[:, D * t : D * (t + 1)], w_in[t], NT)
    dh_ref[...] = grad_normed

    def grad_in(t):
        g_in[t] = dot(n_ref[...], dgu_ref[:, D * t : D * (t + 1)], TN).astype(BF16)
        for target, block in zip(targets, blocks):
            mover.send(g_in.at[t, rows_at(block, r)], target.at[pl.ds((1 + t) * r, r)])

    for j in range(rows):
        part = slice(tok * j, tok * (j + 1))
        grad_hidden = dy[part, :].astype(F32) + norm_backward(
            dh_ref[part, :], unit_ref[part, :], inv_stds[j], gain
        )
        dh_ref[part, :] = grad_hidden
        da_ref[part, :] = grad_hidden.astype(BF16)
        if j < 3:
            grad_in(j)
    for t in range(rows, 3):
        grad_in(t)
    mover.send(dh_ref, dh_out)
    do_ref[...] = dot(da_ref[...], w_out[...], NT).astype(BF16)
    mover.send(do_ref, do_out)
    g_out[...] = dot(low_ref[...], da_ref[...], TN).astype(BF16)
    for target, block in zip(targets, blocks):
        mover.send(g_out.at[rows_at(block, r)], target.at[pl.ds(0, r)])
    mover.finish()


def middle(plan, meta, low, gains, pieces, sources):
    local, rows, tok = plan.local, plan.rows, plan.tok
    count = len(sources)
    total = 4 * D + FF
    if plan.aligned:
        grads = grad_blocks(plan, plan.packed, D)
    else:
        grads = [shape_of((total, D), BF16)]
    return pl.pallas_call(
        functools.partial(middle_kernel, plan),
        in_specs=[SMEM, VMEM] + [ANY] * (HALVES + rows + count),
        out_specs=[ANY] * (rows + 2 + len(grads)),
        out_shape=[shape_of((tok, D), BF16)] * rows
        + [shape_of((local, D), BF16), shape_of((local, D), F32)]
        + grads,
        scratch_shapes=[
            pltpu.VMEM((local, D), BF16),
            pltpu.VMEM((local, D), BF16),
            pltpu.VMEM((local, D), BF16),
            pltpu.VMEM((D, D), BF16),
            pltpu.VMEM((3, D, D), BF16),
            pltpu.VMEM((FF, D), BF16),
            pltpu.VMEM((local, D), F32),
            pltpu.VMEM((local, D), F32),
            pltpu.VMEM((local, D), BF16),
            pltpu.VMEM((local, 2 * FF), F32),
            pltpu.VMEM((local, FF), BF16),
            pltpu.VMEM((local, 2 * FF), BF16),
            pltpu.VMEM((local, D), BF16),
            pltpu.VMEM((local, D), BF16),
            pltpu.VMEM((local, D), F32),
            pltpu.VMEM((local, D), BF16),
            pltpu.VMEM((D, D), BF16),
            pltpu.VMEM((3, D, D), BF16),
            pltpu.VMEM((FF, D), BF16),
            pltpu.SemaphoreType.DMA((HALVES + 3 * rows + 2 + 10 * count,)),
        ],
        compiler_params=params(),
        cost_estimate=cost(COSTS["middle"]),
        name="middle",
    )(meta, gains, *low, *pieces, *sources)


def back_weight_kernel(plan, meta, *refs):
    groups, local = plan.groups, plan.local
    count = len(BACK_PARTS)
    cos_ref, sin_ref, n_in, refs = refs[0], refs[1], refs[2], refs[3:]
    dq_refs, refs = refs[:count], refs[count:]
    dkv, refs = refs[: count * groups], refs[count * groups :]
    dp_out, refs = refs[0], refs[1:]
    grads, refs = refs[: 4 if plan.aligned else 1], refs[4 if plan.aligned else 1 :]
    cos, sin, n_ref, dkv_ref, dp_ref, g_ref, sems = refs
    mover = Mover(sems)
    columns = []
    for half, first, pairs in BACK_PARTS:
        columns.append(pl.ds(HALF * half + 128 * first, 128 * pairs))
    first_in = [mover.start(n_in, n_ref)]
    for i in range(count):
        first_in.append(mover.start(dq_refs[i], dp_ref.at[0, :, columns[i]]))
    rest_in = [mover.start(cos_ref, cos), mover.start(sin_ref, sin)]
    for i in range(count):
        for e in range(groups):
            rest_in.append(
                mover.start(dkv[groups * i + e], dkv_ref.at[e, :, :, columns[i]])
            )
    r, _ = block_size(plan)

    def send_grad(t):
        cols = pl.ds(D * t, D)
        for i in range(source_count(plan)):
            at = rows_at(block_of(plan, meta, i), r)
            mover.send(g_ref.at[at, cols], grad_target(plan, grads, i).at[:, cols])

    wait_all(first_in)
    normed = n_ref[...]
    g_ref[:, :D] = dot(normed, dp_ref[0], TN).astype(BF16)
    send_grad(0)
    wait_all(rest_in)
    dp_ref[2] = sum_pieces([dkv_ref[e, 1] for e in range(groups)]).astype(BF16)
    g_ref[:, 2 * D : 3 * D] = dot(normed, dp_ref[2], TN).astype(BF16)
    send_grad(2)
    grad_keys = sum_pieces([dkv_ref[e, 0] for e in range(groups)])
    dp_ref[1] = rotate_all(grad_keys, cos[...], sin[...], -1.0).astype(BF16)
    mover.send(dp_ref, dp_out)
    g_ref[:, D : 2 * D] = dot(normed, dp_ref[1], TN).astype(BF16)
    send_grad(1)
    mover.finish()


def back_weight(plan, meta, cosine, sine, normed, dq, dkv):
    local, groups, count = plan.local, plan.groups, len(BACK_PARTS)
    if plan.aligned:
        grads = grad_blocks(plan, plan.r, 3 * D)
    else:
        grads = [shape_of((D, 3 * D), BF16)]
    results = pl.pallas_call(
        functools.partial(back_weight_kernel, plan),
        in_specs=[SMEM] + [ANY] * (3 + count * (1 + groups)),
        out_specs=[ANY] * (1 + len(grads)),
        out_shape=[shape_of((3, local, D), BF16)] + grads,
        scratch_shapes=[
            pltpu.VMEM((local, 128), F32),
            pltpu.VMEM((local, 128), F32),
            pltpu.VMEM((local, D), BF16),
            pltpu.VMEM((groups, 2, local, D), BF16),
            pltpu.VMEM((3, local, D), BF16),
            pltpu.VMEM((D, 3 * D), BF16),
            pltpu.SemaphoreType.DMA((4 + count * (1 + groups) + 3 * source_count(plan),)),
        ],
        compiler_params=params(),
        cost_estimate=cost(COSTS["back_weight"]),
        name="back_weight",
    )(meta, cosine, sine, normed, *dq, *dkv)
    return results[0], results[1:]


def back_in_kernel(plan, meta, dp_ref, dh_ref, gain_ref, *refs):
    rows, tok = plan.rows, plan.tok
    count = source_count(plan)
    x_refs, refs = refs[:rows], refs[rows:]
    out_refs, refs = refs[:rows], refs[rows:]
    sources, refs = refs[:count], refs[count:]
    both_refs = refs[:rows]
    w_ref, in_sems = refs[rows:]
    copies = qkv_copies(plan, meta, sources, w_ref, in_sems)
    for copy in copies:
        copy.start()
    for copy in copies:
        copy.wait()
    grad_normed = dot(dp_ref[0], w_ref[:, :D], NT)
    for t in range(1, 3):
        grad_normed = grad_normed + dot(dp_ref[t], w_ref[:, D * t : D * (t + 1)], NT)
    for j in range(rows):
        part = slice(tok * j, tok * (j + 1))
        unit, inv_std = layer_norm(x_refs[j][0].astype(F32))
        grad = grad_normed[part, :]
        back = norm_backward(grad, unit, inv_std, gain_ref[0:1, :])
        both_refs[j][0] = out_refs[j][...]
        both_refs[j][1] = (dh_ref[part, :] + back).astype(BF16)


def back_in(plan, meta, dprojected, dhidden, gains, pieces, outs, sources):
    rows, tok = plan.rows, plan.tok
    count = len(sources)
    return pl.pallas_call(
        functools.partial(back_in_kernel, plan),
        in_specs=[SMEM] + [VMEM] * (3 + 2 * rows) + [ANY] * count,
        out_specs=[VMEM] * rows,
        out_shape=[shape_of((2, tok, D), BF16)] * rows,
        scratch_shapes=[pltpu.VMEM((D, EXT), BF16), pltpu.SemaphoreType.DMA((count,))],
        compiler_params=params(),
        cost_estimate=cost(COSTS["back_in"]),
        name="back_in",
    )(meta, dprojected, dhidden, gains, *pieces, *outs, *sources)


def gain_columns(weight, grad):
    total = jnp.sum(weight.astype(F32) * grad.astype(F32), axis=1, keepdims=True)
    high = total.astype(BF16)
    return high, (total - high.astype(F32)).astype(BF16)


def pad_width(plan):
    return -(-(3 * plan.cw + 2) // 128) * 128


def gain_tail(plan, weight, grad):
    width = pad_width(plan) - 3 * plan.cw
    high, rest = gain_columns(weight, grad)
    lane = lax.broadcasted_iota(jnp.int32, (plan.r, width), 1)
    return jnp.where(lane == 0, high, jnp.where(lane == 1, rest, jnp.zeros_like(high)))


def cut_qkv_kernel(plan, meta, total, weight, *refs):
    outs, held = refs[: plan.nrow], refs[plan.nrow]
    width = 3 * plan.cw
    tail = gain_tail(plan, weight[:, : 3 * D], total[...])
    for z in range(plan.nrow):
        place_at = meta[plan.at_z + z]
        held[place_at, :, :width] = total[:, width * z : width * (z + 1)]
        held[place_at, :, width:] = tail
    for j in range(plan.nrow):
        outs[j][...] = held[j]


def cut_qkv(plan, meta, total, weight):
    width, wide = 3 * plan.cw, pad_width(plan)
    if not plan.aligned:
        tail = gain_tail(plan, weight[:, : 3 * D], total)
        parts = [
            jnp.concatenate([total[:, width * z : width * (z + 1)], tail], axis=1)
            for z in range(plan.nrow)
        ]
        return ordered(plan, meta, parts)
    return pl.pallas_call(
        functools.partial(cut_qkv_kernel, plan),
        in_specs=[SMEM, VMEM, VMEM],
        out_specs=[VMEM] * plan.nrow,
        out_shape=[shape_of((plan.r, wide), BF16)] * plan.nrow,
        scratch_shapes=[pltpu.VMEM((plan.nrow, plan.r, wide), BF16)],
        compiler_params=params(),
        cost_estimate=cost(COSTS["cut_qkv"]),
        name="cut_qkv",
    )(meta, total, weight)


def gain_blank(plan, weight, grad):
    r, blank = plan.r, 2 * plan.r - plan.rf
    cols = [weight[r * t : r * (t + 1)] for t in range(1, 4)]
    grads = [grad[r * t : r * (t + 1)] for t in range(1, 4)]
    high, rest = gain_columns(jnp.concatenate(cols, axis=1), jnp.concatenate(grads, axis=1))
    lane = lax.broadcasted_iota(jnp.int32, (blank, plan.cw), 1)
    found = jnp.zeros((blank, plan.cw), BF16)
    for i in range(r // blank):
        part = slice(blank * i, blank * (i + 1))
        found = jnp.where(lane == 2 * i, high[part], found)
        found = jnp.where(lane == 2 * i + 1, rest[part], found)
    return found


def cut_rest_kernel(plan, meta, total, weight, *refs):
    outs, held = refs[: plan.nrow], refs[plan.nrow]
    r, rf, cw = plan.r, plan.rf, plan.cw
    blank = gain_blank(plan, weight[...], total[...])
    for z in range(plan.nrow):
        place_at = meta[plan.at_z + z]
        cols = slice(cw * z, cw * (z + 1))
        parts = []
        for i in range(3):
            block, at = (3 * z + i) // plan.nrow, (3 * z + i) % plan.nrow
            parts.append(total[r * (1 + block) : r * (2 + block), cw * at : cw * (at + 1)])
        held[place_at, :r, :] = jnp.concatenate([parts[0], parts[2]], axis=1)
        held[place_at, r : 2 * r, :] = jnp.concatenate(
            [parts[1], total[4 * r : 5 * r, cols]], axis=1
        )
        rest = total[5 * r : 4 * r + rf, cols]
        held[place_at, 2 * r :, :] = jnp.concatenate(
            [total[:r, cols], jnp.concatenate([rest, blank], axis=0)], axis=1
        )
    for j in range(plan.nrow):
        outs[j][...] = held[j]


def cut_rest(plan, meta, total, weight):
    r, cw = plan.r, plan.cw
    if not plan.aligned:
        grad_in = jnp.concatenate([total[r * (1 + t) : r * (2 + t)] for t in range(3)], axis=1)
        blank = gain_blank(plan, weight, total)
        parts = [
            pack_rest(
                plan,
                total[:r, cw * z : cw * (z + 1)],
                grad_in[:, 3 * cw * z : 3 * cw * (z + 1)],
                total[4 * r :, cw * z : cw * (z + 1)],
                blank,
            )
            for z in range(plan.nrow)
        ]
        return ordered(plan, meta, parts)
    return pl.pallas_call(
        functools.partial(cut_rest_kernel, plan),
        in_specs=[SMEM, VMEM, VMEM],
        out_specs=[VMEM] * plan.nrow,
        out_shape=[shape_of((3 * r, 2 * cw), BF16)] * plan.nrow,
        scratch_shapes=[pltpu.VMEM((plan.nrow, 3 * r, 2 * cw), BF16)],
        compiler_params=params(),
        cost_estimate=cost(COSTS["cut_rest"]),
        name="cut_rest",
    )(meta, total, weight)


def reduce_z(plan, pieces):
    return [pieces[0]] + [
        lax.ppermute(pieces[j], "row", plan.z_pairs(j)) for j in range(1, plan.nrow)
    ]


def sum_pieces(pieces):
    total = pieces[0].astype(F32)
    for piece in pieces[1:]:
        total = total + piece.astype(F32)
    return total


def end_rest_kernel(plan, *refs):
    pieces, (g_out, g_in, g_down, g_gain) = refs[: plan.nrow], refs[plan.nrow :]
    total = sum_pieces([piece[...] for piece in pieces])
    parts_in, part_out, part_down = unpack_rest(plan, total)
    g_out[...] = part_out
    g_in[...] = jnp.concatenate(parts_in, axis=1)
    g_down[...] = part_down
    blank = 2 * plan.r - plan.rf
    g_gain[...] = total[3 * plan.r - blank :, plan.cw : plan.cw + 128].T[:8, :]


def end_rest(plan, pieces):
    r, blank = plan.r, 2 * plan.r - plan.rf
    if not plan.aligned:
        total = sum_pieces(pieces)
        parts_in, out_grad, down_grad = unpack_rest(plan, total)
        in_grad = jnp.concatenate(parts_in, axis=1)
        gain = total[3 * r - blank :, plan.cw : plan.cw + 8].T
    else:
        out_grad, in_grad, down_grad, gain = pl.pallas_call(
            functools.partial(end_rest_kernel, plan),
            in_specs=[VMEM] * plan.nrow,
            out_specs=[VMEM] * 4,
            out_shape=[
                shape_of((r, plan.cw), F32),
                shape_of((r, 3 * plan.cw), F32),
                shape_of((plan.rf, plan.cw), F32),
                shape_of((8, blank), F32),
            ],
            compiler_params=params(),
            cost_estimate=cost(COSTS["end_rest"]),
            name="end_rest",
        )(*pieces)
    gain = jnp.concatenate([gain[2 * i] + gain[2 * i + 1] for i in range(r // blank)])
    return out_grad, in_grad, down_grad, gain


def end_qkv_kernel(plan, gain_ref, *refs):
    pieces, (g_qkv, g_gain) = refs[: plan.nrow], refs[plan.nrow :]
    width, wide = 3 * plan.cw, pad_width(plan)
    total = sum_pieces([piece[...] for piece in pieces])
    g_qkv[...] = total[:, :width]
    tail = total[:, wide - 128 :].T
    at = width - (wide - 128)
    g_gain[...] = (tail[at : at + 1, :] + tail[at + 1 : at + 2, :]) / gain_ref[...]


def end_qkv(plan, gain, pieces):
    width, wide = 3 * plan.cw, pad_width(plan)
    if not plan.aligned:
        total = sum_pieces(pieces)
        return total[:, :width], (total[:, width] + total[:, width + 1]) / gain[0]
    grad, gain_grad = pl.pallas_call(
        functools.partial(end_qkv_kernel, plan),
        in_specs=[VMEM] * (1 + plan.nrow),
        out_specs=[VMEM] * 2,
        out_shape=[shape_of((plan.r, width), F32), shape_of((1, plan.r), F32)],
        compiler_params=params(),
        cost_estimate=cost(COSTS["end_qkv"]),
        name="end_qkv",
    )(gain, *pieces)
    return grad, gain_grad.reshape(plan.r)


def rotation_tables(plan, meta, lengths):
    ends = jnp.cumsum(lax.dynamic_index_in_dim(lengths, meta[plan.at_lo], 0, keepdims=False))
    starts = jnp.concatenate([jnp.zeros((1,), jnp.int32), ends[:-1]])
    bases = meta[plan.at_base : plan.at_base + plan.rows]
    places = (bases[:, None] + jnp.arange(plan.tok, dtype=jnp.int32)[None, :]).reshape(-1)
    passed = places[:, None] >= starts[None, :]
    positions = places - jnp.max(jnp.where(passed, starts[None, :], 0), axis=1)
    half = HD // 2
    inverse = ROPE_BASE ** (-(jnp.arange(half, dtype=F32) * (2.0 / HD)))
    angles = positions.astype(F32)[:, None] * inverse
    cosine, sine = jnp.cos(angles), jnp.sin(angles)
    return (
        jnp.concatenate([cosine] * 4, axis=1),
        jnp.concatenate([-sine, sine, -sine, sine], axis=1),
    )


def body(
    plan,
    tokens,
    lengths,
    norm_gain,
    qkv_weight,
    out_weight,
    mlp_gain,
    in_weight,
    down_weight,
    cotangent,
):
    blk, row = lax.axis_index("blk"), lax.axis_index("row")
    meta = lax.dynamic_slice(
        jnp.asarray(plan.table), (row, blk, 0), (1, 1, plan.size)
    ).reshape(plan.size)
    qkv_parts = gather_z(plan, qkv_weight)
    cut, packed = prepare(plan, meta, tokens, cotangent, out_weight, in_weight, down_weight)
    pieces = exchange_rows(plan, cut)
    rest_parts = gather_z(plan, packed, behind=qkv_parts)
    gains = jnp.pad(jnp.stack([norm_gain, mlp_gain], axis=1), ((0, 0), (0, 126)))
    cosine, sine = rotation_tables(plan, meta, lengths)
    mask = masks(plan, meta, lengths)
    qkv_joined = join_qkv(plan, meta, gains, qkv_parts)
    qkv_own = gather_start(plan, qkv_joined, pieces[1:])
    qkv_own[1] = tie(qkv_own[1], *rest_parts[2:], cosine, sine, *mask)
    qkv_own = gather_more(plan, qkv_own)
    qkv_own[-1] = tie(qkv_own[-1], rest_parts[1])
    qkv_other = [swap_cores(plan, piece) for piece in qkv_own]
    qkv_from = qkv_sources(plan, meta, qkv_own, qkv_other)
    rest_parts[0] = tie(rest_parts[0], qkv_joined, *qkv_other[:-1])
    joined = join_rest(plan, meta, rest_parts)
    results = project(plan, tie(meta, joined), cosine, sine, pieces, qkv_from)
    queries, kv, (normed, gains) = results[0], results[1 : 1 + HALVES], results[1 + HALVES :]
    kv = [
        [part]
        + [
            lax.ppermute(part, "blk", plan.xor_pairs(plan.member(e)))
            for e in range(1, plan.groups)
        ]
        for part in kv
    ]
    rest_own = gather_start(plan, joined)
    heads, low, lse = [None] * HALVES, [None] * HALVES, [None] * HALVES
    heads[0], low[0], lse[0] = attend(plan, 0, meta, mask, queries, kv[0])
    order = tie(meta, low[0], *rest_own[1:])
    rest_own[1:] = [tie(piece, low[0]) for piece in rest_own[1:]]
    rest_other = [swap_cores(plan, piece) for piece in rest_own]
    rest_more = gather_more(plan, rest_own)[len(rest_own) :]
    heads[1], low[1], lse[1] = attend(plan, 1, order, mask, queries, kv[1])
    rest_more = [tie(piece, low[1]) for piece in rest_more]
    rest_own = rest_own + rest_more
    rest_other = rest_other + [swap_cores(plan, piece) for piece in rest_more]
    rest_from = rest_sources(plan, meta, rest_own, rest_other)
    results = middle(plan, meta, low, gains, pieces, rest_from)
    outs, (dout, dhidden), rest_grads = (
        results[: plan.rows],
        results[plan.rows : plan.rows + 2],
        results[plan.rows + 2 :],
    )
    if not plan.aligned:
        r, rf, nblk = plan.r, plan.rf, plan.nblk
        whole = rest_grads[0]
        blocks = [whole[D * i : D * (i + 1)].reshape(nblk, r, D) for i in range(4)]
        blocks.append(whole[4 * D :].reshape(nblk, rf, D))
        rest_grads = split_blocks(plan, meta, jnp.concatenate(blocks, axis=1))
    keep_low, keep_high, other_low, other_high = reduce_start(plan, rest_grads)
    dq, dkv = [], []
    order = meta
    for i, part in enumerate(BACK_PARTS):
        half = part[0]
        results = attend_back(
            plan, part, order, mask, queries, dout, heads[half], lse[half], cosine, sine, kv[half]
        )
        dq.append(results[0])
        dkv.append(results[1])
        dkv += [
            lax.ppermute(results[1 + e], "blk", plan.xor_pairs(plan.member(e)))
            for e in range(1, plan.groups)
        ]
        if i == 0:
            rest_high = add_low(tie(keep_high, dq[0]), other_high)
            rest_low = add_low(tie(keep_low, dq[0]), other_low)
            order = tie(meta, dq[0], rest_high, rest_low)
        else:
            order = tie(meta, dq[i], *dkv[1 : plan.groups])
    rest_low, rest_high = reduce_step(plan, plan.bits - 1, tie(rest_low, dq[-1]), rest_high)
    order = tie(meta, rest_low) if rest_high is None else tie(meta, rest_low, rest_high)
    dprojected, qkv_grads = back_weight(plan, order, cosine, sine, normed, dq, dkv)
    if not plan.aligned:
        qkv_grads = split_blocks(plan, meta, qkv_grads[0].reshape(plan.nblk, plan.r, 3 * D))
    rest_low = tie(rest_low, dprojected)
    for step in reversed(range(plan.bits - 1)):
        rest_low, rest_high = reduce_step(plan, step, rest_low, rest_high)
    keep_low, keep_high, other_low, other_high = reduce_start(plan, qkv_grads)
    qkv_high = add_low(tie(keep_high, rest_low), other_high)
    qkv_low = add_low(keep_low, other_low)
    rest_cut = cut_rest(plan, meta, tie(rest_low, qkv_high), joined)
    order = tie(meta, qkv_high, qkv_low, *rest_cut)
    both = back_in(plan, order, dprojected, dhidden, gains, pieces, outs, qkv_from)
    rest_pieces = reduce_z(plan, rest_cut)
    qkv_low = tie(qkv_low, both[0], *rest_pieces[1:3])
    for step in reversed(range(plan.bits)):
        if step == 0:
            qkv_low = tie(qkv_low, *rest_pieces[3:])
        qkv_low, qkv_high = reduce_step(plan, step, qkv_low, qkv_high)
    both = exchange_rows(plan, [tie(piece, qkv_low) for piece in both])
    qkv_cut = cut_qkv(plan, meta, tie(qkv_low, *rest_pieces[1:]), qkv_joined)
    qkv_pieces = reduce_z(plan, qkv_cut)
    rest_pieces[0] = tie(rest_pieces[0], *qkv_cut)
    out_grad, in_grad, down_grad, mlp_gain_grad = end_rest(plan, rest_pieces)
    output, input_grad = place(plan, meta, [tie(both[0], *qkv_cut)] + both[1:])
    gain_row = norm_gain.astype(F32)[None]
    qkv_grad, norm_gain_grad = end_qkv(plan, tie(gain_row, output, input_grad, in_grad), qkv_pieces)
    mlp_gain_grad = mlp_gain_grad / mlp_gain.astype(F32)
    return (
        output,
        input_grad,
        norm_gain_grad,
        qkv_grad,
        out_grad,
        mlp_gain_grad,
        in_grad,
        down_grad,
    )


def solution(mesh):
    weights = P("blk", "row")
    acts = P("row", "blk", None)

    def run(*args):
        rows = args[0].shape[0] // mesh.shape["row"]
        tok = args[0].shape[1] // mesh.shape["blk"]
        plan = Plan(mesh, rows, tok)
        return jax.shard_map(
            functools.partial(body, plan),
            mesh=mesh,
            in_specs=(acts, P("row", None), P("blk"), weights, weights, P("blk"), weights, weights, acts),
            out_specs=(acts, acts, P("blk"), weights, weights, P("blk"), weights, weights),
            check_vma=False,
        )(*args)

    return run
```

```python
import functools
import math

import jax
import jax.numpy as jnp
import numpy as np
from jax import lax
from jax.experimental import pallas as pl
from jax.experimental.pallas import tpu as pltpu
from jax.sharding import PartitionSpec as P

D = 768
HEADS = 12
HD = 64
FF = 1152
NDOC = 8
PAIRS = HEADS // 2
EXT = 3 * D + 128

ROPE_BASE = 160000.0
NORM_EPSILON = 1e-05
MASKED = -1e30
F32 = jnp.float32
BF16 = jnp.bfloat16
NN = (((1,), (0,)), ((), ()))
NT = (((1,), (1,)), ((), ()))
TN = (((0,), (0,)), ((), ()))
LIMITS = {
    "prepare": 8,
    "place_rows": 8,
    "join_qkv": 4,
    "join_rest": 6,
    "project": 20,
    "masks": 4,
    "attend": 16,
    "middle": 56,
    "attend_back": 16,
    "back_in": 20,
    "back_weight": 16,
    "cut_qkv": 4,
    "cut_rest": 6,
    "end_rest": 4,
    "end_qkv": 4,
}
HALVES = 2
HALF_PAIRS = PAIRS // HALVES
HALF = D // HALVES
BACK_PARTS = ((0, 0, 1), (0, 1, 2), (1, 0, 3))
COSTS = {
    "prepare": 4,
    "place_rows": 2,
    "join_qkv": 2,
    "join_rest": 2,
    "project": 7,
    "attend": 9,
    "middle": 20,
    "attend_back": 12,
    "back_in": 7,
    "back_weight": 6,
    "cut_qkv": 2,
    "cut_rest": 2,
    "end_rest": 2,
    "end_qkv": 2,
}
SMEM = pl.BlockSpec(memory_space=pltpu.SMEM)
ANY = pl.BlockSpec(memory_space=pl.ANY)
VMEM = pl.BlockSpec(memory_space=pltpu.VMEM)


def dot(a, b, dims):
    return lax.dot_general(a, b, dims, preferred_element_type=F32)


def shape_of(dims, dtype):
    return jax.ShapeDtypeStruct(tuple(dims), dtype)


def params(plan, name):
    size = max(1, plan.groups * plan.local // 1024)
    return pltpu.CompilerParams(vmem_limit_bytes=min(56, LIMITS[name] * size) * 1024 * 1024)


def cost(microseconds):
    return pl.CostEstimate(
        flops=int(microseconds * 1e6), bytes_accessed=1 << 10, transcendentals=0
    )


def tie(value, *others):
    return lax.optimization_barrier((value, *others))[0]


class Plan:
    def __init__(self, mesh, rows, tok):
        self.nrow = mesh.shape["row"]
        self.nblk = mesh.shape["blk"]
        self.rows = rows
        self.tok = tok
        self.local = rows * tok
        self.chips = self.nblk // 2
        self.bits = self.chips.bit_length() - 1
        self.groups = self.nblk // rows
        self.r = D // self.nblk
        self.rf = FF // self.nblk
        self.cw = D // self.nrow
        self.aligned = self.r % 16 == 0 and self.rf % 16 == 0
        self.packed = 4 * self.r + self.rf
        rows_, chips, nrow = self.rows, self.chips, self.nrow
        self.at_pick = 0
        self.at_base = self.at_pick + rows_
        self.at_own = self.at_base + self.groups * rows_
        self.at_other = self.at_own + chips
        self.at_z = self.at_other + chips
        self.at_lo = self.at_z + nrow
        self.size = self.at_lo + 1
        table = np.zeros((nrow, self.nblk, self.size), np.int32)
        for z in range(nrow):
            for blk in range(self.nblk):
                chip, core = blk // 2, blk % 2
                low = chip % rows_
                entry = table[z, blk]
                for j in range(rows_):
                    entry[self.at_pick + j] = low ^ j
                for e in range(self.groups):
                    other = blk ^ self.member(e)
                    for j in range(rows_):
                        entry[self.at_base + e * rows_ + j] = (2 * ((other // 2) ^ j) + other % 2) * tok
                for j in range(chips):
                    entry[self.at_own + j] = 2 * (chip ^ self.order(core, j)) + core
                    entry[self.at_other + j] = 2 * (chip ^ self.order(1 - core, j)) + 1 - core
                for other in range(nrow):
                    entry[self.at_z + other] = other ^ z
                entry[self.at_lo] = low
        self.table = table

    def member(self, e):
        return (e & 1) | ((e >> 1) * 2 * self.rows)

    def order(self, core, j):
        if core == 0:
            return j
        return int(format(j, "0%db" % self.bits)[::-1], 2) if self.bits else 0

    def step_pairs(self, step):
        def flip(blk):
            bit = step if blk % 2 == 0 else self.bits - 1 - step
            return 2 * ((blk // 2) ^ (1 << bit)) + blk % 2

        return [(blk, flip(blk)) for blk in range(self.nblk)]

    def xor_pairs(self, mask):
        return [(blk, blk ^ mask) for blk in range(self.nblk)]

    def z_pairs(self, mask):
        return [(z, z ^ mask) for z in range(self.nrow)]


def swap_cores(plan, value):
    return lax.ppermute(value, "blk", plan.xor_pairs(1))


def gather_z(plan, value, behind=None):
    pieces = [value]
    for j in range(1, plan.nrow):
        source = value if behind is None else tie(value, behind[j])
        pieces.append(lax.ppermute(source, "row", plan.z_pairs(j)))
    return pieces


def exchange_rows(plan, pieces):
    return [pieces[0]] + [
        lax.ppermute(pieces[j], "blk", plan.xor_pairs(2 * j)) for j in range(1, plan.rows)
    ]


def gather_start(plan, value, behind=()):
    pairs = [plan.step_pairs(step) for step in range(plan.bits)]
    first = lax.ppermute(value, "blk", pairs[0])
    second = [lax.ppermute(tie(value, *behind), "blk", pairs[1])] if plan.bits > 1 else []
    return [value, first] + second


def gather_more(plan, pieces):
    for step in range(1, plan.bits):
        have = 1 << step
        missing = pieces[len(pieces) - have :] if step > 1 else pieces[1:2]
        pieces = pieces + [lax.ppermute(piece, "blk", plan.step_pairs(step)) for piece in missing]
    return pieces


def add_low(a, b):
    return (a.astype(F32) + b.astype(F32)).astype(BF16)


def reduce_start(plan, grads):
    keep_low, keep_high, send_low, send_high = grads
    other_high = swap_cores(plan, send_high)
    return keep_low, keep_high, swap_cores(plan, send_low), other_high


def reduce_step(plan, step, low, high):
    moved = lax.ppermute(high, "blk", plan.step_pairs(step))
    half = low.shape[0] // 2
    if half == 0:
        return add_low(low, moved)[0], None
    high = add_low(low[half:], moved[half:])
    return add_low(low[:half], moved[:half]), high


def layer_norm(values):
    average = jnp.mean(values, axis=-1, keepdims=True)
    centred = values - average
    inv_std = lax.rsqrt(jnp.mean(centred * centred, axis=-1, keepdims=True) + NORM_EPSILON)
    return centred * inv_std, inv_std


def norm_backward(grad_out, normalized, inv_std, gain):
    scaled = grad_out * gain
    inner = jnp.mean(scaled * normalized, axis=-1, keepdims=True)
    outer = jnp.mean(scaled, axis=-1, keepdims=True)
    return inv_std * (scaled - outer - normalized * inner)


def swap_halves(values):
    lane = lax.broadcasted_iota(jnp.int32, values.shape, 1)
    width = values.shape[1]
    half = HD // 2
    return jnp.where(
        (lane & half) == 0, pltpu.roll(values, width - half, 1), pltpu.roll(values, half, 1)
    )


def rotate_pair(values, cosine, sine, direction):
    return values * cosine + swap_halves(values) * (direction * sine)


def rotate_all(values, cosine, sine, direction):
    return jnp.concatenate(
        [
            rotate_pair(values[:, 128 * p : 128 * (p + 1)], cosine, sine, direction)
            for p in range(values.shape[1] // 128)
        ],
        axis=1,
    )


def prepare_kernel(plan, meta, tokens, cotangent, w_out, w_in, w_down, *refs):
    rows = plan.rows
    for j in range(rows):
        row = meta[plan.at_pick + j]
        refs[j][0] = tokens[row]
        refs[j][1] = cotangent[row]
    if plan.aligned:
        refs[rows][...] = pack_rest(plan, w_out[...], w_in[...], w_down[...])


def prepare(plan, meta, tokens, cotangent, w_out, w_in, w_down):
    rows = plan.rows
    shapes = [shape_of((2, plan.tok, D), BF16)] * rows
    if plan.aligned:
        shapes.append(shape_of((3 * plan.r, 2 * plan.cw), BF16))
    results = pl.pallas_call(
        functools.partial(prepare_kernel, plan),
        in_specs=[SMEM] + [VMEM] * 5,
        out_specs=[VMEM] * len(shapes),
        out_shape=shapes,
        compiler_params=params(plan, "prepare"),
        cost_estimate=cost(COSTS["prepare"]),
        name="prepare",
    )(meta, tokens, cotangent, w_out, w_in, w_down)
    packed = results[rows] if plan.aligned else pack_rest(plan, w_out, w_in, w_down)
    return results[:rows], packed


def place_kernel(plan, meta, *refs):
    pieces, (out, grad) = refs[: plan.rows], refs[plan.rows :]
    for j in range(plan.rows):
        row = meta[plan.at_pick + j]
        out[row] = pieces[j][0]
        grad[row] = pieces[j][1]


def place(plan, meta, pieces):
    return pl.pallas_call(
        functools.partial(place_kernel, plan),
        in_specs=[SMEM] + [VMEM] * plan.rows,
        out_specs=[VMEM] * 2,
        out_shape=[shape_of((plan.rows, plan.tok, D), BF16)] * 2,
        compiler_params=params(plan, "place_rows"),
        cost_estimate=cost(COSTS["place_rows"]),
        name="place_rows",
    )(meta, *pieces)


def ordered(plan, meta, pieces):
    stacked = jnp.stack(pieces)
    return [
        lax.dynamic_index_in_dim(stacked, meta[plan.at_z + z], 0, keepdims=False)
        for z in range(plan.nrow)
    ]


def join_qkv_kernel(plan, meta, gains, *refs):
    pieces, out, held = refs[: plan.nrow], refs[plan.nrow], refs[plan.nrow + 1]
    width = 3 * plan.cw
    for j in range(plan.nrow):
        held[j] = pieces[j][...]
    for z in range(plan.nrow):
        out[:, width * z : width * (z + 1)] = held[meta[plan.at_z + z]]
    out[:, 3 * D :] = gains[...]


def join_qkv(plan, meta, gains, pieces):
    if not plan.aligned:
        return jnp.concatenate(ordered(plan, meta, pieces) + [gains], axis=1)
    return pl.pallas_call(
        functools.partial(join_qkv_kernel, plan),
        in_specs=[SMEM] + [VMEM] * (1 + plan.nrow),
        out_specs=VMEM,
        out_shape=shape_of((plan.r, EXT), BF16),
        scratch_shapes=[pltpu.VMEM((plan.nrow, plan.r, 3 * plan.cw), BF16)],
        compiler_params=params(plan, "join_qkv"),
        cost_estimate=cost(COSTS["join_qkv"]),
        name="join_qkv",
    )(meta, gains, *pieces)


def pack_rest(plan, w_out, w_in, w_down, blank=None):
    cw = plan.cw
    left = jnp.concatenate([w_in[:, :cw], w_in[:, cw : 2 * cw], w_out], axis=0)
    if blank is None:
        blank = jnp.zeros((2 * plan.r - plan.rf, cw), BF16)
    right = jnp.concatenate([w_in[:, 2 * cw :], w_down, blank], axis=0)
    return jnp.concatenate([left, right], axis=1)


def unpack_rest(plan, piece):
    r, rf, cw = plan.r, plan.rf, plan.cw
    parts_in = [piece[:r, :cw], piece[r : 2 * r, :cw], piece[:r, cw:]]
    return parts_in, piece[2 * r : 3 * r, :cw], piece[r : r + rf, cw:]


def join_rest_kernel(plan, meta, *refs):
    pieces, out, held = refs[: plan.nrow], refs[plan.nrow], refs[plan.nrow + 1]
    r, cw = plan.r, plan.cw
    for j in range(plan.nrow):
        held[j] = pieces[j][...]
    for z in range(plan.nrow):
        parts_in, part_out, part_down = unpack_rest(plan, held[meta[plan.at_z + z]])
        out[:r, cw * z : cw * (z + 1)] = part_out
        for i in range(3):
            block, place_at = (3 * z + i) // plan.nrow, (3 * z + i) % plan.nrow
            out[r * (1 + block) : r * (2 + block), cw * place_at : cw * (place_at + 1)] = parts_in[i]
        out[4 * r :, cw * z : cw * (z + 1)] = part_down


def join_rest(plan, meta, pieces):
    if not plan.aligned:
        parts = [unpack_rest(plan, piece) for piece in ordered(plan, meta, pieces)]
        w_in = jnp.concatenate([part for item in parts for part in item[0]], axis=1)
        blocks = [jnp.concatenate([item[1] for item in parts], axis=1)]
        blocks += [w_in[:, D * t : D * (t + 1)] for t in range(3)]
        blocks += [jnp.concatenate([item[2] for item in parts], axis=1)]
        return jnp.concatenate(blocks, axis=0)
    return pl.pallas_call(
        functools.partial(join_rest_kernel, plan),
        in_specs=[SMEM] + [VMEM] * plan.nrow,
        out_specs=VMEM,
        out_shape=shape_of((plan.packed, D), BF16),
        scratch_shapes=[pltpu.VMEM((plan.nrow, 3 * plan.r, 2 * plan.cw), BF16)],
        compiler_params=params(plan, "join_rest"),
        cost_estimate=cost(COSTS["join_rest"]),
        name="join_rest",
    )(meta, *pieces)


def by_block(plan, meta, own, other):
    stacked = jnp.stack(own + other)
    places = meta[plan.at_own : plan.at_other + plan.chips]
    return jnp.zeros_like(stacked).at[places].set(stacked)


def split_blocks(plan, meta, blocks):
    half = plan.chips // 2
    return [
        jnp.take(blocks, meta[plan.at_own + half * i : plan.at_own + half * (i + 1)], axis=0)
        for i in range(4)
    ]


def qkv_sources(plan, meta, own, other):
    if plan.aligned:
        return own + other
    return [by_block(plan, meta, own, other).reshape(D, EXT)]


def rest_sources(plan, meta, own, other):
    if plan.aligned:
        return own + other
    blocks = by_block(plan, meta, own, other)
    r = plan.r
    parts = [blocks[:, r * i : r * (i + 1)].reshape(D, D) for i in range(4)]
    parts.append(blocks[:, 4 * r :].reshape(FF, D))
    return [jnp.concatenate(parts, axis=0)]


def block_size(plan):
    return (plan.r, plan.rf) if plan.aligned else (D, FF)


def block_of(plan, meta, index):
    return meta[plan.at_own + index] if plan.aligned else 0


def rows_at(index, size):
    if isinstance(index, int):
        return pl.ds(index * size, size)
    return pl.ds(pl.multiple_of(index * size, size), size)


class Mover:
    def __init__(self, sems):
        self.sems = sems
        self.used = 0
        self.open = []

    def start(self, source, target):
        copy = pltpu.make_async_copy(source, target, self.sems.at[self.used])
        self.used += 1
        copy.start()
        return copy

    def send(self, source, target):
        self.open.append(self.start(source, target))

    def finish(self):
        for copy in self.open:
            copy.wait()


def wait_all(copies):
    for copy in copies:
        copy.wait()


def qkv_copies(plan, meta, sources, w_ref, sems):
    r, _ = block_size(plan)
    return [
        pltpu.make_async_copy(source, w_ref.at[rows_at(block_of(plan, meta, i), r)], sems.at[i])
        for i, source in enumerate(sources)
    ]


def grad_target(plan, grads, index):
    if not plan.aligned:
        return grads[0]
    half = plan.chips // 2
    return grads[index // half].at[index % half]


def grad_blocks(plan, height, width):
    return [shape_of((plan.chips // 2, height, width), BF16)] * 4


def source_count(plan):
    return 2 * plan.chips if plan.aligned else 1


def qkv_kernel(plan, meta, cos_ref, sin_ref, *refs):
    x_refs = refs[: plan.rows]
    count = source_count(plan)
    sources = refs[plan.rows : plan.rows + count]
    q_ref = refs[plan.rows + count]
    kv_refs = refs[plan.rows + count + 1 : plan.rows + count + 1 + HALVES]
    n_ref, gain_ref, w_ref, sems = refs[plan.rows + count + 1 + HALVES :]
    copies = qkv_copies(plan, meta, sources, w_ref, sems)
    for copy in copies:
        copy.start()
    units = [layer_norm(x_refs[j][0].astype(F32))[0] for j in range(plan.rows)]
    for copy in copies:
        copy.wait()
    gain_ref[...] = w_ref[:, 3 * D :].astype(F32).T[:8, :]
    for j in range(plan.rows):
        n_ref[plan.tok * j : plan.tok * (j + 1), :] = (units[j] * gain_ref[0:1, :]).astype(BF16)
    cosine, sine = cos_ref[...], sin_ref[...]
    normed = n_ref[...]
    queries = dot(normed, w_ref[:, :D], NN)
    q_ref[...] = rotate_all(queries, cosine, sine, 1.0).astype(BF16)
    keys = rotate_all(dot(normed, w_ref[:, D : 2 * D], NN), cosine, sine, 1.0).astype(BF16)
    values = dot(normed, w_ref[:, 2 * D : 3 * D], NN).astype(BF16)
    for h in range(HALVES):
        kv_refs[h][0] = keys[:, HALF * h : HALF * (h + 1)]
        kv_refs[h][1] = values[:, HALF * h : HALF * (h + 1)]


def project(plan, meta, cosine, sine, pieces, sources):
    local = plan.local
    count = len(sources)
    inputs = [meta, cosine, sine, *pieces, *sources]
    return pl.pallas_call(
        functools.partial(qkv_kernel, plan),
        in_specs=[SMEM, VMEM, VMEM] + [VMEM] * plan.rows + [ANY] * count,
        out_specs=[VMEM] * (3 + HALVES),
        out_shape=[shape_of((local, D), BF16)]
        + [shape_of((2, local, HALF), BF16)] * HALVES
        + [shape_of((local, D), BF16), shape_of((8, D), F32)],
        scratch_shapes=[pltpu.VMEM((D, EXT), BF16), pltpu.SemaphoreType.DMA((count,))],
        compiler_params=params(plan, "project"),
        cost_estimate=cost(COSTS["project"]),
        name="project",
    )(*inputs)


def fill_docs(plan, meta, lengths, kmask, qmask):
    low = meta[plan.at_lo]
    ends = []
    passed = jnp.int32(0)
    for n in range(NDOC):
        passed = passed + lengths[low, n]
        ends.append(passed)

    tok = plan.tok
    lane = lax.broadcasted_iota(jnp.int32, (tok, 128), 1) & (HD - 1)
    for i in range(plan.groups * plan.rows):
        places = meta[plan.at_base + i] + lax.broadcasted_iota(jnp.int32, (tok, 128), 0)
        docs = jnp.zeros((tok, 128), jnp.int32)
        for end in ends:
            docs = docs + (places >= end).astype(jnp.int32)
        part = slice(i * tok, (i + 1) * tok)
        same = docs == lane
        kmask[part, :] = jnp.where((lane < NDOC) & ~same, MASKED, 0.0).astype(BF16)
        if i < plan.rows:
            qmask[part, :] = jnp.where(same, 1.0, 0.0).astype(BF16)


def masks(plan, meta, lengths):
    keys = plan.groups * plan.local
    return pl.pallas_call(
        functools.partial(fill_docs, plan),
        in_specs=[SMEM, SMEM],
        out_specs=[VMEM, VMEM],
        out_shape=[shape_of((keys, 128), BF16), shape_of((plan.local, 128), BF16)],
        compiler_params=params(plan, "masks"),
        cost_estimate=cost(1),
        name="masks",
    )(meta, lengths)


def head_part(pair, head, other=None):
    lane = lax.broadcasted_iota(jnp.int32, pair.shape, 1)
    keep = (lane < HD) if head == 0 else (lane >= HD)
    return jnp.where(keep, pair, jnp.zeros_like(pair) if other is None else other)


def attend_kernel(plan, width, order, kmask, qmask, q_ref, *refs):
    groups, local = plan.groups, plan.local
    kv = refs[:groups]
    o_ref, low_ref, lse_ref, s_ref, p_ref = refs[groups:]
    total_keys = groups * local
    chunk = 128
    values_t = []
    row = lax.broadcasted_iota(jnp.int32, (HD + 8, total_keys), 0)
    pair_t = jnp.concatenate([kv[e][1].T for e in range(groups)], axis=1)
    for h in range(2):
        head = pair_t[h * HD : (h + 1) * HD, :]
        values_t.append(jnp.concatenate([head, jnp.ones((8, total_keys), BF16)], axis=0))
    for first in range(0, local, width):
        rows = slice(first, first + width)
        queries = q_ref[rows, :] * jnp.asarray(1.0 / math.sqrt(HD), BF16)
        tops = []
        for h in range(2):
            head_queries = head_part(queries, h, qmask[rows, :])
            top = jnp.full((8, width), MASKED, F32)
            for e in range(groups):
                for c in range(0, local, 2 * chunk):
                    part = slice(e * local + c, e * local + c + 2 * chunk)
                    keys = head_part(kv[e][0, c : c + 2 * chunk, :], h, kmask[part, :])
                    scores = dot(keys, head_queries, NT)
                    s_ref[h, part, :] = scores
                    top = jnp.maximum(top, jnp.max(scores.reshape(-1, 8, width), axis=0))
            tops.append(jnp.max(top, axis=0, keepdims=True))
        parts = []
        for h in range(2):
            for c in range(0, total_keys, chunk):
                part = slice(c, c + chunk)
                p_ref[h, part, :] = jnp.exp(s_ref[h, part, :] - tops[h]).astype(BF16)
            weighted = dot(values_t[h], p_ref[h], NN)
            total = weighted[HD : HD + 1, :]
            parts.append(weighted[:HD, :] / total)
            lse_ref[0, h : h + 1, rows] = tops[h] + jnp.log(total)
        heads = jnp.concatenate(parts, axis=0).T
        o_ref[rows, :] = heads
        low_ref[rows, :] = heads.astype(BF16)


def attend(plan, part, meta, mask, queries, kv):
    local, groups = plan.local, plan.groups
    width = min(512, local)
    skip = part * HALF_PAIRS
    pair = pl.BlockSpec((local, 128), lambda p: (0, p))
    pair_q = pl.BlockSpec((local, 128), lambda p: (0, p + skip))
    pair_kv = pl.BlockSpec((2, local, 128), lambda p: (0, 0, p))
    whole_k = pl.BlockSpec((groups * local, 128), lambda p: (0, 0))
    whole_q = pl.BlockSpec((local, 128), lambda p: (0, 0))
    inputs = [meta, *mask, queries, *kv]
    return pl.pallas_call(
        functools.partial(attend_kernel, plan, width),
        grid=(HALF_PAIRS,),
        in_specs=[SMEM, whole_k, whole_q, pair_q] + [pair_kv] * groups,
        out_specs=[pair, pair, pl.BlockSpec((1, 2, local), lambda p: (p, 0, 0))],
        out_shape=[
            shape_of((local, HALF), F32),
            shape_of((local, HALF), BF16),
            shape_of((HALF_PAIRS, 2, local), F32),
        ],
        scratch_shapes=[
            pltpu.VMEM((2, groups * local, width), F32),
            pltpu.VMEM((2, groups * local, width), BF16),
        ],
        compiler_params=params(plan, "attend"),
        cost_estimate=cost(COSTS["attend"]),
        name="attend",
    )(*inputs)


def attend_back_kernel(
    plan, width, order, kmask, qmask, q_ref, do_ref, o_ref, lse_ref, cos_ref, sin_ref, *refs
):
    groups, local = plan.groups, plan.local
    kv = refs[:groups]
    dq_ref = refs[groups]
    dkv = refs[groups + 1 : 2 * groups + 1]
    held, p_ref, ds_ref = refs[2 * groups + 1 :]
    keys_t = [kv[e][0].T for e in range(groups)]
    scale = 1.0 / math.sqrt(HD)
    chunk = 128
    for first in range(0, local, width):
        rows = slice(first, first + width)
        queries = q_ref[rows, :] * jnp.asarray(scale, BF16)
        dout = do_ref[rows, :]
        product = (dout.astype(F32) * o_ref[rows, :]).T
        parts = []
        for h in range(2):
            masked_queries = head_part(queries, h, qmask[rows, :])
            head_queries = head_part(queries, h)
            head_dout = head_part(dout, h)
            lse = lse_ref[0, h : h + 1, rows]
            delta = jnp.sum(product[h * HD : (h + 1) * HD, :], axis=0, keepdims=True)
            grad_queries = jnp.zeros((HD, width), F32)
            for e in range(groups):
                for c in range(0, local, chunk):
                    part = slice(c, c + chunk)
                    mask = kmask[e * local + c : e * local + c + chunk, :]
                    scores = dot(head_part(kv[e][0, part, :], h, mask), masked_queries, NT)
                    dprobs = dot(kv[e][1, part, :], head_dout, NT)
                    probs = jnp.exp(scores - lse)
                    p_ref[h, e, part, :] = probs.astype(BF16)
                    ds_ref[h, e, part, :] = (probs * (dprobs - delta)).astype(BF16)
                grad_values = dot(p_ref[h, e], head_dout, NN)
                grad_keys = dot(ds_ref[h, e], head_queries, NN)
                if first == 0 and h == 0:
                    held[e, 0] = grad_keys
                    held[e, 1] = grad_values
                else:
                    held[e, 0] += grad_keys
                    held[e, 1] += grad_values
                grad_queries = grad_queries + dot(
                    keys_t[e][h * HD : (h + 1) * HD, :], ds_ref[h, e], NN
                )
            parts.append(grad_queries)
        grad = jnp.concatenate(parts, axis=0).T * scale
        dq_ref[rows, :] = rotate_pair(grad, cos_ref[rows, :], sin_ref[rows, :], -1.0).astype(BF16)
    for e in range(groups):
        dkv[e][...] = held[e].astype(BF16)


def attend_back(plan, part, meta, mask, queries, dout, heads, lse, cosine, sine, kv):
    local, groups = plan.local, plan.groups
    width = min(512, local)
    half, first, count = part
    skip = half * HALF_PAIRS + first
    wide = 128 * count
    pair = pl.BlockSpec((local, 128), lambda p: (0, p))
    pair_h = pl.BlockSpec((local, 128), lambda p: (0, p + first))
    pair_q = pl.BlockSpec((local, 128), lambda p: (0, p + skip))
    whole_k = pl.BlockSpec((groups * local, 128), lambda p: (0, 0))
    inputs = [meta, *mask, queries, dout, heads, lse, cosine, sine, *kv]
    table = pl.BlockSpec((local, 128), lambda p: (0, 0))
    pair_kv = pl.BlockSpec((2, local, 128), lambda p: (0, 0, p))
    pair_kv_h = pl.BlockSpec((2, local, 128), lambda p: (0, 0, p + first))
    return pl.pallas_call(
        functools.partial(attend_back_kernel, plan, width),
        grid=(count,),
        in_specs=[
            SMEM,
            whole_k,
            table,
            pair_q,
            pair_q,
            pair_h,
            pl.BlockSpec((1, 2, local), lambda p: (p + first, 0, 0)),
            table,
            table,
        ]
        + [pair_kv_h] * groups,
        out_specs=[pair] + [pair_kv] * groups,
        out_shape=[shape_of((local, wide), BF16)] + [shape_of((2, local, wide), BF16)] * groups,
        scratch_shapes=[
            pltpu.VMEM((groups, 2, local, 128), F32),
            pltpu.VMEM((2, groups, local, width), BF16),
            pltpu.VMEM((2, groups, local, width), BF16),
        ],
        compiler_params=params(plan, "attend_back"),
        cost_estimate=cost(4 * count),
        name="attend_back",
    )(*inputs)


def middle_kernel(plan, meta, gain_ref, *refs):
    rows, tok, local = plan.rows, plan.tok, plan.local
    count = source_count(plan)
    low_refs, refs = refs[:HALVES], refs[HALVES:]
    x_refs, refs = refs[:rows], refs[rows:]
    sources, refs = refs[:count], refs[count:]
    out_refs, refs = refs[:rows], refs[rows:]
    do_out, dh_out, refs = refs[0], refs[1], refs[2:]
    grads, refs = refs[: 4 if plan.aligned else 1], refs[4 if plan.aligned else 1 :]
    low_ref, x_ref, dy_ref, w_out, w_in, w_down, h_ref, unit_ref, n_ref, gu_ref = refs[:10]
    mid_ref, dgu_ref, out_ref, do_ref, dh_ref, da_ref, inv_ref, g_out, g_in, g_down, sems = refs[10:]
    mover = Mover(sems)
    r, rf = block_size(plan)
    blocks = [block_of(plan, meta, i) for i in range(count)]
    low_in = [
        mover.start(low_refs[h], low_ref.at[:, pl.ds(HALF * h, HALF)]) for h in range(HALVES)
    ]
    out_in = [
        mover.start(source.at[pl.ds(0, r)], w_out.at[rows_at(block, r)])
        for source, block in zip(sources, blocks)
    ]
    x_in = [mover.start(x_refs[j].at[0], x_ref.at[pl.ds(tok * j, tok)]) for j in range(rows)]

    def fetch_in(t):
        return [
            mover.start(source.at[pl.ds((1 + t) * r, r)], w_in.at[t, rows_at(block, r)])
            for source, block in zip(sources, blocks)
        ]

    in_in = [fetch_in(t) for t in range(3)]
    dy_in = [mover.start(x_refs[j].at[1], dy_ref.at[pl.ds(tok * j, tok)]) for j in range(rows)]
    down_in = [
        mover.start(source.at[pl.ds(4 * r, rf)], w_down.at[rows_at(block, rf)])
        for source, block in zip(sources, blocks)
    ]
    wait_all(low_in)
    wait_all(out_in)
    wait_all(x_in)
    gain = gain_ref[1:2, :]

    h_ref[...] = x_ref[...].astype(F32) + dot(low_ref[...], w_out[...], NN)
    unit, inv_std = layer_norm(h_ref[...])
    unit_ref[...] = unit
    inv_ref[...] = jnp.broadcast_to(inv_std, (local, 128))
    n_ref[...] = (unit * gain).astype(BF16)

    for t in range(3):
        wait_all(in_in[t])

    @pl.loop(0, 3)
    def _(t):
        gu_ref[:, pl.ds(pl.multiple_of(t * D, D), D)] = dot(n_ref[...], w_in[t], NN)

    wait_all(dy_in)
    wait_all(down_in)
    size = FF // 3

    @pl.loop(0, 3)
    def _(f):
        cols = pl.ds(pl.multiple_of(f * size, size), size)
        up_cols = pl.ds(pl.multiple_of(FF + f * size, size), size)
        gate = gu_ref[:, cols]
        up = gu_ref[:, up_cols]
        below = 0.5 + 0.5 * lax.erf(gate * math.sqrt(0.5))
        active = gate * below
        mid_ref[:, cols] = (active * up).astype(BF16)
        slope = below + gate * jnp.exp(-0.5 * gate * gate) * (1.0 / math.sqrt(2.0 * math.pi))
        dmid = dot(dy_ref[...], w_down[cols, :], NT)
        dgu_ref[:, cols] = (dmid * up * slope).astype(BF16)
        dgu_ref[:, up_cols] = (dmid * active).astype(BF16)
        g_down[cols, :] = dot(mid_ref[:, cols], dy_ref[...], TN).astype(BF16)

    targets = [grad_target(plan, grads, i) for i in range(count)]
    for target, block in zip(targets, blocks):
        mover.send(g_down.at[rows_at(block, rf)], target.at[pl.ds(4 * r, rf)])
    step = D // 3

    @pl.loop(0, 3)
    def _(n):
        cols = pl.ds(pl.multiple_of(n * step, step), step)
        mixed = dot(mid_ref[...], w_down[:, cols], NN)
        out_ref[:, cols] = (h_ref[:, cols] + mixed).astype(BF16)
        grad = dot(dgu_ref[:, :D], w_in[0, cols, :], NT)
        for t in range(1, 3):
            grad = grad + dot(dgu_ref[:, D * t : D * (t + 1)], w_in[t, cols, :], NT)
        dh_ref[:, cols] = grad
    for j in range(rows):
        mover.send(out_ref.at[pl.ds(tok * j, tok)], out_refs[j])

    @pl.loop(0, 3)
    def _(t):
        g_in[t] = dot(
            n_ref[...], dgu_ref[:, pl.ds(pl.multiple_of(t * D, D), D)], TN
        ).astype(BF16)

    for t in range(3):
        for target, block in zip(targets, blocks):
            mover.send(g_in.at[t, rows_at(block, r)], target.at[pl.ds((1 + t) * r, r)])

    grad_hidden = dy_ref[...].astype(F32) + norm_backward(
        dh_ref[...], unit_ref[...], inv_ref[:, 0:1], gain
    )
    dh_ref[...] = grad_hidden
    da_ref[...] = grad_hidden.astype(BF16)
    mover.send(dh_ref, dh_out)
    do_ref[...] = dot(da_ref[...], w_out[...], NT).astype(BF16)
    g_out[...] = dot(low_ref[...], da_ref[...], TN).astype(BF16)

    mover.send(do_ref, do_out)
    for target, block in zip(targets, blocks):
        mover.send(g_out.at[rows_at(block, r)], target.at[pl.ds(0, r)])
    mover.finish()


def middle(plan, meta, low, gains, pieces, sources):
    local, rows, tok = plan.local, plan.rows, plan.tok
    count = len(sources)
    total = 4 * D + FF
    if plan.aligned:
        grads = grad_blocks(plan, plan.packed, D)
    else:
        grads = [shape_of((total, D), BF16)]
    return pl.pallas_call(
        functools.partial(middle_kernel, plan),
        in_specs=[SMEM, VMEM] + [ANY] * (HALVES + rows + count),
        out_specs=[ANY] * (rows + 2 + len(grads)),
        out_shape=[shape_of((tok, D), BF16)] * rows
        + [shape_of((local, D), BF16), shape_of((local, D), F32)]
        + grads,
        scratch_shapes=[
            pltpu.VMEM((local, D), BF16),
            pltpu.VMEM((local, D), BF16),
            pltpu.VMEM((local, D), BF16),
            pltpu.VMEM((D, D), BF16),
            pltpu.VMEM((3, D, D), BF16),
            pltpu.VMEM((FF, D), BF16),
            pltpu.VMEM((local, D), F32),
            pltpu.VMEM((local, D), F32),
            pltpu.VMEM((local, D), BF16),
            pltpu.VMEM((local, 2 * FF), F32),
            pltpu.VMEM((local, FF), BF16),
            pltpu.VMEM((local, 2 * FF), BF16),
            pltpu.VMEM((local, D), BF16),
            pltpu.VMEM((local, D), BF16),
            pltpu.VMEM((local, D), F32),
            pltpu.VMEM((local, D), BF16),
            pltpu.VMEM((local, 128), F32),
            pltpu.VMEM((D, D), BF16),
            pltpu.VMEM((3, D, D), BF16),
            pltpu.VMEM((FF, D), BF16),
            pltpu.SemaphoreType.DMA((HALVES + 3 * rows + 2 + 10 * count,)),
        ],
        compiler_params=params(plan, "middle"),
        cost_estimate=cost(COSTS["middle"]),
        name="middle",
    )(meta, gains, *low, *pieces, *sources)


def back_weight_kernel(plan, meta, *refs):
    groups, local = plan.groups, plan.local
    count = len(BACK_PARTS)
    cos_ref, sin_ref, n_in, refs = refs[0], refs[1], refs[2], refs[3:]
    dq_refs, refs = refs[:count], refs[count:]
    dkv, refs = refs[: count * groups], refs[count * groups :]
    dp_out, refs = refs[0], refs[1:]
    grads, refs = refs[: 4 if plan.aligned else 1], refs[4 if plan.aligned else 1 :]
    cos, sin, n_ref, dkv_ref, dp_ref, g_ref, sems = refs
    mover = Mover(sems)
    columns = []
    for half, first, pairs in BACK_PARTS:
        columns.append(pl.ds(HALF * half + 128 * first, 128 * pairs))
    first_in = [mover.start(n_in, n_ref)]
    for i in range(count):
        first_in.append(mover.start(dq_refs[i], dp_ref.at[0, :, columns[i]]))
    rest_in = [mover.start(cos_ref, cos), mover.start(sin_ref, sin)]
    for i in range(count):
        for e in range(groups):
            rest_in.append(
                mover.start(dkv[groups * i + e], dkv_ref.at[e, :, :, columns[i]])
            )
    r, _ = block_size(plan)

    def send_grad(t):
        cols = pl.ds(D * t, D)
        for i in range(source_count(plan)):
            at = rows_at(block_of(plan, meta, i), r)
            mover.send(g_ref.at[at, cols], grad_target(plan, grads, i).at[:, cols])

    wait_all(first_in)
    normed = n_ref[...]
    g_ref[:, :D] = dot(normed, dp_ref[0], TN).astype(BF16)
    send_grad(0)
    wait_all(rest_in)
    dp_ref[2] = sum_pieces([dkv_ref[e, 1] for e in range(groups)]).astype(BF16)
    g_ref[:, 2 * D : 3 * D] = dot(normed, dp_ref[2], TN).astype(BF16)
    send_grad(2)
    grad_keys = sum_pieces([dkv_ref[e, 0] for e in range(groups)])
    dp_ref[1] = rotate_all(grad_keys, cos[...], sin[...], -1.0).astype(BF16)
    mover.send(dp_ref, dp_out)
    g_ref[:, D : 2 * D] = dot(normed, dp_ref[1], TN).astype(BF16)
    send_grad(1)
    mover.finish()


def back_weight(plan, meta, cosine, sine, normed, dq, dkv):
    local, groups, count = plan.local, plan.groups, len(BACK_PARTS)
    if plan.aligned:
        grads = grad_blocks(plan, plan.r, 3 * D)
    else:
        grads = [shape_of((D, 3 * D), BF16)]
    results = pl.pallas_call(
        functools.partial(back_weight_kernel, plan),
        in_specs=[SMEM] + [ANY] * (3 + count * (1 + groups)),
        out_specs=[ANY] * (1 + len(grads)),
        out_shape=[shape_of((3, local, D), BF16)] + grads,
        scratch_shapes=[
            pltpu.VMEM((local, 128), F32),
            pltpu.VMEM((local, 128), F32),
            pltpu.VMEM((local, D), BF16),
            pltpu.VMEM((groups, 2, local, D), BF16),
            pltpu.VMEM((3, local, D), BF16),
            pltpu.VMEM((D, 3 * D), BF16),
            pltpu.SemaphoreType.DMA((4 + count * (1 + groups) + 3 * source_count(plan),)),
        ],
        compiler_params=params(plan, "back_weight"),
        cost_estimate=cost(COSTS["back_weight"]),
        name="back_weight",
    )(meta, cosine, sine, normed, *dq, *dkv)
    return results[0], results[1:]


def back_in_kernel(plan, meta, dp_ref, dh_ref, gain_ref, *refs):
    rows, tok = plan.rows, plan.tok
    count = source_count(plan)
    x_refs, refs = refs[:rows], refs[rows:]
    out_refs, refs = refs[:rows], refs[rows:]
    sources, refs = refs[:count], refs[count:]
    both_refs = refs[:rows]
    w_ref, in_sems = refs[rows:]
    copies = qkv_copies(plan, meta, sources, w_ref, in_sems)
    for copy in copies:
        copy.start()
    for copy in copies:
        copy.wait()
    grad_normed = dot(dp_ref[0], w_ref[:, :D], NT)
    for t in range(1, 3):
        grad_normed = grad_normed + dot(dp_ref[t], w_ref[:, D * t : D * (t + 1)], NT)
    for j in range(rows):
        part = slice(tok * j, tok * (j + 1))
        unit, inv_std = layer_norm(x_refs[j][0].astype(F32))
        grad = grad_normed[part, :]
        back = norm_backward(grad, unit, inv_std, gain_ref[0:1, :])
        both_refs[j][0] = out_refs[j][...]
        both_refs[j][1] = (dh_ref[part, :] + back).astype(BF16)


def back_in(plan, meta, dprojected, dhidden, gains, pieces, outs, sources):
    rows, tok = plan.rows, plan.tok
    count = len(sources)
    return pl.pallas_call(
        functools.partial(back_in_kernel, plan),
        in_specs=[SMEM] + [VMEM] * (3 + 2 * rows) + [ANY] * count,
        out_specs=[VMEM] * rows,
        out_shape=[shape_of((2, tok, D), BF16)] * rows,
        scratch_shapes=[pltpu.VMEM((D, EXT), BF16), pltpu.SemaphoreType.DMA((count,))],
        compiler_params=params(plan, "back_in"),
        cost_estimate=cost(COSTS["back_in"]),
        name="back_in",
    )(meta, dprojected, dhidden, gains, *pieces, *outs, *sources)


def gain_columns(weight, grad):
    total = jnp.sum(weight.astype(F32) * grad.astype(F32), axis=1, keepdims=True)
    high = total.astype(BF16)
    return high, (total - high.astype(F32)).astype(BF16)


def pad_width(plan):
    return -(-(3 * plan.cw + 2) // 128) * 128


def gain_tail(plan, weight, grad):
    width = pad_width(plan) - 3 * plan.cw
    high, rest = gain_columns(weight, grad)
    lane = lax.broadcasted_iota(jnp.int32, (plan.r, width), 1)
    return jnp.where(lane == 0, high, jnp.where(lane == 1, rest, jnp.zeros_like(high)))


def cut_qkv_kernel(plan, meta, total, weight, *refs):
    outs, held = refs[: plan.nrow], refs[plan.nrow]
    width = 3 * plan.cw
    tail = gain_tail(plan, weight[:, : 3 * D], total[...])
    for z in range(plan.nrow):
        place_at = meta[plan.at_z + z]
        held[place_at, :, :width] = total[:, width * z : width * (z + 1)]
        held[place_at, :, width:] = tail
    for j in range(plan.nrow):
        outs[j][...] = held[j]


def cut_qkv(plan, meta, total, weight):
    width, wide = 3 * plan.cw, pad_width(plan)
    if not plan.aligned:
        tail = gain_tail(plan, weight[:, : 3 * D], total)
        parts = [
            jnp.concatenate([total[:, width * z : width * (z + 1)], tail], axis=1)
            for z in range(plan.nrow)
        ]
        return ordered(plan, meta, parts)
    return pl.pallas_call(
        functools.partial(cut_qkv_kernel, plan),
        in_specs=[SMEM, VMEM, VMEM],
        out_specs=[VMEM] * plan.nrow,
        out_shape=[shape_of((plan.r, wide), BF16)] * plan.nrow,
        scratch_shapes=[pltpu.VMEM((plan.nrow, plan.r, wide), BF16)],
        compiler_params=params(plan, "cut_qkv"),
        cost_estimate=cost(COSTS["cut_qkv"]),
        name="cut_qkv",
    )(meta, total, weight)


def gain_blank(plan, weight, grad):
    r, blank = plan.r, 2 * plan.r - plan.rf
    cols = [weight[r * t : r * (t + 1)] for t in range(1, 4)]
    grads = [grad[r * t : r * (t + 1)] for t in range(1, 4)]
    high, rest = gain_columns(jnp.concatenate(cols, axis=1), jnp.concatenate(grads, axis=1))
    lane = lax.broadcasted_iota(jnp.int32, (blank, plan.cw), 1)
    found = jnp.zeros((blank, plan.cw), BF16)
    for i in range(r // blank):
        part = slice(blank * i, blank * (i + 1))
        found = jnp.where(lane == 2 * i, high[part], found)
        found = jnp.where(lane == 2 * i + 1, rest[part], found)
    return found


def cut_rest_kernel(plan, meta, total, weight, *refs):
    outs, held = refs[: plan.nrow], refs[plan.nrow]
    r, rf, cw = plan.r, plan.rf, plan.cw
    blank = gain_blank(plan, weight[...], total[...])
    for z in range(plan.nrow):
        place_at = meta[plan.at_z + z]
        cols = slice(cw * z, cw * (z + 1))
        parts = []
        for i in range(3):
            block, at = (3 * z + i) // plan.nrow, (3 * z + i) % plan.nrow
            parts.append(total[r * (1 + block) : r * (2 + block), cw * at : cw * (at + 1)])
        held[place_at, :r, :] = jnp.concatenate([parts[0], parts[2]], axis=1)
        held[place_at, r : 2 * r, :] = jnp.concatenate(
            [parts[1], total[4 * r : 5 * r, cols]], axis=1
        )
        rest = total[5 * r : 4 * r + rf, cols]
        held[place_at, 2 * r :, :] = jnp.concatenate(
            [total[:r, cols], jnp.concatenate([rest, blank], axis=0)], axis=1
        )
    for j in range(plan.nrow):
        outs[j][...] = held[j]


def cut_rest(plan, meta, total, weight):
    r, cw = plan.r, plan.cw
    if not plan.aligned:
        grad_in = jnp.concatenate([total[r * (1 + t) : r * (2 + t)] for t in range(3)], axis=1)
        blank = gain_blank(plan, weight, total)
        parts = [
            pack_rest(
                plan,
                total[:r, cw * z : cw * (z + 1)],
                grad_in[:, 3 * cw * z : 3 * cw * (z + 1)],
                total[4 * r :, cw * z : cw * (z + 1)],
                blank,
            )
            for z in range(plan.nrow)
        ]
        return ordered(plan, meta, parts)
    return pl.pallas_call(
        functools.partial(cut_rest_kernel, plan),
        in_specs=[SMEM, VMEM, VMEM],
        out_specs=[VMEM] * plan.nrow,
        out_shape=[shape_of((3 * r, 2 * cw), BF16)] * plan.nrow,
        scratch_shapes=[pltpu.VMEM((plan.nrow, 3 * r, 2 * cw), BF16)],
        compiler_params=params(plan, "cut_rest"),
        cost_estimate=cost(COSTS["cut_rest"]),
        name="cut_rest",
    )(meta, total, weight)


def reduce_z(plan, pieces):
    return [pieces[0]] + [
        lax.ppermute(pieces[j], "row", plan.z_pairs(j)) for j in range(1, plan.nrow)
    ]


def sum_pieces(pieces):
    total = pieces[0].astype(F32)
    for piece in pieces[1:]:
        total = total + piece.astype(F32)
    return total


def end_rest_kernel(plan, *refs):
    pieces, (g_out, g_in, g_down, g_gain) = refs[: plan.nrow], refs[plan.nrow :]
    total = sum_pieces([piece[...] for piece in pieces])
    parts_in, part_out, part_down = unpack_rest(plan, total)
    g_out[...] = part_out
    g_in[...] = jnp.concatenate(parts_in, axis=1)
    g_down[...] = part_down
    blank = 2 * plan.r - plan.rf
    g_gain[...] = total[3 * plan.r - blank :, plan.cw : plan.cw + 128].T[:8, :]


def end_rest(plan, pieces):
    r, blank = plan.r, 2 * plan.r - plan.rf
    if not plan.aligned:
        total = sum_pieces(pieces)
        parts_in, out_grad, down_grad = unpack_rest(plan, total)
        in_grad = jnp.concatenate(parts_in, axis=1)
        gain = total[3 * r - blank :, plan.cw : plan.cw + 8].T
    else:
        out_grad, in_grad, down_grad, gain = pl.pallas_call(
            functools.partial(end_rest_kernel, plan),
            in_specs=[VMEM] * plan.nrow,
            out_specs=[VMEM] * 4,
            out_shape=[
                shape_of((r, plan.cw), F32),
                shape_of((r, 3 * plan.cw), F32),
                shape_of((plan.rf, plan.cw), F32),
                shape_of((8, blank), F32),
            ],
            compiler_params=params(plan, "end_rest"),
            cost_estimate=cost(COSTS["end_rest"]),
            name="end_rest",
        )(*pieces)
    gain = jnp.concatenate([gain[2 * i] + gain[2 * i + 1] for i in range(r // blank)])
    return out_grad, in_grad, down_grad, gain


def end_qkv_kernel(plan, gain_ref, *refs):
    pieces, (g_qkv, g_gain) = refs[: plan.nrow], refs[plan.nrow :]
    width, wide = 3 * plan.cw, pad_width(plan)
    total = sum_pieces([piece[...] for piece in pieces])
    g_qkv[...] = total[:, :width]
    tail = total[:, wide - 128 :].T
    at = width - (wide - 128)
    g_gain[...] = (tail[at : at + 1, :] + tail[at + 1 : at + 2, :]) / gain_ref[...]


def end_qkv(plan, gain, pieces):
    width, wide = 3 * plan.cw, pad_width(plan)
    if not plan.aligned:
        total = sum_pieces(pieces)
        return total[:, :width], (total[:, width] + total[:, width + 1]) / gain[0]
    grad, gain_grad = pl.pallas_call(
        functools.partial(end_qkv_kernel, plan),
        in_specs=[VMEM] * (1 + plan.nrow),
        out_specs=[VMEM] * 2,
        out_shape=[shape_of((plan.r, width), F32), shape_of((1, plan.r), F32)],
        compiler_params=params(plan, "end_qkv"),
        cost_estimate=cost(COSTS["end_qkv"]),
        name="end_qkv",
    )(gain, *pieces)
    return grad, gain_grad.reshape(plan.r)


def rotation_tables(plan, meta, lengths):
    ends = jnp.cumsum(lax.dynamic_index_in_dim(lengths, meta[plan.at_lo], 0, keepdims=False))
    starts = jnp.concatenate([jnp.zeros((1,), jnp.int32), ends[:-1]])
    bases = meta[plan.at_base : plan.at_base + plan.rows]
    places = (bases[:, None] + jnp.arange(plan.tok, dtype=jnp.int32)[None, :]).reshape(-1)
    passed = places[:, None] >= starts[None, :]
    positions = places - jnp.max(jnp.where(passed, starts[None, :], 0), axis=1)
    half = HD // 2
    inverse = ROPE_BASE ** (-(jnp.arange(half, dtype=F32) * (2.0 / HD)))
    angles = positions.astype(F32)[:, None] * inverse
    cosine, sine = jnp.cos(angles), jnp.sin(angles)
    return (
        jnp.concatenate([cosine] * 4, axis=1),
        jnp.concatenate([-sine, sine, -sine, sine], axis=1),
    )


def body(
    plan,
    tokens,
    lengths,
    norm_gain,
    qkv_weight,
    out_weight,
    mlp_gain,
    in_weight,
    down_weight,
    cotangent,
):
    blk, row = lax.axis_index("blk"), lax.axis_index("row")
    meta = lax.dynamic_slice(
        jnp.asarray(plan.table), (row, blk, 0), (1, 1, plan.size)
    ).reshape(plan.size)
    qkv_parts = gather_z(plan, qkv_weight)
    cut, packed = prepare(plan, meta, tokens, cotangent, out_weight, in_weight, down_weight)
    pieces = exchange_rows(plan, cut)
    rest_parts = gather_z(plan, packed, behind=qkv_parts)
    gains = jnp.pad(jnp.stack([norm_gain, mlp_gain], axis=1), ((0, 0), (0, 126)))
    cosine, sine = rotation_tables(plan, meta, lengths)
    mask = masks(plan, meta, lengths)
    qkv_joined = join_qkv(plan, meta, gains, qkv_parts)
    qkv_own = gather_start(plan, qkv_joined, pieces[1:])
    qkv_own[1] = tie(qkv_own[1], *rest_parts[2:], cosine, sine, *mask)
    qkv_own = gather_more(plan, qkv_own)
    qkv_own[-1] = tie(qkv_own[-1], rest_parts[1])
    qkv_other = [swap_cores(plan, piece) for piece in qkv_own]
    qkv_from = qkv_sources(plan, meta, qkv_own, qkv_other)
    rest_parts[0] = tie(rest_parts[0], qkv_joined, *qkv_other[:-1])
    joined = join_rest(plan, meta, rest_parts)
    results = project(plan, tie(meta, joined), cosine, sine, pieces, qkv_from)
    queries, kv, (normed, gains) = results[0], results[1 : 1 + HALVES], results[1 + HALVES :]
    kv = [
        [part]
        + [
            lax.ppermute(part, "blk", plan.xor_pairs(plan.member(e)))
            for e in range(1, plan.groups)
        ]
        for part in kv
    ]
    rest_own = gather_start(plan, joined)
    heads, low, lse = [None] * HALVES, [None] * HALVES, [None] * HALVES
    heads[0], low[0], lse[0] = attend(plan, 0, meta, mask, queries, kv[0])
    order = tie(meta, low[0], *rest_own[1:])
    rest_own[1:] = [tie(piece, low[0]) for piece in rest_own[1:]]
    rest_other = [swap_cores(plan, piece) for piece in rest_own]
    rest_more = gather_more(plan, rest_own)[len(rest_own) :]
    heads[1], low[1], lse[1] = attend(plan, 1, order, mask, queries, kv[1])
    rest_more = [tie(piece, low[1]) for piece in rest_more]
    rest_own = rest_own + rest_more
    rest_other = rest_other + [swap_cores(plan, piece) for piece in rest_more]
    rest_from = rest_sources(plan, meta, rest_own, rest_other)
    results = middle(plan, meta, low, gains, pieces, rest_from)
    outs, (dout, dhidden), rest_grads = (
        results[: plan.rows],
        results[plan.rows : plan.rows + 2],
        results[plan.rows + 2 :],
    )
    if not plan.aligned:
        r, rf, nblk = plan.r, plan.rf, plan.nblk
        whole = rest_grads[0]
        blocks = [whole[D * i : D * (i + 1)].reshape(nblk, r, D) for i in range(4)]
        blocks.append(whole[4 * D :].reshape(nblk, rf, D))
        rest_grads = split_blocks(plan, meta, jnp.concatenate(blocks, axis=1))
    keep_low, keep_high, other_low, other_high = reduce_start(plan, rest_grads)
    dq, dkv = [], []
    order = meta
    for i, part in enumerate(BACK_PARTS):
        half = part[0]
        results = attend_back(
            plan, part, order, mask, queries, dout, heads[half], lse[half], cosine, sine, kv[half]
        )
        dq.append(results[0])
        dkv.append(results[1])
        dkv += [
            lax.ppermute(results[1 + e], "blk", plan.xor_pairs(plan.member(e)))
            for e in range(1, plan.groups)
        ]
        if i == 0:
            rest_high = add_low(tie(keep_high, dq[0]), other_high)
            rest_low = add_low(tie(keep_low, dq[0]), other_low)
            order = tie(meta, dq[0], rest_high, rest_low)
        else:
            order = tie(meta, dq[i], *dkv[1 : plan.groups])
    rest_low, rest_high = reduce_step(plan, plan.bits - 1, tie(rest_low, dq[-1]), rest_high)
    order = tie(meta, rest_low) if rest_high is None else tie(meta, rest_low, rest_high)
    dprojected, qkv_grads = back_weight(plan, order, cosine, sine, normed, dq, dkv)
    if not plan.aligned:
        qkv_grads = split_blocks(plan, meta, qkv_grads[0].reshape(plan.nblk, plan.r, 3 * D))
    rest_low = tie(rest_low, dprojected)
    for step in reversed(range(plan.bits - 1)):
        rest_low, rest_high = reduce_step(plan, step, rest_low, rest_high)
    keep_low, keep_high, other_low, other_high = reduce_start(plan, qkv_grads)
    qkv_high = add_low(tie(keep_high, rest_low), other_high)
    qkv_low = add_low(keep_low, other_low)
    rest_cut = cut_rest(plan, meta, tie(rest_low, qkv_high), joined)
    order = tie(meta, qkv_high, qkv_low, *rest_cut)
    both = back_in(plan, order, dprojected, dhidden, gains, pieces, outs, qkv_from)
    rest_pieces = reduce_z(plan, rest_cut)
    qkv_low = tie(qkv_low, both[0], *rest_pieces[1:3])
    for step in reversed(range(plan.bits)):
        if step == 0:
            qkv_low = tie(qkv_low, *rest_pieces[3:])
        qkv_low, qkv_high = reduce_step(plan, step, qkv_low, qkv_high)
    both = exchange_rows(plan, [tie(piece, qkv_low) for piece in both])
    qkv_cut = cut_qkv(plan, meta, tie(qkv_low, *rest_pieces[1:]), qkv_joined)
    qkv_pieces = reduce_z(plan, qkv_cut)
    rest_pieces[0] = tie(rest_pieces[0], *qkv_cut)
    out_grad, in_grad, down_grad, mlp_gain_grad = end_rest(plan, rest_pieces)
    output, input_grad = place(plan, meta, [tie(both[0], *qkv_cut)] + both[1:])
    gain_row = norm_gain.astype(F32)[None]
    qkv_grad, norm_gain_grad = end_qkv(plan, tie(gain_row, output, input_grad, in_grad), qkv_pieces)
    mlp_gain_grad = mlp_gain_grad / mlp_gain.astype(F32)
    return (
        output,
        input_grad,
        norm_gain_grad,
        qkv_grad,
        out_grad,
        mlp_gain_grad,
        in_grad,
        down_grad,
    )


def solution(mesh):
    weights = P("blk", "row")
    acts = P("row", "blk", None)

    def run(*args):
        rows = args[0].shape[0] // mesh.shape["row"]
        tok = args[0].shape[1] // mesh.shape["blk"]
        plan = Plan(mesh, rows, tok)
        return jax.shard_map(
            functools.partial(body, plan),
            mesh=mesh,
            in_specs=(acts, P("row", None), P("blk"), weights, weights, P("blk"), weights, weights, acts),
            out_specs=(acts, acts, P("blk"), weights, weights, P("blk"), weights, weights),
            check_vma=False,
        )(*args)

    return run
```

```python
import functools
import math

import jax
import jax.numpy as jnp
import numpy as np
from jax import lax
from jax.experimental import pallas as pl
from jax.experimental.pallas import tpu as pltpu
from jax.sharding import PartitionSpec as P

D = 768
HEADS = 12
HD = 64
FF = 1152
NDOC = 8
PAIRS = HEADS // 2
EXT = 3 * D + 128

ROPE_BASE = 160000.0
NORM_EPSILON = 1e-05
MASKED = -1e30
F32 = jnp.float32
BF16 = jnp.bfloat16
NN = (((1,), (0,)), ((), ()))
NT = (((1,), (1,)), ((), ()))
TN = (((0,), (0,)), ((), ()))
LIMITS = {
    "prepare": 60,
    "place_rows": 8,
    "join_qkv": 4,
    "join_rest": 6,
    "project": 20,
    "masks": 4,
    "attend": 16,
    "middle": 56,
    "attend_back": 16,
    "back_in": 20,
    "back_weight": 16,
    "cut_qkv": 4,
    "cut_rest": 6,
    "end_rest": 4,
    "end_qkv": 4,
}
HALVES = 2
HALF_PAIRS = PAIRS // HALVES
HALF = D // HALVES
BACK_PARTS = ((0, 0, 1), (0, 1, 2), (1, 0, 3))
COSTS = {
    "prepare": 4,
    "place_rows": 2,
    "join_qkv": 2,
    "join_rest": 2,
    "project": 7,
    "attend": 9,
    "middle": 20,
    "attend_back": 12,
    "back_in": 7,
    "back_weight": 6,
    "cut_qkv": 2,
    "cut_rest": 2,
    "end_rest": 2,
    "end_qkv": 2,
}
SMEM = pl.BlockSpec(memory_space=pltpu.SMEM)
ANY = pl.BlockSpec(memory_space=pl.ANY)
VMEM = pl.BlockSpec(memory_space=pltpu.VMEM)


def dot(a, b, dims):
    return lax.dot_general(a, b, dims, preferred_element_type=F32)


def shape_of(dims, dtype):
    return jax.ShapeDtypeStruct(tuple(dims), dtype)


def params(plan, name):
    size = max(1, plan.groups * plan.local // 1024)
    return pltpu.CompilerParams(vmem_limit_bytes=min(60, LIMITS[name] * size) * 1024 * 1024)


def cost(microseconds):
    return pl.CostEstimate(
        flops=int(microseconds * 1e6), bytes_accessed=1 << 10, transcendentals=0
    )


def tie(value, *others):
    return lax.optimization_barrier((value, *others))[0]


class Plan:
    def __init__(self, mesh, rows, tok):
        self.nrow = mesh.shape["row"]
        self.nblk = mesh.shape["blk"]
        self.rows = rows
        self.tok = tok
        self.local = rows * tok
        self.chips = self.nblk // 2
        self.bits = self.chips.bit_length() - 1
        self.groups = self.nblk // rows
        self.r = D // self.nblk
        self.rf = FF // self.nblk
        self.cw = D // self.nrow
        self.aligned = self.r % 16 == 0 and self.rf % 16 == 0
        self.packed = 4 * self.r + self.rf
        rows_, chips, nrow = self.rows, self.chips, self.nrow
        self.at_pick = 0
        self.at_base = self.at_pick + rows_
        self.at_own = self.at_base + self.groups * rows_
        self.at_other = self.at_own + chips
        self.at_z = self.at_other + chips
        self.at_lo = self.at_z + nrow
        self.size = self.at_lo + 1
        table = np.zeros((nrow, self.nblk, self.size), np.int32)
        for z in range(nrow):
            for blk in range(self.nblk):
                chip, core = blk // 2, blk % 2
                low = chip % rows_
                entry = table[z, blk]
                for j in range(rows_):
                    entry[self.at_pick + j] = low ^ j
                for e in range(self.groups):
                    other = blk ^ self.member(e)
                    for j in range(rows_):
                        entry[self.at_base + e * rows_ + j] = (2 * ((other // 2) ^ j) + other % 2) * tok
                for j in range(chips):
                    entry[self.at_own + j] = 2 * (chip ^ self.order(core, j)) + core
                    entry[self.at_other + j] = 2 * (chip ^ self.order(1 - core, j)) + 1 - core
                for other in range(nrow):
                    entry[self.at_z + other] = other ^ z
                entry[self.at_lo] = low
        self.table = table

    def member(self, e):
        return (e & 1) | ((e >> 1) * 2 * self.rows)

    def order(self, core, j):
        if core == 0:
            return j
        return int(format(j, "0%db" % self.bits)[::-1], 2) if self.bits else 0

    def step_pairs(self, step):
        def flip(blk):
            bit = step if blk % 2 == 0 else self.bits - 1 - step
            return 2 * ((blk // 2) ^ (1 << bit)) + blk % 2

        return [(blk, flip(blk)) for blk in range(self.nblk)]

    def xor_pairs(self, mask):
        return [(blk, blk ^ mask) for blk in range(self.nblk)]

    def z_pairs(self, mask):
        return [(z, z ^ mask) for z in range(self.nrow)]


def swap_cores(plan, value):
    return lax.ppermute(value, "blk", plan.xor_pairs(1))


def gather_z(plan, value, behind=None):
    pieces = [value]
    for j in range(1, plan.nrow):
        source = value if behind is None else tie(value, behind[j])
        pieces.append(lax.ppermute(source, "row", plan.z_pairs(j)))
    return pieces


def exchange_rows(plan, pieces):
    return [pieces[0]] + [
        lax.ppermute(pieces[j], "blk", plan.xor_pairs(2 * j)) for j in range(1, plan.rows)
    ]


def gather_start(plan, value, behind=()):
    pairs = [plan.step_pairs(step) for step in range(plan.bits)]
    first = lax.ppermute(value, "blk", pairs[0])
    second = [lax.ppermute(tie(value, *behind), "blk", pairs[1])] if plan.bits > 1 else []
    return [value, first] + second


def gather_more(plan, pieces):
    for step in range(1, plan.bits):
        have = 1 << step
        missing = pieces[len(pieces) - have :] if step > 1 else pieces[1:2]
        pieces = pieces + [lax.ppermute(piece, "blk", plan.step_pairs(step)) for piece in missing]
    return pieces


def add_low(a, b):
    return (a.astype(F32) + b.astype(F32)).astype(BF16)


def reduce_start(plan, grads):
    keep_low, keep_high, send_low, send_high = grads
    other_high = swap_cores(plan, send_high)
    return keep_low, keep_high, swap_cores(plan, send_low), other_high


def reduce_step(plan, step, low, high):
    moved = lax.ppermute(high, "blk", plan.step_pairs(step))
    half = low.shape[0] // 2
    if half == 0:
        return add_low(low, moved)[0], None
    high = add_low(low[half:], moved[half:])
    return add_low(low[:half], moved[:half]), high


def layer_norm(values):
    average = jnp.mean(values, axis=-1, keepdims=True)
    centred = values - average
    inv_std = lax.rsqrt(jnp.mean(centred * centred, axis=-1, keepdims=True) + NORM_EPSILON)
    return centred * inv_std, inv_std


def norm_backward(grad_out, normalized, inv_std, gain):
    scaled = grad_out * gain
    inner = jnp.mean(scaled * normalized, axis=-1, keepdims=True)
    outer = jnp.mean(scaled, axis=-1, keepdims=True)
    return inv_std * (scaled - outer - normalized * inner)


def swap_halves(values):
    lane = lax.broadcasted_iota(jnp.int32, values.shape, 1)
    width = values.shape[1]
    half = HD // 2
    return jnp.where(
        (lane & half) == 0, pltpu.roll(values, width - half, 1), pltpu.roll(values, half, 1)
    )


def rotate_pair(values, cosine, sine, direction):
    return values * cosine + swap_halves(values) * (direction * sine)


def rotate_all(values, cosine, sine, direction):
    return jnp.concatenate(
        [
            rotate_pair(values[:, 128 * p : 128 * (p + 1)], cosine, sine, direction)
            for p in range(values.shape[1] // 128)
        ],
        axis=1,
    )


def prepare_kernel(plan, meta, tokens, cotangent, w_out, w_in, w_down, *refs):
    rows = plan.rows
    for j in range(rows):
        row = meta[plan.at_pick + j]
        refs[j][0] = tokens[row]
        refs[j][1] = cotangent[row]
    if plan.aligned:
        refs[rows][...] = pack_rest(plan, w_out[...], w_in[...], w_down[...])


def prepare(plan, meta, tokens, cotangent, w_out, w_in, w_down):
    rows = plan.rows
    shapes = [shape_of((2, plan.tok, D), BF16)] * rows
    if plan.aligned:
        shapes.append(shape_of((3 * plan.r, 2 * plan.cw), BF16))
    results = pl.pallas_call(
        functools.partial(prepare_kernel, plan),
        in_specs=[SMEM] + [VMEM] * 5,
        out_specs=[VMEM] * len(shapes),
        out_shape=shapes,
        compiler_params=params(plan, "prepare"),
        cost_estimate=cost(COSTS["prepare"]),
        name="prepare",
    )(meta, tokens, cotangent, w_out, w_in, w_down)
    packed = results[rows] if plan.aligned else pack_rest(plan, w_out, w_in, w_down)
    return results[:rows], packed


def place_kernel(plan, meta, *refs):
    pieces, (out, grad) = refs[: plan.rows], refs[plan.rows :]
    for j in range(plan.rows):
        row = meta[plan.at_pick + j]
        out[row] = pieces[j][0]
        grad[row] = pieces[j][1]


def place(plan, meta, pieces):
    return pl.pallas_call(
        functools.partial(place_kernel, plan),
        in_specs=[SMEM] + [VMEM] * plan.rows,
        out_specs=[VMEM] * 2,
        out_shape=[shape_of((plan.rows, plan.tok, D), BF16)] * 2,
        compiler_params=params(plan, "place_rows"),
        cost_estimate=cost(COSTS["place_rows"]),
        name="place_rows",
    )(meta, *pieces)


def ordered(plan, meta, pieces):
    stacked = jnp.stack(pieces)
    return [
        lax.dynamic_index_in_dim(stacked, meta[plan.at_z + z], 0, keepdims=False)
        for z in range(plan.nrow)
    ]


def join_qkv_kernel(plan, meta, gains, *refs):
    pieces, out, held = refs[: plan.nrow], refs[plan.nrow], refs[plan.nrow + 1]
    width = 3 * plan.cw
    for j in range(plan.nrow):
        held[j] = pieces[j][...]
    for z in range(plan.nrow):
        out[:, width * z : width * (z + 1)] = held[meta[plan.at_z + z]]
    out[:, 3 * D :] = gains[...]


def join_qkv(plan, meta, gains, pieces):
    if not plan.aligned:
        return jnp.concatenate(ordered(plan, meta, pieces) + [gains], axis=1)
    return pl.pallas_call(
        functools.partial(join_qkv_kernel, plan),
        in_specs=[SMEM] + [VMEM] * (1 + plan.nrow),
        out_specs=VMEM,
        out_shape=shape_of((plan.r, EXT), BF16),
        scratch_shapes=[pltpu.VMEM((plan.nrow, plan.r, 3 * plan.cw), BF16)],
        compiler_params=params(plan, "join_qkv"),
        cost_estimate=cost(COSTS["join_qkv"]),
        name="join_qkv",
    )(meta, gains, *pieces)


def pack_rest(plan, w_out, w_in, w_down, blank=None):
    cw = plan.cw
    left = jnp.concatenate([w_in[:, :cw], w_in[:, cw : 2 * cw], w_out], axis=0)
    if blank is None:
        blank = jnp.zeros((2 * plan.r - plan.rf, cw), BF16)
    right = jnp.concatenate([w_in[:, 2 * cw :], w_down, blank], axis=0)
    return jnp.concatenate([left, right], axis=1)


def unpack_rest(plan, piece):
    r, rf, cw = plan.r, plan.rf, plan.cw
    parts_in = [piece[:r, :cw], piece[r : 2 * r, :cw], piece[:r, cw:]]
    return parts_in, piece[2 * r : 3 * r, :cw], piece[r : r + rf, cw:]


def join_rest_kernel(plan, meta, *refs):
    pieces, out, held = refs[: plan.nrow], refs[plan.nrow], refs[plan.nrow + 1]
    r, cw = plan.r, plan.cw
    for j in range(plan.nrow):
        held[j] = pieces[j][...]
    for z in range(plan.nrow):
        parts_in, part_out, part_down = unpack_rest(plan, held[meta[plan.at_z + z]])
        out[:r, cw * z : cw * (z + 1)] = part_out
        for i in range(3):
            block, place_at = (3 * z + i) // plan.nrow, (3 * z + i) % plan.nrow
            out[r * (1 + block) : r * (2 + block), cw * place_at : cw * (place_at + 1)] = parts_in[i]
        out[4 * r :, cw * z : cw * (z + 1)] = part_down


def join_rest(plan, meta, pieces):
    if not plan.aligned:
        parts = [unpack_rest(plan, piece) for piece in ordered(plan, meta, pieces)]
        w_in = jnp.concatenate([part for item in parts for part in item[0]], axis=1)
        blocks = [jnp.concatenate([item[1] for item in parts], axis=1)]
        blocks += [w_in[:, D * t : D * (t + 1)] for t in range(3)]
        blocks += [jnp.concatenate([item[2] for item in parts], axis=1)]
        return jnp.concatenate(blocks, axis=0)
    return pl.pallas_call(
        functools.partial(join_rest_kernel, plan),
        in_specs=[SMEM] + [VMEM] * plan.nrow,
        out_specs=VMEM,
        out_shape=shape_of((plan.packed, D), BF16),
        scratch_shapes=[pltpu.VMEM((plan.nrow, 3 * plan.r, 2 * plan.cw), BF16)],
        compiler_params=params(plan, "join_rest"),
        cost_estimate=cost(COSTS["join_rest"]),
        name="join_rest",
    )(meta, *pieces)


def by_block(plan, meta, own, other):
    stacked = jnp.stack(own + other)
    places = meta[plan.at_own : plan.at_other + plan.chips]
    return jnp.zeros_like(stacked).at[places].set(stacked)


def split_blocks(plan, meta, blocks):
    half = plan.chips // 2
    return [
        jnp.take(blocks, meta[plan.at_own + half * i : plan.at_own + half * (i + 1)], axis=0)
        for i in range(4)
    ]


def qkv_sources(plan, meta, own, other):
    if plan.aligned:
        return own + other
    return [by_block(plan, meta, own, other).reshape(D, EXT)]


def rest_sources(plan, meta, own, other):
    if plan.aligned:
        return own + other
    blocks = by_block(plan, meta, own, other)
    r = plan.r
    parts = [blocks[:, r * i : r * (i + 1)].reshape(D, D) for i in range(4)]
    parts.append(blocks[:, 4 * r :].reshape(FF, D))
    return [jnp.concatenate(parts, axis=0)]


def block_size(plan):
    return (plan.r, plan.rf) if plan.aligned else (D, FF)


def block_of(plan, meta, index):
    return meta[plan.at_own + index] if plan.aligned else 0


def rows_at(index, size):
    if isinstance(index, int):
        return pl.ds(index * size, size)
    return pl.ds(pl.multiple_of(index * size, size), size)


class Mover:
    def __init__(self, sems):
        self.sems = sems
        self.used = 0
        self.open = []

    def start(self, source, target):
        copy = pltpu.make_async_copy(source, target, self.sems.at[self.used])
        self.used += 1
        copy.start()
        return copy

    def send(self, source, target):
        self.open.append(self.start(source, target))

    def finish(self):
        for copy in self.open:
            copy.wait()


def wait_all(copies):
    for copy in copies:
        copy.wait()


def qkv_copies(plan, meta, sources, w_ref, sems):
    r, _ = block_size(plan)
    return [
        pltpu.make_async_copy(source, w_ref.at[rows_at(block_of(plan, meta, i), r)], sems.at[i])
        for i, source in enumerate(sources)
    ]


def grad_target(plan, grads, index):
    if not plan.aligned:
        return grads[0]
    half = plan.chips // 2
    return grads[index // half].at[index % half]


def grad_blocks(plan, height, width):
    return [shape_of((plan.chips // 2, height, width), BF16)] * 4


def source_count(plan):
    return 2 * plan.chips if plan.aligned else 1


def qkv_kernel(plan, meta, cos_ref, sin_ref, *refs):
    x_refs = refs[: plan.rows]
    count = source_count(plan)
    sources = refs[plan.rows : plan.rows + count]
    q_ref = refs[plan.rows + count]
    kv_refs = refs[plan.rows + count + 1 : plan.rows + count + 1 + HALVES]
    n_ref, gain_ref, w_ref, sems = refs[plan.rows + count + 1 + HALVES :]
    copies = qkv_copies(plan, meta, sources, w_ref, sems)
    for copy in copies:
        copy.start()
    units = [layer_norm(x_refs[j][0].astype(F32))[0] for j in range(plan.rows)]
    for copy in copies:
        copy.wait()
    gain_ref[...] = w_ref[:, 3 * D :].astype(F32).T[:8, :]
    for j in range(plan.rows):
        n_ref[plan.tok * j : plan.tok * (j + 1), :] = (units[j] * gain_ref[0:1, :]).astype(BF16)
    cosine, sine = cos_ref[...], sin_ref[...]
    normed = n_ref[...]
    queries = dot(normed, w_ref[:, :D], NN)
    q_ref[...] = rotate_all(queries, cosine, sine, 1.0).astype(BF16)
    keys = rotate_all(dot(normed, w_ref[:, D : 2 * D], NN), cosine, sine, 1.0).astype(BF16)
    values = dot(normed, w_ref[:, 2 * D : 3 * D], NN).astype(BF16)
    for h in range(HALVES):
        kv_refs[h][0] = keys[:, HALF * h : HALF * (h + 1)]
        kv_refs[h][1] = values[:, HALF * h : HALF * (h + 1)]


def project(plan, meta, cosine, sine, pieces, sources):
    local = plan.local
    count = len(sources)
    inputs = [meta, cosine, sine, *pieces, *sources]
    return pl.pallas_call(
        functools.partial(qkv_kernel, plan),
        in_specs=[SMEM, VMEM, VMEM] + [VMEM] * plan.rows + [ANY] * count,
        out_specs=[VMEM] * (3 + HALVES),
        out_shape=[shape_of((local, D), BF16)]
        + [shape_of((2, local, HALF), BF16)] * HALVES
        + [shape_of((local, D), BF16), shape_of((8, D), F32)],
        scratch_shapes=[pltpu.VMEM((D, EXT), BF16), pltpu.SemaphoreType.DMA((count,))],
        compiler_params=params(plan, "project"),
        cost_estimate=cost(COSTS["project"]),
        name="project",
    )(*inputs)


def fill_docs(plan, meta, lengths, kmask, qmask):
    low = meta[plan.at_lo]
    ends = []
    passed = jnp.int32(0)
    for n in range(NDOC):
        passed = passed + lengths[low, n]
        ends.append(passed)

    tok = plan.tok
    lane = lax.broadcasted_iota(jnp.int32, (tok, 128), 1) & (HD - 1)
    for i in range(plan.groups * plan.rows):
        places = meta[plan.at_base + i] + lax.broadcasted_iota(jnp.int32, (tok, 128), 0)
        docs = jnp.zeros((tok, 128), jnp.int32)
        for end in ends:
            docs = docs + (places >= end).astype(jnp.int32)
        part = slice(i * tok, (i + 1) * tok)
        same = docs == lane
        kmask[part, :] = jnp.where((lane < NDOC) & ~same, MASKED, 0.0).astype(BF16)
        if i < plan.rows:
            qmask[part, :] = jnp.where(same, 1.0, 0.0).astype(BF16)


def masks(plan, meta, lengths):
    keys = plan.groups * plan.local
    return pl.pallas_call(
        functools.partial(fill_docs, plan),
        in_specs=[SMEM, SMEM],
        out_specs=[VMEM, VMEM],
        out_shape=[shape_of((keys, 128), BF16), shape_of((plan.local, 128), BF16)],
        compiler_params=params(plan, "masks"),
        cost_estimate=cost(1),
        name="masks",
    )(meta, lengths)


def head_part(pair, head, other=None):
    keep = (lax.broadcasted_iota(jnp.int32, pair.shape, 1) // HD) == head
    return jnp.where(keep, pair, jnp.zeros_like(pair) if other is None else other)


def attend_kernel(plan, width, order, kmask, qmask, q_ref, *refs):
    groups, local = plan.groups, plan.local
    kv = refs[:groups]
    o_ref, low_ref, lse_ref, s_ref, p_ref = refs[groups:]
    total_keys = groups * local
    chunk = 128
    values_t = []
    row = lax.broadcasted_iota(jnp.int32, (HD + 8, total_keys), 0)
    pair_t = jnp.concatenate([kv[e][1].T for e in range(groups)], axis=1)
    for h in range(2):
        head = pair_t[h * HD : (h + 1) * HD, :]
        values_t.append(jnp.concatenate([head, jnp.ones((8, total_keys), BF16)], axis=0))
    for first in range(0, local, width):
        rows = slice(first, first + width)
        queries = q_ref[rows, :] * jnp.asarray(1.0 / math.sqrt(HD), BF16)
        tops = []
        for h in range(2):
            head_queries = head_part(queries, h, qmask[rows, :])
            top = jnp.full((8, width), MASKED, F32)
            for e in range(groups):
                for c in range(0, local, 2 * chunk):
                    part = slice(e * local + c, e * local + c + 2 * chunk)
                    keys = head_part(kv[e][0, c : c + 2 * chunk, :], h, kmask[part, :])
                    scores = dot(keys, head_queries, NT)
                    s_ref[h, part, :] = scores
                    top = jnp.maximum(top, jnp.max(scores.reshape(-1, 8, width), axis=0))
            tops.append(jnp.max(top, axis=0, keepdims=True))
        parts = []
        for h in range(2):
            for c in range(0, total_keys, chunk):
                part = slice(c, c + chunk)
                p_ref[h, part, :] = jnp.exp(s_ref[h, part, :] - tops[h]).astype(BF16)
            weighted = dot(values_t[h], p_ref[h], NN)
            total = weighted[HD : HD + 1, :]
            parts.append(weighted[:HD, :] / total)
            lse_ref[0, h : h + 1, rows] = tops[h] + jnp.log(total)
        heads = jnp.concatenate(parts, axis=0).T
        o_ref[rows, :] = heads
        low_ref[rows, :] = heads.astype(BF16)


def attend(plan, part, meta, mask, queries, kv):
    local, groups = plan.local, plan.groups
    width = min(512, local)
    skip = part * HALF_PAIRS
    pair = pl.BlockSpec((local, 128), lambda p: (0, p))
    pair_q = pl.BlockSpec((local, 128), lambda p: (0, p + skip))
    pair_kv = pl.BlockSpec((2, local, 128), lambda p: (0, 0, p))
    whole_k = pl.BlockSpec((groups * local, 128), lambda p: (0, 0))
    whole_q = pl.BlockSpec((local, 128), lambda p: (0, 0))
    inputs = [meta, *mask, queries, *kv]
    return pl.pallas_call(
        functools.partial(attend_kernel, plan, width),
        grid=(HALF_PAIRS,),
        in_specs=[SMEM, whole_k, whole_q, pair_q] + [pair_kv] * groups,
        out_specs=[pair, pair, pl.BlockSpec((1, 2, local), lambda p: (p, 0, 0))],
        out_shape=[
            shape_of((local, HALF), F32),
            shape_of((local, HALF), BF16),
            shape_of((HALF_PAIRS, 2, local), F32),
        ],
        scratch_shapes=[
            pltpu.VMEM((2, groups * local, width), F32),
            pltpu.VMEM((2, groups * local, width), BF16),
        ],
        compiler_params=params(plan, "attend"),
        cost_estimate=cost(COSTS["attend"]),
        name="attend",
    )(*inputs)


def attend_back_kernel(
    plan, width, order, kmask, qmask, q_ref, do_ref, o_ref, lse_ref, cos_ref, sin_ref, *refs
):
    groups, local = plan.groups, plan.local
    kv = refs[:groups]
    dq_ref = refs[groups]
    dkv = refs[groups + 1 : 2 * groups + 1]
    held, p_ref, ds_ref, keys_t, product, grad_t = refs[2 * groups + 1 :]
    for e in range(groups):
        keys_t[e] = kv[e][0].T
    held[...] = jnp.zeros_like(held)
    scale = 1.0 / math.sqrt(HD)
    chunk = 128
    for first in range(0, local, width):
        rows = slice(first, first + width)
        product[...] = (do_ref[rows, :].astype(F32) * o_ref[rows, :]).T

        @pl.loop(0, 2)
        def _(h):
            head = pl.ds(pl.multiple_of(h * HD, HD), HD)
            queries = q_ref[rows, :] * jnp.asarray(scale, BF16)
            masked_queries = head_part(queries, h, qmask[rows, :])
            head_queries = head_part(queries, h)
            head_dout = head_part(do_ref[rows, :], h)
            lse = lse_ref[0, pl.ds(h, 1), rows]
            delta = jnp.sum(product[head, :], axis=0, keepdims=True)
            grad_queries = jnp.zeros((HD, width), F32)
            for e in range(groups):
                for c in range(0, local, chunk):
                    part = slice(c, c + chunk)
                    mask = kmask[e * local + c : e * local + c + chunk, :]
                    scores = dot(head_part(kv[e][0, part, :], h, mask), masked_queries, NT)
                    dprobs = dot(kv[e][1, part, :], head_dout, NT)
                    probs = jnp.exp(scores - lse)
                    p_ref[e, part, :] = probs.astype(BF16)
                    ds_ref[e, part, :] = (probs * (dprobs - delta)).astype(BF16)
                held[e, 0] += dot(ds_ref[e], head_queries, NN)
                held[e, 1] += dot(p_ref[e], head_dout, NN)
                grad_queries = grad_queries + dot(keys_t[e, head, :], ds_ref[e], NN)
            grad_t[head, :] = grad_queries

        grad = grad_t[...].T * scale
        dq_ref[rows, :] = rotate_pair(grad, cos_ref[rows, :], sin_ref[rows, :], -1.0).astype(BF16)
    for e in range(groups):
        dkv[e][...] = held[e].astype(BF16)


def attend_back(plan, part, meta, mask, queries, dout, heads, lse, cosine, sine, kv):
    local, groups = plan.local, plan.groups
    width = min(512, local)
    half, first, count = part
    skip = half * HALF_PAIRS + first
    wide = 128 * count
    pair = pl.BlockSpec((local, 128), lambda p: (0, p))
    pair_h = pl.BlockSpec((local, 128), lambda p: (0, p + first))
    pair_q = pl.BlockSpec((local, 128), lambda p: (0, p + skip))
    whole_k = pl.BlockSpec((groups * local, 128), lambda p: (0, 0))
    inputs = [meta, *mask, queries, dout, heads, lse, cosine, sine, *kv]
    table = pl.BlockSpec((local, 128), lambda p: (0, 0))
    pair_kv = pl.BlockSpec((2, local, 128), lambda p: (0, 0, p))
    pair_kv_h = pl.BlockSpec((2, local, 128), lambda p: (0, 0, p + first))
    return pl.pallas_call(
        functools.partial(attend_back_kernel, plan, width),
        grid=(count,),
        in_specs=[
            SMEM,
            whole_k,
            table,
            pair_q,
            pair_q,
            pair_h,
            pl.BlockSpec((1, 2, local), lambda p: (p + first, 0, 0)),
            table,
            table,
        ]
        + [pair_kv_h] * groups,
        out_specs=[pair] + [pair_kv] * groups,
        out_shape=[shape_of((local, wide), BF16)] + [shape_of((2, local, wide), BF16)] * groups,
        scratch_shapes=[
            pltpu.VMEM((groups, 2, local, 128), F32),
            pltpu.VMEM((groups, local, width), BF16),
            pltpu.VMEM((groups, local, width), BF16),
            pltpu.VMEM((groups, 128, local), BF16),
            pltpu.VMEM((128, width), F32),
            pltpu.VMEM((128, width), F32),
        ],
        compiler_params=params(plan, "attend_back"),
        cost_estimate=cost(4 * count),
        name="attend_back",
    )(*inputs)


def middle_kernel(plan, meta, gain_ref, *refs):
    rows, tok, local = plan.rows, plan.tok, plan.local
    count = source_count(plan)
    low_refs, refs = refs[:HALVES], refs[HALVES:]
    x_refs, refs = refs[:rows], refs[rows:]
    sources, refs = refs[:count], refs[count:]
    out_refs, refs = refs[:rows], refs[rows:]
    do_out, dh_out, refs = refs[0], refs[1], refs[2:]
    grads, refs = refs[: 4 if plan.aligned else 1], refs[4 if plan.aligned else 1 :]
    low_ref, x_ref, dy_ref, w_out, w_in, w_down, h_ref, unit_ref, n_ref, gu_ref = refs[:10]
    mid_ref, dgu_ref, out_ref, do_ref, dh_ref, da_ref, inv_ref, g_out, g_in, g_down, sems = refs[10:]
    mover = Mover(sems)
    r, rf = block_size(plan)
    blocks = [block_of(plan, meta, i) for i in range(count)]
    low_in = [
        mover.start(low_refs[h], low_ref.at[:, pl.ds(HALF * h, HALF)]) for h in range(HALVES)
    ]
    out_in = [
        mover.start(source.at[pl.ds(0, r)], w_out.at[rows_at(block, r)])
        for source, block in zip(sources, blocks)
    ]
    x_in = [mover.start(x_refs[j].at[0], x_ref.at[pl.ds(tok * j, tok)]) for j in range(rows)]

    def fetch_in(t):
        return [
            mover.start(source.at[pl.ds((1 + t) * r, r)], w_in.at[t, rows_at(block, r)])
            for source, block in zip(sources, blocks)
        ]

    in_in = [fetch_in(t) for t in range(3)]
    dy_in = [mover.start(x_refs[j].at[1], dy_ref.at[pl.ds(tok * j, tok)]) for j in range(rows)]
    down_in = [
        mover.start(source.at[pl.ds(4 * r, rf)], w_down.at[rows_at(block, rf)])
        for source, block in zip(sources, blocks)
    ]
    wait_all(low_in)
    wait_all(out_in)
    wait_all(x_in)
    gain = gain_ref[1:2, :]

    h_ref[...] = x_ref[...].astype(F32) + dot(low_ref[...], w_out[...], NN)
    unit, inv_std = layer_norm(h_ref[...])
    unit_ref[...] = unit
    inv_ref[...] = jnp.broadcast_to(inv_std, (local, 128))
    n_ref[...] = (unit * gain).astype(BF16)

    for t in range(3):
        wait_all(in_in[t])

    @pl.loop(0, 3)
    def _(t):
        gu_ref[:, pl.ds(pl.multiple_of(t * D, D), D)] = dot(n_ref[...], w_in[t], NN)

    wait_all(dy_in)
    wait_all(down_in)
    size = FF // 3

    @pl.loop(0, 3)
    def _(f):
        cols = pl.ds(pl.multiple_of(f * size, size), size)
        up_cols = pl.ds(pl.multiple_of(FF + f * size, size), size)
        gate = gu_ref[:, cols]
        up = gu_ref[:, up_cols]
        below = 0.5 + 0.5 * lax.erf(gate * math.sqrt(0.5))
        active = gate * below
        mid_ref[:, cols] = (active * up).astype(BF16)
        slope = below + gate * jnp.exp(-0.5 * gate * gate) * (1.0 / math.sqrt(2.0 * math.pi))
        dmid = dot(dy_ref[...], w_down[cols, :], NT)
        dgu_ref[:, cols] = (dmid * up * slope).astype(BF16)
        dgu_ref[:, up_cols] = (dmid * active).astype(BF16)
        g_down[cols, :] = dot(mid_ref[:, cols], dy_ref[...], TN).astype(BF16)

    targets = [grad_target(plan, grads, i) for i in range(count)]
    for target, block in zip(targets, blocks):
        mover.send(g_down.at[rows_at(block, rf)], target.at[pl.ds(4 * r, rf)])
    step = D // 3

    @pl.loop(0, 3)
    def _(n):
        cols = pl.ds(pl.multiple_of(n * step, step), step)
        mixed = dot(mid_ref[...], w_down[:, cols], NN)
        out_ref[:, cols] = (h_ref[:, cols] + mixed).astype(BF16)
        grad = dot(dgu_ref[:, :D], w_in[0, cols, :], NT)
        for t in range(1, 3):
            grad = grad + dot(dgu_ref[:, D * t : D * (t + 1)], w_in[t, cols, :], NT)
        dh_ref[:, cols] = grad
    for j in range(rows):
        mover.send(out_ref.at[pl.ds(tok * j, tok)], out_refs[j])

    @pl.loop(0, 3)
    def _(t):
        g_in[t] = dot(
            n_ref[...], dgu_ref[:, pl.ds(pl.multiple_of(t * D, D), D)], TN
        ).astype(BF16)

    for t in range(3):
        for target, block in zip(targets, blocks):
            mover.send(g_in.at[t, rows_at(block, r)], target.at[pl.ds((1 + t) * r, r)])

    grad_hidden = dy_ref[...].astype(F32) + norm_backward(
        dh_ref[...], unit_ref[...], inv_ref[:, 0:1], gain
    )
    dh_ref[...] = grad_hidden
    da_ref[...] = grad_hidden.astype(BF16)
    mover.send(dh_ref, dh_out)
    do_ref[...] = dot(da_ref[...], w_out[...], NT).astype(BF16)
    g_out[...] = dot(low_ref[...], da_ref[...], TN).astype(BF16)

    mover.send(do_ref, do_out)
    for target, block in zip(targets, blocks):
        mover.send(g_out.at[rows_at(block, r)], target.at[pl.ds(0, r)])
    mover.finish()


def middle(plan, meta, low, gains, pieces, sources):
    local, rows, tok = plan.local, plan.rows, plan.tok
    count = len(sources)
    total = 4 * D + FF
    if plan.aligned:
        grads = grad_blocks(plan, plan.packed, D)
    else:
        grads = [shape_of((total, D), BF16)]
    return pl.pallas_call(
        functools.partial(middle_kernel, plan),
        in_specs=[SMEM, VMEM] + [ANY] * (HALVES + rows + count),
        out_specs=[ANY] * (rows + 2 + len(grads)),
        out_shape=[shape_of((tok, D), BF16)] * rows
        + [shape_of((local, D), BF16), shape_of((local, D), F32)]
        + grads,
        scratch_shapes=[
            pltpu.VMEM((local, D), BF16),
            pltpu.VMEM((local, D), BF16),
            pltpu.VMEM((local, D), BF16),
            pltpu.VMEM((D, D), BF16),
            pltpu.VMEM((3, D, D), BF16),
            pltpu.VMEM((FF, D), BF16),
            pltpu.VMEM((local, D), F32),
            pltpu.VMEM((local, D), F32),
            pltpu.VMEM((local, D), BF16),
            pltpu.VMEM((local, 2 * FF), F32),
            pltpu.VMEM((local, FF), BF16),
            pltpu.VMEM((local, 2 * FF), BF16),
            pltpu.VMEM((local, D), BF16),
            pltpu.VMEM((local, D), BF16),
            pltpu.VMEM((local, D), F32),
            pltpu.VMEM((local, D), BF16),
            pltpu.VMEM((local, 128), F32),
            pltpu.VMEM((D, D), BF16),
            pltpu.VMEM((3, D, D), BF16),
            pltpu.VMEM((FF, D), BF16),
            pltpu.SemaphoreType.DMA((HALVES + 3 * rows + 2 + 10 * count,)),
        ],
        compiler_params=params(plan, "middle"),
        cost_estimate=cost(COSTS["middle"]),
        name="middle",
    )(meta, gains, *low, *pieces, *sources)


def back_weight_kernel(plan, meta, *refs):
    groups, local = plan.groups, plan.local
    count = len(BACK_PARTS)
    cos_ref, sin_ref, n_in, refs = refs[0], refs[1], refs[2], refs[3:]
    dq_refs, refs = refs[:count], refs[count:]
    dkv, refs = refs[: count * groups], refs[count * groups :]
    dp_out, refs = refs[0], refs[1:]
    grads, refs = refs[: 4 if plan.aligned else 1], refs[4 if plan.aligned else 1 :]
    cos, sin, n_ref, dkv_ref, dp_ref, g_ref, sems = refs
    mover = Mover(sems)
    columns = []
    for half, first, pairs in BACK_PARTS:
        columns.append(pl.ds(HALF * half + 128 * first, 128 * pairs))
    first_in = [mover.start(n_in, n_ref)]
    for i in range(count):
        first_in.append(mover.start(dq_refs[i], dp_ref.at[0, :, columns[i]]))
    rest_in = [mover.start(cos_ref, cos), mover.start(sin_ref, sin)]
    for i in range(count):
        for e in range(groups):
            rest_in.append(
                mover.start(dkv[groups * i + e], dkv_ref.at[e, :, :, columns[i]])
            )
    r, _ = block_size(plan)

    def send_grad(t):
        cols = pl.ds(D * t, D)
        for i in range(source_count(plan)):
            at = rows_at(block_of(plan, meta, i), r)
            mover.send(g_ref.at[at, cols], grad_target(plan, grads, i).at[:, cols])

    wait_all(first_in)
    normed = n_ref[...]
    g_ref[:, :D] = dot(normed, dp_ref[0], TN).astype(BF16)
    send_grad(0)
    wait_all(rest_in)
    dp_ref[2] = sum_pieces([dkv_ref[e, 1] for e in range(groups)]).astype(BF16)
    g_ref[:, 2 * D : 3 * D] = dot(normed, dp_ref[2], TN).astype(BF16)
    send_grad(2)
    grad_keys = sum_pieces([dkv_ref[e, 0] for e in range(groups)])
    dp_ref[1] = rotate_all(grad_keys, cos[...], sin[...], -1.0).astype(BF16)
    mover.send(dp_ref, dp_out)
    g_ref[:, D : 2 * D] = dot(normed, dp_ref[1], TN).astype(BF16)
    send_grad(1)
    mover.finish()


def back_weight(plan, meta, cosine, sine, normed, dq, dkv):
    local, groups, count = plan.local, plan.groups, len(BACK_PARTS)
    if plan.aligned:
        grads = grad_blocks(plan, plan.r, 3 * D)
    else:
        grads = [shape_of((D, 3 * D), BF16)]
    results = pl.pallas_call(
        functools.partial(back_weight_kernel, plan),
        in_specs=[SMEM] + [ANY] * (3 + count * (1 + groups)),
        out_specs=[ANY] * (1 + len(grads)),
        out_shape=[shape_of((3, local, D), BF16)] + grads,
        scratch_shapes=[
            pltpu.VMEM((local, 128), F32),
            pltpu.VMEM((local, 128), F32),
            pltpu.VMEM((local, D), BF16),
            pltpu.VMEM((groups, 2, local, D), BF16),
            pltpu.VMEM((3, local, D), BF16),
            pltpu.VMEM((D, 3 * D), BF16),
            pltpu.SemaphoreType.DMA((4 + count * (1 + groups) + 3 * source_count(plan),)),
        ],
        compiler_params=params(plan, "back_weight"),
        cost_estimate=cost(COSTS["back_weight"]),
        name="back_weight",
    )(meta, cosine, sine, normed, *dq, *dkv)
    return results[0], results[1:]


def back_in_kernel(plan, meta, dp_ref, dh_ref, gain_ref, *refs):
    rows, tok = plan.rows, plan.tok
    count = source_count(plan)
    x_refs, refs = refs[:rows], refs[rows:]
    out_refs, refs = refs[:rows], refs[rows:]
    sources, refs = refs[:count], refs[count:]
    both_refs = refs[:rows]
    w_ref, in_sems = refs[rows:]
    copies = qkv_copies(plan, meta, sources, w_ref, in_sems)
    for copy in copies:
        copy.start()
    for copy in copies:
        copy.wait()
    grad_normed = dot(dp_ref[0], w_ref[:, :D], NT)
    for t in range(1, 3):
        grad_normed = grad_normed + dot(dp_ref[t], w_ref[:, D * t : D * (t + 1)], NT)
    for j in range(rows):
        part = slice(tok * j, tok * (j + 1))
        unit, inv_std = layer_norm(x_refs[j][0].astype(F32))
        grad = grad_normed[part, :]
        back = norm_backward(grad, unit, inv_std, gain_ref[0:1, :])
        both_refs[j][0] = out_refs[j][...]
        both_refs[j][1] = (dh_ref[part, :] + back).astype(BF16)


def back_in(plan, meta, dprojected, dhidden, gains, pieces, outs, sources):
    rows, tok = plan.rows, plan.tok
    count = len(sources)
    return pl.pallas_call(
        functools.partial(back_in_kernel, plan),
        in_specs=[SMEM] + [VMEM] * (3 + 2 * rows) + [ANY] * count,
        out_specs=[VMEM] * rows,
        out_shape=[shape_of((2, tok, D), BF16)] * rows,
        scratch_shapes=[pltpu.VMEM((D, EXT), BF16), pltpu.SemaphoreType.DMA((count,))],
        compiler_params=params(plan, "back_in"),
        cost_estimate=cost(COSTS["back_in"]),
        name="back_in",
    )(meta, dprojected, dhidden, gains, *pieces, *outs, *sources)


def gain_columns(weight, grad):
    total = jnp.sum(weight.astype(F32) * grad.astype(F32), axis=1, keepdims=True)
    high = total.astype(BF16)
    return high, (total - high.astype(F32)).astype(BF16)


def pad_width(plan):
    return -(-(3 * plan.cw + 2) // 128) * 128


def gain_tail(plan, weight, grad):
    width = pad_width(plan) - 3 * plan.cw
    high, rest = gain_columns(weight, grad)
    lane = lax.broadcasted_iota(jnp.int32, (plan.r, width), 1)
    return jnp.where(lane == 0, high, jnp.where(lane == 1, rest, jnp.zeros_like(high)))


def cut_qkv_kernel(plan, meta, total, weight, *refs):
    outs, held = refs[: plan.nrow], refs[plan.nrow]
    width = 3 * plan.cw
    tail = gain_tail(plan, weight[:, : 3 * D], total[...])
    for z in range(plan.nrow):
        place_at = meta[plan.at_z + z]
        held[place_at, :, :width] = total[:, width * z : width * (z + 1)]
        held[place_at, :, width:] = tail
    for j in range(plan.nrow):
        outs[j][...] = held[j]


def cut_qkv(plan, meta, total, weight):
    width, wide = 3 * plan.cw, pad_width(plan)
    if not plan.aligned:
        tail = gain_tail(plan, weight[:, : 3 * D], total)
        parts = [
            jnp.concatenate([total[:, width * z : width * (z + 1)], tail], axis=1)
            for z in range(plan.nrow)
        ]
        return ordered(plan, meta, parts)
    return pl.pallas_call(
        functools.partial(cut_qkv_kernel, plan),
        in_specs=[SMEM, VMEM, VMEM],
        out_specs=[VMEM] * plan.nrow,
        out_shape=[shape_of((plan.r, wide), BF16)] * plan.nrow,
        scratch_shapes=[pltpu.VMEM((plan.nrow, plan.r, wide), BF16)],
        compiler_params=params(plan, "cut_qkv"),
        cost_estimate=cost(COSTS["cut_qkv"]),
        name="cut_qkv",
    )(meta, total, weight)


def gain_blank(plan, weight, grad):
    r, blank = plan.r, 2 * plan.r - plan.rf
    cols = [weight[r * t : r * (t + 1)] for t in range(1, 4)]
    grads = [grad[r * t : r * (t + 1)] for t in range(1, 4)]
    high, rest = gain_columns(jnp.concatenate(cols, axis=1), jnp.concatenate(grads, axis=1))
    lane = lax.broadcasted_iota(jnp.int32, (blank, plan.cw), 1)
    found = jnp.zeros((blank, plan.cw), BF16)
    for i in range(r // blank):
        part = slice(blank * i, blank * (i + 1))
        found = jnp.where(lane == 2 * i, high[part], found)
        found = jnp.where(lane == 2 * i + 1, rest[part], found)
    return found


def cut_rest_kernel(plan, meta, total, weight, *refs):
    outs, held = refs[: plan.nrow], refs[plan.nrow]
    r, rf, cw = plan.r, plan.rf, plan.cw
    blank = gain_blank(plan, weight[...], total[...])
    for z in range(plan.nrow):
        place_at = meta[plan.at_z + z]
        cols = slice(cw * z, cw * (z + 1))
        parts = []
        for i in range(3):
            block, at = (3 * z + i) // plan.nrow, (3 * z + i) % plan.nrow
            parts.append(total[r * (1 + block) : r * (2 + block), cw * at : cw * (at + 1)])
        held[place_at, :r, :] = jnp.concatenate([parts[0], parts[2]], axis=1)
        held[place_at, r : 2 * r, :] = jnp.concatenate(
            [parts[1], total[4 * r : 5 * r, cols]], axis=1
        )
        rest = total[5 * r : 4 * r + rf, cols]
        held[place_at, 2 * r :, :] = jnp.concatenate(
            [total[:r, cols], jnp.concatenate([rest, blank], axis=0)], axis=1
        )
    for j in range(plan.nrow):
        outs[j][...] = held[j]


def cut_rest(plan, meta, total, weight):
    r, cw = plan.r, plan.cw
    if not plan.aligned:
        grad_in = jnp.concatenate([total[r * (1 + t) : r * (2 + t)] for t in range(3)], axis=1)
        blank = gain_blank(plan, weight, total)
        parts = [
            pack_rest(
                plan,
                total[:r, cw * z : cw * (z + 1)],
                grad_in[:, 3 * cw * z : 3 * cw * (z + 1)],
                total[4 * r :, cw * z : cw * (z + 1)],
                blank,
            )
            for z in range(plan.nrow)
        ]
        return ordered(plan, meta, parts)
    return pl.pallas_call(
        functools.partial(cut_rest_kernel, plan),
        in_specs=[SMEM, VMEM, VMEM],
        out_specs=[VMEM] * plan.nrow,
        out_shape=[shape_of((3 * r, 2 * cw), BF16)] * plan.nrow,
        scratch_shapes=[pltpu.VMEM((plan.nrow, 3 * r, 2 * cw), BF16)],
        compiler_params=params(plan, "cut_rest"),
        cost_estimate=cost(COSTS["cut_rest"]),
        name="cut_rest",
    )(meta, total, weight)


def reduce_z(plan, pieces):
    return [pieces[0]] + [
        lax.ppermute(pieces[j], "row", plan.z_pairs(j)) for j in range(1, plan.nrow)
    ]


def sum_pieces(pieces):
    total = pieces[0].astype(F32)
    for piece in pieces[1:]:
        total = total + piece.astype(F32)
    return total


def end_rest_kernel(plan, *refs):
    pieces, (g_out, g_in, g_down, g_gain) = refs[: plan.nrow], refs[plan.nrow :]
    total = sum_pieces([piece[...] for piece in pieces])
    parts_in, part_out, part_down = unpack_rest(plan, total)
    g_out[...] = part_out
    g_in[...] = jnp.concatenate(parts_in, axis=1)
    g_down[...] = part_down
    blank = 2 * plan.r - plan.rf
    g_gain[...] = total[3 * plan.r - blank :, plan.cw : plan.cw + 128].T[:8, :]


def end_rest(plan, pieces):
    r, blank = plan.r, 2 * plan.r - plan.rf
    if not plan.aligned:
        total = sum_pieces(pieces)
        parts_in, out_grad, down_grad = unpack_rest(plan, total)
        in_grad = jnp.concatenate(parts_in, axis=1)
        gain = total[3 * r - blank :, plan.cw : plan.cw + 8].T
    else:
        out_grad, in_grad, down_grad, gain = pl.pallas_call(
            functools.partial(end_rest_kernel, plan),
            in_specs=[VMEM] * plan.nrow,
            out_specs=[VMEM] * 4,
            out_shape=[
                shape_of((r, plan.cw), F32),
                shape_of((r, 3 * plan.cw), F32),
                shape_of((plan.rf, plan.cw), F32),
                shape_of((8, blank), F32),
            ],
            compiler_params=params(plan, "end_rest"),
            cost_estimate=cost(COSTS["end_rest"]),
            name="end_rest",
        )(*pieces)
    gain = jnp.concatenate([gain[2 * i] + gain[2 * i + 1] for i in range(r // blank)])
    return out_grad, in_grad, down_grad, gain


def end_qkv_kernel(plan, gain_ref, *refs):
    pieces, (g_qkv, g_gain) = refs[: plan.nrow], refs[plan.nrow :]
    width, wide = 3 * plan.cw, pad_width(plan)
    total = sum_pieces([piece[...] for piece in pieces])
    g_qkv[...] = total[:, :width]
    tail = total[:, wide - 128 :].T
    at = width - (wide - 128)
    g_gain[...] = (tail[at : at + 1, :] + tail[at + 1 : at + 2, :]) / gain_ref[...]


def end_qkv(plan, gain, pieces):
    width, wide = 3 * plan.cw, pad_width(plan)
    if not plan.aligned:
        total = sum_pieces(pieces)
        return total[:, :width], (total[:, width] + total[:, width + 1]) / gain[0]
    grad, gain_grad = pl.pallas_call(
        functools.partial(end_qkv_kernel, plan),
        in_specs=[VMEM] * (1 + plan.nrow),
        out_specs=[VMEM] * 2,
        out_shape=[shape_of((plan.r, width), F32), shape_of((1, plan.r), F32)],
        compiler_params=params(plan, "end_qkv"),
        cost_estimate=cost(COSTS["end_qkv"]),
        name="end_qkv",
    )(gain, *pieces)
    return grad, gain_grad.reshape(plan.r)


def rotation_tables(plan, meta, lengths):
    ends = jnp.cumsum(lax.dynamic_index_in_dim(lengths, meta[plan.at_lo], 0, keepdims=False))
    starts = jnp.concatenate([jnp.zeros((1,), jnp.int32), ends[:-1]])
    bases = meta[plan.at_base : plan.at_base + plan.rows]
    places = (bases[:, None] + jnp.arange(plan.tok, dtype=jnp.int32)[None, :]).reshape(-1)
    passed = places[:, None] >= starts[None, :]
    positions = places - jnp.max(jnp.where(passed, starts[None, :], 0), axis=1)
    half = HD // 2
    inverse = ROPE_BASE ** (-(jnp.arange(half, dtype=F32) * (2.0 / HD)))
    angles = positions.astype(F32)[:, None] * inverse
    cosine, sine = jnp.cos(angles), jnp.sin(angles)
    return (
        jnp.concatenate([cosine] * 4, axis=1),
        jnp.concatenate([-sine, sine, -sine, sine], axis=1),
    )


def body(
    plan,
    tokens,
    lengths,
    norm_gain,
    qkv_weight,
    out_weight,
    mlp_gain,
    in_weight,
    down_weight,
    cotangent,
):
    blk, row = lax.axis_index("blk"), lax.axis_index("row")
    meta = lax.dynamic_slice(
        jnp.asarray(plan.table), (row, blk, 0), (1, 1, plan.size)
    ).reshape(plan.size)
    qkv_parts = gather_z(plan, qkv_weight)
    cut, packed = prepare(plan, meta, tokens, cotangent, out_weight, in_weight, down_weight)
    pieces = exchange_rows(plan, cut)
    rest_parts = gather_z(plan, packed, behind=qkv_parts)
    gains = jnp.pad(jnp.stack([norm_gain, mlp_gain], axis=1), ((0, 0), (0, 126)))
    cosine, sine = rotation_tables(plan, meta, lengths)
    mask = masks(plan, meta, lengths)
    qkv_joined = join_qkv(plan, meta, gains, qkv_parts)
    qkv_own = gather_start(plan, qkv_joined, pieces[1:])
    qkv_own[1] = tie(qkv_own[1], *rest_parts[2:], cosine, sine, *mask)
    qkv_own = gather_more(plan, qkv_own)
    qkv_own[-1] = tie(qkv_own[-1], rest_parts[1])
    qkv_other = [swap_cores(plan, piece) for piece in qkv_own]
    qkv_from = qkv_sources(plan, meta, qkv_own, qkv_other)
    rest_parts[0] = tie(rest_parts[0], qkv_joined, *qkv_other[:-1])
    joined = join_rest(plan, meta, rest_parts)
    results = project(plan, tie(meta, joined), cosine, sine, pieces, qkv_from)
    queries, kv, (normed, gains) = results[0], results[1 : 1 + HALVES], results[1 + HALVES :]
    kv = [
        [part]
        + [
            lax.ppermute(part, "blk", plan.xor_pairs(plan.member(e)))
            for e in range(1, plan.groups)
        ]
        for part in kv
    ]
    rest_own = gather_start(plan, joined)
    heads, low, lse = [None] * HALVES, [None] * HALVES, [None] * HALVES
    heads[0], low[0], lse[0] = attend(plan, 0, meta, mask, queries, kv[0])
    order = tie(meta, low[0], *rest_own[1:])
    rest_own[1:] = [tie(piece, low[0]) for piece in rest_own[1:]]
    rest_other = [swap_cores(plan, piece) for piece in rest_own]
    rest_more = gather_more(plan, rest_own)[len(rest_own) :]
    heads[1], low[1], lse[1] = attend(plan, 1, order, mask, queries, kv[1])
    rest_more = [tie(piece, low[1]) for piece in rest_more]
    rest_own = rest_own + rest_more
    rest_other = rest_other + [swap_cores(plan, piece) for piece in rest_more]
    rest_from = rest_sources(plan, meta, rest_own, rest_other)
    results = middle(plan, meta, low, gains, pieces, rest_from)
    outs, (dout, dhidden), rest_grads = (
        results[: plan.rows],
        results[plan.rows : plan.rows + 2],
        results[plan.rows + 2 :],
    )
    if not plan.aligned:
        r, rf, nblk = plan.r, plan.rf, plan.nblk
        whole = rest_grads[0]
        blocks = [whole[D * i : D * (i + 1)].reshape(nblk, r, D) for i in range(4)]
        blocks.append(whole[4 * D :].reshape(nblk, rf, D))
        rest_grads = split_blocks(plan, meta, jnp.concatenate(blocks, axis=1))
    keep_low, keep_high, other_low, other_high = reduce_start(plan, rest_grads)
    dq, dkv = [], []
    order = meta
    for i, part in enumerate(BACK_PARTS):
        half = part[0]
        results = attend_back(
            plan, part, order, mask, queries, dout, heads[half], lse[half], cosine, sine, kv[half]
        )
        dq.append(results[0])
        dkv.append(results[1])
        dkv += [
            lax.ppermute(results[1 + e], "blk", plan.xor_pairs(plan.member(e)))
            for e in range(1, plan.groups)
        ]
        if i == 0:
            rest_high = add_low(tie(keep_high, dq[0]), other_high)
            rest_low = add_low(tie(keep_low, dq[0]), other_low)
            order = tie(meta, dq[0], rest_high, rest_low)
        else:
            order = tie(meta, dq[i], *dkv[1 : plan.groups])
    rest_low, rest_high = reduce_step(plan, plan.bits - 1, tie(rest_low, dq[-1]), rest_high)
    order = tie(meta, rest_low) if rest_high is None else tie(meta, rest_low, rest_high)
    dprojected, qkv_grads = back_weight(plan, order, cosine, sine, normed, dq, dkv)
    if not plan.aligned:
        qkv_grads = split_blocks(plan, meta, qkv_grads[0].reshape(plan.nblk, plan.r, 3 * D))
    rest_low = tie(rest_low, dprojected)
    for step in reversed(range(plan.bits - 1)):
        rest_low, rest_high = reduce_step(plan, step, rest_low, rest_high)
    keep_low, keep_high, other_low, other_high = reduce_start(plan, qkv_grads)
    qkv_high = add_low(tie(keep_high, rest_low), other_high)
    qkv_low = add_low(keep_low, other_low)
    rest_cut = cut_rest(plan, meta, tie(rest_low, qkv_high), joined)
    order = tie(meta, qkv_high, qkv_low, *rest_cut)
    both = back_in(plan, order, dprojected, dhidden, gains, pieces, outs, qkv_from)
    rest_pieces = reduce_z(plan, rest_cut)
    qkv_low = tie(qkv_low, both[0], *rest_pieces[1:3])
    for step in reversed(range(plan.bits)):
        if step == 0:
            qkv_low = tie(qkv_low, *rest_pieces[3:])
        qkv_low, qkv_high = reduce_step(plan, step, qkv_low, qkv_high)
    both = exchange_rows(plan, [tie(piece, qkv_low) for piece in both])
    qkv_cut = cut_qkv(plan, meta, tie(qkv_low, *rest_pieces[1:]), qkv_joined)
    qkv_pieces = reduce_z(plan, qkv_cut)
    rest_pieces[0] = tie(rest_pieces[0], *qkv_cut)
    out_grad, in_grad, down_grad, mlp_gain_grad = end_rest(plan, rest_pieces)
    output, input_grad = place(plan, meta, [tie(both[0], *qkv_cut)] + both[1:])
    gain_row = norm_gain.astype(F32)[None]
    qkv_grad, norm_gain_grad = end_qkv(plan, tie(gain_row, output, input_grad, in_grad), qkv_pieces)
    mlp_gain_grad = mlp_gain_grad / mlp_gain.astype(F32)
    return (
        output,
        input_grad,
        norm_gain_grad,
        qkv_grad,
        out_grad,
        mlp_gain_grad,
        in_grad,
        down_grad,
    )


def solution(mesh):
    weights = P("blk", "row")
    acts = P("row", "blk", None)

    def run(*args):
        rows = args[0].shape[0] // mesh.shape["row"]
        tok = args[0].shape[1] // mesh.shape["blk"]
        plan = Plan(mesh, rows, tok)
        return jax.shard_map(
            functools.partial(body, plan),
            mesh=mesh,
            in_specs=(acts, P("row", None), P("blk"), weights, weights, P("blk"), weights, weights, acts),
            out_specs=(acts, acts, P("blk"), weights, weights, P("blk"), weights, weights),
            check_vma=False,
        )(*args)

    return run
```

```python
import functools
import math

import jax
import jax.numpy as jnp
import numpy as np
from jax import lax
from jax.experimental import pallas as pl
from jax.experimental.pallas import tpu as pltpu
from jax.sharding import PartitionSpec as P

D = 768
HEADS = 12
HD = 64
FF = 1152
NDOC = 8
PAIRS = HEADS // 2
EXT = 3 * D + 128

ROPE_BASE = 160000.0
NORM_EPSILON = 1e-05
MASKED = -1e30
F32 = jnp.float32
BF16 = jnp.bfloat16
NN = (((1,), (0,)), ((), ()))
NT = (((1,), (1,)), ((), ()))
TN = (((0,), (0,)), ((), ()))
LIMITS = {
    "prepare": 60,
    "place_rows": 8,
    "join_qkv": 4,
    "join_rest": 6,
    "project": 20,
    "masks": 4,
    "attend": 16,
    "middle": 56,
    "attend_back": 16,
    "back_in": 20,
    "back_weight": 16,
    "cut_qkv": 4,
    "cut_rest": 6,
    "end_rest": 4,
    "end_qkv": 4,
}
HALVES = 2
HALF_PAIRS = PAIRS // HALVES
HALF = D // HALVES
BACK_PARTS = ((0, 0, 1), (0, 1, 2), (1, 0, 3))
COSTS = {
    "prepare": 4,
    "place_rows": 2,
    "join_qkv": 2,
    "join_rest": 2,
    "project": 7,
    "attend": 9,
    "middle": 20,
    "attend_back": 12,
    "back_in": 7,
    "back_weight": 6,
    "cut_qkv": 2,
    "cut_rest": 2,
    "end_rest": 2,
    "end_qkv": 2,
}
SMEM = pl.BlockSpec(memory_space=pltpu.SMEM)
ANY = pl.BlockSpec(memory_space=pl.ANY)
VMEM = pl.BlockSpec(memory_space=pltpu.VMEM)


def dot(a, b, dims):
    return lax.dot_general(a, b, dims, preferred_element_type=F32)


def shape_of(dims, dtype):
    return jax.ShapeDtypeStruct(tuple(dims), dtype)


def params(plan, name):
    size = max(1, plan.groups * plan.local // 1024)
    return pltpu.CompilerParams(vmem_limit_bytes=min(60, LIMITS[name] * size) * 1024 * 1024)


def cost(microseconds):
    return pl.CostEstimate(
        flops=int(microseconds * 1e6), bytes_accessed=1 << 10, transcendentals=0
    )


def tie(value, *others):
    return lax.optimization_barrier((value, *others))[0]


class Plan:
    def __init__(self, mesh, rows, tok):
        self.nrow = mesh.shape["row"]
        self.nblk = mesh.shape["blk"]
        self.rows = rows
        self.tok = tok
        self.local = rows * tok
        self.chips = self.nblk // 2
        self.bits = self.chips.bit_length() - 1
        self.groups = self.nblk // rows
        self.r = D // self.nblk
        self.rf = FF // self.nblk
        self.cw = D // self.nrow
        self.aligned = self.r % 16 == 0 and self.rf % 16 == 0
        self.packed = 4 * self.r + self.rf
        rows_, chips, nrow = self.rows, self.chips, self.nrow
        self.at_pick = 0
        self.at_base = self.at_pick + rows_
        self.at_own = self.at_base + self.groups * rows_
        self.at_other = self.at_own + chips
        self.at_z = self.at_other + chips
        self.at_lo = self.at_z + nrow
        self.size = self.at_lo + 1
        table = np.zeros((nrow, self.nblk, self.size), np.int32)
        for z in range(nrow):
            for blk in range(self.nblk):
                chip, core = blk // 2, blk % 2
                low = chip % rows_
                entry = table[z, blk]
                for j in range(rows_):
                    entry[self.at_pick + j] = low ^ j
                for e in range(self.groups):
                    other = blk ^ self.member(e)
                    for j in range(rows_):
                        entry[self.at_base + e * rows_ + j] = (2 * ((other // 2) ^ j) + other % 2) * tok
                for j in range(chips):
                    entry[self.at_own + j] = 2 * (chip ^ self.order(core, j)) + core
                    entry[self.at_other + j] = 2 * (chip ^ self.order(1 - core, j)) + 1 - core
                for other in range(nrow):
                    entry[self.at_z + other] = other ^ z
                entry[self.at_lo] = low
        self.table = table

    def member(self, e):
        return (e & 1) | ((e >> 1) * 2 * self.rows)

    def order(self, core, j):
        if core == 0:
            return j
        return int(format(j, "0%db" % self.bits)[::-1], 2) if self.bits else 0

    def step_pairs(self, step):
        def flip(blk):
            bit = step if blk % 2 == 0 else self.bits - 1 - step
            return 2 * ((blk // 2) ^ (1 << bit)) + blk % 2

        return [(blk, flip(blk)) for blk in range(self.nblk)]

    def xor_pairs(self, mask):
        return [(blk, blk ^ mask) for blk in range(self.nblk)]

    def z_pairs(self, mask):
        return [(z, z ^ mask) for z in range(self.nrow)]


def swap_cores(plan, value):
    return lax.ppermute(value, "blk", plan.xor_pairs(1))


def gather_z(plan, value, behind=None):
    pieces = [value]
    for j in range(1, plan.nrow):
        source = value if behind is None else tie(value, behind[j])
        pieces.append(lax.ppermute(source, "row", plan.z_pairs(j)))
    return pieces


def exchange_rows(plan, pieces):
    return [pieces[0]] + [
        lax.ppermute(pieces[j], "blk", plan.xor_pairs(2 * j)) for j in range(1, plan.rows)
    ]


def gather_start(plan, value, behind=()):
    pairs = [plan.step_pairs(step) for step in range(plan.bits)]
    first = lax.ppermute(value, "blk", pairs[0])
    second = [lax.ppermute(tie(value, *behind), "blk", pairs[1])] if plan.bits > 1 else []
    return [value, first] + second


def gather_more(plan, pieces):
    for step in range(1, plan.bits):
        have = 1 << step
        missing = pieces[len(pieces) - have :] if step > 1 else pieces[1:2]
        pieces = pieces + [lax.ppermute(piece, "blk", plan.step_pairs(step)) for piece in missing]
    return pieces


def add_low(a, b):
    return (a.astype(F32) + b.astype(F32)).astype(BF16)


def reduce_start(plan, grads):
    keep_low, keep_high, send_low, send_high = grads
    other_high = swap_cores(plan, send_high)
    return keep_low, keep_high, swap_cores(plan, send_low), other_high


def reduce_step(plan, step, low, high):
    moved = lax.ppermute(high, "blk", plan.step_pairs(step))
    half = low.shape[0] // 2
    if half == 0:
        return add_low(low, moved)[0], None
    high = add_low(low[half:], moved[half:])
    return add_low(low[:half], moved[:half]), high


def layer_norm(values):
    average = jnp.mean(values, axis=-1, keepdims=True)
    centred = values - average
    inv_std = lax.rsqrt(jnp.mean(centred * centred, axis=-1, keepdims=True) + NORM_EPSILON)
    return centred * inv_std, inv_std


def norm_backward(grad_out, normalized, inv_std, gain):
    scaled = grad_out * gain
    inner = jnp.mean(scaled * normalized, axis=-1, keepdims=True)
    outer = jnp.mean(scaled, axis=-1, keepdims=True)
    return inv_std * (scaled - outer - normalized * inner)


def swap_halves(values):
    lane = lax.broadcasted_iota(jnp.int32, values.shape, 1)
    width = values.shape[1]
    half = HD // 2
    return jnp.where(
        (lane & half) == 0, pltpu.roll(values, width - half, 1), pltpu.roll(values, half, 1)
    )


def rotate_pair(values, cosine, sine, direction):
    return values * cosine + swap_halves(values) * (direction * sine)


def rotate_all(values, cosine, sine, direction):
    return jnp.concatenate(
        [
            rotate_pair(values[:, 128 * p : 128 * (p + 1)], cosine, sine, direction)
            for p in range(values.shape[1] // 128)
        ],
        axis=1,
    )


def prepare_kernel(plan, meta, tokens, cotangent, w_out, w_in, w_down, *refs):
    rows = plan.rows
    for j in range(rows):
        row = meta[plan.at_pick + j]
        refs[j][0] = tokens[row]
        refs[j][1] = cotangent[row]
    if plan.aligned:
        refs[rows][...] = pack_rest(plan, w_out[...], w_in[...], w_down[...])


def prepare(plan, meta, tokens, cotangent, w_out, w_in, w_down):
    rows = plan.rows
    shapes = [shape_of((2, plan.tok, D), BF16)] * rows
    if plan.aligned:
        shapes.append(shape_of((3 * plan.r, 2 * plan.cw), BF16))
    results = pl.pallas_call(
        functools.partial(prepare_kernel, plan),
        in_specs=[SMEM] + [VMEM] * 5,
        out_specs=[VMEM] * len(shapes),
        out_shape=shapes,
        compiler_params=params(plan, "prepare"),
        cost_estimate=cost(COSTS["prepare"]),
        name="prepare",
    )(meta, tokens, cotangent, w_out, w_in, w_down)
    packed = results[rows] if plan.aligned else pack_rest(plan, w_out, w_in, w_down)
    return results[:rows], packed


def place_kernel(plan, meta, *refs):
    pieces, (out, grad) = refs[: plan.rows], refs[plan.rows :]
    for j in range(plan.rows):
        row = meta[plan.at_pick + j]
        out[row] = pieces[j][0]
        grad[row] = pieces[j][1]


def place(plan, meta, pieces):
    return pl.pallas_call(
        functools.partial(place_kernel, plan),
        in_specs=[SMEM] + [VMEM] * plan.rows,
        out_specs=[VMEM] * 2,
        out_shape=[shape_of((plan.rows, plan.tok, D), BF16)] * 2,
        compiler_params=params(plan, "place_rows"),
        cost_estimate=cost(COSTS["place_rows"]),
        name="place_rows",
    )(meta, *pieces)


def ordered(plan, meta, pieces):
    stacked = jnp.stack(pieces)
    return [
        lax.dynamic_index_in_dim(stacked, meta[plan.at_z + z], 0, keepdims=False)
        for z in range(plan.nrow)
    ]


def join_qkv_kernel(plan, meta, gains, *refs):
    pieces, out, held = refs[: plan.nrow], refs[plan.nrow], refs[plan.nrow + 1]
    width = 3 * plan.cw
    for j in range(plan.nrow):
        held[j] = pieces[j][...]
    for z in range(plan.nrow):
        out[:, width * z : width * (z + 1)] = held[meta[plan.at_z + z]]
    out[:, 3 * D :] = gains[...]


def join_qkv(plan, meta, gains, pieces):
    if not plan.aligned:
        return jnp.concatenate(ordered(plan, meta, pieces) + [gains], axis=1)
    return pl.pallas_call(
        functools.partial(join_qkv_kernel, plan),
        in_specs=[SMEM] + [VMEM] * (1 + plan.nrow),
        out_specs=VMEM,
        out_shape=shape_of((plan.r, EXT), BF16),
        scratch_shapes=[pltpu.VMEM((plan.nrow, plan.r, 3 * plan.cw), BF16)],
        compiler_params=params(plan, "join_qkv"),
        cost_estimate=cost(COSTS["join_qkv"]),
        name="join_qkv",
    )(meta, gains, *pieces)


def pack_rest(plan, w_out, w_in, w_down, blank=None):
    cw = plan.cw
    left = jnp.concatenate([w_in[:, :cw], w_in[:, cw : 2 * cw], w_out], axis=0)
    if blank is None:
        blank = jnp.zeros((2 * plan.r - plan.rf, cw), BF16)
    right = jnp.concatenate([w_in[:, 2 * cw :], w_down, blank], axis=0)
    return jnp.concatenate([left, right], axis=1)


def unpack_rest(plan, piece):
    r, rf, cw = plan.r, plan.rf, plan.cw
    parts_in = [piece[:r, :cw], piece[r : 2 * r, :cw], piece[:r, cw:]]
    return parts_in, piece[2 * r : 3 * r, :cw], piece[r : r + rf, cw:]


def join_rest_kernel(plan, meta, *refs):
    pieces, out, held = refs[: plan.nrow], refs[plan.nrow], refs[plan.nrow + 1]
    r, cw = plan.r, plan.cw
    for j in range(plan.nrow):
        held[j] = pieces[j][...]
    for z in range(plan.nrow):
        parts_in, part_out, part_down = unpack_rest(plan, held[meta[plan.at_z + z]])
        out[:r, cw * z : cw * (z + 1)] = part_out
        for i in range(3):
            block, place_at = (3 * z + i) // plan.nrow, (3 * z + i) % plan.nrow
            out[r * (1 + block) : r * (2 + block), cw * place_at : cw * (place_at + 1)] = parts_in[i]
        out[4 * r :, cw * z : cw * (z + 1)] = part_down


def join_rest(plan, meta, pieces):
    if not plan.aligned:
        parts = [unpack_rest(plan, piece) for piece in ordered(plan, meta, pieces)]
        w_in = jnp.concatenate([part for item in parts for part in item[0]], axis=1)
        blocks = [jnp.concatenate([item[1] for item in parts], axis=1)]
        blocks += [w_in[:, D * t : D * (t + 1)] for t in range(3)]
        blocks += [jnp.concatenate([item[2] for item in parts], axis=1)]
        return jnp.concatenate(blocks, axis=0)
    return pl.pallas_call(
        functools.partial(join_rest_kernel, plan),
        in_specs=[SMEM] + [VMEM] * plan.nrow,
        out_specs=VMEM,
        out_shape=shape_of((plan.packed, D), BF16),
        scratch_shapes=[pltpu.VMEM((plan.nrow, 3 * plan.r, 2 * plan.cw), BF16)],
        compiler_params=params(plan, "join_rest"),
        cost_estimate=cost(COSTS["join_rest"]),
        name="join_rest",
    )(meta, *pieces)


def by_block(plan, meta, own, other):
    stacked = jnp.stack(own + other)
    places = meta[plan.at_own : plan.at_other + plan.chips]
    return jnp.zeros_like(stacked).at[places].set(stacked)


def split_blocks(plan, meta, blocks):
    half = plan.chips // 2
    return [
        jnp.take(blocks, meta[plan.at_own + half * i : plan.at_own + half * (i + 1)], axis=0)
        for i in range(4)
    ]


def qkv_sources(plan, meta, own, other):
    if plan.aligned:
        return own + other
    return [by_block(plan, meta, own, other).reshape(D, EXT)]


def rest_sources(plan, meta, own, other):
    if plan.aligned:
        return own + other
    blocks = by_block(plan, meta, own, other)
    r = plan.r
    parts = [blocks[:, r * i : r * (i + 1)].reshape(D, D) for i in range(4)]
    parts.append(blocks[:, 4 * r :].reshape(FF, D))
    return [jnp.concatenate(parts, axis=0)]


def block_size(plan):
    return (plan.r, plan.rf) if plan.aligned else (D, FF)


def block_of(plan, meta, index):
    return meta[plan.at_own + index] if plan.aligned else 0


def rows_at(index, size):
    if isinstance(index, int):
        return pl.ds(index * size, size)
    return pl.ds(pl.multiple_of(index * size, size), size)


class Mover:
    def __init__(self, sems):
        self.sems = sems
        self.used = 0
        self.open = []

    def start(self, source, target):
        copy = pltpu.make_async_copy(source, target, self.sems.at[self.used])
        self.used += 1
        copy.start()
        return copy

    def send(self, source, target):
        self.open.append(self.start(source, target))

    def finish(self):
        for copy in self.open:
            copy.wait()


def wait_all(copies):
    for copy in copies:
        copy.wait()


def qkv_copies(plan, meta, sources, w_ref, sems):
    r, _ = block_size(plan)
    return [
        pltpu.make_async_copy(source, w_ref.at[rows_at(block_of(plan, meta, i), r)], sems.at[i])
        for i, source in enumerate(sources)
    ]


def grad_target(plan, grads, index):
    if not plan.aligned:
        return grads[0]
    half = plan.chips // 2
    return grads[index // half].at[index % half]


def grad_blocks(plan, height, width):
    return [shape_of((plan.chips // 2, height, width), BF16)] * 4


def source_count(plan):
    return 2 * plan.chips if plan.aligned else 1


def qkv_kernel(plan, meta, cos_ref, sin_ref, *refs):
    x_refs = refs[: plan.rows]
    count = source_count(plan)
    sources = refs[plan.rows : plan.rows + count]
    q_ref = refs[plan.rows + count]
    kv_refs = refs[plan.rows + count + 1 : plan.rows + count + 1 + HALVES]
    n_ref, gain_ref, w_ref, sems = refs[plan.rows + count + 1 + HALVES :]
    copies = qkv_copies(plan, meta, sources, w_ref, sems)
    for copy in copies:
        copy.start()
    units = [layer_norm(x_refs[j][0].astype(F32))[0] for j in range(plan.rows)]
    for copy in copies:
        copy.wait()
    gain_ref[...] = w_ref[:, 3 * D :].astype(F32).T[:8, :]
    for j in range(plan.rows):
        n_ref[plan.tok * j : plan.tok * (j + 1), :] = (units[j] * gain_ref[0:1, :]).astype(BF16)
    cosine, sine = cos_ref[...], sin_ref[...]
    normed = n_ref[...]
    queries = dot(normed, w_ref[:, :D], NN)
    q_ref[...] = rotate_all(queries, cosine, sine, 1.0).astype(BF16)
    keys = rotate_all(dot(normed, w_ref[:, D : 2 * D], NN), cosine, sine, 1.0).astype(BF16)
    values = dot(normed, w_ref[:, 2 * D : 3 * D], NN).astype(BF16)
    for h in range(HALVES):
        kv_refs[h][0] = keys[:, HALF * h : HALF * (h + 1)]
        kv_refs[h][1] = values[:, HALF * h : HALF * (h + 1)]


def project(plan, meta, cosine, sine, pieces, sources):
    local = plan.local
    count = len(sources)
    inputs = [meta, cosine, sine, *pieces, *sources]
    return pl.pallas_call(
        functools.partial(qkv_kernel, plan),
        in_specs=[SMEM, VMEM, VMEM] + [VMEM] * plan.rows + [ANY] * count,
        out_specs=[VMEM] * (3 + HALVES),
        out_shape=[shape_of((local, D), BF16)]
        + [shape_of((2, local, HALF), BF16)] * HALVES
        + [shape_of((local, D), BF16), shape_of((8, D), F32)],
        scratch_shapes=[pltpu.VMEM((D, EXT), BF16), pltpu.SemaphoreType.DMA((count,))],
        compiler_params=params(plan, "project"),
        cost_estimate=cost(COSTS["project"]),
        name="project",
    )(*inputs)


def fill_docs(plan, meta, lengths, kmask, qmask):
    low = meta[plan.at_lo]
    ends = []
    passed = jnp.int32(0)
    for n in range(NDOC):
        passed = passed + lengths[low, n]
        ends.append(passed)

    tok = plan.tok
    lane = lax.broadcasted_iota(jnp.int32, (tok, 128), 1) & (HD - 1)
    for i in range(plan.groups * plan.rows):
        places = meta[plan.at_base + i] + lax.broadcasted_iota(jnp.int32, (tok, 128), 0)
        docs = jnp.zeros((tok, 128), jnp.int32)
        for end in ends:
            docs = docs + (places >= end).astype(jnp.int32)
        part = slice(i * tok, (i + 1) * tok)
        same = docs == lane
        kmask[part, :] = jnp.where((lane < NDOC) & ~same, MASKED, 0.0).astype(BF16)
        if i < plan.rows:
            qmask[part, :] = jnp.where(same, 1.0, 0.0).astype(BF16)


def masks(plan, meta, lengths):
    keys = plan.groups * plan.local
    return pl.pallas_call(
        functools.partial(fill_docs, plan),
        in_specs=[SMEM, SMEM],
        out_specs=[VMEM, VMEM],
        out_shape=[shape_of((keys, 128), BF16), shape_of((plan.local, 128), BF16)],
        compiler_params=params(plan, "masks"),
        cost_estimate=cost(1),
        name="masks",
    )(meta, lengths)


def head_part(pair, head, other=None):
    keep = (lax.broadcasted_iota(jnp.int32, pair.shape, 1) // HD) == head
    return jnp.where(keep, pair, jnp.zeros_like(pair) if other is None else other)


def attend_kernel(plan, width, order, kmask, qmask, q_ref, *refs):
    groups, local = plan.groups, plan.local
    kv = refs[:groups]
    o_ref, low_ref, lse_ref, s_ref, p_ref = refs[groups:]
    total_keys = groups * local
    chunk = 128
    values_t = []
    row = lax.broadcasted_iota(jnp.int32, (HD + 8, total_keys), 0)
    pair_t = jnp.concatenate([kv[e][1].T for e in range(groups)], axis=1)
    for h in range(2):
        head = pair_t[h * HD : (h + 1) * HD, :]
        values_t.append(jnp.concatenate([head, jnp.ones((8, total_keys), BF16)], axis=0))
    for first in range(0, local, width):
        rows = slice(first, first + width)
        queries = q_ref[rows, :] * jnp.asarray(1.0 / math.sqrt(HD), BF16)
        tops = []
        for h in range(2):
            head_queries = head_part(queries, h, qmask[rows, :])
            top = jnp.full((8, width), MASKED, F32)
            for e in range(groups):
                for c in range(0, local, 2 * chunk):
                    part = slice(e * local + c, e * local + c + 2 * chunk)
                    keys = head_part(kv[e][0, c : c + 2 * chunk, :], h, kmask[part, :])
                    scores = dot(keys, head_queries, NT)
                    s_ref[h, part, :] = scores
                    top = jnp.maximum(top, jnp.max(scores.reshape(-1, 8, width), axis=0))
            tops.append(jnp.max(top, axis=0, keepdims=True))
        parts = []
        for h in range(2):
            for c in range(0, total_keys, chunk):
                part = slice(c, c + chunk)
                p_ref[h, part, :] = jnp.exp(s_ref[h, part, :] - tops[h]).astype(BF16)
            weighted = dot(values_t[h], p_ref[h], NN)
            total = weighted[HD : HD + 1, :]
            parts.append(weighted[:HD, :] / total)
            lse_ref[0, h : h + 1, rows] = tops[h] + jnp.log(total)
        heads = jnp.concatenate(parts, axis=0).T
        o_ref[rows, :] = heads
        low_ref[rows, :] = heads.astype(BF16)


def attend(plan, part, meta, mask, queries, kv):
    local, groups = plan.local, plan.groups
    width = min(512, local)
    skip = part * HALF_PAIRS
    pair = pl.BlockSpec((local, 128), lambda p: (0, p))
    pair_q = pl.BlockSpec((local, 128), lambda p: (0, p + skip))
    pair_kv = pl.BlockSpec((2, local, 128), lambda p: (0, 0, p))
    whole_k = pl.BlockSpec((groups * local, 128), lambda p: (0, 0))
    whole_q = pl.BlockSpec((local, 128), lambda p: (0, 0))
    inputs = [meta, *mask, queries, *kv]
    return pl.pallas_call(
        functools.partial(attend_kernel, plan, width),
        grid=(HALF_PAIRS,),
        in_specs=[SMEM, whole_k, whole_q, pair_q] + [pair_kv] * groups,
        out_specs=[pair, pair, pl.BlockSpec((1, 2, local), lambda p: (p, 0, 0))],
        out_shape=[
            shape_of((local, HALF), F32),
            shape_of((local, HALF), BF16),
            shape_of((HALF_PAIRS, 2, local), F32),
        ],
        scratch_shapes=[
            pltpu.VMEM((2, groups * local, width), F32),
            pltpu.VMEM((2, groups * local, width), BF16),
        ],
        compiler_params=params(plan, "attend"),
        cost_estimate=cost(COSTS["attend"]),
        name="attend",
    )(*inputs)


def attend_back_kernel(
    plan, width, order, kmask, qmask, q_ref, do_ref, o_ref, lse_ref, cos_ref, sin_ref, *refs
):
    groups, local = plan.groups, plan.local
    kv = refs[:groups]
    dq_ref = refs[groups]
    dkv = refs[groups + 1 : 2 * groups + 1]
    held, p_ref, ds_ref, keys_t, product, grad_t = refs[2 * groups + 1 :]
    for e in range(groups):
        keys_t[e] = kv[e][0].T
    held[...] = jnp.zeros_like(held)
    scale = 1.0 / math.sqrt(HD)
    chunk = 128
    for first in range(0, local, width):
        rows = slice(first, first + width)
        product[...] = (do_ref[rows, :].astype(F32) * o_ref[rows, :]).T

        @pl.loop(0, 2)
        def _(h):
            head = pl.ds(pl.multiple_of(h * HD, HD), HD)
            queries = q_ref[rows, :] * jnp.asarray(scale, BF16)
            masked_queries = head_part(queries, h, qmask[rows, :])
            head_queries = head_part(queries, h)
            head_dout = head_part(do_ref[rows, :], h)
            lse = lse_ref[0, pl.ds(h, 1), rows]
            delta = jnp.sum(product[head, :], axis=0, keepdims=True)
            grad_queries = jnp.zeros((HD, width), F32)
            for e in range(groups):
                for c in range(0, local, chunk):
                    part = slice(c, c + chunk)
                    mask = kmask[e * local + c : e * local + c + chunk, :]
                    scores = dot(head_part(kv[e][0, part, :], h, mask), masked_queries, NT)
                    dprobs = dot(kv[e][1, part, :], head_dout, NT)
                    probs = jnp.exp(scores - lse)
                    p_ref[e, part, :] = probs.astype(BF16)
                    ds_ref[e, part, :] = (probs * (dprobs - delta)).astype(BF16)
                held[e, 0] += dot(ds_ref[e], head_queries, NN)
                held[e, 1] += dot(p_ref[e], head_dout, NN)
                grad_queries = grad_queries + dot(keys_t[e, head, :], ds_ref[e], NN)
            grad_t[head, :] = grad_queries

        grad = grad_t[...].T * scale
        dq_ref[rows, :] = rotate_pair(grad, cos_ref[rows, :], sin_ref[rows, :], -1.0).astype(BF16)
    for e in range(groups):
        dkv[e][...] = held[e].astype(BF16)


def attend_back(plan, part, meta, mask, queries, dout, heads, lse, cosine, sine, kv):
    local, groups = plan.local, plan.groups
    width = min(512, local)
    half, first, count = part
    skip = half * HALF_PAIRS + first
    wide = 128 * count
    pair = pl.BlockSpec((local, 128), lambda p: (0, p))
    pair_h = pl.BlockSpec((local, 128), lambda p: (0, p + first))
    pair_q = pl.BlockSpec((local, 128), lambda p: (0, p + skip))
    whole_k = pl.BlockSpec((groups * local, 128), lambda p: (0, 0))
    inputs = [meta, *mask, queries, dout, heads, lse, cosine, sine, *kv]
    table = pl.BlockSpec((local, 128), lambda p: (0, 0))
    pair_kv = pl.BlockSpec((2, local, 128), lambda p: (0, 0, p))
    pair_kv_h = pl.BlockSpec((2, local, 128), lambda p: (0, 0, p + first))
    return pl.pallas_call(
        functools.partial(attend_back_kernel, plan, width),
        grid=(count,),
        in_specs=[
            SMEM,
            whole_k,
            table,
            pair_q,
            pair_q,
            pair_h,
            pl.BlockSpec((1, 2, local), lambda p: (p + first, 0, 0)),
            table,
            table,
        ]
        + [pair_kv_h] * groups,
        out_specs=[pair] + [pair_kv] * groups,
        out_shape=[shape_of((local, wide), BF16)] + [shape_of((2, local, wide), BF16)] * groups,
        scratch_shapes=[
            pltpu.VMEM((groups, 2, local, 128), F32),
            pltpu.VMEM((groups, local, width), BF16),
            pltpu.VMEM((groups, local, width), BF16),
            pltpu.VMEM((groups, 128, local), BF16),
            pltpu.VMEM((128, width), F32),
            pltpu.VMEM((128, width), F32),
        ],
        compiler_params=params(plan, "attend_back"),
        cost_estimate=cost(4 * count),
        name="attend_back",
    )(*inputs)


def middle_kernel(plan, meta, gain_ref, *refs):
    rows, tok, local = plan.rows, plan.tok, plan.local
    count = source_count(plan)
    low_refs, refs = refs[:HALVES], refs[HALVES:]
    x_refs, refs = refs[:rows], refs[rows:]
    sources, refs = refs[:count], refs[count:]
    out_refs, refs = refs[:rows], refs[rows:]
    do_out, dh_out, refs = refs[0], refs[1], refs[2:]
    grads, refs = refs[: 4 if plan.aligned else 1], refs[4 if plan.aligned else 1 :]
    low_ref, x_ref, dy_ref, w_out, w_in, w_down, h_ref, unit_ref, n_ref, gu_ref = refs[:10]
    mid_ref, dgu_ref, out_ref, do_ref, dh_ref, da_ref, inv_ref, g_out, g_in, g_down, sems = refs[10:]
    mover = Mover(sems)
    r, rf = block_size(plan)
    blocks = [block_of(plan, meta, i) for i in range(count)]
    low_in = [
        mover.start(low_refs[h], low_ref.at[:, pl.ds(HALF * h, HALF)]) for h in range(HALVES)
    ]
    out_in = [
        mover.start(source.at[pl.ds(0, r)], w_out.at[rows_at(block, r)])
        for source, block in zip(sources, blocks)
    ]
    x_in = [mover.start(x_refs[j].at[0], x_ref.at[pl.ds(tok * j, tok)]) for j in range(rows)]

    def fetch_in(t):
        return [
            mover.start(source.at[pl.ds((1 + t) * r, r)], w_in.at[t, rows_at(block, r)])
            for source, block in zip(sources, blocks)
        ]

    in_in = [fetch_in(t) for t in range(3)]
    dy_in = [mover.start(x_refs[j].at[1], dy_ref.at[pl.ds(tok * j, tok)]) for j in range(rows)]
    down_in = [
        mover.start(source.at[pl.ds(4 * r, rf)], w_down.at[rows_at(block, rf)])
        for source, block in zip(sources, blocks)
    ]
    wait_all(low_in)
    wait_all(out_in)
    wait_all(x_in)
    gain = gain_ref[1:2, :]

    h_ref[...] = x_ref[...].astype(F32) + dot(low_ref[...], w_out[...], NN)
    unit, inv_std = layer_norm(h_ref[...])
    unit_ref[...] = unit
    inv_ref[...] = jnp.broadcast_to(inv_std, (local, 128))
    n_ref[...] = (unit * gain).astype(BF16)

    for t in range(3):
        wait_all(in_in[t])

    @pl.loop(0, 3)
    def _(t):
        gu_ref[:, pl.ds(pl.multiple_of(t * D, D), D)] = dot(n_ref[...], w_in[t], NN)

    wait_all(dy_in)
    wait_all(down_in)
    size = FF // 3

    @pl.loop(0, 3)
    def _(f):
        cols = pl.ds(pl.multiple_of(f * size, size), size)
        up_cols = pl.ds(pl.multiple_of(FF + f * size, size), size)
        gate = gu_ref[:, cols]
        up = gu_ref[:, up_cols]
        below = 0.5 + 0.5 * lax.erf(gate * math.sqrt(0.5))
        active = gate * below
        mid_ref[:, cols] = (active * up).astype(BF16)
        slope = below + gate * jnp.exp(-0.5 * gate * gate) * (1.0 / math.sqrt(2.0 * math.pi))
        dmid = dot(dy_ref[...], w_down[cols, :], NT)
        dgu_ref[:, cols] = (dmid * up * slope).astype(BF16)
        dgu_ref[:, up_cols] = (dmid * active).astype(BF16)
        g_down[cols, :] = dot(mid_ref[:, cols], dy_ref[...], TN).astype(BF16)

    targets = [grad_target(plan, grads, i) for i in range(count)]
    for target, block in zip(targets, blocks):
        mover.send(g_down.at[rows_at(block, rf)], target.at[pl.ds(4 * r, rf)])
    step = D // 3

    @pl.loop(0, 3)
    def _(n):
        cols = pl.ds(pl.multiple_of(n * step, step), step)
        mixed = dot(mid_ref[...], w_down[:, cols], NN)
        out_ref[:, cols] = (h_ref[:, cols] + mixed).astype(BF16)
        grad = dot(dgu_ref[:, :D], w_in[0, cols, :], NT)
        for t in range(1, 3):
            grad = grad + dot(dgu_ref[:, D * t : D * (t + 1)], w_in[t, cols, :], NT)
        dh_ref[:, cols] = grad
    for j in range(rows):
        mover.send(out_ref.at[pl.ds(tok * j, tok)], out_refs[j])

    @pl.loop(0, 3)
    def _(t):
        g_in[t] = dot(
            n_ref[...], dgu_ref[:, pl.ds(pl.multiple_of(t * D, D), D)], TN
        ).astype(BF16)

    for t in range(3):
        for target, block in zip(targets, blocks):
            mover.send(g_in.at[t, rows_at(block, r)], target.at[pl.ds((1 + t) * r, r)])

    grad_hidden = dy_ref[...].astype(F32) + norm_backward(
        dh_ref[...], unit_ref[...], inv_ref[:, 0:1], gain
    )
    dh_ref[...] = grad_hidden
    da_ref[...] = grad_hidden.astype(BF16)
    mover.send(dh_ref, dh_out)
    do_ref[...] = dot(da_ref[...], w_out[...], NT).astype(BF16)
    g_out[...] = dot(low_ref[...], da_ref[...], TN).astype(BF16)

    mover.send(do_ref, do_out)
    for target, block in zip(targets, blocks):
        mover.send(g_out.at[rows_at(block, r)], target.at[pl.ds(0, r)])
    mover.finish()


def middle(plan, meta, low, gains, pieces, sources):
    local, rows, tok = plan.local, plan.rows, plan.tok
    count = len(sources)
    total = 4 * D + FF
    if plan.aligned:
        grads = grad_blocks(plan, plan.packed, D)
    else:
        grads = [shape_of((total, D), BF16)]
    return pl.pallas_call(
        functools.partial(middle_kernel, plan),
        in_specs=[SMEM, VMEM] + [ANY] * (HALVES + rows + count),
        out_specs=[ANY] * (rows + 2 + len(grads)),
        out_shape=[shape_of((tok, D), BF16)] * rows
        + [shape_of((local, D), BF16), shape_of((local, D), F32)]
        + grads,
        scratch_shapes=[
            pltpu.VMEM((local, D), BF16),
            pltpu.VMEM((local, D), BF16),
            pltpu.VMEM((local, D), BF16),
            pltpu.VMEM((D, D), BF16),
            pltpu.VMEM((3, D, D), BF16),
            pltpu.VMEM((FF, D), BF16),
            pltpu.VMEM((local, D), F32),
            pltpu.VMEM((local, D), F32),
            pltpu.VMEM((local, D), BF16),
            pltpu.VMEM((local, 2 * FF), F32),
            pltpu.VMEM((local, FF), BF16),
            pltpu.VMEM((local, 2 * FF), BF16),
            pltpu.VMEM((local, D), BF16),
            pltpu.VMEM((local, D), BF16),
            pltpu.VMEM((local, D), F32),
            pltpu.VMEM((local, D), BF16),
            pltpu.VMEM((local, 128), F32),
            pltpu.VMEM((D, D), BF16),
            pltpu.VMEM((3, D, D), BF16),
            pltpu.VMEM((FF, D), BF16),
            pltpu.SemaphoreType.DMA((HALVES + 3 * rows + 2 + 10 * count,)),
        ],
        compiler_params=params(plan, "middle"),
        cost_estimate=cost(COSTS["middle"]),
        name="middle",
    )(meta, gains, *low, *pieces, *sources)


def back_weight_kernel(plan, meta, *refs):
    groups, local = plan.groups, plan.local
    count = len(BACK_PARTS)
    cos_ref, sin_ref, n_in, refs = refs[0], refs[1], refs[2], refs[3:]
    dq_refs, refs = refs[:count], refs[count:]
    dkv, refs = refs[: count * groups], refs[count * groups :]
    dp_out, refs = refs[0], refs[1:]
    grads, refs = refs[: 4 if plan.aligned else 1], refs[4 if plan.aligned else 1 :]
    cos, sin, n_ref, dkv_ref, dp_ref, g_ref, sems = refs
    mover = Mover(sems)
    columns = []
    for half, first, pairs in BACK_PARTS:
        columns.append(pl.ds(HALF * half + 128 * first, 128 * pairs))
    first_in = [mover.start(n_in, n_ref)]
    for i in range(count):
        first_in.append(mover.start(dq_refs[i], dp_ref.at[0, :, columns[i]]))
    rest_in = [mover.start(cos_ref, cos), mover.start(sin_ref, sin)]
    for i in range(count):
        for e in range(groups):
            rest_in.append(
                mover.start(dkv[groups * i + e], dkv_ref.at[e, :, :, columns[i]])
            )
    r, _ = block_size(plan)

    def send_grad(t):
        cols = pl.ds(D * t, D)
        for i in range(source_count(plan)):
            at = rows_at(block_of(plan, meta, i), r)
            mover.send(g_ref.at[at, cols], grad_target(plan, grads, i).at[:, cols])

    wait_all(first_in)
    normed = n_ref[...]
    g_ref[:, :D] = dot(normed, dp_ref[0], TN).astype(BF16)
    send_grad(0)
    wait_all(rest_in)
    dp_ref[2] = sum_pieces([dkv_ref[e, 1] for e in range(groups)]).astype(BF16)
    g_ref[:, 2 * D : 3 * D] = dot(normed, dp_ref[2], TN).astype(BF16)
    send_grad(2)
    grad_keys = sum_pieces([dkv_ref[e, 0] for e in range(groups)])
    dp_ref[1] = rotate_all(grad_keys, cos[...], sin[...], -1.0).astype(BF16)
    mover.send(dp_ref, dp_out)
    g_ref[:, D : 2 * D] = dot(normed, dp_ref[1], TN).astype(BF16)
    send_grad(1)
    mover.finish()


def back_weight(plan, meta, cosine, sine, normed, dq, dkv):
    local, groups, count = plan.local, plan.groups, len(BACK_PARTS)
    if plan.aligned:
        grads = grad_blocks(plan, plan.r, 3 * D)
    else:
        grads = [shape_of((D, 3 * D), BF16)]
    results = pl.pallas_call(
        functools.partial(back_weight_kernel, plan),
        in_specs=[SMEM] + [ANY] * (3 + count * (1 + groups)),
        out_specs=[ANY] * (1 + len(grads)),
        out_shape=[shape_of((3, local, D), BF16)] + grads,
        scratch_shapes=[
            pltpu.VMEM((local, 128), F32),
            pltpu.VMEM((local, 128), F32),
            pltpu.VMEM((local, D), BF16),
            pltpu.VMEM((groups, 2, local, D), BF16),
            pltpu.VMEM((3, local, D), BF16),
            pltpu.VMEM((D, 3 * D), BF16),
            pltpu.SemaphoreType.DMA((4 + count * (1 + groups) + 3 * source_count(plan),)),
        ],
        compiler_params=params(plan, "back_weight"),
        cost_estimate=cost(COSTS["back_weight"]),
        name="back_weight",
    )(meta, cosine, sine, normed, *dq, *dkv)
    return results[0], results[1:]


def back_in_kernel(plan, meta, dp_ref, dh_ref, gain_ref, *refs):
    rows, tok = plan.rows, plan.tok
    count = source_count(plan)
    x_refs, refs = refs[:rows], refs[rows:]
    out_refs, refs = refs[:rows], refs[rows:]
    sources, refs = refs[:count], refs[count:]
    both_refs = refs[:rows]
    w_ref, in_sems = refs[rows:]
    copies = qkv_copies(plan, meta, sources, w_ref, in_sems)
    for copy in copies:
        copy.start()
    for copy in copies:
        copy.wait()
    grad_normed = dot(dp_ref[0], w_ref[:, :D], NT)
    for t in range(1, 3):
        grad_normed = grad_normed + dot(dp_ref[t], w_ref[:, D * t : D * (t + 1)], NT)
    for j in range(rows):
        part = slice(tok * j, tok * (j + 1))
        unit, inv_std = layer_norm(x_refs[j][0].astype(F32))
        grad = grad_normed[part, :]
        back = norm_backward(grad, unit, inv_std, gain_ref[0:1, :])
        both_refs[j][0] = out_refs[j][...]
        both_refs[j][1] = (dh_ref[part, :] + back).astype(BF16)


def back_in(plan, meta, dprojected, dhidden, gains, pieces, outs, sources):
    rows, tok = plan.rows, plan.tok
    count = len(sources)
    return pl.pallas_call(
        functools.partial(back_in_kernel, plan),
        in_specs=[SMEM] + [VMEM] * (3 + 2 * rows) + [ANY] * count,
        out_specs=[VMEM] * rows,
        out_shape=[shape_of((2, tok, D), BF16)] * rows,
        scratch_shapes=[pltpu.VMEM((D, EXT), BF16), pltpu.SemaphoreType.DMA((count,))],
        compiler_params=params(plan, "back_in"),
        cost_estimate=cost(COSTS["back_in"]),
        name="back_in",
    )(meta, dprojected, dhidden, gains, *pieces, *outs, *sources)


def gain_columns(weight, grad):
    total = jnp.sum(weight.astype(F32) * grad.astype(F32), axis=1, keepdims=True)
    high = total.astype(BF16)
    return high, (total - high.astype(F32)).astype(BF16)


def pad_width(plan):
    return -(-(3 * plan.cw + 2) // 128) * 128


def gain_tail(plan, weight, grad):
    width = pad_width(plan) - 3 * plan.cw
    high, rest = gain_columns(weight, grad)
    lane = lax.broadcasted_iota(jnp.int32, (plan.r, width), 1)
    return jnp.where(lane == 0, high, jnp.where(lane == 1, rest, jnp.zeros_like(high)))


def cut_qkv_kernel(plan, meta, total, weight, *refs):
    outs, held = refs[: plan.nrow], refs[plan.nrow]
    width = 3 * plan.cw
    tail = gain_tail(plan, weight[:, : 3 * D], total[...])
    for z in range(plan.nrow):
        place_at = meta[plan.at_z + z]
        held[place_at, :, :width] = total[:, width * z : width * (z + 1)]
        held[place_at, :, width:] = tail
    for j in range(plan.nrow):
        outs[j][...] = held[j]


def cut_qkv(plan, meta, total, weight):
    width, wide = 3 * plan.cw, pad_width(plan)
    if not plan.aligned:
        tail = gain_tail(plan, weight[:, : 3 * D], total)
        parts = [
            jnp.concatenate([total[:, width * z : width * (z + 1)], tail], axis=1)
            for z in range(plan.nrow)
        ]
        return ordered(plan, meta, parts)
    return pl.pallas_call(
        functools.partial(cut_qkv_kernel, plan),
        in_specs=[SMEM, VMEM, VMEM],
        out_specs=[VMEM] * plan.nrow,
        out_shape=[shape_of((plan.r, wide), BF16)] * plan.nrow,
        scratch_shapes=[pltpu.VMEM((plan.nrow, plan.r, wide), BF16)],
        compiler_params=params(plan, "cut_qkv"),
        cost_estimate=cost(COSTS["cut_qkv"]),
        name="cut_qkv",
    )(meta, total, weight)


def gain_blank(plan, weight, grad):
    r, blank = plan.r, 2 * plan.r - plan.rf
    cols = [weight[r * t : r * (t + 1)] for t in range(1, 4)]
    grads = [grad[r * t : r * (t + 1)] for t in range(1, 4)]
    high, rest = gain_columns(jnp.concatenate(cols, axis=1), jnp.concatenate(grads, axis=1))
    lane = lax.broadcasted_iota(jnp.int32, (blank, plan.cw), 1)
    found = jnp.zeros((blank, plan.cw), BF16)
    for i in range(r // blank):
        part = slice(blank * i, blank * (i + 1))
        found = jnp.where(lane == 2 * i, high[part], found)
        found = jnp.where(lane == 2 * i + 1, rest[part], found)
    return found


def cut_rest_kernel(plan, meta, total, weight, *refs):
    outs, held = refs[: plan.nrow], refs[plan.nrow]
    r, rf, cw = plan.r, plan.rf, plan.cw
    blank = gain_blank(plan, weight[...], total[...])
    for z in range(plan.nrow):
        place_at = meta[plan.at_z + z]
        cols = slice(cw * z, cw * (z + 1))
        parts = []
        for i in range(3):
            block, at = (3 * z + i) // plan.nrow, (3 * z + i) % plan.nrow
            parts.append(total[r * (1 + block) : r * (2 + block), cw * at : cw * (at + 1)])
        held[place_at, :r, :] = jnp.concatenate([parts[0], parts[2]], axis=1)
        held[place_at, r : 2 * r, :] = jnp.concatenate(
            [parts[1], total[4 * r : 5 * r, cols]], axis=1
        )
        rest = total[5 * r : 4 * r + rf, cols]
        held[place_at, 2 * r :, :] = jnp.concatenate(
            [total[:r, cols], jnp.concatenate([rest, blank], axis=0)], axis=1
        )
    for j in range(plan.nrow):
        outs[j][...] = held[j]


def cut_rest(plan, meta, total, weight):
    r, cw = plan.r, plan.cw
    if not plan.aligned:
        grad_in = jnp.concatenate([total[r * (1 + t) : r * (2 + t)] for t in range(3)], axis=1)
        blank = gain_blank(plan, weight, total)
        parts = [
            pack_rest(
                plan,
                total[:r, cw * z : cw * (z + 1)],
                grad_in[:, 3 * cw * z : 3 * cw * (z + 1)],
                total[4 * r :, cw * z : cw * (z + 1)],
                blank,
            )
            for z in range(plan.nrow)
        ]
        return ordered(plan, meta, parts)
    return pl.pallas_call(
        functools.partial(cut_rest_kernel, plan),
        in_specs=[SMEM, VMEM, VMEM],
        out_specs=[VMEM] * plan.nrow,
        out_shape=[shape_of((3 * r, 2 * cw), BF16)] * plan.nrow,
        scratch_shapes=[pltpu.VMEM((plan.nrow, 3 * r, 2 * cw), BF16)],
        compiler_params=params(plan, "cut_rest"),
        cost_estimate=cost(COSTS["cut_rest"]),
        name="cut_rest",
    )(meta, total, weight)


def reduce_z(plan, pieces):
    return [pieces[0]] + [
        lax.ppermute(pieces[j], "row", plan.z_pairs(j)) for j in range(1, plan.nrow)
    ]


def sum_pieces(pieces):
    total = pieces[0].astype(F32)
    for piece in pieces[1:]:
        total = total + piece.astype(F32)
    return total


def end_rest_kernel(plan, *refs):
    pieces, (g_out, g_in, g_down, g_gain) = refs[: plan.nrow], refs[plan.nrow :]
    total = sum_pieces([piece[...] for piece in pieces])
    parts_in, part_out, part_down = unpack_rest(plan, total)
    g_out[...] = part_out
    g_in[...] = jnp.concatenate(parts_in, axis=1)
    g_down[...] = part_down
    blank = 2 * plan.r - plan.rf
    g_gain[...] = total[3 * plan.r - blank :, plan.cw : plan.cw + 128].T[:8, :]


def end_rest(plan, pieces):
    r, blank = plan.r, 2 * plan.r - plan.rf
    if not plan.aligned:
        total = sum_pieces(pieces)
        parts_in, out_grad, down_grad = unpack_rest(plan, total)
        in_grad = jnp.concatenate(parts_in, axis=1)
        gain = total[3 * r - blank :, plan.cw : plan.cw + 8].T
    else:
        out_grad, in_grad, down_grad, gain = pl.pallas_call(
            functools.partial(end_rest_kernel, plan),
            in_specs=[VMEM] * plan.nrow,
            out_specs=[VMEM] * 4,
            out_shape=[
                shape_of((r, plan.cw), F32),
                shape_of((r, 3 * plan.cw), F32),
                shape_of((plan.rf, plan.cw), F32),
                shape_of((8, blank), F32),
            ],
            compiler_params=params(plan, "end_rest"),
            cost_estimate=cost(COSTS["end_rest"]),
            name="end_rest",
        )(*pieces)
    gain = jnp.concatenate([gain[2 * i] + gain[2 * i + 1] for i in range(r // blank)])
    return out_grad, in_grad, down_grad, gain


def end_qkv_kernel(plan, gain_ref, *refs):
    pieces, (g_qkv, g_gain) = refs[: plan.nrow], refs[plan.nrow :]
    width, wide = 3 * plan.cw, pad_width(plan)
    total = sum_pieces([piece[...] for piece in pieces])
    g_qkv[...] = total[:, :width]
    tail = total[:, wide - 128 :].T
    at = width - (wide - 128)
    g_gain[...] = (tail[at : at + 1, :] + tail[at + 1 : at + 2, :]) / gain_ref[...]


def end_qkv(plan, gain, pieces):
    width, wide = 3 * plan.cw, pad_width(plan)
    if not plan.aligned:
        total = sum_pieces(pieces)
        return total[:, :width], (total[:, width] + total[:, width + 1]) / gain[0]
    grad, gain_grad = pl.pallas_call(
        functools.partial(end_qkv_kernel, plan),
        in_specs=[VMEM] * (1 + plan.nrow),
        out_specs=[VMEM] * 2,
        out_shape=[shape_of((plan.r, width), F32), shape_of((1, plan.r), F32)],
        compiler_params=params(plan, "end_qkv"),
        cost_estimate=cost(COSTS["end_qkv"]),
        name="end_qkv",
    )(gain, *pieces)
    return grad, gain_grad.reshape(plan.r)


def rotation_tables(plan, meta, lengths):
    ends = jnp.cumsum(lax.dynamic_index_in_dim(lengths, meta[plan.at_lo], 0, keepdims=False))
    starts = jnp.concatenate([jnp.zeros((1,), jnp.int32), ends[:-1]])
    bases = meta[plan.at_base : plan.at_base + plan.rows]
    places = (bases[:, None] + jnp.arange(plan.tok, dtype=jnp.int32)[None, :]).reshape(-1)
    passed = places[:, None] >= starts[None, :]
    positions = places - jnp.max(jnp.where(passed, starts[None, :], 0), axis=1)
    half = HD // 2
    inverse = ROPE_BASE ** (-(jnp.arange(half, dtype=F32) * (2.0 / HD)))
    angles = positions.astype(F32)[:, None] * inverse
    cosine, sine = jnp.cos(angles), jnp.sin(angles)
    return (
        jnp.concatenate([cosine] * 4, axis=1),
        jnp.concatenate([-sine, sine, -sine, sine], axis=1),
    )


def body(
    plan,
    tokens,
    lengths,
    norm_gain,
    qkv_weight,
    out_weight,
    mlp_gain,
    in_weight,
    down_weight,
    cotangent,
):
    blk, row = lax.axis_index("blk"), lax.axis_index("row")
    meta = lax.dynamic_slice(
        jnp.asarray(plan.table), (row, blk, 0), (1, 1, plan.size)
    ).reshape(plan.size)
    qkv_parts = gather_z(plan, qkv_weight)
    cut, packed = prepare(plan, meta, tokens, cotangent, out_weight, in_weight, down_weight)
    pieces = exchange_rows(plan, cut)
    rest_parts = gather_z(plan, packed, behind=qkv_parts)
    gains = jnp.pad(jnp.stack([norm_gain, mlp_gain], axis=1), ((0, 0), (0, 126)))
    cosine, sine = rotation_tables(plan, meta, lengths)
    mask = masks(plan, meta, lengths)
    qkv_joined = join_qkv(plan, meta, gains, qkv_parts)
    qkv_own = gather_start(plan, qkv_joined, pieces[1:])
    qkv_own[1] = tie(qkv_own[1], *rest_parts[2:], cosine, sine, *mask)
    qkv_own = gather_more(plan, qkv_own)
    qkv_own[-1] = tie(qkv_own[-1], rest_parts[1])
    qkv_other = [swap_cores(plan, piece) for piece in qkv_own]
    qkv_from = qkv_sources(plan, meta, qkv_own, qkv_other)
    rest_parts[0] = tie(rest_parts[0], qkv_joined, *qkv_other[:-1])
    joined = join_rest(plan, meta, rest_parts)
    results = project(plan, tie(meta, joined), cosine, sine, pieces, qkv_from)
    queries, kv, (normed, gains) = results[0], results[1 : 1 + HALVES], results[1 + HALVES :]
    kv = [
        [part]
        + [
            lax.ppermute(part, "blk", plan.xor_pairs(plan.member(e)))
            for e in range(1, plan.groups)
        ]
        for part in kv
    ]
    rest_own = gather_start(plan, joined)
    heads, low, lse = [None] * HALVES, [None] * HALVES, [None] * HALVES
    heads[0], low[0], lse[0] = attend(plan, 0, meta, mask, queries, kv[0])
    order = tie(meta, low[0], *rest_own[1:])
    rest_own[1:] = [tie(piece, low[0]) for piece in rest_own[1:]]
    rest_other = [swap_cores(plan, piece) for piece in rest_own]
    rest_more = gather_more(plan, rest_own)[len(rest_own) :]
    heads[1], low[1], lse[1] = attend(plan, 1, order, mask, queries, kv[1])
    rest_more = [tie(piece, low[1]) for piece in rest_more]
    rest_own = rest_own + rest_more
    rest_other = rest_other + [swap_cores(plan, piece) for piece in rest_more]
    rest_from = rest_sources(plan, meta, rest_own, rest_other)
    results = middle(plan, meta, low, gains, pieces, rest_from)
    outs, (dout, dhidden), rest_grads = (
        results[: plan.rows],
        results[plan.rows : plan.rows + 2],
        results[plan.rows + 2 :],
    )
    if not plan.aligned:
        r, rf, nblk = plan.r, plan.rf, plan.nblk
        whole = rest_grads[0]
        blocks = [whole[D * i : D * (i + 1)].reshape(nblk, r, D) for i in range(4)]
        blocks.append(whole[4 * D :].reshape(nblk, rf, D))
        rest_grads = split_blocks(plan, meta, jnp.concatenate(blocks, axis=1))
    keep_low, keep_high, other_low, other_high = reduce_start(plan, rest_grads)
    dq, dkv = [], []
    order = meta
    for i, part in enumerate(BACK_PARTS):
        half = part[0]
        results = attend_back(
            plan, part, order, mask, queries, dout, heads[half], lse[half], cosine, sine, kv[half]
        )
        dq.append(results[0])
        dkv.append(results[1])
        dkv += [
            lax.ppermute(results[1 + e], "blk", plan.xor_pairs(plan.member(e)))
            for e in range(1, plan.groups)
        ]
        if i == 0:
            rest_high = add_low(tie(keep_high, dq[0]), other_high)
            rest_low = add_low(tie(keep_low, dq[0]), other_low)
            order = tie(meta, dq[0], rest_high, rest_low)
        else:
            order = tie(meta, dq[i], *dkv[1 : plan.groups])
    rest_low, rest_high = reduce_step(plan, plan.bits - 1, tie(rest_low, dq[-1]), rest_high)
    order = tie(meta, rest_low) if rest_high is None else tie(meta, rest_low, rest_high)
    dprojected, qkv_grads = back_weight(plan, order, cosine, sine, normed, dq, dkv)
    if not plan.aligned:
        qkv_grads = split_blocks(plan, meta, qkv_grads[0].reshape(plan.nblk, plan.r, 3 * D))
    rest_low = tie(rest_low, dprojected)
    for step in reversed(range(plan.bits - 1)):
        rest_low, rest_high = reduce_step(plan, step, rest_low, rest_high)
    keep_low, keep_high, other_low, other_high = reduce_start(plan, qkv_grads)
    qkv_high = add_low(tie(keep_high, rest_low), other_high)
    qkv_low = add_low(keep_low, other_low)
    rest_cut = cut_rest(plan, meta, tie(rest_low, qkv_high), joined)
    order = tie(meta, qkv_high, qkv_low, *rest_cut)
    both = back_in(plan, order, dprojected, dhidden, gains, pieces, outs, qkv_from)
    rest_pieces = reduce_z(plan, rest_cut)
    qkv_low = tie(qkv_low, both[0], *rest_pieces[1:3])
    for step in reversed(range(plan.bits)):
        if step == 0:
            both = [tie(piece, qkv_high) for piece in both]
        qkv_low, qkv_high = reduce_step(plan, step, qkv_low, qkv_high)
    qkv_cut = cut_qkv(plan, meta, tie(qkv_low, *rest_pieces[1:]), qkv_joined)
    both = exchange_rows(plan, both[:3] + [tie(piece, *qkv_cut) for piece in both[3:]])
    qkv_pieces = reduce_z(plan, qkv_cut)
    rest_pieces[0] = tie(rest_pieces[0], *qkv_cut)
    out_grad, in_grad, down_grad, mlp_gain_grad = end_rest(plan, rest_pieces)
    output, input_grad = place(plan, meta, [tie(both[0], *qkv_cut)] + both[1:])
    gain_row = norm_gain.astype(F32)[None]
    qkv_grad, norm_gain_grad = end_qkv(plan, tie(gain_row, output, input_grad, in_grad), qkv_pieces)
    mlp_gain_grad = mlp_gain_grad / mlp_gain.astype(F32)
    return (
        output,
        input_grad,
        norm_gain_grad,
        qkv_grad,
        out_grad,
        mlp_gain_grad,
        in_grad,
        down_grad,
    )


def solution(mesh):
    weights = P("blk", "row")
    acts = P("row", "blk", None)

    def run(*args):
        rows = args[0].shape[0] // mesh.shape["row"]
        tok = args[0].shape[1] // mesh.shape["blk"]
        plan = Plan(mesh, rows, tok)
        return jax.shard_map(
            functools.partial(body, plan),
            mesh=mesh,
            in_specs=(acts, P("row", None), P("blk"), weights, weights, P("blk"), weights, weights, acts),
            out_specs=(acts, acts, P("blk"), weights, weights, P("blk"), weights, weights),
            check_vma=False,
        )(*args)

    return run
```

```python
import functools
import math

import jax
import jax.numpy as jnp
import numpy as np
from jax import lax
from jax.experimental import pallas as pl
from jax.experimental.pallas import tpu as pltpu
from jax.sharding import PartitionSpec as P

D = 768
HEADS = 12
HD = 64
FF = 1152
NDOC = 8
PAIRS = HEADS // 2
EXT = 3 * D + 128

ROPE_BASE = 160000.0
NORM_EPSILON = 1e-05
MASKED = -1e30
F32 = jnp.float32
BF16 = jnp.bfloat16
NN = (((1,), (0,)), ((), ()))
NT = (((1,), (1,)), ((), ()))
TN = (((0,), (0,)), ((), ()))
LIMITS = {
    "prepare": 60,
    "place_rows": 8,
    "join_qkv": 4,
    "join_rest": 6,
    "project": 20,
    "masks": 4,
    "attend": 12,
    "middle": 56,
    "attend_back": 12,
    "back_in": 20,
    "back_weight": 14,
    "cut_qkv": 4,
    "cut_rest": 6,
    "end_rest": 4,
    "end_qkv": 4,
}
HALVES = 2
HALF_PAIRS = PAIRS // HALVES
HALF = D // HALVES
BACK_PARTS = ((0, 0, 1), (0, 1, 2), (1, 0, 3))
COSTS = {
    "prepare": 4,
    "place_rows": 2,
    "join_qkv": 2,
    "join_rest": 2,
    "project": 7,
    "attend": 9,
    "middle": 20,
    "attend_back": 12,
    "back_in": 7,
    "back_weight": 6,
    "cut_qkv": 2,
    "cut_rest": 2,
    "end_rest": 2,
    "end_qkv": 2,
}
SMEM = pl.BlockSpec(memory_space=pltpu.SMEM)
ANY = pl.BlockSpec(memory_space=pl.ANY)
VMEM = pl.BlockSpec(memory_space=pltpu.VMEM)


def dot(a, b, dims):
    return lax.dot_general(a, b, dims, preferred_element_type=F32)


def shape_of(dims, dtype):
    return jax.ShapeDtypeStruct(tuple(dims), dtype)


def params(plan, name):
    size = max(1, plan.groups * plan.local // 1024)
    return pltpu.CompilerParams(vmem_limit_bytes=min(60, LIMITS[name] * size) * 1024 * 1024)


def cost(microseconds):
    return pl.CostEstimate(
        flops=int(microseconds * 1e6), bytes_accessed=1 << 10, transcendentals=0
    )


def tie(value, *others):
    return lax.optimization_barrier((value, *others))[0]


class Plan:
    def __init__(self, mesh, rows, tok):
        self.nrow = mesh.shape["row"]
        self.nblk = mesh.shape["blk"]
        self.rows = rows
        self.tok = tok
        self.local = rows * tok
        self.chips = self.nblk // 2
        self.bits = self.chips.bit_length() - 1
        self.groups = self.nblk // rows
        self.r = D // self.nblk
        self.rf = FF // self.nblk
        self.cw = D // self.nrow
        self.aligned = self.r % 16 == 0 and self.rf % 16 == 0
        self.packed = 4 * self.r + self.rf
        rows_, chips, nrow = self.rows, self.chips, self.nrow
        self.at_pick = 0
        self.at_base = self.at_pick + rows_
        self.at_own = self.at_base + self.groups * rows_
        self.at_other = self.at_own + chips
        self.at_z = self.at_other + chips
        self.at_lo = self.at_z + nrow
        self.size = self.at_lo + 1
        table = np.zeros((nrow, self.nblk, self.size), np.int32)
        for z in range(nrow):
            for blk in range(self.nblk):
                chip, core = blk // 2, blk % 2
                low = chip % rows_
                entry = table[z, blk]
                for j in range(rows_):
                    entry[self.at_pick + j] = low ^ j
                for e in range(self.groups):
                    other = blk ^ self.member(e)
                    for j in range(rows_):
                        entry[self.at_base + e * rows_ + j] = (2 * ((other // 2) ^ j) + other % 2) * tok
                for j in range(chips):
                    entry[self.at_own + j] = 2 * (chip ^ self.order(core, j)) + core
                    entry[self.at_other + j] = 2 * (chip ^ self.order(1 - core, j)) + 1 - core
                for other in range(nrow):
                    entry[self.at_z + other] = other ^ z
                entry[self.at_lo] = low
        self.table = table

    def member(self, e):
        return (e & 1) | ((e >> 1) * 2 * self.rows)

    def order(self, core, j):
        if core == 0:
            return j
        return int(format(j, "0%db" % self.bits)[::-1], 2) if self.bits else 0

    def step_pairs(self, step):
        def flip(blk):
            bit = step if blk % 2 == 0 else self.bits - 1 - step
            return 2 * ((blk // 2) ^ (1 << bit)) + blk % 2

        return [(blk, flip(blk)) for blk in range(self.nblk)]

    def xor_pairs(self, mask):
        return [(blk, blk ^ mask) for blk in range(self.nblk)]

    def z_pairs(self, mask):
        return [(z, z ^ mask) for z in range(self.nrow)]


def swap_cores(plan, value):
    return lax.ppermute(value, "blk", plan.xor_pairs(1))


def gather_z(plan, value, behind=None):
    pieces = [value]
    for j in range(1, plan.nrow):
        source = value if behind is None else tie(value, behind[j])
        pieces.append(lax.ppermute(source, "row", plan.z_pairs(j)))
    return pieces


def exchange_rows(plan, pieces):
    return [pieces[0]] + [
        lax.ppermute(pieces[j], "blk", plan.xor_pairs(2 * j)) for j in range(1, plan.rows)
    ]


def gather_start(plan, value, behind=()):
    pairs = [plan.step_pairs(step) for step in range(plan.bits)]
    first = lax.ppermute(value, "blk", pairs[0])
    second = [lax.ppermute(tie(value, *behind), "blk", pairs[1])] if plan.bits > 1 else []
    return [value, first] + second


def gather_more(plan, pieces):
    for step in range(1, plan.bits):
        have = 1 << step
        missing = pieces[len(pieces) - have :] if step > 1 else pieces[1:2]
        pieces = pieces + [lax.ppermute(piece, "blk", plan.step_pairs(step)) for piece in missing]
    return pieces


def add_low(a, b):
    return (a.astype(F32) + b.astype(F32)).astype(BF16)


def reduce_start(plan, grads):
    keep_low, keep_high, send_low, send_high = grads
    other_high = swap_cores(plan, send_high)
    return keep_low, keep_high, swap_cores(plan, send_low), other_high


def reduce_step(plan, step, low, high):
    moved = lax.ppermute(high, "blk", plan.step_pairs(step))
    half = low.shape[0] // 2
    if half == 0:
        return add_low(low, moved)[0], None
    high = add_low(low[half:], moved[half:])
    return add_low(low[:half], moved[:half]), high


def layer_norm(values):
    average = jnp.mean(values, axis=-1, keepdims=True)
    centred = values - average
    inv_std = lax.rsqrt(jnp.mean(centred * centred, axis=-1, keepdims=True) + NORM_EPSILON)
    return centred * inv_std, inv_std


def norm_backward(grad_out, normalized, inv_std, gain):
    scaled = grad_out * gain
    inner = jnp.mean(scaled * normalized, axis=-1, keepdims=True)
    outer = jnp.mean(scaled, axis=-1, keepdims=True)
    return inv_std * (scaled - outer - normalized * inner)


def swap_halves(values):
    lane = lax.broadcasted_iota(jnp.int32, values.shape, 1)
    width = values.shape[1]
    half = HD // 2
    return jnp.where(
        (lane & half) == 0, pltpu.roll(values, width - half, 1), pltpu.roll(values, half, 1)
    )


def rotate_pair(values, cosine, sine, direction):
    return values * cosine + swap_halves(values) * (direction * sine)


def rotate_all(values, cosine, sine, direction):
    return jnp.concatenate(
        [
            rotate_pair(values[:, 128 * p : 128 * (p + 1)], cosine, sine, direction)
            for p in range(values.shape[1] // 128)
        ],
        axis=1,
    )


def prepare_kernel(plan, meta, tokens, cotangent, w_out, w_in, w_down, *refs):
    rows = plan.rows
    for j in range(rows):
        row = meta[plan.at_pick + j]
        refs[j][0] = tokens[row]
        refs[j][1] = cotangent[row]
    if plan.aligned:
        refs[rows][...] = pack_rest(plan, w_out[...], w_in[...], w_down[...])


def prepare(plan, meta, tokens, cotangent, w_out, w_in, w_down):
    rows = plan.rows
    shapes = [shape_of((2, plan.tok, D), BF16)] * rows
    if plan.aligned:
        shapes.append(shape_of((3 * plan.r, 2 * plan.cw), BF16))
    results = pl.pallas_call(
        functools.partial(prepare_kernel, plan),
        in_specs=[SMEM] + [VMEM] * 5,
        out_specs=[VMEM] * len(shapes),
        out_shape=shapes,
        compiler_params=params(plan, "prepare"),
        cost_estimate=cost(COSTS["prepare"]),
        name="prepare",
    )(meta, tokens, cotangent, w_out, w_in, w_down)
    packed = results[rows] if plan.aligned else pack_rest(plan, w_out, w_in, w_down)
    return results[:rows], packed


def place_kernel(plan, meta, *refs):
    pieces, (out, grad) = refs[: plan.rows], refs[plan.rows :]
    for j in range(plan.rows):
        row = meta[plan.at_pick + j]
        out[row] = pieces[j][0]
        grad[row] = pieces[j][1]


def place(plan, meta, pieces):
    return pl.pallas_call(
        functools.partial(place_kernel, plan),
        in_specs=[SMEM] + [VMEM] * plan.rows,
        out_specs=[VMEM] * 2,
        out_shape=[shape_of((plan.rows, plan.tok, D), BF16)] * 2,
        compiler_params=params(plan, "place_rows"),
        cost_estimate=cost(COSTS["place_rows"]),
        name="place_rows",
    )(meta, *pieces)


def ordered(plan, meta, pieces):
    stacked = jnp.stack(pieces)
    return [
        lax.dynamic_index_in_dim(stacked, meta[plan.at_z + z], 0, keepdims=False)
        for z in range(plan.nrow)
    ]


def join_qkv_kernel(plan, meta, gains, *refs):
    pieces, out, held = refs[: plan.nrow], refs[plan.nrow], refs[plan.nrow + 1]
    width = 3 * plan.cw
    for j in range(plan.nrow):
        held[j] = pieces[j][...]
    for z in range(plan.nrow):
        out[:, width * z : width * (z + 1)] = held[meta[plan.at_z + z]]
    out[:, 3 * D :] = gains[...]


def join_qkv(plan, meta, gains, pieces):
    if not plan.aligned:
        return jnp.concatenate(ordered(plan, meta, pieces) + [gains], axis=1)
    return pl.pallas_call(
        functools.partial(join_qkv_kernel, plan),
        in_specs=[SMEM] + [VMEM] * (1 + plan.nrow),
        out_specs=VMEM,
        out_shape=shape_of((plan.r, EXT), BF16),
        scratch_shapes=[pltpu.VMEM((plan.nrow, plan.r, 3 * plan.cw), BF16)],
        compiler_params=params(plan, "join_qkv"),
        cost_estimate=cost(COSTS["join_qkv"]),
        name="join_qkv",
    )(meta, gains, *pieces)


def pack_rest(plan, w_out, w_in, w_down, blank=None):
    cw = plan.cw
    left = jnp.concatenate([w_in[:, :cw], w_in[:, cw : 2 * cw], w_out], axis=0)
    if blank is None:
        blank = jnp.zeros((2 * plan.r - plan.rf, cw), BF16)
    right = jnp.concatenate([w_in[:, 2 * cw :], w_down, blank], axis=0)
    return jnp.concatenate([left, right], axis=1)


def unpack_rest(plan, piece):
    r, rf, cw = plan.r, plan.rf, plan.cw
    parts_in = [piece[:r, :cw], piece[r : 2 * r, :cw], piece[:r, cw:]]
    return parts_in, piece[2 * r : 3 * r, :cw], piece[r : r + rf, cw:]


def join_rest_kernel(plan, meta, *refs):
    pieces, out, held = refs[: plan.nrow], refs[plan.nrow], refs[plan.nrow + 1]
    r, cw = plan.r, plan.cw
    for j in range(plan.nrow):
        held[j] = pieces[j][...]
    for z in range(plan.nrow):
        parts_in, part_out, part_down = unpack_rest(plan, held[meta[plan.at_z + z]])
        out[:r, cw * z : cw * (z + 1)] = part_out
        for i in range(3):
            block, place_at = (3 * z + i) // plan.nrow, (3 * z + i) % plan.nrow
            out[r * (1 + block) : r * (2 + block), cw * place_at : cw * (place_at + 1)] = parts_in[i]
        out[4 * r :, cw * z : cw * (z + 1)] = part_down


def join_rest(plan, meta, pieces):
    if not plan.aligned:
        parts = [unpack_rest(plan, piece) for piece in ordered(plan, meta, pieces)]
        w_in = jnp.concatenate([part for item in parts for part in item[0]], axis=1)
        blocks = [jnp.concatenate([item[1] for item in parts], axis=1)]
        blocks += [w_in[:, D * t : D * (t + 1)] for t in range(3)]
        blocks += [jnp.concatenate([item[2] for item in parts], axis=1)]
        return jnp.concatenate(blocks, axis=0)
    return pl.pallas_call(
        functools.partial(join_rest_kernel, plan),
        in_specs=[SMEM] + [VMEM] * plan.nrow,
        out_specs=VMEM,
        out_shape=shape_of((plan.packed, D), BF16),
        scratch_shapes=[pltpu.VMEM((plan.nrow, 3 * plan.r, 2 * plan.cw), BF16)],
        compiler_params=params(plan, "join_rest"),
        cost_estimate=cost(COSTS["join_rest"]),
        name="join_rest",
    )(meta, *pieces)


def by_block(plan, meta, own, other):
    stacked = jnp.stack(own + other)
    places = meta[plan.at_own : plan.at_other + plan.chips]
    return jnp.zeros_like(stacked).at[places].set(stacked)


def split_blocks(plan, meta, blocks):
    half = plan.chips // 2
    return [
        jnp.take(blocks, meta[plan.at_own + half * i : plan.at_own + half * (i + 1)], axis=0)
        for i in range(4)
    ]


def qkv_sources(plan, meta, own, other):
    if plan.aligned:
        return own + other
    return [by_block(plan, meta, own, other).reshape(D, EXT)]


def rest_sources(plan, meta, own, other):
    if plan.aligned:
        return own + other
    blocks = by_block(plan, meta, own, other)
    r = plan.r
    parts = [blocks[:, r * i : r * (i + 1)].reshape(D, D) for i in range(4)]
    parts.append(blocks[:, 4 * r :].reshape(FF, D))
    return [jnp.concatenate(parts, axis=0)]


def block_size(plan):
    return (plan.r, plan.rf) if plan.aligned else (D, FF)


def block_of(plan, meta, index):
    return meta[plan.at_own + index] if plan.aligned else 0


def rows_at(index, size):
    if isinstance(index, int):
        return pl.ds(index * size, size)
    return pl.ds(pl.multiple_of(index * size, size), size)


class Mover:
    def __init__(self, sems):
        self.sems = sems
        self.used = 0
        self.open = []

    def start(self, source, target):
        copy = pltpu.make_async_copy(source, target, self.sems.at[self.used])
        self.used += 1
        copy.start()
        return copy

    def send(self, source, target):
        self.open.append(self.start(source, target))

    def finish(self):
        for copy in self.open:
            copy.wait()


def wait_all(copies):
    for copy in copies:
        copy.wait()


def qkv_copies(plan, meta, sources, w_ref, sems):
    r, _ = block_size(plan)
    return [
        pltpu.make_async_copy(source, w_ref.at[rows_at(block_of(plan, meta, i), r)], sems.at[i])
        for i, source in enumerate(sources)
    ]


def grad_target(plan, grads, index):
    if not plan.aligned:
        return grads[0]
    half = plan.chips // 2
    return grads[index // half].at[index % half]


def grad_blocks(plan, height, width):
    return [shape_of((plan.chips // 2, height, width), BF16)] * 4


def source_count(plan):
    return 2 * plan.chips if plan.aligned else 1


def qkv_kernel(plan, meta, cos_ref, sin_ref, *refs):
    x_refs = refs[: plan.rows]
    count = source_count(plan)
    sources = refs[plan.rows : plan.rows + count]
    q_ref = refs[plan.rows + count]
    kv_refs = refs[plan.rows + count + 1 : plan.rows + count + 1 + HALVES]
    n_ref, gain_ref, w_ref, sems = refs[plan.rows + count + 1 + HALVES :]
    copies = qkv_copies(plan, meta, sources, w_ref, sems)
    for copy in copies:
        copy.start()
    units = [layer_norm(x_refs[j][0].astype(F32))[0] for j in range(plan.rows)]
    for copy in copies:
        copy.wait()
    gain_ref[...] = w_ref[:, 3 * D :].astype(F32).T[:8, :]
    for j in range(plan.rows):
        n_ref[plan.tok * j : plan.tok * (j + 1), :] = (units[j] * gain_ref[0:1, :]).astype(BF16)
    cosine, sine = cos_ref[...], sin_ref[...]
    normed = n_ref[...]
    queries = dot(normed, w_ref[:, :D], NN)
    q_ref[...] = rotate_all(queries, cosine, sine, 1.0).astype(BF16)
    keys = rotate_all(dot(normed, w_ref[:, D : 2 * D], NN), cosine, sine, 1.0).astype(BF16)
    values = dot(normed, w_ref[:, 2 * D : 3 * D], NN).astype(BF16)
    for h in range(HALVES):
        kv_refs[h][0] = keys[:, HALF * h : HALF * (h + 1)]
        kv_refs[h][1] = values[:, HALF * h : HALF * (h + 1)]


def project(plan, meta, cosine, sine, pieces, sources):
    local = plan.local
    count = len(sources)
    inputs = [meta, cosine, sine, *pieces, *sources]
    return pl.pallas_call(
        functools.partial(qkv_kernel, plan),
        in_specs=[SMEM, VMEM, VMEM] + [VMEM] * plan.rows + [ANY] * count,
        out_specs=[VMEM] * (3 + HALVES),
        out_shape=[shape_of((local, D), BF16)]
        + [shape_of((2, local, HALF), BF16)] * HALVES
        + [shape_of((local, D), BF16), shape_of((8, D), F32)],
        scratch_shapes=[pltpu.VMEM((D, EXT), BF16), pltpu.SemaphoreType.DMA((count,))],
        compiler_params=params(plan, "project"),
        cost_estimate=cost(COSTS["project"]),
        name="project",
    )(*inputs)


def fill_docs(plan, meta, lengths, kmask, qmask):
    low = meta[plan.at_lo]
    ends = []
    passed = jnp.int32(0)
    for n in range(NDOC):
        passed = passed + lengths[low, n]
        ends.append(passed)

    tok = plan.tok
    lane = lax.broadcasted_iota(jnp.int32, (tok, 128), 1) & (HD - 1)
    for i in range(plan.groups * plan.rows):
        places = meta[plan.at_base + i] + lax.broadcasted_iota(jnp.int32, (tok, 128), 0)
        docs = jnp.zeros((tok, 128), jnp.int32)
        for end in ends:
            docs = docs + (places >= end).astype(jnp.int32)
        part = slice(i * tok, (i + 1) * tok)
        same = docs == lane
        kmask[part, :] = jnp.where((lane < NDOC) & ~same, MASKED, 0.0).astype(BF16)
        if i < plan.rows:
            qmask[part, :] = jnp.where(same, 1.0, 0.0).astype(BF16)


def masks(plan, meta, lengths):
    keys = plan.groups * plan.local
    return pl.pallas_call(
        functools.partial(fill_docs, plan),
        in_specs=[SMEM, SMEM],
        out_specs=[VMEM, VMEM],
        out_shape=[shape_of((keys, 128), BF16), shape_of((plan.local, 128), BF16)],
        compiler_params=params(plan, "masks"),
        cost_estimate=cost(1),
        name="masks",
    )(meta, lengths)


def head_part(pair, head, other=None):
    keep = (lax.broadcasted_iota(jnp.int32, pair.shape, 1) // HD) == head
    return jnp.where(keep, pair, jnp.zeros_like(pair) if other is None else other)


def attend_kernel(plan, width, order, kmask, qmask, q_ref, *refs):
    groups, local = plan.groups, plan.local
    kv = refs[:groups]
    o_ref, low_ref, lse_ref, s_ref, p_ref = refs[groups:]
    total_keys = groups * local
    chunk = 128
    values_t = []
    row = lax.broadcasted_iota(jnp.int32, (HD + 8, total_keys), 0)
    pair_t = jnp.concatenate([kv[e][1].T for e in range(groups)], axis=1)
    for h in range(2):
        head = pair_t[h * HD : (h + 1) * HD, :]
        values_t.append(jnp.concatenate([head, jnp.ones((8, total_keys), BF16)], axis=0))
    for first in range(0, local, width):
        rows = slice(first, first + width)
        queries = q_ref[rows, :] * jnp.asarray(1.0 / math.sqrt(HD), BF16)
        tops = []
        for h in range(2):
            head_queries = head_part(queries, h, qmask[rows, :])
            top = jnp.full((8, width), MASKED, F32)
            for e in range(groups):
                for c in range(0, local, 2 * chunk):
                    part = slice(e * local + c, e * local + c + 2 * chunk)
                    keys = head_part(kv[e][0, c : c + 2 * chunk, :], h, kmask[part, :])
                    scores = dot(keys, head_queries, NT)
                    s_ref[h, part, :] = scores
                    top = jnp.maximum(top, jnp.max(scores.reshape(-1, 8, width), axis=0))
            tops.append(jnp.max(top, axis=0, keepdims=True))
        parts = []
        for h in range(2):
            for c in range(0, total_keys, chunk):
                part = slice(c, c + chunk)
                p_ref[h, part, :] = jnp.exp(s_ref[h, part, :] - tops[h]).astype(BF16)
            weighted = dot(values_t[h], p_ref[h], NN)
            total = weighted[HD : HD + 1, :]
            parts.append(weighted[:HD, :] / total)
            lse_ref[0, h : h + 1, rows] = tops[h] + jnp.log(total)
        heads = jnp.concatenate(parts, axis=0).T
        o_ref[rows, :] = heads
        low_ref[rows, :] = heads.astype(BF16)


def attend(plan, part, meta, mask, queries, kv):
    local, groups = plan.local, plan.groups
    width = min(512, local)
    skip = part * HALF_PAIRS
    pair = pl.BlockSpec((local, 128), lambda p: (0, p))
    pair_q = pl.BlockSpec((local, 128), lambda p: (0, p + skip))
    pair_kv = pl.BlockSpec((2, local, 128), lambda p: (0, 0, p))
    whole_k = pl.BlockSpec((groups * local, 128), lambda p: (0, 0))
    whole_q = pl.BlockSpec((local, 128), lambda p: (0, 0))
    inputs = [meta, *mask, queries, *kv]
    return pl.pallas_call(
        functools.partial(attend_kernel, plan, width),
        grid=(HALF_PAIRS,),
        in_specs=[SMEM, whole_k, whole_q, pair_q] + [pair_kv] * groups,
        out_specs=[pair, pair, pl.BlockSpec((1, 2, local), lambda p: (p, 0, 0))],
        out_shape=[
            shape_of((local, HALF), F32),
            shape_of((local, HALF), BF16),
            shape_of((HALF_PAIRS, 2, local), F32),
        ],
        scratch_shapes=[
            pltpu.VMEM((2, groups * local, width), F32),
            pltpu.VMEM((2, groups * local, width), BF16),
        ],
        compiler_params=params(plan, "attend"),
        cost_estimate=cost(COSTS["attend"]),
        name="attend",
    )(*inputs)


def attend_back_kernel(
    plan, width, order, kmask, qmask, q_ref, do_ref, o_ref, lse_ref, cos_ref, sin_ref, *refs
):
    groups, local = plan.groups, plan.local
    kv = refs[:groups]
    dq_ref = refs[groups]
    dkv = refs[groups + 1 : 2 * groups + 1]
    held, p_ref, ds_ref, keys_t, product, grad_t = refs[2 * groups + 1 :]
    for e in range(groups):
        keys_t[e] = kv[e][0].T
    held[...] = jnp.zeros_like(held)
    scale = 1.0 / math.sqrt(HD)
    chunk = 128
    for first in range(0, local, width):
        rows = slice(first, first + width)
        product[...] = (do_ref[rows, :].astype(F32) * o_ref[rows, :]).T

        @pl.loop(0, 2)
        def _(h):
            head = pl.ds(pl.multiple_of(h * HD, HD), HD)
            queries = q_ref[rows, :] * jnp.asarray(scale, BF16)
            masked_queries = head_part(queries, h, qmask[rows, :])
            head_queries = head_part(queries, h)
            head_dout = head_part(do_ref[rows, :], h)
            lse = lse_ref[0, pl.ds(h, 1), rows]
            delta = jnp.sum(product[head, :], axis=0, keepdims=True)
            grad_queries = jnp.zeros((HD, width), F32)
            for e in range(groups):
                for c in range(0, local, chunk):
                    part = slice(c, c + chunk)
                    mask = kmask[e * local + c : e * local + c + chunk, :]
                    scores = dot(head_part(kv[e][0, part, :], h, mask), masked_queries, NT)
                    dprobs = dot(kv[e][1, part, :], head_dout, NT)
                    probs = jnp.exp(scores - lse)
                    p_ref[e, part, :] = probs.astype(BF16)
                    ds_ref[e, part, :] = (probs * (dprobs - delta)).astype(BF16)
                held[e, 0] += dot(ds_ref[e], head_queries, NN)
                held[e, 1] += dot(p_ref[e], head_dout, NN)
                grad_queries = grad_queries + dot(keys_t[e, head, :], ds_ref[e], NN)
            grad_t[head, :] = grad_queries

        grad = grad_t[...].T * scale
        dq_ref[rows, :] = rotate_pair(grad, cos_ref[rows, :], sin_ref[rows, :], -1.0).astype(BF16)
    for e in range(groups):
        dkv[e][...] = held[e].astype(BF16)


def attend_back(plan, part, meta, mask, queries, dout, heads, lse, cosine, sine, kv):
    local, groups = plan.local, plan.groups
    width = min(512, local)
    half, first, count = part
    skip = half * HALF_PAIRS + first
    wide = 128 * count
    pair = pl.BlockSpec((local, 128), lambda p: (0, p))
    pair_h = pl.BlockSpec((local, 128), lambda p: (0, p + first))
    pair_q = pl.BlockSpec((local, 128), lambda p: (0, p + skip))
    whole_k = pl.BlockSpec((groups * local, 128), lambda p: (0, 0))
    inputs = [meta, *mask, queries, dout, heads, lse, cosine, sine, *kv]
    table = pl.BlockSpec((local, 128), lambda p: (0, 0))
    pair_kv = pl.BlockSpec((2, local, 128), lambda p: (0, 0, p))
    pair_kv_h = pl.BlockSpec((2, local, 128), lambda p: (0, 0, p + first))
    return pl.pallas_call(
        functools.partial(attend_back_kernel, plan, width),
        grid=(count,),
        in_specs=[
            SMEM,
            whole_k,
            table,
            pair_q,
            pair_q,
            pair_h,
            pl.BlockSpec((1, 2, local), lambda p: (p + first, 0, 0)),
            table,
            table,
        ]
        + [pair_kv_h] * groups,
        out_specs=[pair] + [pair_kv] * groups,
        out_shape=[shape_of((local, wide), BF16)] + [shape_of((2, local, wide), BF16)] * groups,
        scratch_shapes=[
            pltpu.VMEM((groups, 2, local, 128), F32),
            pltpu.VMEM((groups, local, width), BF16),
            pltpu.VMEM((groups, local, width), BF16),
            pltpu.VMEM((groups, 128, local), BF16),
            pltpu.VMEM((128, width), F32),
            pltpu.VMEM((128, width), F32),
        ],
        compiler_params=params(plan, "attend_back"),
        cost_estimate=cost(4 * count),
        name="attend_back",
    )(*inputs)


def middle_kernel(plan, meta, gain_ref, *refs):
    rows, tok, local = plan.rows, plan.tok, plan.local
    count = source_count(plan)
    low_refs, refs = refs[:HALVES], refs[HALVES:]
    x_refs, refs = refs[:rows], refs[rows:]
    sources, refs = refs[:count], refs[count:]
    out_refs, refs = refs[:rows], refs[rows:]
    do_out, dh_out, refs = refs[0], refs[1], refs[2:]
    grads, refs = refs[: 4 if plan.aligned else 1], refs[4 if plan.aligned else 1 :]
    low_ref, x_ref, dy_ref, w_out, w_in, w_down, h_ref, unit_ref, n_ref, gu_ref = refs[:10]
    mid_ref, dgu_ref, out_ref, do_ref, dh_ref, da_ref, inv_ref, g_out, g_in, g_down, sems = refs[10:]
    mover = Mover(sems)
    r, rf = block_size(plan)
    blocks = [block_of(plan, meta, i) for i in range(count)]
    low_in = [
        mover.start(low_refs[h], low_ref.at[:, pl.ds(HALF * h, HALF)]) for h in range(HALVES)
    ]
    out_in = [
        mover.start(source.at[pl.ds(0, r)], w_out.at[rows_at(block, r)])
        for source, block in zip(sources, blocks)
    ]
    x_in = [mover.start(x_refs[j].at[0], x_ref.at[pl.ds(tok * j, tok)]) for j in range(rows)]

    def fetch_in(t):
        return [
            mover.start(source.at[pl.ds((1 + t) * r, r)], w_in.at[t, rows_at(block, r)])
            for source, block in zip(sources, blocks)
        ]

    in_in = [fetch_in(t) for t in range(3)]
    dy_in = [mover.start(x_refs[j].at[1], dy_ref.at[pl.ds(tok * j, tok)]) for j in range(rows)]
    down_in = [
        mover.start(source.at[pl.ds(4 * r, rf)], w_down.at[rows_at(block, rf)])
        for source, block in zip(sources, blocks)
    ]
    wait_all(low_in)
    wait_all(out_in)
    wait_all(x_in)
    gain = gain_ref[1:2, :]

    h_ref[...] = x_ref[...].astype(F32) + dot(low_ref[...], w_out[...], NN)
    unit, inv_std = layer_norm(h_ref[...])
    unit_ref[...] = unit
    inv_ref[...] = jnp.broadcast_to(inv_std, (local, 128))
    n_ref[...] = (unit * gain).astype(BF16)

    for t in range(3):
        wait_all(in_in[t])

    @pl.loop(0, 3)
    def _(t):
        gu_ref[:, pl.ds(pl.multiple_of(t * D, D), D)] = dot(n_ref[...], w_in[t], NN)

    wait_all(dy_in)
    wait_all(down_in)
    size = FF // 3

    @pl.loop(0, 3)
    def _(f):
        cols = pl.ds(pl.multiple_of(f * size, size), size)
        up_cols = pl.ds(pl.multiple_of(FF + f * size, size), size)
        gate = gu_ref[:, cols]
        up = gu_ref[:, up_cols]
        below = 0.5 + 0.5 * lax.erf(gate * math.sqrt(0.5))
        active = gate * below
        mid_ref[:, cols] = (active * up).astype(BF16)
        slope = below + gate * jnp.exp(-0.5 * gate * gate) * (1.0 / math.sqrt(2.0 * math.pi))
        dmid = dot(dy_ref[...], w_down[cols, :], NT)
        dgu_ref[:, cols] = (dmid * up * slope).astype(BF16)
        dgu_ref[:, up_cols] = (dmid * active).astype(BF16)
        g_down[cols, :] = dot(mid_ref[:, cols], dy_ref[...], TN).astype(BF16)

    targets = [grad_target(plan, grads, i) for i in range(count)]
    for target, block in zip(targets, blocks):
        mover.send(g_down.at[rows_at(block, rf)], target.at[pl.ds(4 * r, rf)])
    step = D // 3

    @pl.loop(0, 3)
    def _(n):
        cols = pl.ds(pl.multiple_of(n * step, step), step)
        mixed = dot(mid_ref[...], w_down[:, cols], NN)
        out_ref[:, cols] = (h_ref[:, cols] + mixed).astype(BF16)
        grad = dot(dgu_ref[:, :D], w_in[0, cols, :], NT)
        for t in range(1, 3):
            grad = grad + dot(dgu_ref[:, D * t : D * (t + 1)], w_in[t, cols, :], NT)
        dh_ref[:, cols] = grad
        g_in[n] = dot(
            n_ref[...], dgu_ref[:, pl.ds(pl.multiple_of(n * D, D), D)], TN
        ).astype(BF16)
    for j in range(rows):
        mover.send(out_ref.at[pl.ds(tok * j, tok)], out_refs[j])

    for t in range(3):
        for target, block in zip(targets, blocks):
            mover.send(g_in.at[t, rows_at(block, r)], target.at[pl.ds((1 + t) * r, r)])

    grad_hidden = dy_ref[...].astype(F32) + norm_backward(
        dh_ref[...], unit_ref[...], inv_ref[:, 0:1], gain
    )
    dh_ref[...] = grad_hidden
    da_ref[...] = grad_hidden.astype(BF16)
    mover.send(dh_ref, dh_out)
    do_ref[...] = dot(da_ref[...], w_out[...], NT).astype(BF16)
    g_out[...] = dot(low_ref[...], da_ref[...], TN).astype(BF16)

    mover.send(do_ref, do_out)
    for target, block in zip(targets, blocks):
        mover.send(g_out.at[rows_at(block, r)], target.at[pl.ds(0, r)])
    mover.finish()


def middle(plan, meta, low, gains, pieces, sources):
    local, rows, tok = plan.local, plan.rows, plan.tok
    count = len(sources)
    total = 4 * D + FF
    if plan.aligned:
        grads = grad_blocks(plan, plan.packed, D)
    else:
        grads = [shape_of((total, D), BF16)]
    return pl.pallas_call(
        functools.partial(middle_kernel, plan),
        in_specs=[SMEM, VMEM] + [ANY] * (HALVES + rows + count),
        out_specs=[ANY] * (rows + 2 + len(grads)),
        out_shape=[shape_of((tok, D), BF16)] * rows
        + [shape_of((local, D), BF16), shape_of((local, D), F32)]
        + grads,
        scratch_shapes=[
            pltpu.VMEM((local, D), BF16),
            pltpu.VMEM((local, D), BF16),
            pltpu.VMEM((local, D), BF16),
            pltpu.VMEM((D, D), BF16),
            pltpu.VMEM((3, D, D), BF16),
            pltpu.VMEM((FF, D), BF16),
            pltpu.VMEM((local, D), F32),
            pltpu.VMEM((local, D), F32),
            pltpu.VMEM((local, D), BF16),
            pltpu.VMEM((local, 2 * FF), F32),
            pltpu.VMEM((local, FF), BF16),
            pltpu.VMEM((local, 2 * FF), BF16),
            pltpu.VMEM((local, D), BF16),
            pltpu.VMEM((local, D), BF16),
            pltpu.VMEM((local, D), F32),
            pltpu.VMEM((local, D), BF16),
            pltpu.VMEM((local, 128), F32),
            pltpu.VMEM((D, D), BF16),
            pltpu.VMEM((3, D, D), BF16),
            pltpu.VMEM((FF, D), BF16),
            pltpu.SemaphoreType.DMA((HALVES + 3 * rows + 2 + 10 * count,)),
        ],
        compiler_params=params(plan, "middle"),
        cost_estimate=cost(COSTS["middle"]),
        name="middle",
    )(meta, gains, *low, *pieces, *sources)


def back_weight_kernel(plan, meta, *refs):
    groups, local = plan.groups, plan.local
    count = len(BACK_PARTS)
    cos_ref, sin_ref, n_in, refs = refs[0], refs[1], refs[2], refs[3:]
    dq_refs, refs = refs[:count], refs[count:]
    dkv, refs = refs[: count * groups], refs[count * groups :]
    dp_out, refs = refs[0], refs[1:]
    grads, refs = refs[: 4 if plan.aligned else 1], refs[4 if plan.aligned else 1 :]
    cos, sin, n_ref, dkv_ref, dp_ref, g_ref, sems = refs
    mover = Mover(sems)
    columns = []
    for half, first, pairs in BACK_PARTS:
        columns.append(pl.ds(HALF * half + 128 * first, 128 * pairs))
    first_in = [mover.start(n_in, n_ref)]
    for i in range(count):
        first_in.append(mover.start(dq_refs[i], dp_ref.at[0, :, columns[i]]))
    rest_in = [mover.start(cos_ref, cos), mover.start(sin_ref, sin)]
    for i in range(count):
        for e in range(groups):
            rest_in.append(
                mover.start(dkv[groups * i + e], dkv_ref.at[e, :, :, columns[i]])
            )
    r, _ = block_size(plan)

    def send_grad(t):
        cols = pl.ds(D * t, D)
        for i in range(source_count(plan)):
            at = rows_at(block_of(plan, meta, i), r)
            mover.send(g_ref.at[at, cols], grad_target(plan, grads, i).at[:, cols])

    wait_all(first_in)
    normed = n_ref[...]
    g_ref[:, :D] = dot(normed, dp_ref[0], TN).astype(BF16)
    send_grad(0)
    wait_all(rest_in)
    dp_ref[2] = sum_pieces([dkv_ref[e, 1] for e in range(groups)]).astype(BF16)
    g_ref[:, 2 * D : 3 * D] = dot(normed, dp_ref[2], TN).astype(BF16)
    send_grad(2)
    grad_keys = sum_pieces([dkv_ref[e, 0] for e in range(groups)])
    dp_ref[1] = rotate_all(grad_keys, cos[...], sin[...], -1.0).astype(BF16)
    mover.send(dp_ref, dp_out)
    g_ref[:, D : 2 * D] = dot(normed, dp_ref[1], TN).astype(BF16)
    send_grad(1)
    mover.finish()


def back_weight(plan, meta, cosine, sine, normed, dq, dkv):
    local, groups, count = plan.local, plan.groups, len(BACK_PARTS)
    if plan.aligned:
        grads = grad_blocks(plan, plan.r, 3 * D)
    else:
        grads = [shape_of((D, 3 * D), BF16)]
    results = pl.pallas_call(
        functools.partial(back_weight_kernel, plan),
        in_specs=[SMEM] + [ANY] * (3 + count * (1 + groups)),
        out_specs=[ANY] * (1 + len(grads)),
        out_shape=[shape_of((3, local, D), BF16)] + grads,
        scratch_shapes=[
            pltpu.VMEM((local, 128), F32),
            pltpu.VMEM((local, 128), F32),
            pltpu.VMEM((local, D), BF16),
            pltpu.VMEM((groups, 2, local, D), BF16),
            pltpu.VMEM((3, local, D), BF16),
            pltpu.VMEM((D, 3 * D), BF16),
            pltpu.SemaphoreType.DMA((4 + count * (1 + groups) + 3 * source_count(plan),)),
        ],
        compiler_params=params(plan, "back_weight"),
        cost_estimate=cost(COSTS["back_weight"]),
        name="back_weight",
    )(meta, cosine, sine, normed, *dq, *dkv)
    return results[0], results[1:]


def back_in_kernel(plan, meta, dp_ref, dh_ref, gain_ref, *refs):
    rows, tok = plan.rows, plan.tok
    count = source_count(plan)
    x_refs, refs = refs[:rows], refs[rows:]
    out_refs, refs = refs[:rows], refs[rows:]
    sources, refs = refs[:count], refs[count:]
    both_refs = refs[:rows]
    w_ref, in_sems = refs[rows:]
    copies = qkv_copies(plan, meta, sources, w_ref, in_sems)
    for copy in copies:
        copy.start()
    for copy in copies:
        copy.wait()
    grad_normed = dot(dp_ref[0], w_ref[:, :D], NT)
    for t in range(1, 3):
        grad_normed = grad_normed + dot(dp_ref[t], w_ref[:, D * t : D * (t + 1)], NT)
    for j in range(rows):
        part = slice(tok * j, tok * (j + 1))
        unit, inv_std = layer_norm(x_refs[j][0].astype(F32))
        grad = grad_normed[part, :]
        back = norm_backward(grad, unit, inv_std, gain_ref[0:1, :])
        both_refs[j][0] = out_refs[j][...]
        both_refs[j][1] = (dh_ref[part, :] + back).astype(BF16)


def back_in(plan, meta, dprojected, dhidden, gains, pieces, outs, sources):
    rows, tok = plan.rows, plan.tok
    count = len(sources)
    return pl.pallas_call(
        functools.partial(back_in_kernel, plan),
        in_specs=[SMEM] + [VMEM] * (3 + 2 * rows) + [ANY] * count,
        out_specs=[VMEM] * rows,
        out_shape=[shape_of((2, tok, D), BF16)] * rows,
        scratch_shapes=[pltpu.VMEM((D, EXT), BF16), pltpu.SemaphoreType.DMA((count,))],
        compiler_params=params(plan, "back_in"),
        cost_estimate=cost(COSTS["back_in"]),
        name="back_in",
    )(meta, dprojected, dhidden, gains, *pieces, *outs, *sources)


def gain_columns(weight, grad):
    total = jnp.sum(weight.astype(F32) * grad.astype(F32), axis=1, keepdims=True)
    high = total.astype(BF16)
    return high, (total - high.astype(F32)).astype(BF16)


def pad_width(plan):
    return -(-(3 * plan.cw + 2) // 128) * 128


def gain_tail(plan, weight, grad):
    width = pad_width(plan) - 3 * plan.cw
    high, rest = gain_columns(weight, grad)
    lane = lax.broadcasted_iota(jnp.int32, (plan.r, width), 1)
    return jnp.where(lane == 0, high, jnp.where(lane == 1, rest, jnp.zeros_like(high)))


def cut_qkv_kernel(plan, meta, total, weight, *refs):
    outs, held = refs[: plan.nrow], refs[plan.nrow]
    width = 3 * plan.cw
    tail = gain_tail(plan, weight[:, : 3 * D], total[...])
    for z in range(plan.nrow):
        place_at = meta[plan.at_z + z]
        held[place_at, :, :width] = total[:, width * z : width * (z + 1)]
        held[place_at, :, width:] = tail
    for j in range(plan.nrow):
        outs[j][...] = held[j]


def cut_qkv(plan, meta, total, weight):
    width, wide = 3 * plan.cw, pad_width(plan)
    if not plan.aligned:
        tail = gain_tail(plan, weight[:, : 3 * D], total)
        parts = [
            jnp.concatenate([total[:, width * z : width * (z + 1)], tail], axis=1)
            for z in range(plan.nrow)
        ]
        return ordered(plan, meta, parts)
    return pl.pallas_call(
        functools.partial(cut_qkv_kernel, plan),
        in_specs=[SMEM, VMEM, VMEM],
        out_specs=[VMEM] * plan.nrow,
        out_shape=[shape_of((plan.r, wide), BF16)] * plan.nrow,
        scratch_shapes=[pltpu.VMEM((plan.nrow, plan.r, wide), BF16)],
        compiler_params=params(plan, "cut_qkv"),
        cost_estimate=cost(COSTS["cut_qkv"]),
        name="cut_qkv",
    )(meta, total, weight)


def gain_blank(plan, weight, grad):
    r, blank = plan.r, 2 * plan.r - plan.rf
    cols = [weight[r * t : r * (t + 1)] for t in range(1, 4)]
    grads = [grad[r * t : r * (t + 1)] for t in range(1, 4)]
    high, rest = gain_columns(jnp.concatenate(cols, axis=1), jnp.concatenate(grads, axis=1))
    lane = lax.broadcasted_iota(jnp.int32, (blank, plan.cw), 1)
    found = jnp.zeros((blank, plan.cw), BF16)
    for i in range(r // blank):
        part = slice(blank * i, blank * (i + 1))
        found = jnp.where(lane == 2 * i, high[part], found)
        found = jnp.where(lane == 2 * i + 1, rest[part], found)
    return found


def cut_rest_kernel(plan, meta, total, weight, *refs):
    outs, held = refs[: plan.nrow], refs[plan.nrow]
    r, rf, cw = plan.r, plan.rf, plan.cw
    blank = gain_blank(plan, weight[...], total[...])
    for z in range(plan.nrow):
        place_at = meta[plan.at_z + z]
        cols = slice(cw * z, cw * (z + 1))
        parts = []
        for i in range(3):
            block, at = (3 * z + i) // plan.nrow, (3 * z + i) % plan.nrow
            parts.append(total[r * (1 + block) : r * (2 + block), cw * at : cw * (at + 1)])
        held[place_at, :r, :] = jnp.concatenate([parts[0], parts[2]], axis=1)
        held[place_at, r : 2 * r, :] = jnp.concatenate(
            [parts[1], total[4 * r : 5 * r, cols]], axis=1
        )
        rest = total[5 * r : 4 * r + rf, cols]
        held[place_at, 2 * r :, :] = jnp.concatenate(
            [total[:r, cols], jnp.concatenate([rest, blank], axis=0)], axis=1
        )
    for j in range(plan.nrow):
        outs[j][...] = held[j]


def cut_rest(plan, meta, total, weight):
    r, cw = plan.r, plan.cw
    if not plan.aligned:
        grad_in = jnp.concatenate([total[r * (1 + t) : r * (2 + t)] for t in range(3)], axis=1)
        blank = gain_blank(plan, weight, total)
        parts = [
            pack_rest(
                plan,
                total[:r, cw * z : cw * (z + 1)],
                grad_in[:, 3 * cw * z : 3 * cw * (z + 1)],
                total[4 * r :, cw * z : cw * (z + 1)],
                blank,
            )
            for z in range(plan.nrow)
        ]
        return ordered(plan, meta, parts)
    return pl.pallas_call(
        functools.partial(cut_rest_kernel, plan),
        in_specs=[SMEM, VMEM, VMEM],
        out_specs=[VMEM] * plan.nrow,
        out_shape=[shape_of((3 * r, 2 * cw), BF16)] * plan.nrow,
        scratch_shapes=[pltpu.VMEM((plan.nrow, 3 * r, 2 * cw), BF16)],
        compiler_params=params(plan, "cut_rest"),
        cost_estimate=cost(COSTS["cut_rest"]),
        name="cut_rest",
    )(meta, total, weight)


def reduce_z(plan, pieces):
    return [pieces[0]] + [
        lax.ppermute(pieces[j], "row", plan.z_pairs(j)) for j in range(1, plan.nrow)
    ]


def sum_pieces(pieces):
    total = pieces[0].astype(F32)
    for piece in pieces[1:]:
        total = total + piece.astype(F32)
    return total


def end_rest_kernel(plan, *refs):
    pieces, (g_out, g_in, g_down, g_gain) = refs[: plan.nrow], refs[plan.nrow :]
    total = sum_pieces([piece[...] for piece in pieces])
    parts_in, part_out, part_down = unpack_rest(plan, total)
    g_out[...] = part_out
    g_in[...] = jnp.concatenate(parts_in, axis=1)
    g_down[...] = part_down
    blank = 2 * plan.r - plan.rf
    g_gain[...] = total[3 * plan.r - blank :, plan.cw : plan.cw + 128].T[:8, :]


def end_rest(plan, pieces):
    r, blank = plan.r, 2 * plan.r - plan.rf
    if not plan.aligned:
        total = sum_pieces(pieces)
        parts_in, out_grad, down_grad = unpack_rest(plan, total)
        in_grad = jnp.concatenate(parts_in, axis=1)
        gain = total[3 * r - blank :, plan.cw : plan.cw + 8].T
    else:
        out_grad, in_grad, down_grad, gain = pl.pallas_call(
            functools.partial(end_rest_kernel, plan),
            in_specs=[VMEM] * plan.nrow,
            out_specs=[VMEM] * 4,
            out_shape=[
                shape_of((r, plan.cw), F32),
                shape_of((r, 3 * plan.cw), F32),
                shape_of((plan.rf, plan.cw), F32),
                shape_of((8, blank), F32),
            ],
            compiler_params=params(plan, "end_rest"),
            cost_estimate=cost(COSTS["end_rest"]),
            name="end_rest",
        )(*pieces)
    gain = jnp.concatenate([gain[2 * i] + gain[2 * i + 1] for i in range(r // blank)])
    return out_grad, in_grad, down_grad, gain


def end_qkv_kernel(plan, gain_ref, *refs):
    pieces, (g_qkv, g_gain) = refs[: plan.nrow], refs[plan.nrow :]
    width, wide = 3 * plan.cw, pad_width(plan)
    total = sum_pieces([piece[...] for piece in pieces])
    g_qkv[...] = total[:, :width]
    tail = total[:, wide - 128 :].T
    at = width - (wide - 128)
    g_gain[...] = (tail[at : at + 1, :] + tail[at + 1 : at + 2, :]) / gain_ref[...]


def end_qkv(plan, gain, pieces):
    width, wide = 3 * plan.cw, pad_width(plan)
    if not plan.aligned:
        total = sum_pieces(pieces)
        return total[:, :width], (total[:, width] + total[:, width + 1]) / gain[0]
    grad, gain_grad = pl.pallas_call(
        functools.partial(end_qkv_kernel, plan),
        in_specs=[VMEM] * (1 + plan.nrow),
        out_specs=[VMEM] * 2,
        out_shape=[shape_of((plan.r, width), F32), shape_of((1, plan.r), F32)],
        compiler_params=params(plan, "end_qkv"),
        cost_estimate=cost(COSTS["end_qkv"]),
        name="end_qkv",
    )(gain, *pieces)
    return grad, gain_grad.reshape(plan.r)


def rotation_tables(plan, meta, lengths):
    ends = jnp.cumsum(lax.dynamic_index_in_dim(lengths, meta[plan.at_lo], 0, keepdims=False))
    starts = jnp.concatenate([jnp.zeros((1,), jnp.int32), ends[:-1]])
    bases = meta[plan.at_base : plan.at_base + plan.rows]
    places = (bases[:, None] + jnp.arange(plan.tok, dtype=jnp.int32)[None, :]).reshape(-1)
    passed = places[:, None] >= starts[None, :]
    positions = places - jnp.max(jnp.where(passed, starts[None, :], 0), axis=1)
    half = HD // 2
    inverse = ROPE_BASE ** (-(jnp.arange(half, dtype=F32) * (2.0 / HD)))
    angles = positions.astype(F32)[:, None] * inverse
    cosine, sine = jnp.cos(angles), jnp.sin(angles)
    return (
        jnp.concatenate([cosine] * 4, axis=1),
        jnp.concatenate([-sine, sine, -sine, sine], axis=1),
    )


def body(
    plan,
    tokens,
    lengths,
    norm_gain,
    qkv_weight,
    out_weight,
    mlp_gain,
    in_weight,
    down_weight,
    cotangent,
):
    blk, row = lax.axis_index("blk"), lax.axis_index("row")
    meta = lax.dynamic_slice(
        jnp.asarray(plan.table), (row, blk, 0), (1, 1, plan.size)
    ).reshape(plan.size)
    qkv_parts = gather_z(plan, qkv_weight)
    cut, packed = prepare(plan, meta, tokens, cotangent, out_weight, in_weight, down_weight)
    pieces = exchange_rows(plan, cut)
    rest_parts = gather_z(plan, packed, behind=qkv_parts)
    gains = jnp.pad(jnp.stack([norm_gain, mlp_gain], axis=1), ((0, 0), (0, 126)))
    cosine, sine = rotation_tables(plan, meta, lengths)
    mask = masks(plan, meta, lengths)
    qkv_joined = join_qkv(plan, meta, gains, qkv_parts)
    qkv_own = gather_start(plan, qkv_joined, pieces[1:])
    qkv_own[1] = tie(qkv_own[1], *rest_parts[2:], cosine, sine, *mask)
    qkv_own = gather_more(plan, qkv_own)
    qkv_own[-1] = tie(qkv_own[-1], rest_parts[1])
    qkv_other = [swap_cores(plan, piece) for piece in qkv_own]
    qkv_from = qkv_sources(plan, meta, qkv_own, qkv_other)
    rest_parts[0] = tie(rest_parts[0], qkv_joined, *qkv_other[:-1])
    joined = join_rest(plan, meta, rest_parts)
    results = project(plan, tie(meta, joined), cosine, sine, pieces, qkv_from)
    queries, kv, (normed, gains) = results[0], results[1 : 1 + HALVES], results[1 + HALVES :]
    kv = [
        [part]
        + [
            lax.ppermute(part, "blk", plan.xor_pairs(plan.member(e)))
            for e in range(1, plan.groups)
        ]
        for part in kv
    ]
    rest_own = gather_start(plan, joined)
    heads, low, lse = [None] * HALVES, [None] * HALVES, [None] * HALVES
    heads[0], low[0], lse[0] = attend(plan, 0, meta, mask, queries, kv[0])
    order = tie(meta, low[0], *rest_own[1:])
    rest_own[1:] = [tie(piece, low[0]) for piece in rest_own[1:]]
    rest_other = [swap_cores(plan, piece) for piece in rest_own]
    rest_more = gather_more(plan, rest_own)[len(rest_own) :]
    heads[1], low[1], lse[1] = attend(plan, 1, order, mask, queries, kv[1])
    rest_more = [tie(piece, low[1]) for piece in rest_more]
    rest_own = rest_own + rest_more
    rest_other = rest_other + [swap_cores(plan, piece) for piece in rest_more]
    rest_from = rest_sources(plan, meta, rest_own, rest_other)
    results = middle(plan, meta, low, gains, pieces, rest_from)
    outs, (dout, dhidden), rest_grads = (
        results[: plan.rows],
        results[plan.rows : plan.rows + 2],
        results[plan.rows + 2 :],
    )
    if not plan.aligned:
        r, rf, nblk = plan.r, plan.rf, plan.nblk
        whole = rest_grads[0]
        blocks = [whole[D * i : D * (i + 1)].reshape(nblk, r, D) for i in range(4)]
        blocks.append(whole[4 * D :].reshape(nblk, rf, D))
        rest_grads = split_blocks(plan, meta, jnp.concatenate(blocks, axis=1))
    keep_low, keep_high, other_low, other_high = reduce_start(plan, rest_grads)
    dq, dkv = [], []
    order = meta
    for i, part in enumerate(BACK_PARTS):
        half = part[0]
        results = attend_back(
            plan, part, order, mask, queries, dout, heads[half], lse[half], cosine, sine, kv[half]
        )
        dq.append(results[0])
        dkv.append(results[1])
        dkv += [
            lax.ppermute(results[1 + e], "blk", plan.xor_pairs(plan.member(e)))
            for e in range(1, plan.groups)
        ]
        if i == 0:
            rest_high = add_low(tie(keep_high, dq[0]), other_high)
            rest_low = add_low(tie(keep_low, dq[0]), other_low)
            order = tie(meta, dq[0], rest_high, rest_low)
        else:
            order = tie(meta, dq[i], *dkv[1 : plan.groups])
    rest_low, rest_high = reduce_step(plan, plan.bits - 1, tie(rest_low, dq[-1]), rest_high)
    order = tie(meta, rest_low) if rest_high is None else tie(meta, rest_low, rest_high)
    dprojected, qkv_grads = back_weight(plan, order, cosine, sine, normed, dq, dkv)
    if not plan.aligned:
        qkv_grads = split_blocks(plan, meta, qkv_grads[0].reshape(plan.nblk, plan.r, 3 * D))
    rest_low = tie(rest_low, dprojected)
    for step in reversed(range(plan.bits - 1)):
        rest_low, rest_high = reduce_step(plan, step, rest_low, rest_high)
    keep_low, keep_high, other_low, other_high = reduce_start(plan, qkv_grads)
    qkv_high = add_low(tie(keep_high, rest_low), other_high)
    qkv_low = add_low(keep_low, other_low)
    rest_cut = cut_rest(plan, meta, tie(rest_low, qkv_high), joined)
    order = tie(meta, qkv_high, qkv_low, *rest_cut)
    both = back_in(plan, order, dprojected, dhidden, gains, pieces, outs, qkv_from)
    rest_pieces = reduce_z(plan, rest_cut)
    qkv_low = tie(qkv_low, both[0], *rest_pieces[1:3])
    for step in reversed(range(plan.bits)):
        if step == 0:
            both = [tie(piece, qkv_high) for piece in both]
        qkv_low, qkv_high = reduce_step(plan, step, qkv_low, qkv_high)
    qkv_cut = cut_qkv(plan, meta, tie(qkv_low, *rest_pieces[1:]), qkv_joined)
    both = exchange_rows(plan, both[:3] + [tie(piece, *qkv_cut) for piece in both[3:]])
    qkv_pieces = reduce_z(plan, qkv_cut)
    rest_pieces[0] = tie(rest_pieces[0], *qkv_cut)
    out_grad, in_grad, down_grad, mlp_gain_grad = end_rest(plan, rest_pieces)
    output, input_grad = place(plan, meta, [tie(both[0], *qkv_cut)] + both[1:])
    gain_row = norm_gain.astype(F32)[None]
    qkv_grad, norm_gain_grad = end_qkv(plan, tie(gain_row, output, input_grad, in_grad), qkv_pieces)
    mlp_gain_grad = mlp_gain_grad / mlp_gain.astype(F32)
    return (
        output,
        input_grad,
        norm_gain_grad,
        qkv_grad,
        out_grad,
        mlp_gain_grad,
        in_grad,
        down_grad,
    )


def solution(mesh):
    weights = P("blk", "row")
    acts = P("row", "blk", None)

    def run(*args):
        rows = args[0].shape[0] // mesh.shape["row"]
        tok = args[0].shape[1] // mesh.shape["blk"]
        plan = Plan(mesh, rows, tok)
        return jax.shard_map(
            functools.partial(body, plan),
            mesh=mesh,
            in_specs=(acts, P("row", None), P("blk"), weights, weights, P("blk"), weights, weights, acts),
            out_specs=(acts, acts, P("blk"), weights, weights, P("blk"), weights, weights),
            check_vma=False,
        )(*args)

    return run
```
